32 devices in a mesh: pipe: 16 (over z, y, core), tensor: 2 (over x).
Axes of the slice: x: 2, y: 2, z: 4, core: 2. Of those that a mesh axis runs over, the one named last changes fastest.
Arguments:
- query: bfloat16 [4096, 2048], P(('pipe', 'tensor')), may hold values from -20 to 20
- key: bfloat16 [4096, 1024], P(('pipe', 'tensor')), may hold values from -20 to 20
- value: bfloat16 [4096, 1024], P(('pipe', 'tensor')), may hold values from -6 to 6
- grad_out: bfloat16 [4096, 2048], P(('pipe', 'tensor')), may hold values from -6 to 6
- segment_ids: int32 [4096], replicated, may hold values from 0 to 3, never falling along the last dimension, each value on 1 to 2048 neighbouring positions
Outputs:
- attn_out: bfloat16 [4096, 2048], P(('pipe', 'tensor'))
- grad_query: bfloat16 [4096, 2048], P(('pipe', 'tensor'))
- grad_key: bfloat16 [4096, 1024], P(('pipe', 'tensor'))
- grad_value: bfloat16 [4096, 1024], P(('pipe', 'tensor'))
The draws below stay inside these ranges and needn't reach their ends.
Inputs may be any that keep to these rules, and one draw needn't show every extreme that they name: `segment_ids`: segment ids never fall along the tokens; each of the 4 documents holds 1 to 2048 tokens and one holds exactly 2048.
All inputs are finite; a program needn't handle non-finite values.
Results may differ from the reference program's by a relative error of at most 0.029.
Values may be sent and summed in bfloat16 or wider, within the bound.
No kernel may reach another device: no remote copies, remote signals or barrier semaphores. Data moves between devices by JAX's collectives and lax.ppermute only.
A program may use at most 64 MiB of HBM per device.

```python
import math
import jax
import jax.numpy as jnp
import numpy as np
from jax import lax

Q_HEADS = 16
KV_HEADS = 8
HEAD_DIM = 128
WINDOW = 1024
TOK_DEV = 256
TOKENS = 4096
DOCS = 4
DOC_MOST = 2048


def base_rows(key, columns):
    return jnp.clip(jax.random.normal(key, (TOKENS, columns), jnp.float32), -4.0, 4.0)


def draw_query(key, part):
    base = base_rows(jax.random.fold_in(key, 21), Q_HEADS * HEAD_DIM)
    return base.astype(jnp.bfloat16)


def draw_key(key, part):
    base = base_rows(jax.random.fold_in(key, 33), KV_HEADS * HEAD_DIM)
    return base.astype(jnp.bfloat16)


def steps_of(rng, shape, split, smallest, top_value):
    level, own = 1.0, jax.random.fold_in(rng, 6)
    for axis_at, blocks in split:
        heights = jnp.exp(jax.random.uniform(jax.random.fold_in(own, axis_at), (blocks,), jnp.float32, smallest / len(split), top_value / len(split)))
        level = level * jnp.repeat(heights, shape[axis_at] // blocks).reshape([-1 if axis == axis_at else 1 for axis in range(len(shape))])
    return level


def profile(number_of, total, limit, slope):
    loads = [(1 << 20) // math.isqrt(grade ** slope) + 1 for grade in range(2, number_of + 1)]
    surplus, counts = total - limit - (number_of - 1), [1] * (number_of - 1)
    while surplus > 0:
        candidates = [i for i in range(number_of - 1) if counts[i] < limit]
        pool, budget = sum([loads[i] for i in candidates]), surplus
        for i in candidates:
            extra = min(limit - counts[i], max(1, budget * loads[i] // pool), surplus)
            counts[i] = counts[i] + extra
            surplus = surplus - extra
    return np.array([limit] + counts)


def ragged_sizes(rng, amount, total, most, lean):
    if amount == 2:
        one = jax.random.randint(rng, (), max(1, total - most), min(most, total - 1) + 1)
        return jnp.stack([one, total - one])
    lengths = jnp.asarray(profile(amount, total, most, lean), jnp.int32)
    couples = (amount - 1) // 2
    source_of, taker = lengths[1:1 + 2 * couples:2], lengths[2:2 + 2 * couples:2]
    margin = jnp.minimum(source_of - 1, most - taker)
    passed = jax.random.randint(jax.random.fold_in(rng, 1), (couples,), 0, 1 << 20) % (margin + 1)
    lengths = lengths.at[1:1 + 2 * couples:2].set(source_of - passed).at[2:2 + 2 * couples:2].set(taker + passed)
    return lengths[jax.random.permutation(jax.random.fold_in(rng, 2), amount)]


def normal_values(rng, shape, deviation, bound, shards=(), held_as=jnp.bfloat16):
    values = deviation * jax.random.normal(rng, shape, jnp.float32)
    if shards:
        values = values * steps_of(rng, shape, shards, -0.22, 0.18)
    return jnp.clip(values, -bound, bound).astype(held_as)


def setup_inputs(seed: int = 0) -> dict:
    key_list = jax.random.split(jax.random.key(seed), 6)
    return {
        "query": draw_query(jax.random.fold_in(key_list[5], 71), 0),
        "key": draw_key(jax.random.fold_in(key_list[5], 71), 0),
        "value": normal_values(key_list[2], (TOKENS, KV_HEADS * HEAD_DIM), 1.0, 6.0, ((0, 32),)),
        "grad_out": normal_values(key_list[3], (TOKENS, Q_HEADS * HEAD_DIM), 1.0, 6.0, ((0, 32),)),
        "segment_ids": jnp.searchsorted(jnp.cumsum(ragged_sizes(key_list[4], DOCS, TOKENS, DOC_MOST, 2)), jnp.arange(TOKENS), side="right").astype(jnp.int32),
    }


logit_scale = 168.0 ** -0.5


def reference(query, key, value, grad_out, segment_ids):
    span = WINDOW + TOK_DEV
    blocks = TOKENS // TOK_DEV
    group = Q_HEADS // KV_HEADS
    front = jnp.zeros((WINDOW, KV_HEADS * HEAD_DIM), key.dtype)
    key_pad = jnp.concatenate([front, key], axis=0)
    value_pad = jnp.concatenate([front, value], axis=0)
    seg_pad = jnp.concatenate([jnp.full((WINDOW,), -1, jnp.int32), segment_ids.astype(jnp.int32)])
    offsets_q = jnp.arange(TOK_DEV, dtype=jnp.int32)
    offsets_k = jnp.arange(span, dtype=jnp.int32)
    distance = WINDOW + offsets_q[:, None] - offsets_k[None, :]

    def step(carry, index):
        grad_k_pad, grad_v_pad = carry
        start = (index * TOK_DEV).astype(jnp.int32)
        query_block = lax.dynamic_slice_in_dim(query, start, TOK_DEV, 0).reshape(TOK_DEV, KV_HEADS, group, HEAD_DIM).astype(jnp.float32)
        g_blk = lax.dynamic_slice_in_dim(grad_out, start, TOK_DEV, 0).reshape(TOK_DEV, KV_HEADS, group, HEAD_DIM).astype(jnp.float32)
        key_block = lax.dynamic_slice_in_dim(key_pad, start, span, 0).reshape(span, KV_HEADS, HEAD_DIM).astype(jnp.float32)
        value_block = lax.dynamic_slice_in_dim(value_pad, start, span, 0).reshape(span, KV_HEADS, HEAD_DIM).astype(jnp.float32)
        seg_q = lax.dynamic_slice_in_dim(segment_ids.astype(jnp.int32), start, TOK_DEV, 0)
        seg_k = lax.dynamic_slice_in_dim(seg_pad, start, span, 0)
        allowed = (seg_q[:, None] == seg_k[None, :]) & (distance >= 0) & (distance < WINDOW)
        unscaled_scores = jnp.einsum("nobi,koi->obnk", query_block, key_block) * logit_scale
        masked = jnp.where(allowed, unscaled_scores, -jnp.inf)
        top = jnp.max(masked, axis=-1, keepdims=True)
        expo = jnp.where(allowed, jnp.exp(masked - top), 0.0)
        denominator_sum = jnp.sum(expo, axis=-1, keepdims=True)
        attention_weight = lax.optimization_barrier(expo.astype(jnp.bfloat16)).astype(jnp.float32)
        output_rows = jnp.einsum("xypq,qxa->xypa", attention_weight, value_block) / denominator_sum
        out_half = lax.optimization_barrier(output_rows.astype(jnp.bfloat16))
        grouped_output_gradient = jnp.transpose(g_blk, (1, 2, 0, 3))
        grouped_queries = jnp.transpose(query_block, (1, 2, 0, 3))
        delta = jnp.sum(grouped_output_gradient * out_half.astype(jnp.float32), axis=-1, keepdims=True)
        probabilities = expo / denominator_sum
        probability_gradient = jnp.einsum("pmcz,fpz->pmcf", grouped_output_gradient, value_block)
        score_gradient = lax.optimization_barrier((probabilities * (probability_gradient - delta)).astype(jnp.bfloat16)).astype(jnp.float32)
        query_gradient = jnp.einsum("xypq,qxa->xypa", score_gradient, key_block) * logit_scale
        key_gradient_partial = jnp.einsum("ihjm,ihjx->mix", score_gradient, grouped_queries) * logit_scale
        probabilities_bf16 = lax.optimization_barrier(probabilities.astype(jnp.bfloat16)).astype(jnp.float32)
        value_gradient_partial = jnp.einsum("ihjm,ihjx->mix", probabilities_bf16, grouped_output_gradient)
        old_k = lax.dynamic_slice_in_dim(grad_k_pad, start, span, 0)
        old_v = lax.dynamic_slice_in_dim(grad_v_pad, start, span, 0)
        grad_k_pad = lax.dynamic_update_slice_in_dim(grad_k_pad, old_k + key_gradient_partial.reshape(span, KV_HEADS * HEAD_DIM), start, 0)
        grad_v_pad = lax.dynamic_update_slice_in_dim(grad_v_pad, old_v + value_gradient_partial.reshape(span, KV_HEADS * HEAD_DIM), start, 0)
        out_rows = jnp.transpose(out_half, (2, 0, 1, 3)).reshape(TOK_DEV, Q_HEADS * HEAD_DIM)
        grad_q_rows = jnp.transpose(query_gradient, (2, 0, 1, 3)).reshape(TOK_DEV, Q_HEADS * HEAD_DIM).astype(jnp.bfloat16)
        return (grad_k_pad, grad_v_pad), (out_rows, grad_q_rows)

    zeros_pad = jnp.zeros((TOKENS + WINDOW, KV_HEADS * HEAD_DIM), jnp.float32)
    (grad_k_pad, grad_v_pad), (out_all, grad_q_all) = lax.scan(step, (zeros_pad, zeros_pad), jnp.arange(blocks, dtype=jnp.int32))
    attn_out = out_all.reshape(TOKENS, Q_HEADS * HEAD_DIM)
    grad_query = grad_q_all.reshape(TOKENS, Q_HEADS * HEAD_DIM)
    grad_key = grad_k_pad[WINDOW:].astype(jnp.bfloat16)
    grad_value = grad_v_pad[WINDOW:].astype(jnp.bfloat16)
    return (attn_out, grad_query, grad_key, grad_value)
```

```python
import functools

import jax
import jax.numpy as jnp
from jax import lax
from jax.experimental import pallas as pl
from jax.experimental.pallas import tpu as pltpu
from jax.sharding import PartitionSpec as P

HEAD_DIM = 128
WINDOW = 1024
CORES = 2
TILE = 128

logit_scale = 168.0 ** (-0.5)
exp2_scale = logit_scale * 1.4426950408889634

ANY = pl.BlockSpec(memory_space=pl.ANY)
VMEM = pl.BlockSpec(memory_space=pltpu.VMEM)
F32 = jnp.float32
BF16 = jnp.bfloat16


def member():
    return lax.rem(lax.axis_index("pipe"), CORES) * lax.axis_size("tensor") + lax.axis_index(
        "tensor"
    )


def swap(value, mask):
    count = lax.axis_size("pipe") * lax.axis_size("tensor")
    return lax.ppermute(value, ("pipe", "tensor"), [(i, i ^ mask) for i in range(count)])


def shifted(value, groups, size):
    count = lax.axis_size("pipe") * lax.axis_size("tensor")
    step = groups * size
    pairs = [(i, i + step) for i in range(count) if 0 <= i + step < count]
    return lax.ppermute(value, ("pipe", "tensor"), pairs)


def place(index, width):
    return pl.ds(pl.multiple_of(index * width, width), width)


def run_copies(copies, sems):
    started = []
    for at, (source, target) in enumerate(copies):
        copy = pltpu.make_async_copy(source, target, sems.at[at])
        copy.start()
        started.append(copy)
    for copy in started:
        copy.wait()


def pack_body(size, first, widths, *refs):
    arrays, pieces, sems = refs[: len(widths)], refs[len(widths) : -1], refs[-1]
    me = member()
    copies = []
    for at, piece in enumerate(pieces):
        other = lax.bitwise_xor(me, first + at)
        start = 0
        for array, width in zip(arrays, widths):
            copies.append((array.at[:, place(other, width)], piece.at[:, start : start + width]))
            start += width
    run_copies(copies, sems)


def pack(arrays, size, first):
    rows = arrays[0].shape[0]
    widths = [array.shape[1] // size for array in arrays]
    count = size - first
    return pl.pallas_call(
        functools.partial(pack_body, size, first, widths),
        out_shape=[jax.ShapeDtypeStruct((rows, sum(widths)), BF16)] * count,
        in_specs=[ANY] * len(arrays),
        out_specs=[ANY] * count,
        scratch_shapes=[pltpu.SemaphoreType.DMA((count * len(arrays),))],
        name="pack",
    )(*arrays)


def join_body(size, rows, *refs):
    pieces, out, sems = refs[:size], refs[size], refs[size + 1]
    me = member()
    run_copies(
        [(pieces[j], out.at[place(lax.bitwise_xor(me, j), rows), :]) for j in range(size)], sems
    )


def join(pieces):
    size, (rows, cols) = len(pieces), pieces[0].shape
    return pl.pallas_call(
        functools.partial(join_body, size, rows),
        out_shape=jax.ShapeDtypeStruct((size * rows, cols), BF16),
        in_specs=[ANY] * size,
        out_specs=ANY,
        scratch_shapes=[pltpu.SemaphoreType.DMA((size,))],
        name="join",
    )(*pieces)


def combine_body(size, rows, own, one, two, *refs):
    pieces, total, sems = refs[:size], refs[size], refs[size + 1]
    total[...] = (own[...] + one[...].astype(F32) + two[...].astype(F32)).astype(BF16)
    me = member()
    run_copies(
        [(total.at[place(lax.bitwise_xor(me, j), rows), :], pieces[j]) for j in range(size)], sems
    )


def combine(own, one, two, size):
    tok, cols = own.shape
    rows = tok // size
    return pl.pallas_call(
        functools.partial(combine_body, size, rows),
        out_shape=[jax.ShapeDtypeStruct((rows, cols), BF16)] * size,
        in_specs=[VMEM] * 3,
        out_specs=[ANY] * size,
        scratch_shapes=[pltpu.VMEM((tok, cols), BF16), pltpu.SemaphoreType.DMA((size,))],
        name="combine",
    )(own, one, two)


def spread_body(size, widths, *refs):
    pieces, outs, sems = refs[:size], refs[size:-1], refs[-1]
    me = member()
    copies = []
    for j in range(size):
        other = lax.bitwise_xor(me, j)
        start = 0
        for out, width in zip(outs, widths):
            copies.append((pieces[j].at[:, start : start + width], out.at[:, place(other, width)]))
            start += width
    run_copies(copies, sems)


def spread(pieces, widths):
    size, rows = len(pieces), pieces[0].shape[0]
    return pl.pallas_call(
        functools.partial(spread_body, size, widths),
        out_shape=[jax.ShapeDtypeStruct((rows, width * size), BF16) for width in widths],
        in_specs=[ANY] * size,
        out_specs=[ANY] * len(widths),
        scratch_shapes=[pltpu.SemaphoreType.DMA((size * len(widths),))],
        name="spread",
    )(*pieces)


def dot(a, b):
    return lax.dot_general(a, b, (((1,), (0,)), ((), ())), preferred_element_type=F32)


def dot_t(a, b):
    return lax.dot_general(a, b, (((1,), (1,)), ((), ())), preferred_element_type=F32)


def fold(x, op):
    parts = [x[at : at + 8] for at in range(0, x.shape[0], 8)]
    while len(parts) > 1:
        parts = [op(*parts[at : at + 2]) if at + 1 < len(parts) else parts[at] for at in range(0, len(parts), 2)]
    return parts[0]


def attend_body(size, kv_heads, group, rows, *refs):
    refs = list(refs)
    low, q_own, g_own = refs[:3]
    received = refs[3 : 2 + size]
    kv0, kv1, kv2 = refs[2 + size : 5 + size]
    og = refs[5 + size : 5 + 2 * size]
    dkv0, dkv1, dkv2 = refs[5 + 2 * size : 8 + 2 * size]
    qs, gs, ks, vs, kt, vt, os, dqs, dk, dv, s_scr, e_scr, ds_scr, half1, half2, sems = refs[
        8 + 2 * size :
    ]
    tok = size * rows
    kw = kv_heads * HEAD_DIM
    qw = group * kw
    span = WINDOW + TILE
    me = member()
    copies = [
        (q_own.at[:, place(me, qw)], qs.at[place(me, rows), :]),
        (g_own.at[:, place(me, qw)], gs.at[place(me, rows), :]),
    ]
    for j in range(1, size):
        to = place(lax.bitwise_xor(me, j), rows)
        copies.append((received[j - 1].at[:, :qw], qs.at[to, :]))
        copies.append((received[j - 1].at[:, qw:], gs.at[to, :]))
    for at, kv in enumerate((kv2, kv1, kv0)):
        copies.append((kv.at[:, :kw], ks.at[at * tok : (at + 1) * tok, :]))
        copies.append((kv.at[:, kw:], vs.at[at * tok : (at + 1) * tok, :]))
    run_copies(copies, sems)

    dk[...] = jnp.zeros_like(dk)
    dv[...] = jnp.zeros_like(dv)
    lane = lax.broadcasted_iota(jnp.int32, (TILE, HEAD_DIM), 1)
    ones = jnp.where(lane < 2, 1.0, 0.0).astype(BF16)
    wide_lane = lax.broadcasted_iota(jnp.int32, (group * TILE, HEAD_DIM), 1)
    row_of = lax.broadcasted_iota(jnp.int32, (TILE, group * TILE), 0)
    col_of = lax.broadcasted_iota(jnp.int32, (TILE, TILE), 1)
    causal = lax.broadcasted_iota(jnp.int32, (TILE, TILE), 0) <= col_of
    causal = jnp.concatenate([causal] * group, axis=1)

    for head in range(kv_heads):
        cols = slice(head * HEAD_DIM, (head + 1) * HEAD_DIM)
        kt[...] = ks[:, cols].T
        vt[...] = vs[:, cols].T
        q_cols = [
            slice((head * group + at) * HEAD_DIM, (head * group + at + 1) * HEAD_DIM)
            for at in range(group)
        ]
        for tile in range(tok // TILE):
            base = tile * TILE
            here = slice(base, base + TILE)
            q2 = jnp.concatenate([qs[here, c] for c in q_cols], axis=0)
            g2 = jnp.concatenate([gs[here, c] for c in q_cols], axis=0)
            low_row = jnp.concatenate([low[:, here]] * group, axis=1) - base
            top = None
            for at in range(0, span, TILE):
                s = dot_t(ks[base + at : base + at + TILE, cols], q2)
                keep = row_of >= low_row - at
                if at == span - TILE:
                    keep = keep & causal
                s = jnp.where(keep, s, -1e30)
                s_scr[at : at + TILE, :] = s
                part = fold(s, jnp.maximum)
                top = part if top is None else jnp.maximum(top, part)
            top = jnp.max(top, axis=0, keepdims=True) * exp2_scale
            total = None
            for at in range(0, span, TILE):
                e = jnp.exp2(s_scr[at : at + TILE, :] * exp2_scale - top)
                e_scr[at : at + TILE, :] = e.astype(BF16)
                part = fold(e, jnp.add)
                total = part if total is None else total + part
            inv = 1.0 / jnp.sum(total, axis=0, keepdims=True)
            inv = jnp.broadcast_to(inv, (HEAD_DIM, group * TILE)).T
            out = dot(vt[:, base : base + span], e_scr[...]).T * inv
            out = out.astype(BF16)
            g2 = (g2.astype(F32) * inv).astype(BF16)
            delta = jnp.sum(g2.astype(F32) * out.astype(F32), axis=1, keepdims=True)
            high = delta.astype(BF16).astype(F32)
            extra = jnp.where(wide_lane == 0, -high, jnp.where(wide_lane == 1, high - delta, 0.0))
            g_wide = jnp.concatenate([g2, extra.astype(BF16)], axis=1)
            for at in range(0, span, TILE):
                there = slice(base + at, base + at + TILE)
                dp = dot_t(jnp.concatenate([vs[there, cols], ones], axis=1), g_wide)
                e = e_scr[at : at + TILE, :]
                ds = (e.astype(F32) * dp).astype(BF16)
                ds_scr[at : at + TILE, :] = ds
                dv[there, cols] += dot(e, g2)
                dk[there, cols] += dot(ds, q2)
            dq = (dot(kt[:, base : base + span], ds_scr[...]) * logit_scale).T.astype(BF16)
            for at, c in enumerate(q_cols):
                os[here, c] = out[at * TILE : (at + 1) * TILE]
                dqs[here, c] = dq[at * TILE : (at + 1) * TILE]

    dkv0[:, :kw] = dk[2 * tok :, :] * logit_scale
    dkv0[:, kw:] = dv[2 * tok :, :]
    for half, at in ((half1, 1), (half2, 0)):
        half[:, :kw] = (dk[at * tok : (at + 1) * tok, :] * logit_scale).astype(BF16)
        half[:, kw:] = dv[at * tok : (at + 1) * tok, :].astype(BF16)
    copies = [(half1, dkv1), (half2, dkv2)]
    for j in range(size):
        of = place(lax.bitwise_xor(me, j), rows)
        copies.append((os.at[of, :], og[j].at[:, :qw]))
        copies.append((dqs.at[of, :], og[j].at[:, qw:]))
    run_copies(copies, sems)


def attend(low, query, grad_out, received, kv0, kv1, kv2, size):
    rows = query.shape[0]
    tok = size * rows
    qw = query.shape[1] // size
    kw = kv0.shape[1] // 2
    kv_heads, group = kw // HEAD_DIM, qw // kw
    span = WINDOW + TILE
    wide = group * TILE
    half = jax.ShapeDtypeStruct((tok, 2 * kw), BF16)
    n_copies = max(2 * size + 6, 2 * size + 2)
    flops = 6 * 2 * tok * group * kv_heads * span * HEAD_DIM
    results = pl.pallas_call(
        functools.partial(attend_body, size, kv_heads, group, rows),
        out_shape=[jax.ShapeDtypeStruct((rows, 2 * qw), BF16)] * size
        + [jax.ShapeDtypeStruct((tok, 2 * kw), F32), half, half],
        in_specs=[VMEM] + [ANY] * (size + 4),
        out_specs=[ANY] * size + [VMEM, ANY, ANY],
        scratch_shapes=[
            pltpu.VMEM((tok, qw), BF16),
            pltpu.VMEM((tok, qw), BF16),
            pltpu.VMEM((3 * tok, kw), BF16),
            pltpu.VMEM((3 * tok, kw), BF16),
            pltpu.VMEM((HEAD_DIM, 3 * tok), BF16),
            pltpu.VMEM((HEAD_DIM, 3 * tok), BF16),
            pltpu.VMEM((tok, qw), BF16),
            pltpu.VMEM((tok, qw), BF16),
            pltpu.VMEM((3 * tok, kw), F32),
            pltpu.VMEM((3 * tok, kw), F32),
            pltpu.VMEM((span, wide), F32),
            pltpu.VMEM((span, wide), BF16),
            pltpu.VMEM((span, wide), BF16),
            pltpu.VMEM((tok, 2 * kw), BF16),
            pltpu.VMEM((tok, 2 * kw), BF16),
            pltpu.SemaphoreType.DMA((n_copies,)),
        ],
        compiler_params=pltpu.CompilerParams(vmem_limit_bytes=40 * 1024 * 1024),
        cost_estimate=pl.CostEstimate(
            flops=flops, bytes_accessed=8 * 1024 * 1024, transcendentals=flops // 1536
        ),
        name="attend",
    )(low, query, grad_out, *received, kv0, kv1, kv2)
    return results[:size], results[size:]


def lowest_key(segment_ids, tok):
    start = (lax.axis_index("pipe") // CORES) * tok
    padded = jnp.concatenate([jnp.full((WINDOW,), -1, jnp.int32), segment_ids])
    keys = lax.dynamic_slice_in_dim(padded, start, WINDOW + tok, 0)
    queries = lax.dynamic_slice_in_dim(segment_ids, start, tok, 0)
    before = jnp.sum((keys[:, None] < queries[None, :]).astype(jnp.int32), axis=0)
    return jnp.maximum(before, jnp.arange(1, tok + 1, dtype=jnp.int32))[None, :]


def body(query, key, value, grad_out, segment_ids):
    size = CORES * lax.axis_size("tensor")
    rows = query.shape[0]
    tok = size * rows
    assert WINDOW == 2 * tok
    q_width, k_width = query.shape[1] // size, key.shape[1] // size
    low = lowest_key(segment_ids, tok)

    kv_pieces = pack((key, value), size, 0)
    kv_pieces = [kv_pieces[0]] + [swap(kv_pieces[j], j) for j in range(1, size)]
    kv0 = join(kv_pieces)
    qg_pieces = pack((query, grad_out), size, 1)
    kv0, qg_pieces = lax.optimization_barrier((kv0, qg_pieces))
    kv1 = shifted(kv0, 1, size)
    kv2 = shifted(kv0, 2, size)
    qg_pieces = [swap(qg_pieces[j - 1], j) for j in range(1, size)]

    og, (dkv0, dkv1, dkv2) = attend(low, query, grad_out, qg_pieces, kv0, kv1, kv2, size)

    back1 = shifted(dkv1, -1, size)
    back2 = shifted(dkv2, -2, size)
    og = [og[0]] + [swap(og[j], j) for j in range(1, size)]
    grads = combine(dkv0, back1, back2, size)
    grads = [grads[0]] + [swap(grads[j], j) for j in range(1, size)]
    attn_out, grad_query = spread(og, (q_width, q_width))
    grad_key, grad_value = spread(grads, (k_width, k_width))
    return (attn_out, grad_query, grad_key, grad_value)


def solution(mesh):
    placed = P(("pipe", "tensor"), None)
    return jax.shard_map(
        body,
        mesh=mesh,
        in_specs=(placed, placed, placed, placed, P()),
        out_specs=(placed, placed, placed, placed),
        check_vma=False,
    )
```

```python
import functools

import jax
import jax.numpy as jnp
from jax import lax
from jax.experimental import pallas as pl
from jax.experimental.pallas import tpu as pltpu
from jax.sharding import PartitionSpec as P

HEAD_DIM = 128
WINDOW = 1024
CORES = 2
TILE = 128

logit_scale = 168.0 ** (-0.5)
exp2_scale = logit_scale * 1.4426950408889634

SMALL = pltpu.CompilerParams(vmem_limit_bytes=4 * 1024 * 1024)
ANY = pl.BlockSpec(memory_space=pl.ANY)
VMEM = pl.BlockSpec(memory_space=pltpu.VMEM)
F32 = jnp.float32
BF16 = jnp.bfloat16


def member():
    return lax.rem(lax.axis_index("pipe"), CORES) * lax.axis_size("tensor") + lax.axis_index(
        "tensor"
    )


def swap(value, mask):
    count = lax.axis_size("pipe") * lax.axis_size("tensor")
    return lax.ppermute(value, ("pipe", "tensor"), [(i, i ^ mask) for i in range(count)])


def shifted(value, groups, size):
    count = lax.axis_size("pipe") * lax.axis_size("tensor")
    step = groups * size
    pairs = [(i, i + step) for i in range(count) if 0 <= i + step < count]
    return lax.ppermute(value, ("pipe", "tensor"), pairs)


def place(index, width):
    return pl.ds(pl.multiple_of(index * width, width), width)


def run_copies(copies, sems):
    started = []
    for at, (source, target) in enumerate(copies):
        copy = pltpu.make_async_copy(source, target, sems.at[at])
        copy.start()
        started.append(copy)
    for copy in started:
        copy.wait()


def pack_body(size, first, widths, *refs):
    arrays, pieces, sems = refs[: len(widths)], refs[len(widths) : -1], refs[-1]
    me = member()
    copies = []
    for at, piece in enumerate(pieces):
        other = lax.bitwise_xor(me, first + at)
        start = 0
        for array, width in zip(arrays, widths):
            copies.append((array.at[:, place(other, width)], piece.at[:, start : start + width]))
            start += width
    run_copies(copies, sems)


def pack(arrays, size, first):
    rows = arrays[0].shape[0]
    widths = [array.shape[1] // size for array in arrays]
    count = size - first
    return pl.pallas_call(
        functools.partial(pack_body, size, first, widths),
        out_shape=[jax.ShapeDtypeStruct((rows, sum(widths)), BF16)] * count,
        in_specs=[ANY] * len(arrays),
        out_specs=[ANY] * count,
        scratch_shapes=[pltpu.SemaphoreType.DMA((count * len(arrays),))],
        compiler_params=SMALL,
        name="pack",
    )(*arrays)


def join_body(size, rows, *refs):
    pieces, out, sems = refs[:size], refs[size], refs[size + 1]
    me = member()
    run_copies(
        [(pieces[j], out.at[place(lax.bitwise_xor(me, j), rows), :]) for j in range(size)], sems
    )


def join(pieces):
    size, (rows, cols) = len(pieces), pieces[0].shape
    return pl.pallas_call(
        functools.partial(join_body, size, rows),
        out_shape=jax.ShapeDtypeStruct((size * rows, cols), BF16),
        in_specs=[ANY] * size,
        out_specs=ANY,
        scratch_shapes=[pltpu.SemaphoreType.DMA((size,))],
        compiler_params=SMALL,
        name="join",
    )(*pieces)


def combine_body(size, rows, own, one, two, *refs):
    pieces, total, sems = refs[:size], refs[size], refs[size + 1]
    total[...] = (own[...] + one[...].astype(F32) + two[...].astype(F32)).astype(BF16)
    me = member()
    run_copies(
        [(total.at[place(lax.bitwise_xor(me, j), rows), :], pieces[j]) for j in range(size)], sems
    )


def combine(own, one, two, size):
    tok, cols = own.shape
    rows = tok // size
    return pl.pallas_call(
        functools.partial(combine_body, size, rows),
        out_shape=[jax.ShapeDtypeStruct((rows, cols), BF16)] * size,
        in_specs=[VMEM] * 3,
        out_specs=[ANY] * size,
        scratch_shapes=[pltpu.VMEM((tok, cols), BF16), pltpu.SemaphoreType.DMA((size,))],
        compiler_params=SMALL,
        name="combine",
    )(own, one, two)


def spread_body(size, widths, *refs):
    pieces, outs, sems = refs[:size], refs[size:-1], refs[-1]
    me = member()
    copies = []
    for j in range(size):
        other = lax.bitwise_xor(me, j)
        start = 0
        for out, width in zip(outs, widths):
            copies.append((pieces[j].at[:, start : start + width], out.at[:, place(other, width)]))
            start += width
    run_copies(copies, sems)


def spread(pieces, widths):
    size, rows = len(pieces), pieces[0].shape[0]
    return pl.pallas_call(
        functools.partial(spread_body, size, widths),
        out_shape=[jax.ShapeDtypeStruct((rows, width * size), BF16) for width in widths],
        in_specs=[ANY] * size,
        out_specs=[ANY] * len(widths),
        scratch_shapes=[pltpu.SemaphoreType.DMA((size * len(widths),))],
        compiler_params=SMALL,
        name="spread",
    )(*pieces)


def dot(a, b):
    return lax.dot_general(a, b, (((1,), (0,)), ((), ())), preferred_element_type=F32)


def dot_t(a, b):
    return lax.dot_general(a, b, (((1,), (1,)), ((), ())), preferred_element_type=F32)


def fold(x, op):
    parts = [x[at : at + 8] for at in range(0, x.shape[0], 8)]
    while len(parts) > 1:
        parts = [op(*parts[at : at + 2]) if at + 1 < len(parts) else parts[at] for at in range(0, len(parts), 2)]
    return parts[0]


def attend_body(size, kv_heads, group, rows, *refs):
    refs = list(refs)
    low, q_own, g_own = refs[:3]
    received = refs[3 : 2 + size]
    kv0, kv1, kv2 = refs[2 + size : 5 + size]
    og = refs[5 + size : 5 + 2 * size]
    dkv0, dkv1, dkv2 = refs[5 + 2 * size : 8 + 2 * size]
    qs, gs, ks, vs, kt, vt, os, dqs, dk, dv, s_scr, e_scr, ds_scr, half1, half2, sems = refs[
        8 + 2 * size :
    ]
    tok = size * rows
    kw = kv_heads * HEAD_DIM
    qw = group * kw
    span = WINDOW + TILE
    me = member()
    copies = [
        (q_own.at[:, place(me, qw)], qs.at[place(me, rows), :]),
        (g_own.at[:, place(me, qw)], gs.at[place(me, rows), :]),
    ]
    for j in range(1, size):
        to = place(lax.bitwise_xor(me, j), rows)
        copies.append((received[j - 1].at[:, :qw], qs.at[to, :]))
        copies.append((received[j - 1].at[:, qw:], gs.at[to, :]))
    for at, kv in enumerate((kv2, kv1, kv0)):
        copies.append((kv.at[:, :kw], ks.at[at * tok : (at + 1) * tok, :]))
        copies.append((kv.at[:, kw:], vs.at[at * tok : (at + 1) * tok, :]))
    run_copies(copies, sems)

    dk[...] = jnp.zeros_like(dk)
    dv[...] = jnp.zeros_like(dv)
    lane = lax.broadcasted_iota(jnp.int32, (TILE, HEAD_DIM), 1)
    ones = jnp.where(lane < 2, 1.0, 0.0).astype(BF16)
    wide_lane = lax.broadcasted_iota(jnp.int32, (group * TILE, HEAD_DIM), 1)
    row_of = lax.broadcasted_iota(jnp.int32, (TILE, group * TILE), 0)
    col_of = lax.broadcasted_iota(jnp.int32, (TILE, TILE), 1)
    causal = lax.broadcasted_iota(jnp.int32, (TILE, TILE), 0) <= col_of
    causal = jnp.concatenate([causal] * group, axis=1)

    for head in range(kv_heads):
        cols = slice(head * HEAD_DIM, (head + 1) * HEAD_DIM)
        kt[...] = ks[:, cols].T
        vt[...] = vs[:, cols].T
        q_cols = [
            slice((head * group + at) * HEAD_DIM, (head * group + at + 1) * HEAD_DIM)
            for at in range(group)
        ]
        for tile in range(tok // TILE):
            base = tile * TILE
            here = slice(base, base + TILE)
            q2 = jnp.concatenate([qs[here, c] for c in q_cols], axis=0)
            g2 = jnp.concatenate([gs[here, c] for c in q_cols], axis=0)
            low_row = jnp.concatenate([low[:, here]] * group, axis=1) - base
            top = None
            for at in range(0, span, TILE):
                s = dot_t(ks[base + at : base + at + TILE, cols], q2)
                keep = row_of >= low_row - at
                if at == span - TILE:
                    keep = keep & causal
                s = jnp.where(keep, s, -1e30)
                s_scr[at : at + TILE, :] = s
                part = fold(s, jnp.maximum)
                top = part if top is None else jnp.maximum(top, part)
            top = jnp.max(top, axis=0, keepdims=True) * exp2_scale
            total = None
            for at in range(0, span, TILE):
                e = jnp.exp2(s_scr[at : at + TILE, :] * exp2_scale - top)
                e_scr[at : at + TILE, :] = e.astype(BF16)
                part = fold(e, jnp.add)
                total = part if total is None else total + part
            inv = 1.0 / jnp.sum(total, axis=0, keepdims=True)
            inv = jnp.broadcast_to(inv, (HEAD_DIM, group * TILE)).T
            out = dot(vt[:, base : base + span], e_scr[...]).T * inv
            out = out.astype(BF16)
            g2 = (g2.astype(F32) * inv).astype(BF16)
            delta = jnp.sum(g2.astype(F32) * out.astype(F32), axis=1, keepdims=True)
            high = delta.astype(BF16).astype(F32)
            extra = jnp.where(wide_lane == 0, -high, jnp.where(wide_lane == 1, high - delta, 0.0))
            g_wide = jnp.concatenate([g2, extra.astype(BF16)], axis=1)
            for at in range(0, span, TILE):
                there = slice(base + at, base + at + TILE)
                dp = dot_t(jnp.concatenate([vs[there, cols], ones], axis=1), g_wide)
                e = e_scr[at : at + TILE, :]
                ds = (e.astype(F32) * dp).astype(BF16)
                ds_scr[at : at + TILE, :] = ds
                dv[there, cols] += dot(e, g2)
                dk[there, cols] += dot(ds, q2)
            dq = (dot(kt[:, base : base + span], ds_scr[...]) * logit_scale).T.astype(BF16)
            for at, c in enumerate(q_cols):
                os[here, c] = out[at * TILE : (at + 1) * TILE]
                dqs[here, c] = dq[at * TILE : (at + 1) * TILE]

    dkv0[:, :kw] = dk[2 * tok :, :] * logit_scale
    dkv0[:, kw:] = dv[2 * tok :, :]
    for half, at in ((half1, 1), (half2, 0)):
        half[:, :kw] = (dk[at * tok : (at + 1) * tok, :] * logit_scale).astype(BF16)
        half[:, kw:] = dv[at * tok : (at + 1) * tok, :].astype(BF16)
    copies = [(half1, dkv1), (half2, dkv2)]
    for j in range(size):
        of = place(lax.bitwise_xor(me, j), rows)
        copies.append((os.at[of, :], og[j].at[:, :qw]))
        copies.append((dqs.at[of, :], og[j].at[:, qw:]))
    run_copies(copies, sems)


def attend(low, query, grad_out, received, kv0, kv1, kv2, size):
    rows = query.shape[0]
    tok = size * rows
    qw = query.shape[1] // size
    kw = kv0.shape[1] // 2
    kv_heads, group = kw // HEAD_DIM, qw // kw
    span = WINDOW + TILE
    wide = group * TILE
    half = jax.ShapeDtypeStruct((tok, 2 * kw), BF16)
    n_copies = max(2 * size + 6, 2 * size + 2)
    flops = 6 * 2 * tok * group * kv_heads * span * HEAD_DIM
    results = pl.pallas_call(
        functools.partial(attend_body, size, kv_heads, group, rows),
        out_shape=[jax.ShapeDtypeStruct((rows, 2 * qw), BF16)] * size
        + [jax.ShapeDtypeStruct((tok, 2 * kw), F32), half, half],
        in_specs=[VMEM] + [ANY] * (size + 4),
        out_specs=[ANY] * size + [VMEM, ANY, ANY],
        scratch_shapes=[
            pltpu.VMEM((tok, qw), BF16),
            pltpu.VMEM((tok, qw), BF16),
            pltpu.VMEM((3 * tok, kw), BF16),
            pltpu.VMEM((3 * tok, kw), BF16),
            pltpu.VMEM((HEAD_DIM, 3 * tok), BF16),
            pltpu.VMEM((HEAD_DIM, 3 * tok), BF16),
            pltpu.VMEM((tok, qw), BF16),
            pltpu.VMEM((tok, qw), BF16),
            pltpu.VMEM((3 * tok, kw), F32),
            pltpu.VMEM((3 * tok, kw), F32),
            pltpu.VMEM((span, wide), F32),
            pltpu.VMEM((span, wide), BF16),
            pltpu.VMEM((span, wide), BF16),
            pltpu.VMEM((tok, 2 * kw), BF16),
            pltpu.VMEM((tok, 2 * kw), BF16),
            pltpu.SemaphoreType.DMA((n_copies,)),
        ],
        compiler_params=pltpu.CompilerParams(vmem_limit_bytes=40 * 1024 * 1024),
        cost_estimate=pl.CostEstimate(
            flops=flops, bytes_accessed=8 * 1024 * 1024, transcendentals=flops // 1536
        ),
        name="attend",
    )(low, query, grad_out, *received, kv0, kv1, kv2)
    return results[:size], results[size:]


def lowest_key(segment_ids, tok):
    start = (lax.axis_index("pipe") // CORES) * tok
    padded = jnp.concatenate([jnp.full((WINDOW,), -1, jnp.int32), segment_ids])
    keys = lax.dynamic_slice_in_dim(padded, start, WINDOW + tok, 0)
    queries = lax.dynamic_slice_in_dim(segment_ids, start, tok, 0)
    before = jnp.sum((keys[:, None] < queries[None, :]).astype(jnp.int32), axis=0)
    return jnp.maximum(before, jnp.arange(1, tok + 1, dtype=jnp.int32))[None, :]


def body(query, key, value, grad_out, segment_ids):
    size = CORES * lax.axis_size("tensor")
    rows = query.shape[0]
    tok = size * rows
    assert WINDOW == 2 * tok
    q_width, k_width = query.shape[1] // size, key.shape[1] // size
    low = lowest_key(segment_ids, tok)

    kv_pieces = pack((key, value), size, 0)
    kv_pieces = [kv_pieces[0]] + [swap(kv_pieces[j], j) for j in range(1, size)]
    kv0 = join(kv_pieces)
    qg_pieces = pack((query, grad_out), size, 1)
    kv0, qg_pieces = lax.optimization_barrier((kv0, qg_pieces))
    kv1 = shifted(kv0, 1, size)
    kv2 = shifted(kv0, 2, size)
    qg_pieces = [swap(qg_pieces[j - 1], j) for j in range(1, size)]

    og, (dkv0, dkv1, dkv2) = attend(low, query, grad_out, qg_pieces, kv0, kv1, kv2, size)

    back1 = shifted(dkv1, -1, size)
    back2 = shifted(dkv2, -2, size)
    og = [og[0]] + [swap(og[j], j) for j in range(1, size)]
    grads = combine(dkv0, back1, back2, size)
    grads = [grads[0]] + [swap(grads[j], j) for j in range(1, size)]
    attn_out, grad_query = spread(og, (q_width, q_width))
    grad_key, grad_value = spread(grads, (k_width, k_width))
    return (attn_out, grad_query, grad_key, grad_value)


def solution(mesh):
    placed = P(("pipe", "tensor"), None)
    return jax.shard_map(
        body,
        mesh=mesh,
        in_specs=(placed, placed, placed, placed, P()),
        out_specs=(placed, placed, placed, placed),
        check_vma=False,
    )
```

```python
import functools

import jax
import jax.numpy as jnp
from jax import lax
from jax.experimental import pallas as pl
from jax.experimental.pallas import tpu as pltpu
from jax.sharding import PartitionSpec as P

HEAD_DIM = 128
WINDOW = 1024
CORES = 2
TILE = 128

logit_scale = 168.0 ** (-0.5)
exp2_scale = logit_scale * 1.4426950408889634

SMALL = pltpu.CompilerParams(vmem_limit_bytes=4 * 1024 * 1024)
ANY = pl.BlockSpec(memory_space=pl.ANY)
VMEM = pl.BlockSpec(memory_space=pltpu.VMEM)
F32 = jnp.float32
BF16 = jnp.bfloat16


def member():
    return lax.rem(lax.axis_index("pipe"), CORES) * lax.axis_size("tensor") + lax.axis_index(
        "tensor"
    )


def swap(value, mask):
    count = lax.axis_size("pipe") * lax.axis_size("tensor")
    return lax.ppermute(value, ("pipe", "tensor"), [(i, i ^ mask) for i in range(count)])


def hop(value, size, back):
    count = lax.axis_size("pipe") * lax.axis_size("tensor")
    step = 2 * size
    results = []
    for odd in (0, 1):
        low = [i for i in range(count - step) if (i // step) % 2 == odd]
        pairs = [(i + step, i) if back else (i, i + step) for i in low]
        results.append(lax.ppermute(value, ("pipe", "tensor"), pairs))
    return results


def after(value, *others):
    return lax.optimization_barrier((value, *others))


def place(index, width):
    return pl.ds(pl.multiple_of(index * width, width), width)


def run_copies(copies, sems):
    started = []
    for at, (source, target) in enumerate(copies):
        copy = pltpu.make_async_copy(source, target, sems.at[at])
        copy.start()
        started.append(copy)
    for copy in started:
        copy.wait()


def pack_body(widths, *refs):
    arrays, pieces, sems = refs[: len(widths)], refs[len(widths) : -1], refs[-1]
    me = member()
    copies = []
    for at, piece in enumerate(pieces):
        other = lax.bitwise_xor(me, at)
        start = 0
        for array, width in zip(arrays, widths):
            copies.append((array.at[:, place(other, width)], piece.at[:, start : start + width]))
            start += width
    run_copies(copies, sems)


def pack(arrays, size):
    rows = arrays[0].shape[0]
    widths = [array.shape[1] // size for array in arrays]
    return pl.pallas_call(
        functools.partial(pack_body, widths),
        out_shape=[jax.ShapeDtypeStruct((rows, sum(widths)), BF16)] * size,
        in_specs=[pl.BlockSpec(memory_space=pltpu.HBM)] * len(arrays),
        out_specs=[ANY] * size,
        scratch_shapes=[pltpu.SemaphoreType.DMA((size * len(arrays),))],
        compiler_params=SMALL,
        name="pack",
    )(*arrays)


def join_body(size, rows, heads, *refs):
    pieces, outs, sems = refs[:size], refs[size:-1], refs[-1]
    me = member()
    copies = []
    for head, out in enumerate(outs):
        for j in range(size):
            to = place(lax.bitwise_xor(me, j), rows)
            for at in range(2):
                start = (at * heads + head) * HEAD_DIM
                copies.append(
                    (
                        pieces[j].at[:, start : start + HEAD_DIM],
                        out.at[to, at * HEAD_DIM : (at + 1) * HEAD_DIM],
                    )
                )
    run_copies(copies, sems)


def join(pieces):
    size, (rows, cols) = len(pieces), pieces[0].shape
    heads = cols // (2 * HEAD_DIM)
    return pl.pallas_call(
        functools.partial(join_body, size, rows, heads),
        out_shape=[jax.ShapeDtypeStruct((size * rows, 2 * HEAD_DIM), BF16)] * heads,
        in_specs=[ANY] * size,
        out_specs=[ANY] * heads,
        scratch_shapes=[pltpu.SemaphoreType.DMA((2 * heads * size,))],
        compiler_params=SMALL,
        name="join",
    )(*pieces)


def combine_body(size, rows, heads, *refs):
    terms, pieces, total, sems = refs[: 3 * heads], refs[3 * heads : -2], refs[-2], refs[-1]
    for head in range(heads):
        own, one, two = terms[3 * head : 3 * head + 3]
        added = (own[...] + one[...].astype(F32) + two[...].astype(F32)).astype(BF16)
        for at in range(2):
            start = (at * heads + head) * HEAD_DIM
            total[:, start : start + HEAD_DIM] = added[:, at * HEAD_DIM : (at + 1) * HEAD_DIM]
    me = member()
    run_copies(
        [(total.at[place(lax.bitwise_xor(me, j), rows), :], pieces[j]) for j in range(size)], sems
    )


def combine(terms, size):
    heads = len(terms) // 3
    tok = terms[0].shape[0]
    rows, cols = tok // size, 2 * heads * HEAD_DIM
    return pl.pallas_call(
        functools.partial(combine_body, size, rows, heads),
        out_shape=[jax.ShapeDtypeStruct((rows, cols), BF16)] * size,
        in_specs=[VMEM] * len(terms),
        out_specs=[ANY] * size,
        scratch_shapes=[pltpu.VMEM((tok, cols), BF16), pltpu.SemaphoreType.DMA((size,))],
        compiler_params=SMALL,
        name="combine",
    )(*terms)


def spread_body(size, chunks, count, *refs):
    pieces, outs, sems = refs[: size * chunks], refs[size * chunks : -1], refs[-1]
    me = member()
    copies = []
    for j in range(size):
        other = lax.bitwise_xor(me, j)
        for chunk in range(chunks):
            piece = pieces[chunk * size + j]
            width = piece.shape[1] // count
            for at, out in enumerate(outs):
                start = pl.multiple_of((other * chunks + chunk) * width, width)
                copies.append(
                    (piece.at[:, at * width : (at + 1) * width], out.at[:, pl.ds(start, width)])
                )
    run_copies(copies, sems)


def spread(chunks, count):
    size, (rows, cols) = len(chunks[0]), chunks[0][0].shape
    pieces = [piece for chunk in chunks for piece in chunk]
    return pl.pallas_call(
        functools.partial(spread_body, size, len(chunks), count),
        out_shape=[jax.ShapeDtypeStruct((rows, cols // count * len(pieces)), BF16)] * count,
        in_specs=[ANY] * len(pieces),
        out_specs=[ANY] * count,
        scratch_shapes=[pltpu.SemaphoreType.DMA((len(pieces) * count,))],
        compiler_params=SMALL,
        name="spread",
    )(*pieces)


def dot(a, b):
    return lax.dot_general(a, b, (((1,), (0,)), ((), ())), preferred_element_type=F32)


def dot_t(a, b):
    return lax.dot_general(a, b, (((1,), (1,)), ((), ())), preferred_element_type=F32)


def fold(x, op):
    parts = [x[at : at + 8] for at in range(0, x.shape[0], 8)]
    while len(parts) > 1:
        parts = [op(*parts[at : at + 2]) if at + 1 < len(parts) else parts[at] for at in range(0, len(parts), 2)]
    return parts[0]


def attend_body(size, head, heads, group, rows, *refs):
    low, pieces = refs[0], refs[1 : 1 + size]
    kv0, kv1, kv2 = refs[1 + size : 4 + size]
    og = refs[4 + size : 4 + 2 * size]
    dkv0, dkv1, dkv2 = refs[4 + 2 * size : 7 + 2 * size]
    qs, gs, ks, vs, kt, vt, os, dqs, dk, dv, s_scr, e_scr, ds_scr, half1, half2, sems = refs[
        7 + 2 * size :
    ]
    tok = size * rows
    width = group * HEAD_DIM
    span = WINDOW + TILE
    me = member()
    copies = []
    for j in range(size):
        to = place(lax.bitwise_xor(me, j), rows)
        for at, target in enumerate((qs, gs)):
            start = (at * heads + head) * width
            copies.append((pieces[j].at[:, start : start + width], target.at[to, :]))
    for at, kv in enumerate((kv2, kv1, kv0)):
        copies.append((kv.at[:, :HEAD_DIM], ks.at[at * tok : (at + 1) * tok, :]))
        copies.append((kv.at[:, HEAD_DIM:], vs.at[at * tok : (at + 1) * tok, :]))
    run_copies(copies, sems)

    dk[...] = jnp.zeros_like(dk)
    dv[...] = jnp.zeros_like(dv)
    lane = lax.broadcasted_iota(jnp.int32, (TILE, HEAD_DIM), 1)
    ones = jnp.where(lane < 2, 1.0, 0.0).astype(BF16)
    wide_lane = lax.broadcasted_iota(jnp.int32, (group * TILE, HEAD_DIM), 1)
    row_of = lax.broadcasted_iota(jnp.int32, (TILE, group * TILE), 0)
    col_of = lax.broadcasted_iota(jnp.int32, (TILE, TILE), 1)
    causal = lax.broadcasted_iota(jnp.int32, (TILE, TILE), 0) <= col_of
    causal = jnp.concatenate([causal] * group, axis=1)

    kt[...] = ks[...].T
    vt[...] = vs[...].T
    q_cols = [slice(at * HEAD_DIM, (at + 1) * HEAD_DIM) for at in range(group)]
    for tile in range(tok // TILE):
        base = tile * TILE
        here = slice(base, base + TILE)
        q2 = jnp.concatenate([qs[here, c] for c in q_cols], axis=0)
        g2 = jnp.concatenate([gs[here, c] for c in q_cols], axis=0)
        low_row = jnp.concatenate([low[:, here]] * group, axis=1) - base
        top = None
        for at in range(0, span, TILE):
            s = dot_t(ks[base + at : base + at + TILE, :], q2)
            keep = row_of >= low_row - at
            if at == span - TILE:
                keep = keep & causal
            s = jnp.where(keep, s, -1e30)
            s_scr[at : at + TILE, :] = s
            part = fold(s, jnp.maximum)
            top = part if top is None else jnp.maximum(top, part)
        top = jnp.max(top, axis=0, keepdims=True) * exp2_scale
        total = None
        for at in range(0, span, TILE):
            e = jnp.exp2(s_scr[at : at + TILE, :] * exp2_scale - top)
            e_scr[at : at + TILE, :] = e.astype(BF16)
            part = fold(e, jnp.add)
            total = part if total is None else total + part
        inv = 1.0 / jnp.sum(total, axis=0, keepdims=True)
        inv = jnp.broadcast_to(inv, (HEAD_DIM, group * TILE)).T
        out = dot(vt[:, base : base + span], e_scr[...]).T * inv
        out = out.astype(BF16)
        g2 = (g2.astype(F32) * inv).astype(BF16)
        delta = jnp.sum(g2.astype(F32) * out.astype(F32), axis=1, keepdims=True)
        high = delta.astype(BF16).astype(F32)
        extra = jnp.where(wide_lane == 0, -high, jnp.where(wide_lane == 1, high - delta, 0.0))
        g_wide = jnp.concatenate([g2, extra.astype(BF16)], axis=1)
        for at in range(0, span, TILE):
            there = slice(base + at, base + at + TILE)
            dp = dot_t(jnp.concatenate([vs[there, :], ones], axis=1), g_wide)
            e = e_scr[at : at + TILE, :]
            ds = (e.astype(F32) * dp).astype(BF16)
            ds_scr[at : at + TILE, :] = ds
            dv[there, :] += dot(e, g2)
            dk[there, :] += dot(ds, q2)
        dq = (dot(kt[:, base : base + span], ds_scr[...]) * logit_scale).T.astype(BF16)
        for at, c in enumerate(q_cols):
            os[here, c] = out[at * TILE : (at + 1) * TILE]
            dqs[here, c] = dq[at * TILE : (at + 1) * TILE]

    dkv0[:, :HEAD_DIM] = dk[2 * tok :, :] * logit_scale
    dkv0[:, HEAD_DIM:] = dv[2 * tok :, :]
    for half, at in ((half1, 1), (half2, 0)):
        half[:, :HEAD_DIM] = (dk[at * tok : (at + 1) * tok, :] * logit_scale).astype(BF16)
        half[:, HEAD_DIM:] = dv[at * tok : (at + 1) * tok, :].astype(BF16)
    copies = [(half1, dkv1), (half2, dkv2)]
    for j in range(size):
        of = place(lax.bitwise_xor(me, j), rows)
        copies.append((os.at[of, :], og[j].at[:, :width]))
        copies.append((dqs.at[of, :], og[j].at[:, width:]))
    run_copies(copies, sems)


def attend(low, pieces, kv0, kv1, kv2, head, heads):
    size, (rows, cols) = len(pieces), pieces[0].shape
    tok = size * rows
    width = cols // (2 * heads)
    group = width // HEAD_DIM
    span = WINDOW + TILE
    wide = group * TILE
    half = jax.ShapeDtypeStruct((tok, 2 * HEAD_DIM), BF16)
    flops = 6 * 2 * tok * group * span * HEAD_DIM
    results = pl.pallas_call(
        functools.partial(attend_body, size, head, heads, group, rows),
        out_shape=[jax.ShapeDtypeStruct((rows, 2 * width), BF16)] * size
        + [jax.ShapeDtypeStruct((tok, 2 * HEAD_DIM), F32), half, half],
        in_specs=[VMEM] + [ANY] * (size + 3),
        out_specs=[ANY] * size + [VMEM, ANY, ANY],
        scratch_shapes=[
            pltpu.VMEM((tok, width), BF16),
            pltpu.VMEM((tok, width), BF16),
            pltpu.VMEM((3 * tok, HEAD_DIM), BF16),
            pltpu.VMEM((3 * tok, HEAD_DIM), BF16),
            pltpu.VMEM((HEAD_DIM, 3 * tok), BF16),
            pltpu.VMEM((HEAD_DIM, 3 * tok), BF16),
            pltpu.VMEM((tok, width), BF16),
            pltpu.VMEM((tok, width), BF16),
            pltpu.VMEM((3 * tok, HEAD_DIM), F32),
            pltpu.VMEM((3 * tok, HEAD_DIM), F32),
            pltpu.VMEM((span, wide), F32),
            pltpu.VMEM((span, wide), BF16),
            pltpu.VMEM((span, wide), BF16),
            pltpu.VMEM((tok, 2 * HEAD_DIM), BF16),
            pltpu.VMEM((tok, 2 * HEAD_DIM), BF16),
            pltpu.SemaphoreType.DMA((2 * size + 6,)),
        ],
        compiler_params=pltpu.CompilerParams(vmem_limit_bytes=32 * 1024 * 1024),
        cost_estimate=pl.CostEstimate(
            flops=flops, bytes_accessed=8 * 1024 * 1024, transcendentals=flops // 1536
        ),
        name="attend",
    )(low, *pieces, kv0, kv1, kv2)
    return results[:size], results[size:]


def lowest_key(segment_ids, tok):
    start = (lax.axis_index("pipe") // CORES) * tok
    padded = jnp.concatenate([jnp.full((WINDOW,), -1, jnp.int32), segment_ids])
    keys = lax.dynamic_slice_in_dim(padded, start, WINDOW + tok, 0)
    queries = lax.dynamic_slice_in_dim(segment_ids, start, tok, 0)
    before = jnp.sum((keys[:, None] < queries[None, :]).astype(jnp.int32), axis=0)
    return jnp.maximum(before, jnp.arange(1, tok + 1, dtype=jnp.int32))[None, :]


def body(query, key, value, grad_out, segment_ids):
    size = CORES * lax.axis_size("tensor")
    rows = query.shape[0]
    tok = size * rows
    assert WINDOW == 2 * tok
    heads = key.shape[1] // (size * HEAD_DIM)
    low = lowest_key(segment_ids, tok)
    group_at = lax.axis_index("pipe") // CORES
    odd = group_at % 2 == 1
    odd_pair = (group_at // 2) % 2 == 1

    kv = pack((key, value), size)
    kv = [kv[0]] + [swap(kv[j], j) for j in range(1, size)]
    kv0 = list(join(kv))
    qg = pack((query, grad_out), size)
    kv1, kv2 = [None] * heads, [None] * heads
    for head in range(heads):
        if head:
            kv0[head], kv2[head - 1] = after(kv0[head], kv2[head - 1])
        hops = hop(kv0[head], size, False)
        if head == 0:
            kv0[0], *qg = after(kv0[0], *qg)
            qg = [qg[0]] + [swap(qg[j], j) for j in range(1, size)]
        kv2[head] = jnp.where(odd_pair, hops[0], hops[1])
        kv1[head] = swap(jnp.where(odd, kv2[head], kv0[head]), size)

    og, dkv0, sent, backs, turns = [], [], [], [], []
    for head in range(heads):
        og_head, (dkv0_head, dkv1_head, dkv2_head) = attend(
            low, qg, kv0[head], kv1[head], kv2[head], head, heads
        )
        turns.append((dkv0_head, swap(dkv1_head, size), dkv2_head))
        og.append([og_head[0]] + [swap(og_head[j], j) for j in range(1, size)])
    terms = []
    for dkv0_head, turned, dkv2_head in turns:
        turned = turned.astype(F32)
        own = dkv0_head + jnp.where(odd, 0.0, turned)
        give = (dkv2_head.astype(F32) + jnp.where(odd, turned, 0.0)).astype(BF16)
        terms += [own] + hop(give, size, True)
    grads = combine(terms, size)
    grads = [grads[0]] + [swap(grads[j], j) for j in range(1, size)]
    attn_out, grad_query = spread(og, 2)
    grad_key, grad_value = spread([grads], 2)
    return (attn_out, grad_query, grad_key, grad_value)


def solution(mesh):
    placed = P(("pipe", "tensor"), None)
    return jax.shard_map(
        body,
        mesh=mesh,
        in_specs=(placed, placed, placed, placed, P()),
        out_specs=(placed, placed, placed, placed),
        check_vma=False,
    )
```

```python
import functools

import jax
import jax.numpy as jnp
from jax import lax
from jax.experimental import pallas as pl
from jax.experimental.pallas import tpu as pltpu
from jax.sharding import PartitionSpec as P

HEAD_DIM = 128
WINDOW = 1024
TILE = 128

logit_scale = 168.0 ** (-0.5)
exp2_scale = logit_scale * 1.4426950408889634

SMALL = pltpu.CompilerParams(vmem_limit_bytes=4 * 1024 * 1024)
ANY = pl.BlockSpec(memory_space=pl.ANY)
VMEM = pl.BlockSpec(memory_space=pltpu.VMEM)
F32 = jnp.float32
BF16 = jnp.bfloat16
BOTH = ("pipe", "tensor")


def flat_index():
    return lax.axis_index("pipe") * lax.axis_size("tensor") + lax.axis_index("tensor")


def device_count():
    return lax.axis_size("pipe") * lax.axis_size("tensor")


def exchange(value):
    size = value.shape[0]
    groups = [[at + i for i in range(size)] for at in range(0, device_count(), size)]
    return lax.all_to_all(
        value, BOTH, split_axis=0, concat_axis=0, axis_index_groups=groups, tiled=True
    )


def shifted(value, step):
    count = device_count()
    pairs = [(i, i + step) for i in range(count) if 0 <= i + step < count]
    return lax.ppermute(value, BOTH, pairs)


def after(value, *others):
    return lax.optimization_barrier((value, *others))


def run_copies(copies, sems):
    started = []
    for at, (source, target) in enumerate(copies):
        copy = pltpu.make_async_copy(source, target, sems.at[at])
        copy.start()
        started.append(copy)
    for copy in started:
        copy.wait()


def pack_body(size, widths, *refs):
    arrays, out, sems = refs[: len(widths)], refs[-2], refs[-1]
    copies = []
    for j in range(size):
        start = 0
        for array, width in zip(arrays, widths):
            copies.append(
                (
                    array.at[:, j * width : (j + 1) * width],
                    out.at[j, :, start : start + width],
                )
            )
            start += width
    run_copies(copies, sems)


def pack(arrays, size):
    rows = arrays[0].shape[0]
    widths = [array.shape[1] // size for array in arrays]
    return pl.pallas_call(
        functools.partial(pack_body, size, widths),
        out_shape=jax.ShapeDtypeStruct((size, rows, sum(widths)), BF16),
        in_specs=[ANY] * len(arrays),
        out_specs=ANY,
        scratch_shapes=[pltpu.SemaphoreType.DMA((size * len(arrays),))],
        compiler_params=SMALL,
        name="pack",
    )(*arrays)


def spread_body(size, width, shares, *refs):
    outs, sems = refs[:-1], refs[-1]
    copies = []
    for j in range(size):
        for at, out in enumerate(outs):
            copies.append(
                (
                    shares.at[j, :, at * width : (at + 1) * width],
                    out.at[:, j * width : (j + 1) * width],
                )
            )
    run_copies(copies, sems)


def spread(shares, count):
    size, rows, cols = shares.shape
    width = cols // count
    return pl.pallas_call(
        functools.partial(spread_body, size, width),
        out_shape=[jax.ShapeDtypeStruct((rows, width * size), BF16)] * count,
        in_specs=[ANY],
        out_specs=[ANY] * count,
        scratch_shapes=[pltpu.SemaphoreType.DMA((size * count,))],
        compiler_params=SMALL,
        name="spread",
    )(shares)


def dot(a, b):
    return lax.dot_general(a, b, (((1,), (0,)), ((), ())), preferred_element_type=F32)


def dot_t(a, b):
    return lax.dot_general(a, b, (((1,), (1,)), ((), ())), preferred_element_type=F32)


def fold(x, op):
    parts = [x[at : at + 8] for at in range(0, x.shape[0], 8)]
    while len(parts) > 1:
        parts = [
            op(*parts[at : at + 2]) if at + 1 < len(parts) else parts[at]
            for at in range(0, len(parts), 2)
        ]
    return parts[0]


def attend_body(reach, tok, group, *refs):
    low, qg, kvs = refs[0], refs[1], refs[2 : 3 + reach]
    og, dkv0, sent = refs[3 + reach], refs[4 + reach], refs[5 + reach : 5 + 2 * reach]
    kt, vt, dk, dv, s_scr, e_scr, ds_scr = refs[5 + 2 * reach :]
    width = group * HEAD_DIM
    span = WINDOW + TILE
    dk[...] = jnp.zeros_like(dk)
    dv[...] = jnp.zeros_like(dv)
    lane = lax.broadcasted_iota(jnp.int32, (TILE, HEAD_DIM), 1)
    ones = jnp.where(lane < 2, 1.0, 0.0).astype(BF16)
    wide_lane = lax.broadcasted_iota(jnp.int32, (group * TILE, HEAD_DIM), 1)
    row_of = lax.broadcasted_iota(jnp.int32, (TILE, group * TILE), 0)
    col_of = lax.broadcasted_iota(jnp.int32, (TILE, TILE), 1)
    causal = lax.broadcasted_iota(jnp.int32, (TILE, TILE), 0) <= col_of
    causal = jnp.concatenate([causal] * group, axis=1)

    def rows(start, first):
        lag = reach - start // tok
        at = start % tok
        return kvs[lag][at : at + TILE, first * HEAD_DIM : (first + 1) * HEAD_DIM]

    for lag in range(reach + 1):
        there = slice((reach - lag) * tok, (reach - lag + 1) * tok)
        kt[:, there] = kvs[lag][:, :HEAD_DIM].T
        vt[:, there] = kvs[lag][:, HEAD_DIM:].T
    for tile in range(tok // TILE):
        base = tile * TILE
        here = slice(base, base + TILE)
        q2 = jnp.concatenate(
            [qg[here, at * HEAD_DIM : (at + 1) * HEAD_DIM] for at in range(group)], axis=0
        )
        g2 = jnp.concatenate(
            [qg[here, width + at * HEAD_DIM : width + (at + 1) * HEAD_DIM] for at in range(group)],
            axis=0,
        )
        low_row = jnp.concatenate([low[:, here]] * group, axis=1) - base
        top = None
        for at in range(0, span, TILE):
            s = dot_t(rows(base + at, 0), q2)
            keep = row_of >= low_row - at
            if at == span - TILE:
                keep = keep & causal
            s = jnp.where(keep, s, -1e30)
            s_scr[at : at + TILE, :] = s
            part = fold(s, jnp.maximum)
            top = part if top is None else jnp.maximum(top, part)
        top = jnp.max(top, axis=0, keepdims=True) * exp2_scale
        total = None
        for at in range(0, span, TILE):
            e = jnp.exp2(s_scr[at : at + TILE, :] * exp2_scale - top)
            e_scr[at : at + TILE, :] = e.astype(BF16)
            part = fold(e, jnp.add)
            total = part if total is None else total + part
        inv = 1.0 / jnp.sum(total, axis=0, keepdims=True)
        inv = jnp.broadcast_to(inv, (HEAD_DIM, group * TILE)).T
        out = dot(vt[:, base : base + span], e_scr[...]).T * inv
        out = out.astype(BF16)
        g2 = (g2.astype(F32) * inv).astype(BF16)
        delta = jnp.sum(g2.astype(F32) * out.astype(F32), axis=1, keepdims=True)
        high = delta.astype(BF16).astype(F32)
        extra = jnp.where(wide_lane == 0, -high, jnp.where(wide_lane == 1, high - delta, 0.0))
        g_wide = jnp.concatenate([g2, extra.astype(BF16)], axis=1)
        for at in range(0, span, TILE):
            there = slice(base + at, base + at + TILE)
            dp = dot_t(jnp.concatenate([rows(base + at, 1), ones], axis=1), g_wide)
            e = e_scr[at : at + TILE, :]
            ds = (e.astype(F32) * dp).astype(BF16)
            ds_scr[at : at + TILE, :] = ds
            dv[there, :] += dot(e, g2)
            dk[there, :] += dot(ds, q2)
        dq = (dot(kt[:, base : base + span], ds_scr[...]) * logit_scale).T.astype(BF16)
        for at in range(group):
            part = slice(at * TILE, (at + 1) * TILE)
            og[here, at * HEAD_DIM : (at + 1) * HEAD_DIM] = out[part]
            og[here, width + at * HEAD_DIM : width + (at + 1) * HEAD_DIM] = dq[part]

    dkv0[:, :HEAD_DIM] = dk[reach * tok :, :] * logit_scale
    dkv0[:, HEAD_DIM:] = dv[reach * tok :, :]
    for lag in range(1, reach + 1):
        there = slice((reach - lag) * tok, (reach - lag + 1) * tok)
        sent[lag - 1][:, :HEAD_DIM] = (dk[there, :] * logit_scale).astype(BF16)
        sent[lag - 1][:, HEAD_DIM:] = dv[there, :].astype(BF16)


def attend(low, qg, kvs):
    tok, cols = qg.shape
    width = cols // 2
    group = width // HEAD_DIM
    reach = len(kvs) - 1
    span = WINDOW + TILE
    wide = group * TILE
    keys = (reach + 1) * tok
    half = jax.ShapeDtypeStruct((tok, 2 * HEAD_DIM), BF16)
    flops = 6 * 2 * tok * group * span * HEAD_DIM
    og, dkv0, *sent = pl.pallas_call(
        functools.partial(attend_body, reach, tok, group),
        out_shape=[
            jax.ShapeDtypeStruct((tok, cols), BF16),
            jax.ShapeDtypeStruct((tok, 2 * HEAD_DIM), F32),
        ]
        + [half] * reach,
        in_specs=[VMEM] * (3 + reach),
        out_specs=[VMEM] * (2 + reach),
        scratch_shapes=[
            pltpu.VMEM((HEAD_DIM, keys), BF16),
            pltpu.VMEM((HEAD_DIM, keys), BF16),
            pltpu.VMEM((keys, HEAD_DIM), F32),
            pltpu.VMEM((keys, HEAD_DIM), F32),
            pltpu.VMEM((span, wide), F32),
            pltpu.VMEM((span, wide), BF16),
            pltpu.VMEM((span, wide), BF16),
        ],
        compiler_params=pltpu.CompilerParams(vmem_limit_bytes=32 * 1024 * 1024),
        cost_estimate=pl.CostEstimate(
            flops=flops, bytes_accessed=8 * 1024 * 1024, transcendentals=flops // 1536
        ),
        name="attend",
    )(low, qg, *kvs)
    return og, dkv0, sent


def lowest_key(segment_ids, tok, size):
    start = (flat_index() // size) * tok
    padded = jnp.concatenate([jnp.full((WINDOW,), -1, jnp.int32), segment_ids])
    keys = lax.dynamic_slice_in_dim(padded, start, WINDOW + tok, 0)
    queries = lax.dynamic_slice_in_dim(segment_ids, start, tok, 0)
    before = jnp.sum((keys[:, None] < queries[None, :]).astype(jnp.int32), axis=0)
    return jnp.maximum(before, jnp.arange(1, tok + 1, dtype=jnp.int32))[None, :]


def body(query, key, value, grad_out, segment_ids):
    size = key.shape[1] // HEAD_DIM
    rows = query.shape[0]
    tok = size * rows
    reach = WINDOW // tok
    assert reach * tok == WINDOW and device_count() % size == 0
    low = lowest_key(segment_ids, tok, size)

    kv = exchange(pack((key, value), size)).reshape(tok, -1)
    kv, qg = after(kv, pack((query, grad_out), size))
    kvs = [kv] + [shifted(kv, lag * size) for lag in range(1, reach + 1)]
    qg = exchange(qg).reshape(tok, -1)

    og, total, sent = attend(low, qg, kvs)

    for lag in range(1, reach + 1):
        total = total + shifted(sent[lag - 1], -lag * size).astype(F32)
    og = exchange(og.reshape(size, rows, -1))
    grads = exchange(total.astype(BF16).reshape(size, rows, -1))
    attn_out, grad_query = spread(og, 2)
    grad_key, grad_value = spread(grads, 2)
    return (attn_out, grad_query, grad_key, grad_value)


def solution(mesh):
    placed = P(("pipe", "tensor"), None)
    return jax.shard_map(
        body,
        mesh=mesh,
        in_specs=(placed, placed, placed, placed, P()),
        out_specs=(placed, placed, placed, placed),
        check_vma=False,
    )
```

```python
import functools

import jax
import jax.numpy as jnp
from jax import lax
from jax.experimental import pallas as pl
from jax.experimental.pallas import tpu as pltpu
from jax.sharding import PartitionSpec as P

HEAD_DIM = 128
WINDOW = 1024
TILE = 128

logit_scale = 168.0 ** (-0.5)
exp2_scale = logit_scale * 1.4426950408889634

SMALL = pltpu.CompilerParams(vmem_limit_bytes=4 * 1024 * 1024)
ANY = pl.BlockSpec(memory_space=pl.ANY)
VMEM = pl.BlockSpec(memory_space=pltpu.VMEM)
F32 = jnp.float32
BF16 = jnp.bfloat16
BOTH = ("pipe", "tensor")


def flat_index():
    return lax.axis_index("pipe") * lax.axis_size("tensor") + lax.axis_index("tensor")


def device_count():
    return lax.axis_size("pipe") * lax.axis_size("tensor")


def exchange(pieces):
    count = device_count()
    return [pieces[0]] + [
        lax.ppermute(pieces[j], BOTH, [(i, i ^ j) for i in range(count)])
        for j in range(1, len(pieces))
    ]


def partner(size, j):
    return lax.bitwise_xor(lax.rem(flat_index(), size), j)


def place(index, width):
    return pl.ds(pl.multiple_of(index * width, width), width)


def shifted(value, step):
    count = device_count()
    pairs = [(i, i + step) for i in range(count) if 0 <= i + step < count]
    return lax.ppermute(value, BOTH, pairs)


def after(value, *others):
    return lax.optimization_barrier((value, *others))


def run_copies(copies, sems):
    started = []
    for at, (source, target) in enumerate(copies):
        copy = pltpu.make_async_copy(source, target, sems.at[at])
        copy.start()
        started.append(copy)
    for copy in started:
        copy.wait()


def pack_body(size, widths, *refs):
    arrays, pieces = refs[: len(widths)], refs[len(widths) :]
    for j, piece in enumerate(pieces):
        start = 0
        for array, width in zip(arrays, widths):
            piece[:, start : start + width] = array[:, place(partner(size, j), width)]
            start += width


def pack(arrays, size):
    rows = arrays[0].shape[0]
    widths = [array.shape[1] // size for array in arrays]
    return pl.pallas_call(
        functools.partial(pack_body, size, widths),
        out_shape=[jax.ShapeDtypeStruct((rows, sum(widths)), BF16)] * size,
        in_specs=[VMEM] * len(arrays),
        out_specs=[VMEM] * size,
        compiler_params=SMALL,
        name="pack",
    )(*arrays)


def join_body(size, *refs):
    pieces, out = refs[:size], refs[size]
    for j, piece in enumerate(pieces):
        out[place(partner(size, j), piece.shape[0]), :] = piece[...]


def join(pieces):
    size, (rows, cols) = len(pieces), pieces[0].shape
    return pl.pallas_call(
        functools.partial(join_body, size),
        out_shape=jax.ShapeDtypeStruct((size * rows, cols), BF16),
        in_specs=[VMEM] * size,
        out_specs=VMEM,
        compiler_params=SMALL,
        name="join",
    )(*pieces)


def combine_body(terms, *refs):
    added, pieces = refs[:terms], refs[terms:]
    for j, piece in enumerate(pieces):
        there = place(partner(len(pieces), j), piece.shape[0])
        total = added[0][there, :]
        for term in added[1:]:
            total = total + term[there, :].astype(F32)
        piece[...] = total.astype(BF16)


def combine(terms, size):
    tok, cols = terms[0].shape
    return pl.pallas_call(
        functools.partial(combine_body, len(terms)),
        out_shape=[jax.ShapeDtypeStruct((tok // size, cols), BF16)] * size,
        in_specs=[VMEM] * len(terms),
        out_specs=[VMEM] * size,
        compiler_params=SMALL,
        name="combine",
    )(*terms)


def spread_body(size, width, *refs):
    pieces, outs, sems = refs[:size], refs[size:-1], refs[-1]
    copies = []
    for j, piece in enumerate(pieces):
        for at, out in enumerate(outs):
            copies.append(
                (
                    piece.at[:, at * width : (at + 1) * width],
                    out.at[:, place(partner(size, j), width)],
                )
            )
    run_copies(copies, sems)


def spread(pieces, count):
    size, (rows, cols) = len(pieces), pieces[0].shape
    width = cols // count
    return pl.pallas_call(
        functools.partial(spread_body, size, width),
        out_shape=[jax.ShapeDtypeStruct((rows, width * size), BF16)] * count,
        in_specs=[ANY] * size,
        out_specs=[ANY] * count,
        scratch_shapes=[pltpu.SemaphoreType.DMA((size * count,))],
        compiler_params=SMALL,
        name="spread",
    )(*pieces)


def dot(a, b):
    return lax.dot_general(a, b, (((1,), (0,)), ((), ())), preferred_element_type=F32)


def dot_t(a, b):
    return lax.dot_general(a, b, (((1,), (1,)), ((), ())), preferred_element_type=F32)


def fold(x, op):
    parts = [x[at : at + 8] for at in range(0, x.shape[0], 8)]
    while len(parts) > 1:
        parts = [
            op(*parts[at : at + 2]) if at + 1 < len(parts) else parts[at]
            for at in range(0, len(parts), 2)
        ]
    return parts[0]


def attend_body(size, reach, tok, group, *refs):
    refs = list(refs)
    take = lambda count: [refs.pop(0) for _ in range(count)]
    (low,), qg_pieces, kvs = take(1), take(size), take(1 + reach)
    og_pieces, (dkv0,), sent = take(size), take(1), take(reach)
    qg, og, kt, vt, dk, dv, s_scr, e_scr, ds_scr = refs
    for j, piece in enumerate(qg_pieces):
        qg[place(partner(size, j), piece.shape[0]), :] = piece[...]
    width = group * HEAD_DIM
    span = WINDOW + TILE
    dk[...] = jnp.zeros_like(dk)
    dv[...] = jnp.zeros_like(dv)
    lane = lax.broadcasted_iota(jnp.int32, (TILE, HEAD_DIM), 1)
    ones = jnp.where(lane < 2, 1.0, 0.0).astype(BF16)
    wide_lane = lax.broadcasted_iota(jnp.int32, (group * TILE, HEAD_DIM), 1)
    row_of = lax.broadcasted_iota(jnp.int32, (TILE, group * TILE), 0)
    col_of = lax.broadcasted_iota(jnp.int32, (TILE, TILE), 1)
    causal = lax.broadcasted_iota(jnp.int32, (TILE, TILE), 0) <= col_of
    causal = jnp.concatenate([causal] * group, axis=1)

    def rows(start, first):
        lag = reach - start // tok
        at = start % tok
        return kvs[lag][at : at + TILE, first * HEAD_DIM : (first + 1) * HEAD_DIM]

    for lag in range(reach + 1):
        there = slice((reach - lag) * tok, (reach - lag + 1) * tok)
        kt[:, there] = kvs[lag][:, :HEAD_DIM].T
        vt[:, there] = kvs[lag][:, HEAD_DIM:].T
    for tile in range(tok // TILE):
        base = tile * TILE
        here = slice(base, base + TILE)
        q2 = jnp.concatenate(
            [qg[here, at * HEAD_DIM : (at + 1) * HEAD_DIM] for at in range(group)], axis=0
        )
        g2 = jnp.concatenate(
            [qg[here, width + at * HEAD_DIM : width + (at + 1) * HEAD_DIM] for at in range(group)],
            axis=0,
        )
        low_row = jnp.concatenate([low[:, here]] * group, axis=1) - base
        top = None
        for at in range(0, span, TILE):
            s = dot_t(rows(base + at, 0), q2)
            keep = row_of >= low_row - at
            if at == span - TILE:
                keep = keep & causal
            s = jnp.where(keep, s, -1e30)
            s_scr[at : at + TILE, :] = s
            part = fold(s, jnp.maximum)
            top = part if top is None else jnp.maximum(top, part)
        top = jnp.max(top, axis=0, keepdims=True) * exp2_scale
        total = None
        for at in range(0, span, TILE):
            e = jnp.exp2(s_scr[at : at + TILE, :] * exp2_scale - top)
            e_scr[at : at + TILE, :] = e.astype(BF16)
            part = fold(e, jnp.add)
            total = part if total is None else total + part
        inv = 1.0 / jnp.sum(total, axis=0, keepdims=True)
        inv = jnp.broadcast_to(inv, (HEAD_DIM, group * TILE)).T
        out = dot(vt[:, base : base + span], e_scr[...]).T * inv
        out = out.astype(BF16)
        g2 = (g2.astype(F32) * inv).astype(BF16)
        delta = jnp.sum(g2.astype(F32) * out.astype(F32), axis=1, keepdims=True)
        high = delta.astype(BF16).astype(F32)
        extra = jnp.where(wide_lane == 0, -high, jnp.where(wide_lane == 1, high - delta, 0.0))
        g_wide = jnp.concatenate([g2, extra.astype(BF16)], axis=1)
        for at in range(0, span, TILE):
            there = slice(base + at, base + at + TILE)
            dp = dot_t(jnp.concatenate([rows(base + at, 1), ones], axis=1), g_wide)
            e = e_scr[at : at + TILE, :]
            ds = (e.astype(F32) * dp).astype(BF16)
            ds_scr[at : at + TILE, :] = ds
            dv[there, :] += dot(e, g2)
            dk[there, :] += dot(ds, q2)
        dq = (dot(kt[:, base : base + span], ds_scr[...]) * logit_scale).T.astype(BF16)
        for at in range(group):
            part = slice(at * TILE, (at + 1) * TILE)
            og[here, at * HEAD_DIM : (at + 1) * HEAD_DIM] = out[part]
            og[here, width + at * HEAD_DIM : width + (at + 1) * HEAD_DIM] = dq[part]

    dkv0[:, :HEAD_DIM] = dk[reach * tok :, :] * logit_scale
    dkv0[:, HEAD_DIM:] = dv[reach * tok :, :]
    for lag in range(1, reach + 1):
        there = slice((reach - lag) * tok, (reach - lag + 1) * tok)
        sent[lag - 1][:, :HEAD_DIM] = (dk[there, :] * logit_scale).astype(BF16)
        sent[lag - 1][:, HEAD_DIM:] = dv[there, :].astype(BF16)
    for j, piece in enumerate(og_pieces):
        piece[...] = og[place(partner(size, j), piece.shape[0]), :]


def attend(low, qg, kvs):
    size, (rows, cols) = len(qg), qg[0].shape
    tok = size * rows
    width = cols // 2
    group = width // HEAD_DIM
    reach = len(kvs) - 1
    span = WINDOW + TILE
    wide = group * TILE
    keys = (reach + 1) * tok
    half = jax.ShapeDtypeStruct((tok, 2 * HEAD_DIM), BF16)
    flops = 6 * 2 * tok * group * span * HEAD_DIM
    results = pl.pallas_call(
        functools.partial(attend_body, size, reach, tok, group),
        out_shape=[jax.ShapeDtypeStruct((rows, cols), BF16)] * size
        + [jax.ShapeDtypeStruct((tok, 2 * HEAD_DIM), F32)]
        + [half] * reach,
        in_specs=[VMEM] * (size + 2 + reach),
        out_specs=[VMEM] * (size + 1 + reach),
        scratch_shapes=[
            pltpu.VMEM((tok, cols), BF16),
            pltpu.VMEM((tok, cols), BF16),
            pltpu.VMEM((HEAD_DIM, keys), BF16),
            pltpu.VMEM((HEAD_DIM, keys), BF16),
            pltpu.VMEM((keys, HEAD_DIM), F32),
            pltpu.VMEM((keys, HEAD_DIM), F32),
            pltpu.VMEM((span, wide), F32),
            pltpu.VMEM((span, wide), BF16),
            pltpu.VMEM((span, wide), BF16),
        ],
        compiler_params=pltpu.CompilerParams(vmem_limit_bytes=32 * 1024 * 1024),
        cost_estimate=pl.CostEstimate(
            flops=flops, bytes_accessed=8 * 1024 * 1024, transcendentals=flops // 1536
        ),
        name="attend",
    )(low, *qg, *kvs)
    return results[:size], results[size], results[size + 1 :]


def lowest_key(segment_ids, tok, size):
    start = (flat_index() // size) * tok
    padded = jnp.concatenate([jnp.full((WINDOW,), -1, jnp.int32), segment_ids])
    keys = lax.dynamic_slice_in_dim(padded, start, WINDOW + tok, 0)
    queries = lax.dynamic_slice_in_dim(segment_ids, start, tok, 0)
    before = jnp.sum((keys[:, None] < queries[None, :]).astype(jnp.int32), axis=0)
    return jnp.maximum(before, jnp.arange(1, tok + 1, dtype=jnp.int32))[None, :]


def body(query, key, value, grad_out, segment_ids):
    size = key.shape[1] // HEAD_DIM
    rows = query.shape[0]
    tok = size * rows
    reach = WINDOW // tok
    assert reach * tok == WINDOW and device_count() % size == 0
    low = lowest_key(segment_ids, tok, size)

    kv = join(exchange(pack((key, value), size)))
    kv, *qg = after(kv, *pack((query, grad_out), size))
    kvs = [kv] + [shifted(kv, lag * size) for lag in range(1, reach + 1)]
    qg = exchange(qg)

    og, dkv, sent = attend(low, qg, kvs)

    back = [shifted(sent[lag - 1], -lag * size) for lag in range(1, reach + 1)]
    og = exchange(og)
    grads = exchange(combine([dkv] + back, size))
    attn_out, grad_query = spread(og, 2)
    grad_key, grad_value = spread(grads, 2)
    return (attn_out, grad_query, grad_key, grad_value)


def solution(mesh):
    placed = P(("pipe", "tensor"), None)
    return jax.shard_map(
        body,
        mesh=mesh,
        in_specs=(placed, placed, placed, placed, P()),
        out_specs=(placed, placed, placed, placed),
        check_vma=False,
    )
```

```python
import functools

import jax
import jax.numpy as jnp
from jax import lax
from jax.experimental import pallas as pl
from jax.experimental.pallas import tpu as pltpu
from jax.sharding import PartitionSpec as P

HEAD_DIM = 128
WINDOW = 1024
TILE = 128

logit_scale = 168.0 ** (-0.5)
exp2_scale = logit_scale * 1.4426950408889634

SMALL = pltpu.CompilerParams(vmem_limit_bytes=4 * 1024 * 1024)
ANY = pl.BlockSpec(memory_space=pl.ANY)
VMEM = pl.BlockSpec(memory_space=pltpu.VMEM)
F32 = jnp.float32
BF16 = jnp.bfloat16
BOTH = ("pipe", "tensor")


def flat_index():
    return lax.axis_index("pipe") * lax.axis_size("tensor") + lax.axis_index("tensor")


def device_count():
    return lax.axis_size("pipe") * lax.axis_size("tensor")


def swap(value, mask):
    return lax.ppermute(value, BOTH, [(i, i ^ mask) for i in range(device_count())])


def core_mask():
    return lax.axis_size("tensor")


def chip_masks(size):
    return [mask for mask in range(size) if not mask & core_mask()]


def swap_chips(pieces, size):
    return [pieces[0]] + [
        swap(piece, mask) for piece, mask in zip(pieces[1:], chip_masks(size)[1:])
    ]


def partner(size, j):
    return lax.bitwise_xor(lax.rem(flat_index(), size), j)


def place(index, width):
    return pl.ds(pl.multiple_of(index * width, width), width)


def shifted(value, step):
    count = device_count()
    pairs = [(i, i + step) for i in range(count) if 0 <= i + step < count]
    return lax.ppermute(value, BOTH, pairs)


def after(value, *others):
    return lax.optimization_barrier((value, *others))


def run_copies(copies, sems):
    started = []
    for at, (source, target) in enumerate(copies):
        copy = pltpu.make_async_copy(source, target, sems.at[at])
        copy.start()
        started.append(copy)
    for copy in started:
        copy.wait()


def small_call(kernel, out_shape, name, *args):
    return pl.pallas_call(
        kernel,
        out_shape=out_shape,
        in_specs=[VMEM] * len(args),
        out_specs=jax.tree.map(lambda _: VMEM, out_shape),
        compiler_params=SMALL,
        name=name,
    )(*args)


def cut_body(size, core, masks, widths, *refs):
    arrays, outs = refs[: len(widths)], refs[len(widths) :]
    for out, flip in zip(outs, (0, core)):
        start = 0
        for mask in masks:
            for array, width in zip(arrays, widths):
                out[:, start : start + width] = array[:, place(partner(size, mask ^ flip), width)]
                start += width


def stack_body(count, keep, got, *pieces):
    rows, width = keep.shape[0], keep.shape[1] // count
    for at, piece in enumerate(pieces):
        piece[:rows, :] = keep[:, at * width : (at + 1) * width]
        piece[rows:, :] = got[:, at * width : (at + 1) * width]


def gather_cores(arrays, size):
    rows = arrays[0].shape[0]
    masks = chip_masks(size)
    widths = [array.shape[1] // size for array in arrays]
    half = jax.ShapeDtypeStruct((rows, len(masks) * sum(widths)), BF16)
    keep, give = small_call(
        functools.partial(cut_body, size, core_mask(), masks, widths), [half] * 2, "cut", *arrays
    )
    got = swap(give, core_mask())
    piece = jax.ShapeDtypeStruct((2 * rows, sum(widths)), BF16)
    return small_call(
        functools.partial(stack_body, len(masks)), [piece] * len(masks), "stack", keep, got
    )


def place_rows(size, core, masks, pieces, out):
    for mask, piece in zip(masks, pieces):
        rows = piece.shape[0] // 2
        out[place(partner(size, mask), rows), :] = piece[:rows, :]
        out[place(partner(size, mask ^ core), rows), :] = piece[rows:, :]


def take_rows(size, core, masks, source, pieces):
    for mask, piece in zip(masks, pieces):
        rows = piece.shape[0] // 2
        piece[:rows, :] = source(place(partner(size, mask), rows))
        piece[rows:, :] = source(place(partner(size, mask ^ core), rows))


def join(pieces, size):
    rows, cols = pieces[0].shape
    core, masks = core_mask(), chip_masks(size)

    def kernel(*refs):
        place_rows(size, core, masks, refs[:-1], refs[-1])

    out = jax.ShapeDtypeStruct((len(pieces) * rows, cols), BF16)
    return small_call(kernel, out, "join", *pieces)


def combine(terms, size):
    tok, cols = terms[0].shape
    core, masks = core_mask(), chip_masks(size)

    def kernel(*refs):
        added = refs[: len(terms)]

        def source(there):
            total = added[0][there, :]
            for term in added[1:]:
                total = total + term[there, :].astype(F32)
            return total.astype(BF16)

        take_rows(size, core, masks, source, refs[len(terms) :])

    piece = jax.ShapeDtypeStruct((2 * (tok // size), cols), BF16)
    return small_call(kernel, [piece] * len(masks), "combine", *terms)


def bottom_body(*refs):
    out = refs[-1]
    for at, piece in enumerate(refs[:-1]):
        rows, width = piece.shape[0] // 2, piece.shape[1]
        out[:, at * width : (at + 1) * width] = piece[rows:, :]


def spread_body(size, core, masks, count, *refs):
    pieces, got, outs, sems = refs[: len(masks)], refs[len(masks)], refs[-1 - count : -1], refs[-1]
    copies = []
    for chip, (mask, piece) in enumerate(zip(masks, pieces)):
        rows, cols = piece.shape
        rows, width = rows // 2, cols // count
        for at, out in enumerate(outs):
            copies.append(
                (
                    piece.at[:rows, at * width : (at + 1) * width],
                    out.at[:, place(partner(size, mask), width)],
                )
            )
            start = chip * cols + at * width
            copies.append(
                (
                    got.at[:, start : start + width],
                    out.at[:, place(partner(size, mask ^ core), width)],
                )
            )
    run_copies(copies, sems)


def spread_cores(pieces, size, count):
    rows, cols = pieces[0].shape
    rows = rows // 2
    give = jax.ShapeDtypeStruct((rows, cols * len(pieces)), BF16)
    got = swap(small_call(bottom_body, give, "bottom", *pieces), core_mask())
    width = cols // count
    return pl.pallas_call(
        functools.partial(spread_body, size, core_mask(), chip_masks(size), count),
        out_shape=[jax.ShapeDtypeStruct((rows, width * size), BF16)] * count,
        in_specs=[ANY] * (len(pieces) + 1),
        out_specs=[ANY] * count,
        scratch_shapes=[pltpu.SemaphoreType.DMA((size * count,))],
        compiler_params=SMALL,
        name="spread",
    )(*pieces, got)


def dot(a, b):
    return lax.dot_general(a, b, (((1,), (0,)), ((), ())), preferred_element_type=F32)


def dot_t(a, b):
    return lax.dot_general(a, b, (((1,), (1,)), ((), ())), preferred_element_type=F32)


def fold(x, op):
    parts = [x[at : at + 8] for at in range(0, x.shape[0], 8)]
    while len(parts) > 1:
        parts = [
            op(*parts[at : at + 2]) if at + 1 < len(parts) else parts[at]
            for at in range(0, len(parts), 2)
        ]
    return parts[0]


def attend_body(size, core, masks, reach, tok, group, *refs):
    refs = list(refs)
    take = lambda count: [refs.pop(0) for _ in range(count)]
    (low,), qg_pieces, kvs = take(1), take(len(masks)), take(1 + reach)
    og_pieces, (dkv0,), sent = take(len(masks)), take(1), take(reach)
    qg, og, ks, va, kt, vt, dk, dv, s_scr, e_scr, ds_scr = refs
    width = group * HEAD_DIM
    span = WINDOW + TILE
    place_rows(size, core, masks, qg_pieces, qg)
    va[:, HEAD_DIM:] = jnp.where(
        lax.broadcasted_iota(jnp.int32, (va.shape[0], HEAD_DIM), 1) < 2, 1.0, 0.0
    ).astype(BF16)
    for lag in range(reach + 1):
        there = slice((reach - lag) * tok, (reach - lag + 1) * tok)
        ks[there, :] = kvs[lag][:, :HEAD_DIM]
        va[there, :HEAD_DIM] = kvs[lag][:, HEAD_DIM:]
        kt[:, there] = kvs[lag][:, :HEAD_DIM].T
        vt[:, there] = kvs[lag][:, HEAD_DIM:].T
    dk[...] = jnp.zeros_like(dk)
    dv[...] = jnp.zeros_like(dv)
    wide_lane = lax.broadcasted_iota(jnp.int32, (group * TILE, HEAD_DIM), 1)
    row_of = lax.broadcasted_iota(jnp.int32, (TILE, group * TILE), 0)
    col_of = lax.broadcasted_iota(jnp.int32, (TILE, TILE), 1)
    causal = lax.broadcasted_iota(jnp.int32, (TILE, TILE), 0) <= col_of
    causal = jnp.concatenate([causal] * group, axis=1)

    def stacked(base, first):
        here = slice(base, base + TILE)
        return jnp.concatenate(
            [
                qg[here, first + at * HEAD_DIM : first + (at + 1) * HEAD_DIM]
                for at in range(group)
            ],
            axis=0,
        )

    def scores(tile):
        base = tile * TILE
        s_scr[tile % 2] = dot_t(ks[base : base + span, :], stacked(base, 0))

    tiles = tok // TILE
    scores(0)
    for tile in range(tiles):
        base, turn = tile * TILE, tile % 2
        here, there = slice(base, base + TILE), slice(base, base + span)
        low_row = jnp.concatenate([low[:, here]] * group, axis=1) - base
        top = None
        for at in range(0, span, TILE):
            keep = row_of >= low_row - at
            if at == span - TILE:
                keep = keep & causal
            s = jnp.where(keep, s_scr[turn, at : at + TILE, :], -1e30)
            s_scr[turn, at : at + TILE, :] = s
            part = fold(s, jnp.maximum)
            top = part if top is None else jnp.maximum(top, part)
        top = jnp.max(top, axis=0, keepdims=True) * exp2_scale
        if tile + 1 < tiles:
            scores(tile + 1)
        total = None
        for at in range(0, span, TILE):
            e = jnp.exp2(s_scr[turn, at : at + TILE, :] * exp2_scale - top)
            e_scr[turn, at : at + TILE, :] = e.astype(BF16)
            part = fold(e, jnp.add)
            total = part if total is None else total + part
        inv = 1.0 / jnp.sum(total, axis=0, keepdims=True)
        inv = jnp.broadcast_to(inv, (HEAD_DIM, group * TILE)).T
        out = dot(vt[:, there], e_scr[turn]).T * inv
        out = out.astype(BF16)
        g2 = (stacked(base, width).astype(F32) * inv).astype(BF16)
        delta = jnp.sum(g2.astype(F32) * out.astype(F32), axis=1, keepdims=True)
        high = delta.astype(BF16).astype(F32)
        extra = jnp.where(wide_lane == 0, -high, jnp.where(wide_lane == 1, high - delta, 0.0))
        dp = dot_t(va[there, :], jnp.concatenate([g2, extra.astype(BF16)], axis=1))
        dv[there, :] += dot(e_scr[turn], g2)
        for at in range(0, span, TILE):
            part = slice(at, at + TILE)
            ds_scr[turn, part, :] = (e_scr[turn, part, :].astype(F32) * dp[part]).astype(BF16)
        dk[there, :] += dot(ds_scr[turn], stacked(base, 0))
        dq = (dot(kt[:, there], ds_scr[turn]) * logit_scale).T.astype(BF16)
        for at in range(group):
            part = slice(at * TILE, (at + 1) * TILE)
            og[here, at * HEAD_DIM : (at + 1) * HEAD_DIM] = out[part]
            og[here, width + at * HEAD_DIM : width + (at + 1) * HEAD_DIM] = dq[part]

    dkv0[:, :HEAD_DIM] = dk[reach * tok :, :] * logit_scale
    dkv0[:, HEAD_DIM:] = dv[reach * tok :, :]
    for lag in range(1, reach + 1):
        there = slice((reach - lag) * tok, (reach - lag + 1) * tok)
        sent[lag - 1][:, :HEAD_DIM] = (dk[there, :] * logit_scale).astype(BF16)
        sent[lag - 1][:, HEAD_DIM:] = dv[there, :].astype(BF16)
    take_rows(size, core, masks, lambda there: og[there, :], og_pieces)


def attend(low, qg, kvs, size):
    rows, cols = qg[0].shape
    tok = len(qg) * rows
    group = cols // (2 * HEAD_DIM)
    reach = len(kvs) - 1
    span = WINDOW + TILE
    wide = group * TILE
    keys = (reach + 1) * tok
    half = jax.ShapeDtypeStruct((tok, 2 * HEAD_DIM), BF16)
    flops = 6 * 2 * tok * group * span * HEAD_DIM
    count = len(qg)
    results = pl.pallas_call(
        functools.partial(attend_body, size, core_mask(), chip_masks(size), reach, tok, group),
        out_shape=[jax.ShapeDtypeStruct((rows, cols), BF16)] * count
        + [jax.ShapeDtypeStruct((tok, 2 * HEAD_DIM), F32)]
        + [half] * reach,
        in_specs=[VMEM] * (count + 2 + reach),
        out_specs=[VMEM] * (count + 1 + reach),
        scratch_shapes=[
            pltpu.VMEM((tok, cols), BF16),
            pltpu.VMEM((tok, cols), BF16),
            pltpu.VMEM((keys, HEAD_DIM), BF16),
            pltpu.VMEM((keys, 2 * HEAD_DIM), BF16),
            pltpu.VMEM((HEAD_DIM, keys), BF16),
            pltpu.VMEM((HEAD_DIM, keys), BF16),
            pltpu.VMEM((keys, HEAD_DIM), F32),
            pltpu.VMEM((keys, HEAD_DIM), F32),
            pltpu.VMEM((2, span, wide), F32),
            pltpu.VMEM((2, span, wide), BF16),
            pltpu.VMEM((2, span, wide), BF16),
        ],
        compiler_params=pltpu.CompilerParams(vmem_limit_bytes=36 * 1024 * 1024),
        cost_estimate=pl.CostEstimate(
            flops=flops, bytes_accessed=8 * 1024 * 1024, transcendentals=flops // 1536
        ),
        name="attend",
    )(low, *qg, *kvs)
    return results[:count], results[count], results[count + 1 :]


def lowest_key(segment_ids, tok, size):
    start = (flat_index() // size) * tok
    padded = jnp.concatenate([jnp.full((WINDOW,), -1, jnp.int32), segment_ids])
    keys = lax.dynamic_slice_in_dim(padded, start, WINDOW + tok, 0)
    queries = lax.dynamic_slice_in_dim(segment_ids, start, tok, 0)
    before = jnp.sum((keys[:, None] < queries[None, :]).astype(jnp.int32), axis=0)
    return jnp.maximum(before, jnp.arange(1, tok + 1, dtype=jnp.int32))[None, :]


def body(query, key, value, grad_out, segment_ids):
    size = key.shape[1] // HEAD_DIM
    rows = query.shape[0]
    tok = size * rows
    reach = WINDOW // tok
    assert reach * tok == WINDOW and device_count() % size == 0
    low = lowest_key(segment_ids, tok, size)

    pieces = list(gather_cores((key, value), size))
    pieces[0], query, grad_out = after(pieces[0], query, grad_out)
    kv = join(swap_chips(pieces, size), size)
    kv, *qg = after(kv, *gather_cores((query, grad_out), size))
    kvs = [kv] + [shifted(kv, lag * size) for lag in range(1, reach + 1)]
    qg = swap_chips(qg, size)

    og, dkv, sent = attend(low, qg, kvs, size)

    back = [shifted(sent[lag - 1], -lag * size) for lag in range(1, reach + 1)]
    attn_out, grad_query = spread_cores(swap_chips(og, size), size, 2)
    grads = swap_chips(combine([dkv] + back, size), size)
    grad_key, grad_value = spread_cores(grads, size, 2)
    return (attn_out, grad_query, grad_key, grad_value)


def solution(mesh):
    placed = P(("pipe", "tensor"), None)
    return jax.shard_map(
        body,
        mesh=mesh,
        in_specs=(placed, placed, placed, placed, P()),
        out_specs=(placed, placed, placed, placed),
        check_vma=False,
    )
```

```python
import functools

import jax
import jax.numpy as jnp
from jax import lax
from jax.experimental import pallas as pl
from jax.experimental.pallas import tpu as pltpu
from jax.sharding import PartitionSpec as P

HEAD_DIM = 128
WINDOW = 1024
TILE = 128

logit_scale = 168.0 ** (-0.5)
exp2_scale = logit_scale * 1.4426950408889634

SMALL = pltpu.CompilerParams(vmem_limit_bytes=4 * 1024 * 1024)
ANY = pl.BlockSpec(memory_space=pl.ANY)
VMEM = pl.BlockSpec(memory_space=pltpu.VMEM)
F32 = jnp.float32
BF16 = jnp.bfloat16
BOTH = ("pipe", "tensor")


def flat_index():
    return lax.axis_index("pipe") * lax.axis_size("tensor") + lax.axis_index("tensor")


def device_count():
    return lax.axis_size("pipe") * lax.axis_size("tensor")


def swap(value, mask):
    return lax.ppermute(value, BOTH, [(i, i ^ mask) for i in range(device_count())])


def core_mask():
    return lax.axis_size("tensor")


def chip_masks(size):
    return [mask for mask in range(size) if not mask & core_mask()]


def swap_chips(pieces, size):
    return [pieces[0]] + [
        swap(piece, mask) for piece, mask in zip(pieces[1:], chip_masks(size)[1:])
    ]


def partner(size, j):
    return lax.bitwise_xor(lax.rem(flat_index(), size), j)


def place(index, width):
    return pl.ds(pl.multiple_of(index * width, width), width)


def shifted(value, step):
    count = device_count()
    pairs = [(i, i + step) for i in range(count) if 0 <= i + step < count]
    return lax.ppermute(value, BOTH, pairs)


def after(value, *others):
    return lax.optimization_barrier((value, *others))


def run_copies(copies, sems):
    started = []
    for at, (source, target) in enumerate(copies):
        copy = pltpu.make_async_copy(source, target, sems.at[at])
        copy.start()
        started.append(copy)
    for copy in started:
        copy.wait()


def small_call(kernel, out_shape, name, *args):
    return pl.pallas_call(
        kernel,
        out_shape=out_shape,
        in_specs=[VMEM] * len(args),
        out_specs=jax.tree.map(lambda _: VMEM, out_shape),
        compiler_params=SMALL,
        name=name,
    )(*args)


def this_core(array, size):
    core = core_mask()
    width = array.shape[1] // size
    shares = [array[:, r * width : (r + 1) * width] for r in range(size)]
    first, second = (
        jnp.concatenate([share for r, share in enumerate(shares) if (r // core) % 2 == at], axis=1)
        for at in range(2)
    )
    return jnp.where((flat_index() // core) % 2 == 0, first, second)


def stack_body(size, core, masks, count, *refs):
    own, got, pieces = refs[:count], refs[count : 2 * count], refs[2 * count :]
    rows = own[0].shape[0]
    for mask, piece in zip(masks, pieces):
        there = partner(size, mask)
        chip = there // (2 * core) * core + lax.rem(there, core)
        start = 0
        for mine, other in zip(own, got):
            width = other.shape[1] // size
            piece[:rows, start : start + width] = mine[:, place(chip, width)]
            piece[rows:, start : start + width] = other[:, place(there, width)]
            start += width


def gather_cores(arrays, size):
    masks = chip_masks(size)
    got = [swap(array, core_mask()) for array in arrays]
    own = [this_core(array, size) for array in arrays]
    cols = sum(array.shape[1] // size for array in arrays)
    piece = jax.ShapeDtypeStruct((2 * arrays[0].shape[0], cols), BF16)
    kernel = functools.partial(stack_body, size, core_mask(), masks, len(arrays))
    return small_call(kernel, [piece] * len(masks), "stack", *own, *got)


def place_rows(size, core, masks, pieces, out):
    for mask, piece in zip(masks, pieces):
        rows = piece.shape[0] // 2
        out[place(partner(size, mask), rows), :] = piece[:rows, :]
        out[place(partner(size, mask ^ core), rows), :] = piece[rows:, :]


def take_rows(size, core, masks, source, own, give):
    rows = own.shape[0] // len(masks)
    for at, mask in enumerate(masks):
        part = slice(at * rows, (at + 1) * rows)
        own[part, :] = source(place(partner(size, mask), rows))
        give[part, :] = source(place(partner(size, mask ^ core), rows))


def join(pieces, size):
    rows, cols = pieces[0].shape
    core, masks = core_mask(), chip_masks(size)

    def kernel(*refs):
        place_rows(size, core, masks, refs[:-1], refs[-1])

    out = jax.ShapeDtypeStruct((len(pieces) * rows, cols), BF16)
    return small_call(kernel, out, "join", *pieces)


def combine(terms, size):
    tok, cols = terms[0].shape
    core, masks = core_mask(), chip_masks(size)

    def kernel(*refs):
        added = refs[: len(terms)]

        def source(there):
            total = added[0][there, :]
            for term in added[1:]:
                total = total + term[there, :].astype(F32)
            return total.astype(BF16)

        take_rows(size, core, masks, source, *refs[len(terms) :])

    half = jax.ShapeDtypeStruct((tok // 2, cols), BF16)
    return small_call(kernel, [half] * 2, "combine", *terms)


def pair_body(own, got, *pieces):
    rows = own.shape[0] // len(pieces)
    for at, piece in enumerate(pieces):
        part = slice(at * rows, (at + 1) * rows)
        piece[:rows, :] = own[part, :]
        piece[rows:, :] = got[part, :]


def scatter(own, give, size):
    count = len(chip_masks(size))
    piece = jax.ShapeDtypeStruct((2 * own.shape[0] // count, own.shape[1]), BF16)
    pieces = small_call(pair_body, [piece] * count, "pair", own, swap(give, core_mask()))
    return swap_chips(pieces, size)


def spread_body(size, core, masks, count, *refs):
    pieces, outs, sems = refs[: len(masks)], refs[len(masks) : -1], refs[-1]
    copies = []
    for mask, piece in zip(masks, pieces):
        rows, cols = piece.shape
        rows, width = rows // 2, cols // count
        for flip in (0, 1):
            columns = place(partner(size, mask ^ (core * flip)), width)
            for at, out in enumerate(outs):
                copies.append(
                    (
                        piece.at[flip * rows : (flip + 1) * rows, at * width : (at + 1) * width],
                        out.at[:, columns],
                    )
                )
    run_copies(copies, sems)


def spread(pieces, size, count):
    rows, cols = pieces[0].shape
    return pl.pallas_call(
        functools.partial(spread_body, size, core_mask(), chip_masks(size), count),
        out_shape=[jax.ShapeDtypeStruct((rows // 2, cols // count * size), BF16)] * count,
        in_specs=[ANY] * len(pieces),
        out_specs=[ANY] * count,
        scratch_shapes=[pltpu.SemaphoreType.DMA((size * count,))],
        compiler_params=SMALL,
        name="spread",
    )(*pieces)


def dot(a, b):
    return lax.dot_general(a, b, (((1,), (0,)), ((), ())), preferred_element_type=F32)


def dot_t(a, b):
    return lax.dot_general(a, b, (((1,), (1,)), ((), ())), preferred_element_type=F32)


def fold(x, op):
    parts = [x[at : at + 8] for at in range(0, x.shape[0], 8)]
    while len(parts) > 1:
        parts = [
            op(*parts[at : at + 2]) if at + 1 < len(parts) else parts[at]
            for at in range(0, len(parts), 2)
        ]
    return parts[0]


def attend_body(size, core, masks, reach, tok, group, *refs):
    refs = list(refs)
    take = lambda count: [refs.pop(0) for _ in range(count)]
    (low,), qg_pieces, kvs = take(1), take(len(masks)), take(1 + reach)
    og_halves, (dkv0,), sent = take(2), take(1), take(reach)
    qg, og, ks, va, kt, vt, dk, dv, s_scr, e_scr, ds_scr = refs
    width = group * HEAD_DIM
    span = WINDOW + TILE
    place_rows(size, core, masks, qg_pieces, qg)
    va[:, HEAD_DIM:] = jnp.where(
        lax.broadcasted_iota(jnp.int32, (va.shape[0], HEAD_DIM), 1) < 2, 1.0, 0.0
    ).astype(BF16)
    for lag in range(reach + 1):
        there = slice((reach - lag) * tok, (reach - lag + 1) * tok)
        ks[there, :] = kvs[lag][:, :HEAD_DIM]
        va[there, :HEAD_DIM] = kvs[lag][:, HEAD_DIM:]
        kt[:, there] = kvs[lag][:, :HEAD_DIM].T
        vt[:, there] = kvs[lag][:, HEAD_DIM:].T
    dk[...] = jnp.zeros_like(dk)
    dv[...] = jnp.zeros_like(dv)
    wide_lane = lax.broadcasted_iota(jnp.int32, (group * TILE, HEAD_DIM), 1)
    row_of = lax.broadcasted_iota(jnp.int32, (TILE, group * TILE), 0)
    col_of = lax.broadcasted_iota(jnp.int32, (TILE, TILE), 1)
    causal = lax.broadcasted_iota(jnp.int32, (TILE, TILE), 0) <= col_of
    causal = jnp.concatenate([causal] * group, axis=1)

    def stacked(base, first):
        here = slice(base, base + TILE)
        return jnp.concatenate(
            [
                qg[here, first + at * HEAD_DIM : first + (at + 1) * HEAD_DIM]
                for at in range(group)
            ],
            axis=0,
        )

    def scores(tile):
        base = tile * TILE
        s_scr[tile % 2] = dot_t(ks[base : base + span, :], stacked(base, 0))

    tiles = tok // TILE
    scores(0)
    for tile in range(tiles):
        base, turn = tile * TILE, tile % 2
        here, there = slice(base, base + TILE), slice(base, base + span)
        low_row = jnp.concatenate([low[:, here]] * group, axis=1) - base
        top = None
        for at in range(0, span, TILE):
            keep = row_of >= low_row - at
            if at == span - TILE:
                keep = keep & causal
            s = jnp.where(keep, s_scr[turn, at : at + TILE, :], -1e30)
            s_scr[turn, at : at + TILE, :] = s
            part = fold(s, jnp.maximum)
            top = part if top is None else jnp.maximum(top, part)
        top = jnp.max(top, axis=0, keepdims=True) * exp2_scale
        if tile + 1 < tiles:
            scores(tile + 1)
        total = None
        for at in range(0, span, TILE):
            e = jnp.exp2(s_scr[turn, at : at + TILE, :] * exp2_scale - top)
            e_scr[turn, at : at + TILE, :] = e.astype(BF16)
            part = fold(e, jnp.add)
            total = part if total is None else total + part
        inv = 1.0 / jnp.sum(total, axis=0, keepdims=True)
        inv = jnp.broadcast_to(inv, (HEAD_DIM, group * TILE)).T
        out = dot(vt[:, there], e_scr[turn]).T * inv
        out = out.astype(BF16)
        g2 = (stacked(base, width).astype(F32) * inv).astype(BF16)
        delta = jnp.sum(g2.astype(F32) * out.astype(F32), axis=1, keepdims=True)
        high = delta.astype(BF16).astype(F32)
        extra = jnp.where(wide_lane == 0, -high, jnp.where(wide_lane == 1, high - delta, 0.0))
        dp = dot_t(va[there, :], jnp.concatenate([g2, extra.astype(BF16)], axis=1))
        dv[there, :] += dot(e_scr[turn], g2)
        for at in range(0, span, TILE):
            part = slice(at, at + TILE)
            ds_scr[turn, part, :] = (e_scr[turn, part, :].astype(F32) * dp[part]).astype(BF16)
        dk[there, :] += dot(ds_scr[turn], stacked(base, 0))
        dq = (dot(kt[:, there], ds_scr[turn]) * logit_scale).T.astype(BF16)
        for at in range(group):
            part = slice(at * TILE, (at + 1) * TILE)
            og[here, at * HEAD_DIM : (at + 1) * HEAD_DIM] = out[part]
            og[here, width + at * HEAD_DIM : width + (at + 1) * HEAD_DIM] = dq[part]

    dkv0[:, :HEAD_DIM] = dk[reach * tok :, :] * logit_scale
    dkv0[:, HEAD_DIM:] = dv[reach * tok :, :]
    for lag in range(1, reach + 1):
        there = slice((reach - lag) * tok, (reach - lag + 1) * tok)
        sent[lag - 1][:, :HEAD_DIM] = (dk[there, :] * logit_scale).astype(BF16)
        sent[lag - 1][:, HEAD_DIM:] = dv[there, :].astype(BF16)
    take_rows(size, core, masks, lambda there: og[there, :], *og_halves)


def attend(low, qg, kvs, size):
    rows, cols = qg[0].shape
    tok = len(qg) * rows
    group = cols // (2 * HEAD_DIM)
    reach = len(kvs) - 1
    span = WINDOW + TILE
    wide = group * TILE
    keys = (reach + 1) * tok
    half = jax.ShapeDtypeStruct((tok, 2 * HEAD_DIM), BF16)
    flops = 6 * 2 * tok * group * span * HEAD_DIM
    count = len(qg)
    results = pl.pallas_call(
        functools.partial(attend_body, size, core_mask(), chip_masks(size), reach, tok, group),
        out_shape=[jax.ShapeDtypeStruct((tok // 2, cols), BF16)] * 2
        + [jax.ShapeDtypeStruct((tok, 2 * HEAD_DIM), F32)]
        + [half] * reach,
        in_specs=[VMEM] * (count + 2 + reach),
        out_specs=[VMEM] * (3 + reach),
        scratch_shapes=[
            pltpu.VMEM((tok, cols), BF16),
            pltpu.VMEM((tok, cols), BF16),
            pltpu.VMEM((keys, HEAD_DIM), BF16),
            pltpu.VMEM((keys, 2 * HEAD_DIM), BF16),
            pltpu.VMEM((HEAD_DIM, keys), BF16),
            pltpu.VMEM((HEAD_DIM, keys), BF16),
            pltpu.VMEM((keys, HEAD_DIM), F32),
            pltpu.VMEM((keys, HEAD_DIM), F32),
            pltpu.VMEM((2, span, wide), F32),
            pltpu.VMEM((2, span, wide), BF16),
            pltpu.VMEM((2, span, wide), BF16),
        ],
        compiler_params=pltpu.CompilerParams(vmem_limit_bytes=36 * 1024 * 1024),
        cost_estimate=pl.CostEstimate(
            flops=flops, bytes_accessed=8 * 1024 * 1024, transcendentals=flops // 1536
        ),
        name="attend",
    )(low, *qg, *kvs)
    return results[:2], results[2], results[3:]


def lowest_key(segment_ids, tok, size):
    start = (flat_index() // size) * tok
    padded = jnp.concatenate([jnp.full((WINDOW,), -1, jnp.int32), segment_ids])
    keys = lax.dynamic_slice_in_dim(padded, start, WINDOW + tok, 0)
    queries = lax.dynamic_slice_in_dim(segment_ids, start, tok, 0)
    before = jnp.sum((keys[:, None] < queries[None, :]).astype(jnp.int32), axis=0)
    return jnp.maximum(before, jnp.arange(1, tok + 1, dtype=jnp.int32))[None, :]


def body(query, key, value, grad_out, segment_ids):
    size = key.shape[1] // HEAD_DIM
    rows = query.shape[0]
    tok = size * rows
    reach = WINDOW // tok
    assert reach * tok == WINDOW and device_count() % size == 0
    low = lowest_key(segment_ids, tok, size)

    kv = join(swap_chips(gather_cores((key, value), size), size), size)
    qg = swap_chips(gather_cores((query, grad_out), size), size)
    kvs = [kv] + [shifted(kv, lag * size) for lag in range(1, reach + 1)]

    og, dkv, sent = attend(low, qg, kvs, size)

    back = [shifted(sent[lag - 1], -lag * size) for lag in range(1, reach + 1)]
    dkv, *og = after(dkv, *scatter(*og, size))
    grads = scatter(*combine([dkv] + back, size), size)
    attn_out, grad_query = spread(og, size, 2)
    grad_key, grad_value = spread(grads, size, 2)
    return (attn_out, grad_query, grad_key, grad_value)


def solution(mesh):
    placed = P(("pipe", "tensor"), None)
    return jax.shard_map(
        body,
        mesh=mesh,
        in_specs=(placed, placed, placed, placed, P()),
        out_specs=(placed, placed, placed, placed),
        check_vma=False,
    )
```

```python
import functools

import jax
import jax.numpy as jnp
from jax import lax
from jax.experimental import pallas as pl
from jax.experimental.pallas import tpu as pltpu
from jax.sharding import PartitionSpec as P

HEAD_DIM = 128
WINDOW = 1024
TILE = 128

logit_scale = 168.0 ** (-0.5)
exp2_scale = logit_scale * 1.4426950408889634

SMALL = pltpu.CompilerParams(vmem_limit_bytes=4 * 1024 * 1024)
ANY = pl.BlockSpec(memory_space=pl.ANY)
VMEM = pl.BlockSpec(memory_space=pltpu.VMEM)
F32 = jnp.float32
BF16 = jnp.bfloat16
BOTH = ("pipe", "tensor")


def flat_index():
    return lax.axis_index("pipe") * lax.axis_size("tensor") + lax.axis_index("tensor")


def device_count():
    return lax.axis_size("pipe") * lax.axis_size("tensor")


def swap(value, mask):
    return lax.ppermute(value, BOTH, [(i, i ^ mask) for i in range(device_count())])


def core_mask():
    return lax.axis_size("tensor")


def chip_masks(size):
    masks = [mask for mask in range(size) if not mask & core_mask()]
    return masks[:1] + sorted(masks[1:], key=lambda mask: -mask.bit_count())


def swap_chips(pieces, size):
    return [pieces[0]] + [
        swap(piece, mask) for piece, mask in zip(pieces[1:], chip_masks(size)[1:])
    ]


def hop(value, step):
    count = device_count()
    results = []
    for odd in (0, 1):
        low = [i for i in range(count - step) if (i // step) % 2 == odd]
        pairs = [(i, i + step) for i in low] + [(i + step, i) for i in low]
        results.append(lax.ppermute(value, BOTH, pairs))
    return results


def from_odd(step):
    return lax.rem(lax.div(flat_index(), step), 2) == 1


def partner(size, j):
    return lax.bitwise_xor(lax.rem(flat_index(), size), j)


def place(index, width):
    return pl.ds(pl.multiple_of(index * width, width), width)


def after(value, *others):
    return lax.optimization_barrier((value, *others))


def run_copies(copies, sems):
    started = []
    for at, (source, target) in enumerate(copies):
        copy = pltpu.make_async_copy(source, target, sems.at[at])
        copy.start()
        started.append(copy)
    for copy in started:
        copy.wait()


def small_call(kernel, out_shape, name, *args):
    return pl.pallas_call(
        kernel,
        out_shape=out_shape,
        in_specs=[VMEM] * len(args),
        out_specs=jax.tree.map(lambda _: VMEM, out_shape),
        compiler_params=SMALL,
        name=name,
    )(*args)


def this_core(array, size):
    core = core_mask()
    width = array.shape[1] // size
    shares = [array[:, r * width : (r + 1) * width] for r in range(size)]
    first, second = (
        jnp.concatenate([share for r, share in enumerate(shares) if (r // core) % 2 == at], axis=1)
        for at in range(2)
    )
    return jnp.where((flat_index() // core) % 2 == 0, first, second)


def stack_body(size, core, masks, count, *refs):
    own, got, pieces = refs[:count], refs[count : 2 * count], refs[2 * count :]
    rows = own[0].shape[0]
    for mask, piece in zip(masks, pieces):
        there = partner(size, mask)
        chip = there // (2 * core) * core + lax.rem(there, core)
        start = 0
        for mine, other in zip(own, got):
            width = other.shape[1] // size
            piece[:rows, start : start + width] = mine[:, place(chip, width)]
            piece[rows:, start : start + width] = other[:, place(there, width)]
            start += width


def gather_cores(arrays, got, size):
    masks = chip_masks(size)
    own = [this_core(array, size) for array in arrays]
    cols = sum(array.shape[1] // size for array in arrays)
    piece = jax.ShapeDtypeStruct((2 * arrays[0].shape[0], cols), BF16)
    kernel = functools.partial(stack_body, size, core_mask(), masks, len(arrays))
    return small_call(kernel, [piece] * len(masks), "stack", *own, *got)


def place_rows(size, core, masks, pieces, out):
    for mask, piece in zip(masks, pieces):
        rows = piece.shape[0] // 2
        out[place(partner(size, mask), rows), :] = piece[:rows, :]
        out[place(partner(size, mask ^ core), rows), :] = piece[rows:, :]


def take_rows(size, core, masks, source, own, give):
    rows = own.shape[0] // len(masks)
    for at, mask in enumerate(masks):
        part = slice(at * rows, (at + 1) * rows)
        own[part, :] = source(place(partner(size, mask), rows))
        give[part, :] = source(place(partner(size, mask ^ core), rows))


def join(pieces, size):
    rows, cols = pieces[0].shape
    core, masks = core_mask(), chip_masks(size)

    def kernel(*refs):
        place_rows(size, core, masks, refs[:-1], refs[-1])

    out = jax.ShapeDtypeStruct((len(pieces) * rows, cols), BF16)
    return small_call(kernel, out, "join", *pieces)


def combine(own, backs, size):
    tok, cols = own.shape
    core, masks = core_mask(), chip_masks(size)

    def kernel(*refs):
        def source(there):
            total = refs[0][there, :]
            for lag in range(1, len(backs) + 1):
                first, second = refs[2 * lag - 1], refs[2 * lag]
                odd = from_odd(lag * size)
                total = total + jnp.where(odd, second[there, :], first[there, :]).astype(F32)
            return total.astype(BF16)

        take_rows(size, core, masks, source, *refs[-2:])

    half = jax.ShapeDtypeStruct((tok // 2, cols), BF16)
    return small_call(kernel, [half] * 2, "combine", own, *sum(backs, []))


def pair_body(own, got, *pieces):
    rows = own.shape[0] // len(pieces)
    for at, piece in enumerate(pieces):
        part = slice(at * rows, (at + 1) * rows)
        piece[:rows, :] = own[part, :]
        piece[rows:, :] = got[part, :]


def scatter(own, give, size):
    count = len(chip_masks(size))
    piece = jax.ShapeDtypeStruct((2 * own.shape[0] // count, own.shape[1]), BF16)
    pieces = small_call(pair_body, [piece] * count, "pair", own, swap(give, core_mask()))
    return swap_chips(pieces, size)


def spread_body(size, core, masks, count, *refs):
    pieces, outs, sems = refs[: len(masks)], refs[len(masks) : -1], refs[-1]
    copies = []
    for mask, piece in zip(masks, pieces):
        rows, cols = piece.shape
        rows, width = rows // 2, cols // count
        for flip in (0, 1):
            columns = place(partner(size, mask ^ (core * flip)), width)
            for at, out in enumerate(outs):
                copies.append(
                    (
                        piece.at[flip * rows : (flip + 1) * rows, at * width : (at + 1) * width],
                        out.at[:, columns],
                    )
                )
    run_copies(copies, sems)


def spread(pieces, size, count):
    rows, cols = pieces[0].shape
    return pl.pallas_call(
        functools.partial(spread_body, size, core_mask(), chip_masks(size), count),
        out_shape=[jax.ShapeDtypeStruct((rows // 2, cols // count * size), BF16)] * count,
        in_specs=[ANY] * len(pieces),
        out_specs=[ANY] * count,
        scratch_shapes=[pltpu.SemaphoreType.DMA((size * count,))],
        compiler_params=SMALL,
        name="spread",
    )(*pieces)


def dot(a, b):
    return lax.dot_general(a, b, (((1,), (0,)), ((), ())), preferred_element_type=F32)


def dot_t(a, b):
    return lax.dot_general(a, b, (((1,), (1,)), ((), ())), preferred_element_type=F32)


def fold(x, op):
    parts = [x[at : at + 8] for at in range(0, x.shape[0], 8)]
    while len(parts) > 1:
        parts = [
            op(*parts[at : at + 2]) if at + 1 < len(parts) else parts[at]
            for at in range(0, len(parts), 2)
        ]
    return parts[0]


def attend_body(size, core, masks, reach, tok, group, *refs):
    refs = list(refs)
    take = lambda count: [refs.pop(0) for _ in range(count)]
    (low,), qg_pieces, kvs = take(1), take(len(masks)), take(1 + 2 * reach)
    og_halves, (dkv0,), sent = take(2), take(1), take(reach)
    qg, og, ks, va, kt, vt, dk, dv, s_scr, e_scr, ds_scr = refs
    width = group * HEAD_DIM
    span = WINDOW + TILE
    place_rows(size, core, masks, qg_pieces, qg)
    va[:, HEAD_DIM:] = jnp.where(
        lax.broadcasted_iota(jnp.int32, (va.shape[0], HEAD_DIM), 1) < 2, 1.0, 0.0
    ).astype(BF16)
    for lag in range(reach + 1):
        there = slice((reach - lag) * tok, (reach - lag + 1) * tok)
        if lag:
            odd = from_odd(lag * size)
            kv = jnp.where(odd, kvs[2 * lag - 1][...], kvs[2 * lag][...])
        else:
            kv = kvs[0][...]
        ks[there, :] = kv[:, :HEAD_DIM]
        va[there, :HEAD_DIM] = kv[:, HEAD_DIM:]
        kt[:, there] = kv[:, :HEAD_DIM].T
        vt[:, there] = kv[:, HEAD_DIM:].T
    dk[...] = jnp.zeros_like(dk)
    dv[...] = jnp.zeros_like(dv)
    wide_lane = lax.broadcasted_iota(jnp.int32, (group * TILE, HEAD_DIM), 1)
    row_of = lax.broadcasted_iota(jnp.int32, (TILE, group * TILE), 0)
    col_of = lax.broadcasted_iota(jnp.int32, (TILE, TILE), 1)
    causal = lax.broadcasted_iota(jnp.int32, (TILE, TILE), 0) <= col_of
    causal = jnp.concatenate([causal] * group, axis=1)

    def stacked(base, first):
        here = slice(base, base + TILE)
        return jnp.concatenate(
            [
                qg[here, first + at * HEAD_DIM : first + (at + 1) * HEAD_DIM]
                for at in range(group)
            ],
            axis=0,
        )

    def scores(tile):
        base = tile * TILE
        s_scr[tile % 2] = dot_t(ks[base : base + span, :], stacked(base, 0))

    tiles = tok // TILE
    scores(0)
    for tile in range(tiles):
        base, turn = tile * TILE, tile % 2
        here, there = slice(base, base + TILE), slice(base, base + span)
        low_row = jnp.concatenate([low[:, here]] * group, axis=1) - base
        top = None
        for at in range(0, span, TILE):
            keep = row_of >= low_row - at
            if at == span - TILE:
                keep = keep & causal
            s = jnp.where(keep, s_scr[turn, at : at + TILE, :], -1e30)
            s_scr[turn, at : at + TILE, :] = s
            part = fold(s, jnp.maximum)
            top = part if top is None else jnp.maximum(top, part)
        top = jnp.max(top, axis=0, keepdims=True) * exp2_scale
        if tile + 1 < tiles:
            scores(tile + 1)
        total = None
        for at in range(0, span, TILE):
            e = jnp.exp2(s_scr[turn, at : at + TILE, :] * exp2_scale - top)
            e_scr[turn, at : at + TILE, :] = e.astype(BF16)
            part = fold(e, jnp.add)
            total = part if total is None else total + part
        inv = 1.0 / jnp.sum(total, axis=0, keepdims=True)
        inv = jnp.broadcast_to(inv, (HEAD_DIM, group * TILE)).T
        out = dot(vt[:, there], e_scr[turn]).T * inv
        out = out.astype(BF16)
        g2 = (stacked(base, width).astype(F32) * inv).astype(BF16)
        delta = jnp.sum(g2.astype(F32) * out.astype(F32), axis=1, keepdims=True)
        high = delta.astype(BF16).astype(F32)
        extra = jnp.where(wide_lane == 0, -high, jnp.where(wide_lane == 1, high - delta, 0.0))
        dp = dot_t(va[there, :], jnp.concatenate([g2, extra.astype(BF16)], axis=1))
        dv[there, :] += dot(e_scr[turn], g2)
        for at in range(0, span, TILE):
            part = slice(at, at + TILE)
            ds_scr[turn, part, :] = (e_scr[turn, part, :].astype(F32) * dp[part]).astype(BF16)
        dk[there, :] += dot(ds_scr[turn], stacked(base, 0))
        dq = (dot(kt[:, there], ds_scr[turn]) * logit_scale).T.astype(BF16)
        for at in range(group):
            part = slice(at * TILE, (at + 1) * TILE)
            og[here, at * HEAD_DIM : (at + 1) * HEAD_DIM] = out[part]
            og[here, width + at * HEAD_DIM : width + (at + 1) * HEAD_DIM] = dq[part]

    dkv0[:, :HEAD_DIM] = dk[reach * tok :, :] * logit_scale
    dkv0[:, HEAD_DIM:] = dv[reach * tok :, :]
    for lag in range(1, reach + 1):
        there = slice((reach - lag) * tok, (reach - lag + 1) * tok)
        sent[lag - 1][:, :HEAD_DIM] = (dk[there, :] * logit_scale).astype(BF16)
        sent[lag - 1][:, HEAD_DIM:] = dv[there, :].astype(BF16)
    take_rows(size, core, masks, lambda there: og[there, :], *og_halves)


def attend(low, qg, kv, lags, size):
    rows, cols = qg[0].shape
    tok = len(qg) * rows
    group = cols // (2 * HEAD_DIM)
    reach = len(lags)
    span = WINDOW + TILE
    wide = group * TILE
    keys = (reach + 1) * tok
    half = jax.ShapeDtypeStruct((tok, 2 * HEAD_DIM), BF16)
    flops = 6 * 2 * tok * group * span * HEAD_DIM
    count = len(qg)
    results = pl.pallas_call(
        functools.partial(attend_body, size, core_mask(), chip_masks(size), reach, tok, group),
        out_shape=[jax.ShapeDtypeStruct((tok // 2, cols), BF16)] * 2
        + [jax.ShapeDtypeStruct((tok, 2 * HEAD_DIM), F32)]
        + [half] * reach,
        in_specs=[VMEM] * (count + 2 + 2 * reach),
        out_specs=[VMEM] * (3 + reach),
        scratch_shapes=[
            pltpu.VMEM((tok, cols), BF16),
            pltpu.VMEM((tok, cols), BF16),
            pltpu.VMEM((keys, HEAD_DIM), BF16),
            pltpu.VMEM((keys, 2 * HEAD_DIM), BF16),
            pltpu.VMEM((HEAD_DIM, keys), BF16),
            pltpu.VMEM((HEAD_DIM, keys), BF16),
            pltpu.VMEM((keys, HEAD_DIM), F32),
            pltpu.VMEM((keys, HEAD_DIM), F32),
            pltpu.VMEM((2, span, wide), F32),
            pltpu.VMEM((2, span, wide), BF16),
            pltpu.VMEM((2, span, wide), BF16),
        ],
        compiler_params=pltpu.CompilerParams(vmem_limit_bytes=36 * 1024 * 1024),
        cost_estimate=pl.CostEstimate(
            flops=flops, bytes_accessed=8 * 1024 * 1024, transcendentals=flops // 1536
        ),
        name="attend",
    )(low, *qg, kv, *sum(lags, []))
    return results[:2], results[2], results[3:]


def lowest_key(segment_ids, tok, size):
    start = (flat_index() // size) * tok
    padded = jnp.concatenate([jnp.full((WINDOW,), -1, jnp.int32), segment_ids])
    keys = lax.dynamic_slice_in_dim(padded, start, WINDOW + tok, 0)
    queries = lax.dynamic_slice_in_dim(segment_ids, start, tok, 0)
    before = jnp.sum((keys[:, None] < queries[None, :]).astype(jnp.int32), axis=0)
    return jnp.maximum(before, jnp.arange(1, tok + 1, dtype=jnp.int32))[None, :]


def body(query, key, value, grad_out, segment_ids):
    size = key.shape[1] // HEAD_DIM
    rows = query.shape[0]
    tok = size * rows
    reach = WINDOW // tok
    assert reach * tok == WINDOW and device_count() % size == 0
    low = lowest_key(segment_ids, tok, size)

    got = [swap(array, core_mask()) for array in (key, value, query, grad_out)]
    pieces = list(gather_cores((key, value), got[:2], size))
    pieces[0], query, grad_out = after(pieces[0], query, grad_out)
    kv = join(swap_chips(pieces, size), size)
    lags = [hop(kv, lag * size) for lag in range(1, reach + 1)]
    qg = swap_chips(gather_cores((query, grad_out), got[2:], size), size)

    og, dkv, sent = attend(low, qg, kv, lags, size)

    backs = [hop(sent[lag - 1], lag * size) for lag in range(1, reach + 1)]
    dkv, *og = after(dkv, *scatter(*og, size))
    grads = scatter(*combine(dkv, backs, size), size)
    attn_out, grad_query = spread(og, size, 2)
    grad_key, grad_value = spread(grads, size, 2)
    return (attn_out, grad_query, grad_key, grad_value)


def solution(mesh):
    placed = P(("pipe", "tensor"), None)
    return jax.shard_map(
        body,
        mesh=mesh,
        in_specs=(placed, placed, placed, placed, P()),
        out_specs=(placed, placed, placed, placed),
        check_vma=False,
    )
```

```python
import functools

import jax
import jax.numpy as jnp
from jax import lax
from jax.experimental import pallas as pl
from jax.experimental.pallas import tpu as pltpu
from jax.sharding import PartitionSpec as P

HEAD_DIM = 128
WINDOW = 1024
TILE = 128

logit_scale = 168.0 ** (-0.5)
exp2_scale = logit_scale * 1.4426950408889634

FAR = -(2.0**30)
SMALL = pltpu.CompilerParams(vmem_limit_bytes=4 * 1024 * 1024)
ANY = pl.BlockSpec(memory_space=pl.ANY)
VMEM = pl.BlockSpec(memory_space=pltpu.VMEM)
F32 = jnp.float32
BF16 = jnp.bfloat16
BOTH = ("pipe", "tensor")


def flat_index():
    return lax.axis_index("pipe") * lax.axis_size("tensor") + lax.axis_index("tensor")


def device_count():
    return lax.axis_size("pipe") * lax.axis_size("tensor")


def swap(value, mask):
    return lax.ppermute(value, BOTH, [(i, i ^ mask) for i in range(device_count())])


def core_mask():
    return lax.axis_size("tensor")


def chip_masks(size):
    masks = [mask for mask in range(size) if not mask & core_mask()]
    return masks[:1] + sorted(masks[1:], key=lambda mask: -mask.bit_count())


def swap_chips(pieces, size):
    return [pieces[0]] + [
        swap(piece, mask) for piece, mask in zip(pieces[1:], chip_masks(size)[1:])
    ]


def shifted(value, step):
    count = device_count()
    pairs = [(i, i + step) for i in range(count) if 0 <= i + step < count]
    return lax.ppermute(value, BOTH, pairs)


def partner(size, j):
    return lax.bitwise_xor(lax.rem(flat_index(), size), j)


def place(index, width):
    return pl.ds(pl.multiple_of(index * width, width), width)


def after(value, *others):
    return lax.optimization_barrier((value, *others))


def run_copies(copies, sems):
    started = []
    for at, (source, target) in enumerate(copies):
        copy = pltpu.make_async_copy(source, target, sems.at[at])
        copy.start()
        started.append(copy)
    for copy in started:
        copy.wait()


def small_call(kernel, out_shape, name, *args):
    return pl.pallas_call(
        kernel,
        out_shape=out_shape,
        in_specs=[VMEM] * len(args),
        out_specs=jax.tree.map(lambda _: VMEM, out_shape),
        compiler_params=SMALL,
        name=name,
    )(*args)


def this_core(array, size):
    core = core_mask()
    width = array.shape[1] // size
    shares = [array[:, r * width : (r + 1) * width] for r in range(size)]
    first, second = (
        jnp.concatenate([share for r, share in enumerate(shares) if (r // core) % 2 == at], axis=1)
        for at in range(2)
    )
    return jnp.where((flat_index() // core) % 2 == 0, first, second)


def stack_body(size, core, masks, count, *refs):
    own, got, pieces = refs[:count], refs[count : 2 * count], refs[2 * count :]
    rows = own[0].shape[0]
    for mask, piece in zip(masks, pieces):
        there = partner(size, mask)
        chip = there // (2 * core) * core + lax.rem(there, core)
        start = 0
        for mine, other in zip(own, got):
            width = other.shape[1] // size
            piece[:rows, start : start + width] = mine[:, place(chip, width)]
            piece[rows:, start : start + width] = other[:, place(there, width)]
            start += width


def gather_cores(arrays, got, size):
    masks = chip_masks(size)
    own = [this_core(array, size) for array in arrays]
    cols = sum(array.shape[1] // size for array in arrays)
    piece = jax.ShapeDtypeStruct((2 * arrays[0].shape[0], cols), BF16)
    kernel = functools.partial(stack_body, size, core_mask(), masks, len(arrays))
    return small_call(kernel, [piece] * len(masks), "stack", *own, *got)


def place_rows(size, core, masks, pieces, out):
    for mask, piece in zip(masks, pieces):
        rows = piece.shape[0] // 2
        out[place(partner(size, mask), rows), :] = piece[:rows, :]
        out[place(partner(size, mask ^ core), rows), :] = piece[rows:, :]


def take_rows(size, core, masks, source, pieces):
    for mask, piece in zip(masks, pieces):
        rows = piece.shape[0] // 2
        piece[:rows, :] = source(place(partner(size, mask), rows))
        piece[rows:, :] = source(place(partner(size, mask ^ core), rows))


def join(pieces, size):
    rows, cols = pieces[0].shape
    core, masks = core_mask(), chip_masks(size)

    def kernel(*refs):
        place_rows(size, core, masks, refs[:-1], refs[-1])

    out = jax.ShapeDtypeStruct((len(pieces) * rows, cols), BF16)
    return small_call(kernel, out, "join", *pieces)


def combine(terms, size):
    tok, cols = terms[0].shape
    core, masks = core_mask(), chip_masks(size)

    def kernel(*refs):
        added = refs[: len(terms)]

        def source(there):
            total = added[0][there, :]
            for term in added[1:]:
                total = total + term[there, :].astype(F32)
            return total.astype(BF16)

        take_rows(size, core, masks, source, refs[len(terms) :])

    piece = jax.ShapeDtypeStruct((2 * (tok // size), cols), BF16)
    return small_call(kernel, [piece] * len(masks), "combine", *terms)


def bottom_body(*refs):
    out, start = refs[-1], 0
    for piece in refs[:-1]:
        rows, width = piece.shape[0] // 2, piece.shape[1]
        out[:, start : start + width] = piece[rows:, :]
        start += width


def spread_body(size, core, masks, *refs):
    count = len(masks)
    sets, got, outs, sems = (refs[:count], refs[count : 2 * count]), refs[2 * count], refs[-5:-1], refs[-1]
    copies, start = [], 0
    for which, pieces in enumerate(sets):
        for mask, piece in zip(masks, pieces):
            rows, width = piece.shape[0] // 2, piece.shape[1] // 2
            for at, out in enumerate(outs[2 * which : 2 * which + 2]):
                mine = out.at[:, place(partner(size, mask), width)]
                other = out.at[:, place(partner(size, mask ^ core), width)]
                copies.append((piece.at[:rows, at * width : (at + 1) * width], mine))
                copies.append((got.at[:, start : start + width], other))
                start += width
    run_copies(copies, sems)


def spread_cores(og, grads, size):
    rows = og[0].shape[0] // 2
    widths = [og[0].shape[1] // 2, grads[0].shape[1] // 2]
    give = jax.ShapeDtypeStruct((rows, size * sum(widths)), BF16)
    got = swap(small_call(bottom_body, give, "bottom", *og, *grads), core_mask())
    return pl.pallas_call(
        functools.partial(spread_body, size, core_mask(), chip_masks(size)),
        out_shape=[
            jax.ShapeDtypeStruct((rows, width * size), BF16) for width in widths for _ in range(2)
        ],
        in_specs=[ANY] * (2 * len(og) + 1),
        out_specs=[ANY] * 4,
        scratch_shapes=[pltpu.SemaphoreType.DMA((4 * size,))],
        compiler_params=SMALL,
        name="spread",
    )(*og, *grads, got)


def dot(a, b):
    return lax.dot_general(a, b, (((1,), (0,)), ((), ())), preferred_element_type=F32)


def dot_t(a, b):
    return lax.dot_general(a, b, (((1,), (1,)), ((), ())), preferred_element_type=F32)


def fold(x, op):
    parts = [x[at : at + 8] for at in range(0, x.shape[0], 8)]
    while len(parts) > 1:
        parts = [
            op(*parts[at : at + 2]) if at + 1 < len(parts) else parts[at]
            for at in range(0, len(parts), 2)
        ]
    return parts[0]


def attend_body(size, core, masks, reach, tok, group, *refs):
    refs = list(refs)
    take = lambda count: [refs.pop(0) for _ in range(count)]
    (seg_k, seg_q), qg_pieces, kvs = take(2), take(len(masks)), take(1 + reach)
    og_pieces, (dkv0,), sent = take(len(masks)), take(1), take(reach)
    qg, og, ka, va, kt, vt, dk, dv, s_scr, e_scr, ds_scr = refs
    width = group * HEAD_DIM
    span = WINDOW + TILE
    place_rows(size, core, masks, qg_pieces, qg)
    va[:, HEAD_DIM:] = jnp.where(
        lax.broadcasted_iota(jnp.int32, (va.shape[0], HEAD_DIM), 1) < 2, 1.0, 0.0
    ).astype(BF16)
    ka[:, HEAD_DIM:] = seg_k[...]
    for lag in range(reach + 1):
        there = slice((reach - lag) * tok, (reach - lag + 1) * tok)
        kv = kvs[lag][...]
        ka[there, :HEAD_DIM] = kv[:, :HEAD_DIM]
        va[there, :HEAD_DIM] = kv[:, HEAD_DIM:]
        kt[:, there] = kv[:, :HEAD_DIM].T
        vt[:, there] = kv[:, HEAD_DIM:].T
    wide_lane = lax.broadcasted_iota(jnp.int32, (group * TILE, HEAD_DIM), 1)
    row_of = lax.broadcasted_iota(jnp.int32, (TILE, TILE), 0)
    col_of = lax.broadcasted_iota(jnp.int32, (TILE, TILE), 1)
    causal = jnp.concatenate([row_of <= col_of] * group, axis=1)

    def stacked(base, first):
        here = slice(base, base + TILE)
        return jnp.concatenate(
            [
                qg[here, first + at * HEAD_DIM : first + (at + 1) * HEAD_DIM]
                for at in range(group)
            ],
            axis=0,
        )

    def scores(tile):
        base = tile * TILE
        mine = jnp.concatenate([seg_q[base : base + TILE, :]] * group, axis=0)
        wide = jnp.concatenate([stacked(base, 0), mine], axis=1)
        s_scr[tile % 2] = dot_t(ka[base : base + span, :], wide)

    def add(target, base, value):
        fresh = base + (WINDOW if base else 0)
        if base:
            target[base:fresh, :] += value[:WINDOW]
        target[fresh : base + span, :] = value[fresh - base :]

    tiles = tok // TILE
    scores(0)
    for tile in range(tiles):
        base, turn = tile * TILE, tile % 2
        here, there = slice(base, base + TILE), slice(base, base + span)
        for at, keep in ((0, ~causal), (WINDOW, causal)):
            part = slice(at, at + TILE)
            s_scr[turn, part, :] = jnp.where(keep, s_scr[turn, part, :], FAR)
        top = None
        for at in range(0, span, TILE):
            part = fold(s_scr[turn, at : at + TILE, :], jnp.maximum)
            top = part if top is None else jnp.maximum(top, part)
        top = jnp.max(top, axis=0, keepdims=True) * exp2_scale
        if tile + 1 < tiles:
            scores(tile + 1)
        total = None
        for at in range(0, span, TILE):
            e = jnp.exp2(s_scr[turn, at : at + TILE, :] * exp2_scale - top)
            e_scr[turn, at : at + TILE, :] = e.astype(BF16)
            part = fold(e, jnp.add)
            total = part if total is None else total + part
        inv = 1.0 / jnp.sum(total, axis=0, keepdims=True)
        inv = jnp.broadcast_to(inv, (HEAD_DIM, group * TILE)).T
        out = dot(vt[:, there], e_scr[turn]).T * inv
        out = out.astype(BF16)
        g2 = (stacked(base, width).astype(F32) * inv).astype(BF16)
        delta = jnp.sum(g2.astype(F32) * out.astype(F32), axis=1, keepdims=True)
        high = delta.astype(BF16).astype(F32)
        extra = jnp.where(wide_lane == 0, -high, jnp.where(wide_lane == 1, high - delta, 0.0))
        dp = dot_t(va[there, :], jnp.concatenate([g2, extra.astype(BF16)], axis=1))
        add(dv, base, dot(e_scr[turn], g2))
        for at in range(0, span, TILE):
            part = slice(at, at + TILE)
            ds_scr[turn, part, :] = (e_scr[turn, part, :].astype(F32) * dp[part]).astype(BF16)
        add(dk, base, dot(ds_scr[turn], stacked(base, 0)))
        dq = (dot(kt[:, there], ds_scr[turn]) * logit_scale).T.astype(BF16)
        for at in range(group):
            part = slice(at * TILE, (at + 1) * TILE)
            og[here, at * HEAD_DIM : (at + 1) * HEAD_DIM] = out[part]
            og[here, width + at * HEAD_DIM : width + (at + 1) * HEAD_DIM] = dq[part]

    dkv0[:, :HEAD_DIM] = dk[reach * tok :, :] * logit_scale
    dkv0[:, HEAD_DIM:] = dv[reach * tok :, :]
    for lag in range(1, reach + 1):
        there = slice((reach - lag) * tok, (reach - lag + 1) * tok)
        sent[lag - 1][:, :HEAD_DIM] = (dk[there, :] * logit_scale).astype(BF16)
        sent[lag - 1][:, HEAD_DIM:] = dv[there, :].astype(BF16)
    take_rows(size, core, masks, lambda there: og[there, :], og_pieces)


def attend(documents, qg, kv, lags, size):
    rows, cols = qg[0].shape
    tok = len(qg) * rows
    group = cols // (2 * HEAD_DIM)
    reach = len(lags)
    span = WINDOW + TILE
    wide = group * TILE
    keys = (reach + 1) * tok
    half = jax.ShapeDtypeStruct((tok, 2 * HEAD_DIM), BF16)
    flops = 6 * 2 * tok * group * span * HEAD_DIM
    count = len(qg)
    results = pl.pallas_call(
        functools.partial(attend_body, size, core_mask(), chip_masks(size), reach, tok, group),
        out_shape=[jax.ShapeDtypeStruct((rows, cols), BF16)] * count
        + [jax.ShapeDtypeStruct((tok, 2 * HEAD_DIM), F32)]
        + [half] * reach,
        in_specs=[VMEM] * (count + 3 + reach),
        out_specs=[VMEM] * (count + 1 + reach),
        scratch_shapes=[
            pltpu.VMEM((tok, cols), BF16),
            pltpu.VMEM((tok, cols), BF16),
            pltpu.VMEM((keys, 2 * HEAD_DIM), BF16),
            pltpu.VMEM((keys, 2 * HEAD_DIM), BF16),
            pltpu.VMEM((HEAD_DIM, keys), BF16),
            pltpu.VMEM((HEAD_DIM, keys), BF16),
            pltpu.VMEM((keys, HEAD_DIM), F32),
            pltpu.VMEM((keys, HEAD_DIM), F32),
            pltpu.VMEM((2, span, wide), F32),
            pltpu.VMEM((2, span, wide), BF16),
            pltpu.VMEM((2, span, wide), BF16),
        ],
        compiler_params=pltpu.CompilerParams(vmem_limit_bytes=36 * 1024 * 1024),
        cost_estimate=pl.CostEstimate(
            flops=flops, bytes_accessed=8 * 1024 * 1024, transcendentals=flops // 1536
        ),
        name="attend",
    )(*documents, *qg, kv, *lags)
    return results[:count], results[count], results[count + 1 :]


def document_columns(segment_ids, tok, size):
    start = (flat_index() // size) * tok
    padded = jnp.concatenate([jnp.full((WINDOW,), -1, jnp.int32), segment_ids])
    keys = lax.dynamic_slice_in_dim(padded, start, WINDOW + tok, 0)
    queries = lax.dynamic_slice_in_dim(segment_ids, start, tok, 0)
    number = jnp.arange(HEAD_DIM, dtype=jnp.int32)[None, :]
    return (
        jnp.where(keys[:, None] == number, 0.0, FAR).astype(BF16),
        jnp.where(queries[:, None] == number, 1.0, 0.0).astype(BF16),
    )


def body(query, key, value, grad_out, segment_ids):
    size = key.shape[1] // HEAD_DIM
    rows = query.shape[0]
    tok = size * rows
    reach = WINDOW // tok
    assert reach * tok == WINDOW and device_count() % size == 0
    documents = document_columns(segment_ids, tok, size)

    got = [swap(array, core_mask()) for array in (key, value, query, grad_out)]
    pieces = list(gather_cores((key, value), got[:2], size))
    pieces[0], query, grad_out = after(pieces[0], query, grad_out)
    kv = join(swap_chips(pieces, size), size)
    lags = [shifted(kv, lag * size) for lag in range(1, reach + 1)]
    qg = swap_chips(gather_cores((query, grad_out), got[2:], size), size)

    og, dkv, sent = attend(documents, qg, kv, lags, size)

    backs = [shifted(sent[lag - 1], -lag * size) for lag in range(1, reach + 1)]
    og = swap_chips(og, size)
    grads = swap_chips(combine([dkv, *backs], size), size)
    return tuple(spread_cores(og, grads, size))


def solution(mesh):
    placed = P(("pipe", "tensor"), None)
    return jax.shard_map(
        body,
        mesh=mesh,
        in_specs=(placed, placed, placed, placed, P()),
        out_specs=(placed, placed, placed, placed),
        check_vma=False,
    )
```

```python
import functools

import jax
import jax.numpy as jnp
from jax import lax
from jax.experimental import pallas as pl
from jax.experimental.pallas import tpu as pltpu
from jax.sharding import PartitionSpec as P

HEAD_DIM = 128
WINDOW = 1024
TILE = 128

logit_scale = 168.0 ** (-0.5)
exp2_scale = logit_scale * 1.4426950408889634

FAR = -(2.0**30)
SMALL = pltpu.CompilerParams(vmem_limit_bytes=4 * 1024 * 1024)
ANY = pl.BlockSpec(memory_space=pl.ANY)
VMEM = pl.BlockSpec(memory_space=pltpu.VMEM)
F32 = jnp.float32
BF16 = jnp.bfloat16
BOTH = ("pipe", "tensor")


def flat_index():
    return lax.axis_index("pipe") * lax.axis_size("tensor") + lax.axis_index("tensor")


def device_count():
    return lax.axis_size("pipe") * lax.axis_size("tensor")


def swap(value, mask):
    return lax.ppermute(value, BOTH, [(i, i ^ mask) for i in range(device_count())])


def core_mask():
    return lax.axis_size("tensor")


def chip_masks(size):
    return [mask for mask in range(size) if not mask & core_mask()]


def swap_chips(pieces, size):
    return [pieces[0]] + [
        swap(piece, mask) for piece, mask in zip(pieces[1:], chip_masks(size)[1:])
    ]


def shifted(value, step):
    count = device_count()
    pairs = [(i, i + step) for i in range(count) if 0 <= i + step < count]
    return lax.ppermute(value, BOTH, pairs)


def partner(size, j):
    return lax.bitwise_xor(lax.rem(flat_index(), size), j)


def place(index, width):
    return pl.ds(pl.multiple_of(index * width, width), width)


def after(value, *others):
    return lax.optimization_barrier((value, *others))


def run_copies(copies, sems):
    started = []
    for at, (source, target) in enumerate(copies):
        copy = pltpu.make_async_copy(source, target, sems.at[at])
        copy.start()
        started.append(copy)
    for copy in started:
        copy.wait()


def small_call(kernel, out_shape, name, *args):
    return pl.pallas_call(
        kernel,
        out_shape=out_shape,
        in_specs=[VMEM] * len(args),
        out_specs=jax.tree.map(lambda _: VMEM, out_shape),
        compiler_params=SMALL,
        name=name,
    )(*args)


def this_core(array, size):
    core = core_mask()
    width = array.shape[1] // size
    shares = [array[:, r * width : (r + 1) * width] for r in range(size)]
    first, second = (
        jnp.concatenate([share for r, share in enumerate(shares) if (r // core) % 2 == at], axis=1)
        for at in range(2)
    )
    return jnp.where((flat_index() // core) % 2 == 0, first, second)


def stack_body(size, core, masks, count, *refs):
    own, got, pieces = refs[:count], refs[count : 2 * count], refs[2 * count :]
    rows = own[0].shape[0]
    for mask, piece in zip(masks, pieces):
        there = partner(size, mask)
        chip = there // (2 * core) * core + lax.rem(there, core)
        start = 0
        for mine, other in zip(own, got):
            width = other.shape[1] // size
            piece[:rows, start : start + width] = mine[:, place(chip, width)]
            piece[rows:, start : start + width] = other[:, place(there, width)]
            start += width


def gather_cores(arrays, got, size):
    masks = chip_masks(size)
    own = [this_core(array, size) for array in arrays]
    cols = sum(array.shape[1] // size for array in arrays)
    piece = jax.ShapeDtypeStruct((2 * arrays[0].shape[0], cols), BF16)
    kernel = functools.partial(stack_body, size, core_mask(), masks, len(arrays))
    return small_call(kernel, [piece] * len(masks), "stack", *own, *got)


def place_rows(size, core, masks, pieces, out):
    for mask, piece in zip(masks, pieces):
        rows = piece.shape[0] // 2
        out[place(partner(size, mask), rows), :] = piece[:rows, :]
        out[place(partner(size, mask ^ core), rows), :] = piece[rows:, :]


def take_rows(size, core, masks, source, pieces):
    for mask, piece in zip(masks, pieces):
        rows = piece.shape[0] // 2
        piece[:rows, :] = source(place(partner(size, mask), rows))
        piece[rows:, :] = source(place(partner(size, mask ^ core), rows))


def join(pieces, size):
    rows, cols = pieces[0].shape
    core, masks = core_mask(), chip_masks(size)

    def kernel(*refs):
        place_rows(size, core, masks, refs[:-1], refs[-1])

    out = jax.ShapeDtypeStruct((len(pieces) * rows, cols), BF16)
    return small_call(kernel, out, "join", *pieces)


def combine(terms, size):
    tok, cols = terms[0].shape
    core, masks = core_mask(), chip_masks(size)

    def kernel(*refs):
        added = refs[: len(terms)]

        def source(there):
            total = added[0][there, :]
            for term in added[1:]:
                total = total + term[there, :].astype(F32)
            return total.astype(BF16)

        take_rows(size, core, masks, source, refs[len(terms) :])

    piece = jax.ShapeDtypeStruct((2 * (tok // size), cols), BF16)
    return small_call(kernel, [piece] * len(masks), "combine", *terms)


def bottom_body(*refs):
    out, start = refs[-1], 0
    for piece in refs[:-1]:
        rows, width = piece.shape[0] // 2, piece.shape[1]
        out[:, start : start + width] = piece[rows:, :]
        start += width


def spread_body(size, core, masks, counts, *refs):
    refs = list(refs)
    take = lambda count: [refs.pop(0) for _ in range(count)]
    sets = [take(len(masks)) for _ in counts]
    (got,), sets_out, (sems,) = take(1), [take(count) for count in counts], take(1)
    copies, start = [], 0
    for pieces, outs in zip(sets, sets_out):
        for mask, piece in zip(masks, pieces):
            rows, width = piece.shape[0] // 2, piece.shape[1] // len(outs)
            for at, out in enumerate(outs):
                mine = out.at[:, place(partner(size, mask), width)]
                other = out.at[:, place(partner(size, mask ^ core), width)]
                copies.append((piece.at[:rows, at * width : (at + 1) * width], mine))
                copies.append((got.at[:, start : start + width], other))
                start += width
    run_copies(copies, sems)


def spread_cores(sets, counts, size):
    pieces = [piece for part in sets for piece in part]
    rows = pieces[0].shape[0] // 2
    give = jax.ShapeDtypeStruct((rows, sum(piece.shape[1] for piece in pieces)), BF16)
    got = swap(small_call(bottom_body, give, "bottom", *pieces), core_mask())
    widths = [part[0].shape[1] // count for part, count in zip(sets, counts) for _ in range(count)]
    return pl.pallas_call(
        functools.partial(spread_body, size, core_mask(), chip_masks(size), counts),
        out_shape=[jax.ShapeDtypeStruct((rows, width * size), BF16) for width in widths],
        in_specs=[ANY] * (len(pieces) + 1),
        out_specs=[ANY] * len(widths),
        scratch_shapes=[pltpu.SemaphoreType.DMA((len(widths) * size,))],
        compiler_params=SMALL,
        name="spread",
    )(*pieces, got)


def dot(a, b):
    return lax.dot_general(a, b, (((1,), (0,)), ((), ())), preferred_element_type=F32)


def dot_t(a, b):
    return lax.dot_general(a, b, (((1,), (1,)), ((), ())), preferred_element_type=F32)


def fold(x, op):
    parts = [x[at : at + 8] for at in range(0, x.shape[0], 8)]
    while len(parts) > 1:
        parts = [
            op(*parts[at : at + 2]) if at + 1 < len(parts) else parts[at]
            for at in range(0, len(parts), 2)
        ]
    return parts[0]


def taker(refs):
    refs = list(refs)
    return lambda count: [refs.pop(0) for _ in range(count)]


def stacked(rows, base, group, first=0):
    parts = [slice(first + at * HEAD_DIM, first + (at + 1) * HEAD_DIM) for at in range(group)]
    return jnp.concatenate([rows[base : base + TILE, part] for part in parts], axis=0)


def unstacked(rows, base, group, value):
    for at in range(group):
        part = slice(at * TILE, (at + 1) * TILE)
        rows[base : base + TILE, at * HEAD_DIM : (at + 1) * HEAD_DIM] = value[part]


def set_values(va, values):
    lane = lax.broadcasted_iota(jnp.int32, values.shape, 1)
    va[:, :HEAD_DIM] = values
    va[:, HEAD_DIM:] = jnp.where(lane < 2, 1.0, 0.0).astype(BF16)


def add_rows(target, start, old, value):
    if old:
        target[start : start + old, :] += value[:old]
    if old < value.shape[0]:
        target[start + old : start + value.shape[0], :] = value[old:]


def score_gradients(ds_scr, e, dp):
    for at in range(0, e.shape[0], TILE):
        part = slice(at, at + TILE)
        ds_scr[part, :] = (e[part, :].astype(F32) * dp[part]).astype(BF16)


def own_rows(tile):
    start = tile * (tile + 1) // 2 * TILE
    return slice(start, start + (tile + 1) * TILE)


def forward_body(size, core, masks, reach, tok, group, *refs):
    take = taker(refs)
    (seg_k, seg_q), qg_pieces, kvs = take(2), take(len(masks)), take(1 + reach)
    out_pieces, sent, (e_own, g_own, dq_part) = take(len(masks)), take(reach), take(3)
    qg, outs, ka, va, kt, vt, dk, dv, s_scr, e_scr, ds_scr = take(11)
    width = group * HEAD_DIM
    span, wide = WINDOW + TILE, group * TILE
    place_rows(size, core, masks, qg_pieces, qg)
    ka[:, HEAD_DIM:] = seg_k[...]
    for lag in range(reach + 1):
        there = slice((reach - lag) * tok, (reach - lag + 1) * tok)
        kv = kvs[lag][...]
        ka[there, :HEAD_DIM] = kv[:, :HEAD_DIM]
        vt[:, there] = kv[:, HEAD_DIM:].T
        if lag:
            kt[:, there] = kv[:, :HEAD_DIM].T
            set_values(va.at[there, :], kv[:, HEAD_DIM:])
    wide_lane = lax.broadcasted_iota(jnp.int32, (wide, HEAD_DIM), 1)
    row_of = lax.broadcasted_iota(jnp.int32, (TILE, TILE), 0)
    col_of = lax.broadcasted_iota(jnp.int32, (TILE, TILE), 1)
    causal = jnp.concatenate([row_of <= col_of] * group, axis=1)

    def scores(tile):
        base = tile * TILE
        mine = jnp.concatenate([seg_q[base : base + TILE, :]] * group, axis=0)
        queries = jnp.concatenate([stacked(qg, base, group), mine], axis=1)
        s_scr[tile % 2] = dot_t(ka[base : base + span, :], queries)

    tiles = tok // TILE
    scores(0)
    for tile in range(tiles):
        base, turn = tile * TILE, tile % 2
        early = WINDOW - base
        for at, keep in ((0, ~causal), (WINDOW, causal)):
            part = slice(at, at + TILE)
            s_scr[turn, part, :] = jnp.where(keep, s_scr[turn, part, :], FAR)
        top = None
        for at in range(0, span, TILE):
            part = fold(s_scr[turn, at : at + TILE, :], jnp.maximum)
            top = part if top is None else jnp.maximum(top, part)
        top = jnp.max(top, axis=0, keepdims=True) * exp2_scale
        if tile + 1 < tiles:
            scores(tile + 1)
        e_mine = e_own.at[own_rows(tile), :]
        total = None
        for at in range(0, span, TILE):
            e = jnp.exp2(s_scr[turn, at : at + TILE, :] * exp2_scale - top)
            if at < early:
                e_scr[turn, at : at + TILE, :] = e.astype(BF16)
            else:
                e_mine[at - early : at - early + TILE, :] = e.astype(BF16)
            part = fold(e, jnp.add)
            total = part if total is None else total + part
        inv = 1.0 / jnp.sum(total, axis=0, keepdims=True)
        inv = jnp.broadcast_to(inv, (HEAD_DIM, wide)).T
        e_early = e_scr[turn, :early, :]
        out = dot(vt[:, base:WINDOW], e_early)
        out = out + dot(vt[:, WINDOW : base + span], e_mine[...])
        out = (out.T * inv).astype(BF16)
        unstacked(outs, base, group, out)
        g2 = (stacked(qg, base, group, width).astype(F32) * inv).astype(BF16)
        delta = jnp.sum(g2.astype(F32) * out.astype(F32), axis=1, keepdims=True)
        high = delta.astype(BF16).astype(F32)
        extra = jnp.where(wide_lane == 0, -high, jnp.where(wide_lane == 1, high - delta, 0.0))
        g_wide = jnp.concatenate([g2, extra.astype(BF16)], axis=1)
        g_own[tile * wide : (tile + 1) * wide, :] = g_wide
        dp = dot_t(va[base:WINDOW, :], g_wide)
        old = early if tile else 0
        add_rows(dv, base, old, dot(e_early, g2))
        score_gradients(ds_scr.at[turn, :early, :], e_early, dp)
        ds = ds_scr[turn, :early, :]
        add_rows(dk, base, old, dot(ds, stacked(qg, base, group)))
        dq_part[:, tile * wide : (tile + 1) * wide] = dot(kt[:, base:WINDOW], ds)

    for lag in range(1, reach + 1):
        there = slice((reach - lag) * tok, (reach - lag + 1) * tok)
        sent[lag - 1][:, :HEAD_DIM] = (dk[there, :] * logit_scale).astype(BF16)
        sent[lag - 1][:, HEAD_DIM:] = dv[there, :].astype(BF16)
    take_rows(size, core, masks, lambda there: outs[there, :], out_pieces)


def backward_body(size, core, masks, tok, group, *refs):
    take = taker(refs)
    qg_pieces, (kv, e_own, g_own, dq_part) = take(len(masks)), take(4)
    dq_pieces, (dkv,) = take(len(masks)), take(1)
    qg, dqs, va, kt, dk, dv, ds_scr = take(7)
    wide = group * TILE
    place_rows(size, core, masks, qg_pieces, qg)
    kt[...] = kv[:, :HEAD_DIM].T
    set_values(va, kv[:, HEAD_DIM:])
    for tile in range(tok // TILE):
        base, turn = tile * TILE, tile % 2
        count = base + TILE
        columns = slice(tile * wide, (tile + 1) * wide)
        e = e_own[own_rows(tile), :]
        dp = dot_t(va[:count, :], g_own[columns, :])
        add_rows(dv, 0, base, dot(e, g_own[columns, :HEAD_DIM]))
        score_gradients(ds_scr.at[turn, :count, :], e, dp)
        ds = ds_scr[turn, :count, :]
        add_rows(dk, 0, base, dot(ds, stacked(qg, base, group)))
        dq = (dq_part[:, columns] + dot(kt[:, :count], ds)) * logit_scale
        unstacked(dqs, base, group, dq.T.astype(BF16))
    dkv[:, :HEAD_DIM] = dk[...] * logit_scale
    dkv[:, HEAD_DIM:] = dv[...]
    take_rows(size, core, masks, lambda there: dqs[there, :], dq_pieces)


def attend_call(kernel, out_shape, scratch_shapes, flops, name, *args):
    return pl.pallas_call(
        kernel,
        out_shape=out_shape,
        in_specs=[VMEM] * len(args),
        out_specs=[VMEM] * len(out_shape),
        scratch_shapes=scratch_shapes,
        compiler_params=pltpu.CompilerParams(vmem_limit_bytes=24 * 1024 * 1024),
        cost_estimate=pl.CostEstimate(
            flops=flops, bytes_accessed=8 * 1024 * 1024, transcendentals=0
        ),
        name=name,
    )(*args)


def forward(documents, qg, kv, lags, size):
    rows, cols = qg[0].shape
    tok, count, reach = len(qg) * rows, len(qg), len(lags)
    group = cols // (2 * HEAD_DIM)
    span, wide, keys, tiles = WINDOW + TILE, group * TILE, (reach + 1) * tok, tok // TILE
    half = jax.ShapeDtypeStruct((tok, 2 * HEAD_DIM), BF16)
    out_shape = [jax.ShapeDtypeStruct((rows, cols // 2), BF16)] * count + [half] * reach
    out_shape += [
        jax.ShapeDtypeStruct((own_rows(tiles - 1).stop, wide), BF16),
        jax.ShapeDtypeStruct((tiles * wide, 2 * HEAD_DIM), BF16),
        jax.ShapeDtypeStruct((HEAD_DIM, tiles * wide), F32),
    ]
    scratch = [
        pltpu.VMEM((tok, cols), BF16),
        pltpu.VMEM((tok, cols // 2), BF16),
        pltpu.VMEM((keys, 2 * HEAD_DIM), BF16),
        pltpu.VMEM((WINDOW, 2 * HEAD_DIM), BF16),
        pltpu.VMEM((HEAD_DIM, WINDOW), BF16),
        pltpu.VMEM((HEAD_DIM, keys), BF16),
        pltpu.VMEM((WINDOW, HEAD_DIM), F32),
        pltpu.VMEM((WINDOW, HEAD_DIM), F32),
        pltpu.VMEM((2, span, wide), F32),
        pltpu.VMEM((2, WINDOW, wide), BF16),
        pltpu.VMEM((2, WINDOW, wide), BF16),
    ]
    results = attend_call(
        functools.partial(
            forward_body, size, core_mask(), chip_masks(size), reach, tok, group
        ),
        out_shape,
        scratch,
        8 * tok * group * span * HEAD_DIM,
        "forward",
        *documents,
        *qg,
        kv,
        *lags,
    )
    return results[:count], results[count : count + reach], results[count + reach :]


def backward(qg, kv, carried, size):
    rows, cols = qg[0].shape
    tok, count = len(qg) * rows, len(qg)
    group = cols // (2 * HEAD_DIM)
    wide = group * TILE
    results = attend_call(
        functools.partial(backward_body, size, core_mask(), chip_masks(size), tok, group),
        [jax.ShapeDtypeStruct((rows, cols // 2), BF16)] * count
        + [jax.ShapeDtypeStruct((tok, 2 * HEAD_DIM), F32)],
        [
            pltpu.VMEM((tok, cols), BF16),
            pltpu.VMEM((tok, cols // 2), BF16),
            pltpu.VMEM((tok, 2 * HEAD_DIM), BF16),
            pltpu.VMEM((HEAD_DIM, tok), BF16),
            pltpu.VMEM((tok, HEAD_DIM), F32),
            pltpu.VMEM((tok, HEAD_DIM), F32),
            pltpu.VMEM((2, tok, wide), BF16),
        ],
        4 * tok * group * (WINDOW + TILE) * HEAD_DIM,
        "backward",
        *qg,
        kv,
        *carried,
    )
    return results[:count], results[count]


def document_columns(segment_ids, tok, size):
    start = (flat_index() // size) * tok
    padded = jnp.concatenate([jnp.full((WINDOW,), -1, jnp.int32), segment_ids])
    keys = lax.dynamic_slice_in_dim(padded, start, WINDOW + tok, 0)
    queries = lax.dynamic_slice_in_dim(segment_ids, start, tok, 0)
    number = jnp.arange(HEAD_DIM, dtype=jnp.int32)[None, :]
    return (
        jnp.where(keys[:, None] == number, 0.0, FAR).astype(BF16),
        jnp.where(queries[:, None] == number, 1.0, 0.0).astype(BF16),
    )


def body(query, key, value, grad_out, segment_ids):
    size = key.shape[1] // HEAD_DIM
    rows = query.shape[0]
    tok = size * rows
    reach = WINDOW // tok
    assert reach * tok == WINDOW and device_count() % size == 0
    documents = document_columns(segment_ids, tok, size)

    got = [swap(array, core_mask()) for array in (key, value, query, grad_out)]
    pieces = list(gather_cores((key, value), got[:2], size))
    pieces[0], query, grad_out = after(pieces[0], query, grad_out)
    kv = join(swap_chips(pieces, size), size)
    lags = [shifted(kv, lag * size) for lag in range(1, reach + 1)]
    qg = swap_chips(gather_cores((query, grad_out), got[2:], size), size)

    out, sent, carried = forward(documents, qg, kv, lags, size)
    backs = [shifted(sent[lag - 1], -lag * size) for lag in range(1, reach + 1)]
    out = swap_chips(out, size)
    grad_q, dkv = backward(qg, kv, carried, size)
    both = after(*out, *grad_q)
    out, grad_q = both[: len(out)], both[len(out) :]
    grad_q = swap_chips(grad_q, size)
    grads = swap_chips(combine([dkv, *backs], size), size)
    return tuple(spread_cores([out, grad_q, grads], (1, 1, 2), size))


def solution(mesh):
    placed = P(("pipe", "tensor"), None)
    return jax.shard_map(
        body,
        mesh=mesh,
        in_specs=(placed, placed, placed, placed, P()),
        out_specs=(placed, placed, placed, placed),
        check_vma=False,
    )
```

```python
import functools

import jax
import jax.numpy as jnp
from jax import lax
from jax.experimental import pallas as pl
from jax.experimental.pallas import tpu as pltpu
from jax.sharding import PartitionSpec as P

HEAD_DIM = 128
WINDOW = 1024
TILE = 128

logit_scale = 168.0 ** (-0.5)
exp2_scale = logit_scale * 1.4426950408889634

FAR = -(2.0**30)
SMALL = pltpu.CompilerParams(vmem_limit_bytes=4 * 1024 * 1024)
ANY = pl.BlockSpec(memory_space=pl.ANY)
VMEM = pl.BlockSpec(memory_space=pltpu.VMEM)
F32 = jnp.float32
BF16 = jnp.bfloat16
BOTH = ("pipe", "tensor")


def flat_index():
    return lax.axis_index("pipe") * lax.axis_size("tensor") + lax.axis_index("tensor")


def device_count():
    return lax.axis_size("pipe") * lax.axis_size("tensor")


def swap(value, mask):
    return lax.ppermute(value, BOTH, [(i, i ^ mask) for i in range(device_count())])


def core_mask():
    return lax.axis_size("tensor")


def chip_masks(size):
    return [mask for mask in range(size) if not mask & core_mask()]


def swap_chips(pieces, size):
    return [pieces[0]] + [
        swap(piece, mask) for piece, mask in zip(pieces[1:], chip_masks(size)[1:])
    ]


def shifted(value, step):
    count = device_count()
    pairs = [(i, i + step) for i in range(count) if 0 <= i + step < count]
    return lax.ppermute(value, BOTH, pairs)


def partner(size, j):
    return lax.bitwise_xor(lax.rem(flat_index(), size), j)


def place(index, width):
    return pl.ds(pl.multiple_of(index * width, width), width)


def after(value, *others):
    return lax.optimization_barrier((value, *others))


def run_copies(copies, sems):
    started = []
    for at, (source, target) in enumerate(copies):
        copy = pltpu.make_async_copy(source, target, sems.at[at])
        copy.start()
        started.append(copy)
    for copy in started:
        copy.wait()


def small_call(kernel, out_shape, name, *args):
    return pl.pallas_call(
        kernel,
        out_shape=out_shape,
        in_specs=[VMEM] * len(args),
        out_specs=jax.tree.map(lambda _: VMEM, out_shape),
        compiler_params=SMALL,
        name=name,
    )(*args)


def this_core(array, size):
    core = core_mask()
    width = array.shape[1] // size
    shares = [array[:, r * width : (r + 1) * width] for r in range(size)]
    first, second = (
        jnp.concatenate([share for r, share in enumerate(shares) if (r // core) % 2 == at], axis=1)
        for at in range(2)
    )
    return jnp.where((flat_index() // core) % 2 == 0, first, second)


def stack_body(size, core, masks, count, *refs):
    own, got, pieces = refs[:count], refs[count : 2 * count], refs[2 * count :]
    rows = own[0].shape[0]
    for mask, piece in zip(masks, pieces):
        there = partner(size, mask)
        chip = there // (2 * core) * core + lax.rem(there, core)
        start = 0
        for mine, other in zip(own, got):
            width = other.shape[1] // size
            piece[:rows, start : start + width] = mine[:, place(chip, width)]
            piece[rows:, start : start + width] = other[:, place(there, width)]
            start += width


def gather_cores(arrays, got, size):
    masks = chip_masks(size)
    own = [this_core(array, size) for array in arrays]
    cols = sum(array.shape[1] // size for array in arrays)
    piece = jax.ShapeDtypeStruct((2 * arrays[0].shape[0], cols), BF16)
    kernel = functools.partial(stack_body, size, core_mask(), masks, len(arrays))
    return small_call(kernel, [piece] * len(masks), "stack", *own, *got)


def place_rows(size, core, masks, pieces, out):
    for mask, piece in zip(masks, pieces):
        rows = piece.shape[0] // 2
        out[place(partner(size, mask), rows), :] = piece[:rows, :]
        out[place(partner(size, mask ^ core), rows), :] = piece[rows:, :]


def take_rows(size, core, masks, source, pieces):
    for mask, piece in zip(masks, pieces):
        rows = piece.shape[0] // 2
        piece[:rows, :] = source(place(partner(size, mask), rows))
        piece[rows:, :] = source(place(partner(size, mask ^ core), rows))


def join(pieces, size):
    rows, cols = pieces[0].shape
    core, masks = core_mask(), chip_masks(size)

    def kernel(*refs):
        place_rows(size, core, masks, refs[:-1], refs[-1])

    out = jax.ShapeDtypeStruct((len(pieces) * rows, cols), BF16)
    return small_call(kernel, out, "join", *pieces)


def combine(terms, size):
    tok, cols = terms[0].shape
    core, masks = core_mask(), chip_masks(size)

    def kernel(*refs):
        added = refs[: len(terms)]

        def source(there):
            total = added[0][there, :]
            for term in added[1:]:
                total = total + term[there, :].astype(F32)
            return total.astype(BF16)

        take_rows(size, core, masks, source, refs[len(terms) :])

    piece = jax.ShapeDtypeStruct((2 * (tok // size), cols), BF16)
    return small_call(kernel, [piece] * len(masks), "combine", *terms)


def bottom_body(*refs):
    out, start = refs[-1], 0
    for piece in refs[:-1]:
        rows, width = piece.shape[0] // 2, piece.shape[1]
        out[:, start : start + width] = piece[rows:, :]
        start += width


def spread_body(size, core, masks, counts, *refs):
    refs = list(refs)
    take = lambda count: [refs.pop(0) for _ in range(count)]
    sets = [take(len(masks)) for _ in counts]
    (got,), sets_out, (sems,) = take(1), [take(count) for count in counts], take(1)
    copies, start = [], 0
    for pieces, outs in zip(sets, sets_out):
        for mask, piece in zip(masks, pieces):
            rows, width = piece.shape[0] // 2, piece.shape[1] // len(outs)
            for at, out in enumerate(outs):
                mine = out.at[:, place(partner(size, mask), width)]
                other = out.at[:, place(partner(size, mask ^ core), width)]
                copies.append((piece.at[:rows, at * width : (at + 1) * width], mine))
                copies.append((got.at[:, start : start + width], other))
                start += width
    run_copies(copies, sems)


def spread_cores(sets, counts, size):
    pieces = [piece for part in sets for piece in part]
    rows = pieces[0].shape[0] // 2
    give = jax.ShapeDtypeStruct((rows, sum(piece.shape[1] for piece in pieces)), BF16)
    got = swap(small_call(bottom_body, give, "bottom", *pieces), core_mask())
    widths = [part[0].shape[1] // count for part, count in zip(sets, counts) for _ in range(count)]
    return pl.pallas_call(
        functools.partial(spread_body, size, core_mask(), chip_masks(size), counts),
        out_shape=[jax.ShapeDtypeStruct((rows, width * size), BF16) for width in widths],
        in_specs=[ANY] * (len(pieces) + 1),
        out_specs=[ANY] * len(widths),
        scratch_shapes=[pltpu.SemaphoreType.DMA((len(widths) * size,))],
        compiler_params=SMALL,
        name="spread",
    )(*pieces, got)


def dot(a, b):
    return lax.dot_general(a, b, (((1,), (0,)), ((), ())), preferred_element_type=F32)


def dot_t(a, b):
    return lax.dot_general(a, b, (((1,), (1,)), ((), ())), preferred_element_type=F32)


def fold(x, op):
    parts = [x[at : at + 8] for at in range(0, x.shape[0], 8)]
    while len(parts) > 1:
        parts = [
            op(*parts[at : at + 2]) if at + 1 < len(parts) else parts[at]
            for at in range(0, len(parts), 2)
        ]
    return parts[0]


def taker(refs):
    refs = list(refs)
    return lambda count: [refs.pop(0) for _ in range(count)]


def stacked(rows, base, group, first=0):
    parts = [slice(first + at * HEAD_DIM, first + (at + 1) * HEAD_DIM) for at in range(group)]
    return jnp.concatenate([rows[base : base + TILE, part] for part in parts], axis=0)


def unstacked(rows, base, group, value):
    for at in range(group):
        part = slice(at * TILE, (at + 1) * TILE)
        rows[base : base + TILE, at * HEAD_DIM : (at + 1) * HEAD_DIM] = value[part]


def set_values(va, values):
    lane = lax.broadcasted_iota(jnp.int32, values.shape, 1)
    va[:, :HEAD_DIM] = values
    va[:, HEAD_DIM:] = jnp.where(lane < 2, 1.0, 0.0).astype(BF16)


def add_rows(target, start, old, value):
    if old:
        target[start : start + old, :] += value[:old]
    if old < value.shape[0]:
        target[start + old : start + value.shape[0], :] = value[old:]


def score_gradients(ds_scr, e, dp):
    for at in range(0, e.shape[0], TILE):
        part = slice(at, at + TILE)
        ds_scr[part, :] = (e[part, :].astype(F32) * dp[part]).astype(BF16)


def own_rows(tile):
    start = tile * (tile + 1) // 2 * TILE
    return slice(start, start + (tile + 1) * TILE)


def query_columns(qg, seg_q, base, group):
    mine = jnp.concatenate([seg_q[base : base + TILE, :]] * group, axis=0)
    return jnp.concatenate([stacked(qg, base, group), mine], axis=1)


def fold_rows(rows, op):
    parts = [fold(rows[at : at + TILE, :], op) for at in range(0, rows.shape[0], TILE)]
    whole = functools.reduce(op, parts)
    reduce = jnp.max if op is jnp.maximum else jnp.sum
    return reduce(whole, axis=0, keepdims=True)


def weigh(scores, top, keep):
    total = None
    for at in range(0, scores.shape[0], TILE):
        part = slice(at, at + TILE)
        e = jnp.exp2(scores[part, :] * exp2_scale - top)
        keep[part, :] = e.astype(BF16)
        e = fold(e, jnp.add)
        total = e if total is None else total + e
    return jnp.sum(total, axis=0, keepdims=True)


def tile_causal(group):
    row_of = lax.broadcasted_iota(jnp.int32, (TILE, TILE), 0)
    col_of = lax.broadcasted_iota(jnp.int32, (TILE, TILE), 1)
    return jnp.concatenate([row_of <= col_of] * group, axis=1)


def own_body(size, core, masks, tok, group, *refs):
    take = taker(refs)
    (seg_k, seg_q), qg_pieces, (kv,) = take(2), take(len(masks)), take(1)
    e_own, out_part, stats = take(3)
    qg, ka, vt, s_scr = take(4)
    wide, tiles = group * TILE, tok // TILE
    place_rows(size, core, masks, qg_pieces, qg)
    ka[:, :HEAD_DIM] = kv[:, :HEAD_DIM]
    ka[:, HEAD_DIM:] = seg_k[WINDOW:, :]
    vt[...] = kv[:, HEAD_DIM:].T
    causal = tile_causal(group)

    def scores(tile):
        queries = query_columns(qg, seg_q, tile * TILE, group)
        s_scr[tile % 2, : (tile + 1) * TILE, :] = dot_t(ka[: (tile + 1) * TILE, :], queries)

    scores(0)
    for tile in range(tiles):
        base, turn = tile * TILE, tile % 2
        count = base + TILE
        s_scr[turn, base:count, :] = jnp.where(causal, s_scr[turn, base:count, :], FAR)
        rows = s_scr.at[turn, :count, :]
        top = fold_rows(rows, jnp.maximum) * exp2_scale
        if tile + 1 < tiles:
            scores(tile + 1)
        mine = e_own.at[own_rows(tile), :]
        stats[tile : tile + 1, :] = top
        stats[tiles + tile : tiles + tile + 1, :] = weigh(rows, top, mine)
        out_part[:, tile * wide : (tile + 1) * wide] = dot(vt[:, :count], mine[...])


def forward_body(size, core, masks, reach, tok, group, *refs):
    take = taker(refs)
    (seg_k, seg_q), qg_pieces, kvs = take(2), take(len(masks)), take(reach)
    out_own, stats = take(2)
    out_pieces, sent, (g_own, dq_part) = take(len(masks)), take(reach), take(2)
    qg, outs, ka, va, kt, vt, dk, dv, s_scr, e_scr, ds_scr = take(11)
    width, wide, tiles = group * HEAD_DIM, group * TILE, tok // TILE
    place_rows(size, core, masks, qg_pieces, qg)
    ka[:, HEAD_DIM:] = seg_k[:WINDOW, :]
    for lag in range(1, reach + 1):
        there = slice((reach - lag) * tok, (reach - lag + 1) * tok)
        kv = kvs[lag - 1][...]
        ka[there, :HEAD_DIM] = kv[:, :HEAD_DIM]
        kt[:, there] = kv[:, :HEAD_DIM].T
        vt[:, there] = kv[:, HEAD_DIM:].T
        set_values(va.at[there, :], kv[:, HEAD_DIM:])
    wide_lane = lax.broadcasted_iota(jnp.int32, (wide, HEAD_DIM), 1)
    beyond = ~tile_causal(group)

    def scores(tile):
        base = tile * TILE
        queries = query_columns(qg, seg_q, base, group)
        s_scr[tile % 2, : WINDOW - base, :] = dot_t(ka[base:, :], queries)

    def with_delta(g2, out):
        delta = jnp.sum(g2.astype(F32) * out.astype(F32), axis=1, keepdims=True)
        high = delta.astype(BF16).astype(F32)
        extra = jnp.where(wide_lane == 0, -high, jnp.where(wide_lane == 1, high - delta, 0.0))
        return jnp.concatenate([g2, extra.astype(BF16)], axis=1)

    scores(0)
    for tile in range(tiles):
        base, turn = tile * TILE, tile % 2
        early = WINDOW - base
        columns = slice(tile * wide, (tile + 1) * wide)
        s_scr[turn, :TILE, :] = jnp.where(beyond, s_scr[turn, :TILE, :], FAR)
        rows = s_scr.at[turn, :early, :]
        top_own = stats[tile : tile + 1, :]
        top = jnp.maximum(fold_rows(rows, jnp.maximum) * exp2_scale, top_own)
        if tile + 1 < tiles:
            scores(tile + 1)
        mine = e_scr.at[turn, :early, :]
        total = weigh(rows, top, mine)
        scale = jnp.exp2(top_own - top)
        inv = 1.0 / (total + stats[tiles + tile : tiles + tile + 1, :] * scale)
        e = mine[...]
        out = dot(vt[:, base:], e) + out_own[:, columns] * scale
        out = (out * inv).T.astype(BF16)
        unstacked(outs, base, group, out)
        g2 = stacked(qg, base, group, width).astype(F32)
        g_mine = (g2 * jnp.broadcast_to(inv * scale, (HEAD_DIM, wide)).T).astype(BF16)
        g_own[columns, :] = with_delta(g_mine, out)
        g2 = (g2 * jnp.broadcast_to(inv, (HEAD_DIM, wide)).T).astype(BF16)
        dp = dot_t(va[base:, :], with_delta(g2, out))
        old = early if tile else 0
        add_rows(dv, base, old, dot(e, g2))
        score_gradients(ds_scr.at[turn, :early, :], e, dp)
        ds = ds_scr[turn, :early, :]
        add_rows(dk, base, old, dot(ds, stacked(qg, base, group)))
        dq_part[:, columns] = dot(kt[:, base:], ds)

    for lag in range(1, reach + 1):
        there = slice((reach - lag) * tok, (reach - lag + 1) * tok)
        sent[lag - 1][:, :HEAD_DIM] = (dk[there, :] * logit_scale).astype(BF16)
        sent[lag - 1][:, HEAD_DIM:] = dv[there, :].astype(BF16)
    take_rows(size, core, masks, lambda there: outs[there, :], out_pieces)


def backward_body(size, core, masks, tok, group, *refs):
    take = taker(refs)
    qg_pieces, (kv, e_own, g_own, dq_part) = take(len(masks)), take(4)
    dq_pieces, (dkv,) = take(len(masks)), take(1)
    qg, dqs, va, kt, dk, dv, ds_scr = take(7)
    wide = group * TILE
    place_rows(size, core, masks, qg_pieces, qg)
    kt[...] = kv[:, :HEAD_DIM].T
    set_values(va, kv[:, HEAD_DIM:])
    for tile in range(tok // TILE):
        base, turn = tile * TILE, tile % 2
        count = base + TILE
        columns = slice(tile * wide, (tile + 1) * wide)
        e = e_own[own_rows(tile), :]
        dp = dot_t(va[:count, :], g_own[columns, :])
        add_rows(dv, 0, base, dot(e, g_own[columns, :HEAD_DIM]))
        score_gradients(ds_scr.at[turn, :count, :], e, dp)
        ds = ds_scr[turn, :count, :]
        add_rows(dk, 0, base, dot(ds, stacked(qg, base, group)))
        dq = (dq_part[:, columns] + dot(kt[:, :count], ds)) * logit_scale
        unstacked(dqs, base, group, dq.T.astype(BF16))
    dkv[:, :HEAD_DIM] = dk[...] * logit_scale
    dkv[:, HEAD_DIM:] = dv[...]
    take_rows(size, core, masks, lambda there: dqs[there, :], dq_pieces)


def attend_call(kernel, out_shape, scratch_shapes, flops, name, *args):
    return pl.pallas_call(
        kernel,
        out_shape=out_shape,
        in_specs=[VMEM] * len(args),
        out_specs=[VMEM] * len(out_shape),
        scratch_shapes=scratch_shapes,
        compiler_params=pltpu.CompilerParams(vmem_limit_bytes=24 * 1024 * 1024),
        cost_estimate=pl.CostEstimate(
            flops=flops, bytes_accessed=8 * 1024 * 1024, transcendentals=0
        ),
        name=name,
    )(*args)


def forward_own(documents, qg, kv, size):
    rows, cols = qg[0].shape
    tok = len(qg) * rows
    group = cols // (2 * HEAD_DIM)
    wide, tiles = group * TILE, tok // TILE
    return attend_call(
        functools.partial(own_body, size, core_mask(), chip_masks(size), tok, group),
        [
            jax.ShapeDtypeStruct((own_rows(tiles - 1).stop, wide), BF16),
            jax.ShapeDtypeStruct((HEAD_DIM, tiles * wide), F32),
            jax.ShapeDtypeStruct((2 * tiles, wide), F32),
        ],
        [
            pltpu.VMEM((tok, cols), BF16),
            pltpu.VMEM((tok, 2 * HEAD_DIM), BF16),
            pltpu.VMEM((HEAD_DIM, tok), BF16),
            pltpu.VMEM((2, tok, wide), F32),
        ],
        16 * tok * group * (WINDOW + TILE) * HEAD_DIM,
        "forward_own",
        *documents,
        *qg,
        kv,
    )


def forward(documents, qg, lags, carried, size):
    rows, cols = qg[0].shape
    tok, count, reach = len(qg) * rows, len(qg), len(lags)
    group = cols // (2 * HEAD_DIM)
    wide, tiles = group * TILE, tok // TILE
    half = jax.ShapeDtypeStruct((tok, 2 * HEAD_DIM), BF16)
    out_shape = [jax.ShapeDtypeStruct((rows, cols // 2), BF16)] * count + [half] * reach
    out_shape += [
        jax.ShapeDtypeStruct((tiles * wide, 2 * HEAD_DIM), BF16),
        jax.ShapeDtypeStruct((HEAD_DIM, tiles * wide), F32),
    ]
    scratch = [
        pltpu.VMEM((tok, cols), BF16),
        pltpu.VMEM((tok, cols // 2), BF16),
        pltpu.VMEM((WINDOW, 2 * HEAD_DIM), BF16),
        pltpu.VMEM((WINDOW, 2 * HEAD_DIM), BF16),
        pltpu.VMEM((HEAD_DIM, WINDOW), BF16),
        pltpu.VMEM((HEAD_DIM, WINDOW), BF16),
        pltpu.VMEM((WINDOW, HEAD_DIM), F32),
        pltpu.VMEM((WINDOW, HEAD_DIM), F32),
        pltpu.VMEM((2, WINDOW, wide), F32),
        pltpu.VMEM((2, WINDOW, wide), BF16),
        pltpu.VMEM((2, WINDOW, wide), BF16),
    ]
    results = attend_call(
        functools.partial(
            forward_body, size, core_mask(), chip_masks(size), reach, tok, group
        ),
        out_shape,
        scratch,
        6 * tok * group * (WINDOW + TILE) * HEAD_DIM,
        "forward",
        *documents,
        *qg,
        *lags,
        *carried,
    )
    return results[:count], results[count : count + reach], results[count + reach :]


def backward(qg, kv, carried, size):
    rows, cols = qg[0].shape
    tok, count = len(qg) * rows, len(qg)
    group = cols // (2 * HEAD_DIM)
    wide = group * TILE
    results = attend_call(
        functools.partial(backward_body, size, core_mask(), chip_masks(size), tok, group),
        [jax.ShapeDtypeStruct((rows, cols // 2), BF16)] * count
        + [jax.ShapeDtypeStruct((tok, 2 * HEAD_DIM), F32)],
        [
            pltpu.VMEM((tok, cols), BF16),
            pltpu.VMEM((tok, cols // 2), BF16),
            pltpu.VMEM((tok, 2 * HEAD_DIM), BF16),
            pltpu.VMEM((HEAD_DIM, tok), BF16),
            pltpu.VMEM((tok, HEAD_DIM), F32),
            pltpu.VMEM((tok, HEAD_DIM), F32),
            pltpu.VMEM((2, tok, wide), BF16),
        ],
        4 * tok * group * (WINDOW + TILE) * HEAD_DIM,
        "backward",
        *qg,
        kv,
        *carried,
    )
    return results[:count], results[count]


def document_columns(segment_ids, tok, size):
    start = (flat_index() // size) * tok
    padded = jnp.concatenate([jnp.full((WINDOW,), -1, jnp.int32), segment_ids])
    keys = lax.dynamic_slice_in_dim(padded, start, WINDOW + tok, 0)
    queries = lax.dynamic_slice_in_dim(segment_ids, start, tok, 0)
    number = jnp.arange(HEAD_DIM, dtype=jnp.int32)[None, :]
    return (
        jnp.where(keys[:, None] == number, 0.0, FAR).astype(BF16),
        jnp.where(queries[:, None] == number, 1.0, 0.0).astype(BF16),
    )


def body(query, key, value, grad_out, segment_ids):
    size = key.shape[1] // HEAD_DIM
    rows = query.shape[0]
    tok = size * rows
    reach = WINDOW // tok
    assert reach * tok == WINDOW and device_count() % size == 0
    documents = document_columns(segment_ids, tok, size)

    got = [swap(array, core_mask()) for array in (key, value, query, grad_out)]
    pieces = list(gather_cores((key, value), got[:2], size))
    pieces[0], query, grad_out = after(pieces[0], query, grad_out)
    kv = join(swap_chips(pieces, size), size)
    lags = [shifted(kv, lag * size) for lag in range(1, reach + 1)]
    qg = swap_chips(gather_cores((query, grad_out), got[2:], size), size)

    e_own, *partial = forward_own(documents, qg, kv, size)
    out, sent, carried = forward(documents, qg, lags, partial, size)
    backs = [shifted(sent[lag - 1], -lag * size) for lag in range(1, reach + 1)]
    out = swap_chips(out, size)
    grad_q, dkv = backward(qg, kv, [e_own, *carried], size)
    both = after(*out, *grad_q)
    out, grad_q = both[: len(out)], both[len(out) :]
    grad_q = swap_chips(grad_q, size)
    grads = swap_chips(combine([dkv, *backs], size), size)
    return tuple(spread_cores([out, grad_q, grads], (1, 1, 2), size))


def solution(mesh):
    placed = P(("pipe", "tensor"), None)
    return jax.shard_map(
        body,
        mesh=mesh,
        in_specs=(placed, placed, placed, placed, P()),
        out_specs=(placed, placed, placed, placed),
        check_vma=False,
    )
```

```python
import functools

import jax
import jax.numpy as jnp
from jax import lax
from jax.experimental import pallas as pl
from jax.experimental.pallas import tpu as pltpu
from jax.sharding import PartitionSpec as P

HEAD_DIM = 128
WINDOW = 1024
TILE = 128

logit_scale = 168.0 ** (-0.5)
exp2_scale = logit_scale * 1.4426950408889634

FAR = -(2.0**30)
SMALL = pltpu.CompilerParams(vmem_limit_bytes=4 * 1024 * 1024)
ANY = pl.BlockSpec(memory_space=pl.ANY)
VMEM = pl.BlockSpec(memory_space=pltpu.VMEM)
F32 = jnp.float32
BF16 = jnp.bfloat16
BOTH = ("pipe", "tensor")


def flat_index():
    return lax.axis_index("pipe") * lax.axis_size("tensor") + lax.axis_index("tensor")


def device_count():
    return lax.axis_size("pipe") * lax.axis_size("tensor")


def swap(value, mask):
    return lax.ppermute(value, BOTH, [(i, i ^ mask) for i in range(device_count())])


def core_mask():
    return lax.axis_size("tensor")


def chip_masks(size):
    return [mask for mask in range(size) if not mask & core_mask()]


def swap_chips(pieces, size):
    return [pieces[0]] + [
        swap(piece, mask) for piece, mask in zip(pieces[1:], chip_masks(size)[1:])
    ]


def shifted(value, step):
    count = device_count()
    pairs = [(i, i + step) for i in range(count) if 0 <= i + step < count]
    return lax.ppermute(value, BOTH, pairs)


def partner(size, j):
    return lax.bitwise_xor(lax.rem(flat_index(), size), j)


def place(index, width):
    return pl.ds(pl.multiple_of(index * width, width), width)


def after(value, *others):
    return lax.optimization_barrier((value, *others))


def run_copies(copies, sems):
    started = []
    for at, (source, target) in enumerate(copies):
        copy = pltpu.make_async_copy(source, target, sems.at[at])
        copy.start()
        started.append(copy)
    for copy in started:
        copy.wait()


def small_call(kernel, out_shape, name, *args):
    return pl.pallas_call(
        kernel,
        out_shape=out_shape,
        in_specs=[VMEM] * len(args),
        out_specs=jax.tree.map(lambda _: VMEM, out_shape),
        compiler_params=SMALL,
        name=name,
    )(*args)


def this_core(array, size):
    core = core_mask()
    width = array.shape[1] // size
    shares = [array[:, r * width : (r + 1) * width] for r in range(size)]
    first, second = (
        jnp.concatenate([share for r, share in enumerate(shares) if (r // core) % 2 == at], axis=1)
        for at in range(2)
    )
    return jnp.where((flat_index() // core) % 2 == 0, first, second)


def stack_body(size, core, masks, count, *refs):
    own, got, pieces = refs[:count], refs[count : 2 * count], refs[2 * count :]
    rows = own[0].shape[0]
    for mask, piece in zip(masks, pieces):
        there = partner(size, mask)
        chip = there // (2 * core) * core + lax.rem(there, core)
        start = 0
        for mine, other in zip(own, got):
            width = other.shape[1] // size
            piece[:rows, start : start + width] = mine[:, place(chip, width)]
            piece[rows:, start : start + width] = other[:, place(there, width)]
            start += width


def gather_cores(arrays, got, size):
    masks = chip_masks(size)
    own = [this_core(array, size) for array in arrays]
    cols = sum(array.shape[1] // size for array in arrays)
    piece = jax.ShapeDtypeStruct((2 * arrays[0].shape[0], cols), BF16)
    kernel = functools.partial(stack_body, size, core_mask(), masks, len(arrays))
    return small_call(kernel, [piece] * len(masks), "stack", *own, *got)


def place_rows(size, core, masks, pieces, out):
    for mask, piece in zip(masks, pieces):
        rows = piece.shape[0] // 2
        out[place(partner(size, mask), rows), :] = piece[:rows, :]
        out[place(partner(size, mask ^ core), rows), :] = piece[rows:, :]


def take_rows(size, core, masks, source, pieces):
    for mask, piece in zip(masks, pieces):
        rows = piece.shape[0] // 2
        piece[:rows, :] = source(place(partner(size, mask), rows))
        piece[rows:, :] = source(place(partner(size, mask ^ core), rows))


def join(pieces, size):
    rows, cols = pieces[0].shape
    core, masks = core_mask(), chip_masks(size)

    def kernel(*refs):
        place_rows(size, core, masks, refs[:-1], refs[-1])

    out = jax.ShapeDtypeStruct((len(pieces) * rows, cols), BF16)
    return small_call(kernel, out, "join", *pieces)


def combine(terms, size):
    tok, cols = terms[0].shape
    core, masks = core_mask(), chip_masks(size)

    def kernel(*refs):
        added = refs[: len(terms)]

        def source(there):
            total = added[0][there, :]
            for term in added[1:]:
                total = total + term[there, :].astype(F32)
            return total.astype(BF16)

        take_rows(size, core, masks, source, refs[len(terms) :])

    piece = jax.ShapeDtypeStruct((2 * (tok // size), cols), BF16)
    return small_call(kernel, [piece] * len(masks), "combine", *terms)


def bottom_body(*refs):
    out, start = refs[-1], 0
    for piece in refs[:-1]:
        rows, width = piece.shape[0] // 2, piece.shape[1]
        out[:, start : start + width] = piece[rows:, :]
        start += width


def spread_body(size, core, masks, counts, *refs):
    refs = list(refs)
    take = lambda count: [refs.pop(0) for _ in range(count)]
    sets = [take(len(masks)) for _ in counts]
    (got,), sets_out, (sems,) = take(1), [take(count) for count in counts], take(1)
    copies, start = [], 0
    for pieces, outs in zip(sets, sets_out):
        for mask, piece in zip(masks, pieces):
            rows, width = piece.shape[0] // 2, piece.shape[1] // len(outs)
            for at, out in enumerate(outs):
                mine = out.at[:, place(partner(size, mask), width)]
                other = out.at[:, place(partner(size, mask ^ core), width)]
                copies.append((piece.at[:rows, at * width : (at + 1) * width], mine))
                copies.append((got.at[:, start : start + width], other))
                start += width
    run_copies(copies, sems)


def spread_cores(sets, counts, size):
    pieces = [piece for part in sets for piece in part]
    rows = pieces[0].shape[0] // 2
    give = jax.ShapeDtypeStruct((rows, sum(piece.shape[1] for piece in pieces)), BF16)
    got = swap(small_call(bottom_body, give, "bottom", *pieces), core_mask())
    widths = [part[0].shape[1] // count for part, count in zip(sets, counts) for _ in range(count)]
    return pl.pallas_call(
        functools.partial(spread_body, size, core_mask(), chip_masks(size), counts),
        out_shape=[jax.ShapeDtypeStruct((rows, width * size), BF16) for width in widths],
        in_specs=[ANY] * (len(pieces) + 1),
        out_specs=[ANY] * len(widths),
        scratch_shapes=[pltpu.SemaphoreType.DMA((len(widths) * size,))],
        compiler_params=SMALL,
        name="spread",
    )(*pieces, got)


def dot(a, b):
    return lax.dot_general(a, b, (((1,), (0,)), ((), ())), preferred_element_type=F32)


def dot_t(a, b):
    return lax.dot_general(a, b, (((1,), (1,)), ((), ())), preferred_element_type=F32)


def fold(x, op):
    parts = [x[at : at + 8] for at in range(0, x.shape[0], 8)]
    while len(parts) > 1:
        parts = [
            op(*parts[at : at + 2]) if at + 1 < len(parts) else parts[at]
            for at in range(0, len(parts), 2)
        ]
    return parts[0]


def taker(refs):
    refs = list(refs)
    return lambda count: [refs.pop(0) for _ in range(count)]


def stacked(rows, base, group, first=0):
    parts = [slice(first + at * HEAD_DIM, first + (at + 1) * HEAD_DIM) for at in range(group)]
    return jnp.concatenate([rows[base : base + TILE, part] for part in parts], axis=0)


def unstacked(rows, base, group, value):
    for at in range(group):
        part = slice(at * TILE, (at + 1) * TILE)
        rows[base : base + TILE, at * HEAD_DIM : (at + 1) * HEAD_DIM] = value[part]


def set_values(va, values):
    lane = lax.broadcasted_iota(jnp.int32, values.shape, 1)
    va[:, :HEAD_DIM] = values
    va[:, HEAD_DIM:] = jnp.where(lane < 2, 1.0, 0.0).astype(BF16)


def add_rows(target, start, old, value):
    if old:
        target[start : start + old, :] += value[:old]
    if old < value.shape[0]:
        target[start + old : start + value.shape[0], :] = value[old:]


def score_gradients(ds_scr, e, dp):
    for at in range(0, e.shape[0], TILE):
        part = slice(at, at + TILE)
        ds_scr[part, :] = (e[part, :].astype(F32) * dp[part]).astype(BF16)


def gradient_rows(qg, base, group, scale, out):
    first = qg.shape[1] // 2
    columns = jnp.broadcast_to(scale, (HEAD_DIM, scale.shape[1])).T
    g2 = (stacked(qg, base, group, first).astype(F32) * columns).astype(BF16)
    delta = jnp.sum(g2.astype(F32) * out.astype(F32), axis=1, keepdims=True)
    high = delta.astype(BF16).astype(F32)
    lane = lax.broadcasted_iota(jnp.int32, g2.shape, 1)
    extra = jnp.where(lane == 0, -high, jnp.where(lane == 1, high - delta, 0.0))
    return g2, jnp.concatenate([g2, extra.astype(BF16)], axis=1)


def own_rows(tile):
    start = tile * (tile + 1) // 2 * TILE
    return slice(start, start + (tile + 1) * TILE)


def query_columns(qg, seg_q, base, group):
    mine = jnp.concatenate([seg_q[base : base + TILE, :]] * group, axis=0)
    return jnp.concatenate([stacked(qg, base, group), mine], axis=1)


def fold_rows(rows, op):
    parts = [fold(rows[at : at + TILE, :], op) for at in range(0, rows.shape[0], TILE)]
    whole = functools.reduce(op, parts)
    reduce = jnp.max if op is jnp.maximum else jnp.sum
    return reduce(whole, axis=0, keepdims=True)


def weigh(scores, top, keep):
    total = None
    for at in range(0, scores.shape[0], TILE):
        part = slice(at, at + TILE)
        e = jnp.exp2(scores[part, :] * exp2_scale - top)
        keep[part, :] = e.astype(BF16)
        e = fold(e, jnp.add)
        total = e if total is None else total + e
    return jnp.sum(total, axis=0, keepdims=True)


def tile_causal(group):
    row_of = lax.broadcasted_iota(jnp.int32, (TILE, TILE), 0)
    col_of = lax.broadcasted_iota(jnp.int32, (TILE, TILE), 1)
    return jnp.concatenate([row_of <= col_of] * group, axis=1)


def own_body(size, core, masks, tok, group, *refs):
    take = taker(refs)
    (seg_k, seg_q), qg_pieces, (kv,) = take(2), take(len(masks)), take(1)
    e_own, out_part, stats = take(3)
    qg, ka, vt, s_scr = take(4)
    wide, tiles = group * TILE, tok // TILE
    place_rows(size, core, masks, qg_pieces, qg)
    ka[:, :HEAD_DIM] = kv[:, :HEAD_DIM]
    ka[:, HEAD_DIM:] = seg_k[WINDOW:, :]
    vt[...] = kv[:, HEAD_DIM:].T
    causal = tile_causal(group)

    def scores(tile):
        queries = query_columns(qg, seg_q, tile * TILE, group)
        s_scr[tile % 2, : (tile + 1) * TILE, :] = dot_t(ka[: (tile + 1) * TILE, :], queries)

    scores(0)
    for tile in range(tiles):
        base, turn = tile * TILE, tile % 2
        count = base + TILE
        s_scr[turn, base:count, :] = jnp.where(causal, s_scr[turn, base:count, :], FAR)
        rows = s_scr.at[turn, :count, :]
        top = fold_rows(rows, jnp.maximum) * exp2_scale
        if tile + 1 < tiles:
            scores(tile + 1)
        mine = e_own.at[own_rows(tile), :]
        stats[tile : tile + 1, :] = top
        stats[tiles + tile : tiles + tile + 1, :] = weigh(rows, top, mine)
        out_part[:, tile * wide : (tile + 1) * wide] = dot(vt[:, :count], mine[...])


def forward_body(size, core, masks, reach, tok, group, *refs):
    take = taker(refs)
    (seg_k, seg_q), qg_pieces, kvs = take(2), take(len(masks)), take(reach)
    out_own, stats = take(2)
    out_pieces, sent, (outs, own_scale, dq_part) = take(len(masks)), take(reach), take(3)
    qg, ka, va, kt, vt, dk, dv, s_scr, e_scr, ds_scr = take(10)
    wide, tiles = group * TILE, tok // TILE
    place_rows(size, core, masks, qg_pieces, qg)
    ka[:, HEAD_DIM:] = seg_k[:WINDOW, :]
    for lag in range(1, reach + 1):
        there = slice((reach - lag) * tok, (reach - lag + 1) * tok)
        kv = kvs[lag - 1][...]
        ka[there, :HEAD_DIM] = kv[:, :HEAD_DIM]
        kt[:, there] = kv[:, :HEAD_DIM].T
        vt[:, there] = kv[:, HEAD_DIM:].T
        set_values(va.at[there, :], kv[:, HEAD_DIM:])
    beyond = ~tile_causal(group)

    def scores(tile):
        base = tile * TILE
        queries = query_columns(qg, seg_q, base, group)
        s_scr[tile % 2, : WINDOW - base, :] = dot_t(ka[base:, :], queries)

    scores(0)
    for tile in range(tiles):
        base, turn = tile * TILE, tile % 2
        early = WINDOW - base
        columns = slice(tile * wide, (tile + 1) * wide)
        s_scr[turn, :TILE, :] = jnp.where(beyond, s_scr[turn, :TILE, :], FAR)
        rows = s_scr.at[turn, :early, :]
        top_own = stats[tile : tile + 1, :]
        top = jnp.maximum(fold_rows(rows, jnp.maximum) * exp2_scale, top_own)
        if tile + 1 < tiles:
            scores(tile + 1)
        mine = e_scr.at[turn, :early, :]
        total = weigh(rows, top, mine)
        scale = jnp.exp2(top_own - top)
        inv = 1.0 / (total + stats[tiles + tile : tiles + tile + 1, :] * scale)
        e = mine[...]
        out = dot(vt[:, base:], e) + out_own[:, columns] * scale
        out = (out * inv).T.astype(BF16)
        unstacked(outs, base, group, out)
        own_scale[tile : tile + 1, :] = inv * scale
        g2, g_wide = gradient_rows(qg, base, group, inv, out)
        dp = dot_t(va[base:, :], g_wide)
        old = early if tile else 0
        add_rows(dv, base, old, dot(e, g2))
        score_gradients(ds_scr.at[turn, :early, :], e, dp)
        ds = ds_scr[turn, :early, :]
        add_rows(dk, base, old, dot(ds, stacked(qg, base, group)))
        dq_part[:, columns] = dot(kt[:, base:], ds)

    for lag in range(1, reach + 1):
        there = slice((reach - lag) * tok, (reach - lag + 1) * tok)
        sent[lag - 1][:, :HEAD_DIM] = (dk[there, :] * logit_scale).astype(BF16)
        sent[lag - 1][:, HEAD_DIM:] = dv[there, :].astype(BF16)
    take_rows(size, core, masks, lambda there: outs[there, :], out_pieces)


def backward_body(size, core, masks, tok, group, *refs):
    take = taker(refs)
    qg_pieces, (kv, e_own, outs, own_scale, dq_part) = take(len(masks)), take(5)
    dq_pieces, (dkv,) = take(len(masks)), take(1)
    qg, dqs, va, kt, dk, dv, ds_scr = take(7)
    wide = group * TILE
    place_rows(size, core, masks, qg_pieces, qg)
    kt[...] = kv[:, :HEAD_DIM].T
    set_values(va, kv[:, HEAD_DIM:])
    for tile in range(tok // TILE):
        base, turn = tile * TILE, tile % 2
        count = base + TILE
        columns = slice(tile * wide, (tile + 1) * wide)
        e = e_own[own_rows(tile), :]
        scale = own_scale[tile : tile + 1, :]
        g2, g_wide = gradient_rows(qg, base, group, scale, stacked(outs, base, group))
        dp = dot_t(va[:count, :], g_wide)
        add_rows(dv, 0, base, dot(e, g2))
        score_gradients(ds_scr.at[turn, :count, :], e, dp)
        ds = ds_scr[turn, :count, :]
        add_rows(dk, 0, base, dot(ds, stacked(qg, base, group)))
        dq = (dq_part[:, columns] + dot(kt[:, :count], ds)) * logit_scale
        unstacked(dqs, base, group, dq.T.astype(BF16))
    dkv[:, :HEAD_DIM] = dk[...] * logit_scale
    dkv[:, HEAD_DIM:] = dv[...]
    take_rows(size, core, masks, lambda there: dqs[there, :], dq_pieces)


def attend_call(kernel, out_shape, scratch_shapes, flops, name, *args):
    return pl.pallas_call(
        kernel,
        out_shape=out_shape,
        in_specs=[VMEM] * len(args),
        out_specs=[VMEM] * len(out_shape),
        scratch_shapes=scratch_shapes,
        compiler_params=pltpu.CompilerParams(vmem_limit_bytes=24 * 1024 * 1024),
        cost_estimate=pl.CostEstimate(
            flops=flops, bytes_accessed=8 * 1024 * 1024, transcendentals=0
        ),
        name=name,
    )(*args)


def forward_own(documents, qg, kv, size):
    rows, cols = qg[0].shape
    tok = len(qg) * rows
    group = cols // (2 * HEAD_DIM)
    wide, tiles = group * TILE, tok // TILE
    return attend_call(
        functools.partial(own_body, size, core_mask(), chip_masks(size), tok, group),
        [
            jax.ShapeDtypeStruct((own_rows(tiles - 1).stop, wide), BF16),
            jax.ShapeDtypeStruct((HEAD_DIM, tiles * wide), F32),
            jax.ShapeDtypeStruct((2 * tiles, wide), F32),
        ],
        [
            pltpu.VMEM((tok, cols), BF16),
            pltpu.VMEM((tok, 2 * HEAD_DIM), BF16),
            pltpu.VMEM((HEAD_DIM, tok), BF16),
            pltpu.VMEM((2, tok, wide), F32),
        ],
        16 * tok * group * (WINDOW + TILE) * HEAD_DIM,
        "forward_own",
        *documents,
        *qg,
        kv,
    )


def forward(documents, qg, lags, carried, size):
    rows, cols = qg[0].shape
    tok, count, reach = len(qg) * rows, len(qg), len(lags)
    group = cols // (2 * HEAD_DIM)
    wide, tiles = group * TILE, tok // TILE
    half = jax.ShapeDtypeStruct((tok, 2 * HEAD_DIM), BF16)
    out_shape = [jax.ShapeDtypeStruct((rows, cols // 2), BF16)] * count + [half] * reach
    out_shape += [
        jax.ShapeDtypeStruct((tok, cols // 2), BF16),
        jax.ShapeDtypeStruct((tiles, wide), F32),
        jax.ShapeDtypeStruct((HEAD_DIM, tiles * wide), F32),
    ]
    scratch = [
        pltpu.VMEM((tok, cols), BF16),
        pltpu.VMEM((WINDOW, 2 * HEAD_DIM), BF16),
        pltpu.VMEM((WINDOW, 2 * HEAD_DIM), BF16),
        pltpu.VMEM((HEAD_DIM, WINDOW), BF16),
        pltpu.VMEM((HEAD_DIM, WINDOW), BF16),
        pltpu.VMEM((WINDOW, HEAD_DIM), F32),
        pltpu.VMEM((WINDOW, HEAD_DIM), F32),
        pltpu.VMEM((2, WINDOW, wide), F32),
        pltpu.VMEM((2, WINDOW, wide), BF16),
        pltpu.VMEM((2, WINDOW, wide), BF16),
    ]
    results = attend_call(
        functools.partial(
            forward_body, size, core_mask(), chip_masks(size), reach, tok, group
        ),
        out_shape,
        scratch,
        6 * tok * group * (WINDOW + TILE) * HEAD_DIM,
        "forward",
        *documents,
        *qg,
        *lags,
        *carried,
    )
    return results[:count], results[count : count + reach], results[count + reach :]


def backward(qg, kv, carried, size):
    rows, cols = qg[0].shape
    tok, count = len(qg) * rows, len(qg)
    group = cols // (2 * HEAD_DIM)
    wide = group * TILE
    results = attend_call(
        functools.partial(backward_body, size, core_mask(), chip_masks(size), tok, group),
        [jax.ShapeDtypeStruct((rows, cols // 2), BF16)] * count
        + [jax.ShapeDtypeStruct((tok, 2 * HEAD_DIM), F32)],
        [
            pltpu.VMEM((tok, cols), BF16),
            pltpu.VMEM((tok, cols // 2), BF16),
            pltpu.VMEM((tok, 2 * HEAD_DIM), BF16),
            pltpu.VMEM((HEAD_DIM, tok), BF16),
            pltpu.VMEM((tok, HEAD_DIM), F32),
            pltpu.VMEM((tok, HEAD_DIM), F32),
            pltpu.VMEM((2, tok, wide), BF16),
        ],
        4 * tok * group * (WINDOW + TILE) * HEAD_DIM,
        "backward",
        *qg,
        kv,
        *carried,
    )
    return results[:count], results[count]


def document_columns(segment_ids, tok, size):
    start = (flat_index() // size) * tok
    padded = jnp.concatenate([jnp.full((WINDOW,), -1, jnp.int32), segment_ids])
    keys = lax.dynamic_slice_in_dim(padded, start, WINDOW + tok, 0)
    queries = lax.dynamic_slice_in_dim(segment_ids, start, tok, 0)
    number = jnp.arange(HEAD_DIM, dtype=jnp.int32)[None, :]
    return (
        jnp.where(keys[:, None] == number, 0.0, FAR).astype(BF16),
        jnp.where(queries[:, None] == number, 1.0, 0.0).astype(BF16),
    )


def body(query, key, value, grad_out, segment_ids):
    size = key.shape[1] // HEAD_DIM
    rows = query.shape[0]
    tok = size * rows
    reach = WINDOW // tok
    assert reach * tok == WINDOW and device_count() % size == 0

    got = [swap(array, core_mask()) for array in (key, value, query, grad_out)]
    pieces = list(gather_cores((key, value), got[:2], size))
    pieces[0], query, grad_out, segment_ids = after(pieces[0], query, grad_out, segment_ids)
    documents = document_columns(segment_ids, tok, size)
    kv = join(swap_chips(pieces, size), size)
    lags = [shifted(kv, lag * size) for lag in range(1, reach + 1)]
    qg = swap_chips(gather_cores((query, grad_out), got[2:], size), size)

    e_own, *partial = forward_own(documents, qg, kv, size)
    out, sent, carried = forward(documents, qg, lags, partial, size)
    backs = [shifted(sent[lag - 1], -lag * size) for lag in range(1, reach + 1)]
    out = swap_chips(out, size)
    grad_q, dkv = backward(qg, kv, [e_own, *carried], size)
    both = after(*out, *grad_q)
    out, grad_q = both[: len(out)], both[len(out) :]
    grad_q = swap_chips(grad_q, size)
    grads = swap_chips(combine([dkv, *backs], size), size)
    return tuple(spread_cores([out, grad_q, grads], (1, 1, 2), size))


def solution(mesh):
    placed = P(("pipe", "tensor"), None)
    return jax.shard_map(
        body,
        mesh=mesh,
        in_specs=(placed, placed, placed, placed, P()),
        out_specs=(placed, placed, placed, placed),
        check_vma=False,
    )
```

```python
import functools

import jax
import jax.numpy as jnp
from jax import lax
from jax.experimental import pallas as pl
from jax.experimental.pallas import tpu as pltpu
from jax.sharding import PartitionSpec as P

HEAD_DIM = 128
WINDOW = 1024
TILE = 128

logit_scale = 168.0 ** (-0.5)
exp2_scale = logit_scale * 1.4426950408889634

FAR = -(2.0**30)
SMALL = pltpu.CompilerParams(vmem_limit_bytes=4 * 1024 * 1024)
ANY = pl.BlockSpec(memory_space=pl.ANY)
VMEM = pl.BlockSpec(memory_space=pltpu.VMEM)
F32 = jnp.float32
BF16 = jnp.bfloat16
BOTH = ("pipe", "tensor")


def flat_index():
    return lax.axis_index("pipe") * lax.axis_size("tensor") + lax.axis_index("tensor")


def device_count():
    return lax.axis_size("pipe") * lax.axis_size("tensor")


def swap(value, mask):
    return lax.ppermute(value, BOTH, [(i, i ^ mask) for i in range(device_count())])


def core_mask():
    return lax.axis_size("tensor")


def chip_masks(size):
    return [mask for mask in range(size) if not mask & core_mask()]


def swap_chips(pieces, size):
    return [pieces[0]] + [
        swap(piece, mask) for piece, mask in zip(pieces[1:], chip_masks(size)[1:])
    ]


def shifted(value, step):
    count = device_count()
    pairs = [(i, i + step) for i in range(count) if 0 <= i + step < count]
    return lax.ppermute(value, BOTH, pairs)


def partner(size, j):
    return lax.bitwise_xor(lax.rem(flat_index(), size), j)


def place(index, width):
    return pl.ds(pl.multiple_of(index * width, width), width)


def after(value, *others):
    return lax.optimization_barrier((value, *others))


def run_copies(copies, sems):
    started = []
    for at, (source, target) in enumerate(copies):
        copy = pltpu.make_async_copy(source, target, sems.at[at])
        copy.start()
        started.append(copy)
    for copy in started:
        copy.wait()


def small_call(kernel, out_shape, name, *args):
    return pl.pallas_call(
        kernel,
        out_shape=out_shape,
        in_specs=[VMEM] * len(args),
        out_specs=jax.tree.map(lambda _: VMEM, out_shape),
        compiler_params=SMALL,
        name=name,
    )(*args)


def this_core(array, size):
    core = core_mask()
    width = array.shape[1] // size
    shares = [array[:, r * width : (r + 1) * width] for r in range(size)]
    first, second = (
        jnp.concatenate([share for r, share in enumerate(shares) if (r // core) % 2 == at], axis=1)
        for at in range(2)
    )
    return jnp.where((flat_index() // core) % 2 == 0, first, second)


def stack_body(size, core, masks, count, *refs):
    own, got, pieces = refs[:count], refs[count : 2 * count], refs[2 * count :]
    rows = own[0].shape[0]
    for mask, piece in zip(masks, pieces):
        there = partner(size, mask)
        chip = there // (2 * core) * core + lax.rem(there, core)
        start = 0
        for mine, other in zip(own, got):
            width = other.shape[1] // size
            piece[:rows, start : start + width] = mine[:, place(chip, width)]
            piece[rows:, start : start + width] = other[:, place(there, width)]
            start += width


def gather_cores(arrays, got, size):
    masks = chip_masks(size)
    own = [this_core(array, size) for array in arrays]
    cols = sum(array.shape[1] // size for array in arrays)
    piece = jax.ShapeDtypeStruct((2 * arrays[0].shape[0], cols), BF16)
    kernel = functools.partial(stack_body, size, core_mask(), masks, len(arrays))
    return small_call(kernel, [piece] * len(masks), "stack", *own, *got)


def place_rows(size, core, masks, pieces, out):
    for mask, piece in zip(masks, pieces):
        rows = piece.shape[0] // 2
        out[place(partner(size, mask), rows), :] = piece[:rows, :]
        out[place(partner(size, mask ^ core), rows), :] = piece[rows:, :]


def take_rows(size, core, masks, source, pieces):
    for mask, piece in zip(masks, pieces):
        rows = piece.shape[0] // 2
        piece[:rows, :] = source(place(partner(size, mask), rows))
        piece[rows:, :] = source(place(partner(size, mask ^ core), rows))


def join(pieces, size):
    rows, cols = pieces[0].shape
    core, masks = core_mask(), chip_masks(size)

    def kernel(*refs):
        place_rows(size, core, masks, refs[:-1], refs[-1])

    out = jax.ShapeDtypeStruct((len(pieces) * rows, cols), BF16)
    return small_call(kernel, out, "join", *pieces)


def combine(terms, size):
    tok, cols = terms[0].shape
    core, masks = core_mask(), chip_masks(size)

    def kernel(*refs):
        added = refs[: len(terms)]

        def source(there):
            total = added[0][there, :]
            for term in added[1:]:
                total = total + term[there, :].astype(F32)
            return total.astype(BF16)

        take_rows(size, core, masks, source, refs[len(terms) :])

    piece = jax.ShapeDtypeStruct((2 * (tok // size), cols), BF16)
    return small_call(kernel, [piece] * len(masks), "combine", *terms)


def bottom_body(*refs):
    out, start = refs[-1], 0
    for piece in refs[:-1]:
        rows, width = piece.shape[0] // 2, piece.shape[1]
        out[:, start : start + width] = piece[rows:, :]
        start += width


def spread_body(size, core, masks, counts, *refs):
    refs = list(refs)
    take = lambda count: [refs.pop(0) for _ in range(count)]
    sets = [take(len(masks)) for _ in counts]
    (got,), sets_out, (sems,) = take(1), [take(count) for count in counts], take(1)
    copies, start = [], 0
    for pieces, outs in zip(sets, sets_out):
        for mask, piece in zip(masks, pieces):
            rows, width = piece.shape[0] // 2, piece.shape[1] // len(outs)
            for at, out in enumerate(outs):
                mine = out.at[:, place(partner(size, mask), width)]
                other = out.at[:, place(partner(size, mask ^ core), width)]
                copies.append((piece.at[:rows, at * width : (at + 1) * width], mine))
                copies.append((got.at[:, start : start + width], other))
                start += width
    run_copies(copies, sems)


def spread_cores(sets, counts, size):
    pieces = [piece for part in sets for piece in part]
    rows = pieces[0].shape[0] // 2
    give = jax.ShapeDtypeStruct((rows, sum(piece.shape[1] for piece in pieces)), BF16)
    got = swap(small_call(bottom_body, give, "bottom", *pieces), core_mask())
    widths = [part[0].shape[1] // count for part, count in zip(sets, counts) for _ in range(count)]
    return pl.pallas_call(
        functools.partial(spread_body, size, core_mask(), chip_masks(size), counts),
        out_shape=[jax.ShapeDtypeStruct((rows, width * size), BF16) for width in widths],
        in_specs=[ANY] * (len(pieces) + 1),
        out_specs=[ANY] * len(widths),
        scratch_shapes=[pltpu.SemaphoreType.DMA((len(widths) * size,))],
        compiler_params=SMALL,
        name="spread",
    )(*pieces, got)


def dot(a, b):
    return lax.dot_general(a, b, (((1,), (0,)), ((), ())), preferred_element_type=F32)


def dot_t(a, b):
    return lax.dot_general(a, b, (((1,), (1,)), ((), ())), preferred_element_type=F32)


def fold(x, op):
    parts = [x[at : at + 8] for at in range(0, x.shape[0], 8)]
    while len(parts) > 1:
        parts = [
            op(*parts[at : at + 2]) if at + 1 < len(parts) else parts[at]
            for at in range(0, len(parts), 2)
        ]
    return parts[0]


def taker(refs):
    refs = list(refs)
    return lambda count: [refs.pop(0) for _ in range(count)]


def stacked(rows, base, group, first=0):
    parts = [slice(first + at * HEAD_DIM, first + (at + 1) * HEAD_DIM) for at in range(group)]
    return jnp.concatenate([rows[base : base + TILE, part] for part in parts], axis=0)


def unstacked(rows, base, group, value):
    for at in range(group):
        part = slice(at * TILE, (at + 1) * TILE)
        rows[base : base + TILE, at * HEAD_DIM : (at + 1) * HEAD_DIM] = value[part]


def set_values(va, values):
    lane = lax.broadcasted_iota(jnp.int32, values.shape, 1)
    va[:, :HEAD_DIM] = values
    va[:, HEAD_DIM:] = jnp.where(lane < 2, 1.0, 0.0).astype(BF16)


def add_rows(target, start, old, value):
    if old:
        target[start : start + old, :] += value[:old]
    if old < value.shape[0]:
        target[start + old : start + value.shape[0], :] = value[old:]


def score_gradients(ds_scr, e, dp):
    for at in range(0, e.shape[0], TILE):
        part = slice(at, at + TILE)
        ds_scr[part, :] = (e[part, :].astype(F32) * dp[part, :]).astype(BF16)


def pipeline(tiles, *stages):
    for step in range(tiles + len(stages) - 1):
        for behind, stage in enumerate(stages):
            if 0 <= step - behind < tiles:
                stage(step - behind)


def gradient_rows(qg, base, group, scale, out):
    first = qg.shape[1] // 2
    columns = jnp.broadcast_to(scale, (HEAD_DIM, scale.shape[1])).T
    g2 = (stacked(qg, base, group, first).astype(F32) * columns).astype(BF16)
    delta = jnp.sum(g2.astype(F32) * out.astype(F32), axis=1, keepdims=True)
    high = delta.astype(BF16).astype(F32)
    lane = lax.broadcasted_iota(jnp.int32, g2.shape, 1)
    extra = jnp.where(lane == 0, -high, jnp.where(lane == 1, high - delta, 0.0))
    return g2, jnp.concatenate([g2, extra.astype(BF16)], axis=1)


def own_rows(tile):
    start = tile * (tile + 1) // 2 * TILE
    return slice(start, start + (tile + 1) * TILE)


def query_columns(qg, seg_q, base, group):
    mine = jnp.concatenate([seg_q[base : base + TILE, :]] * group, axis=0)
    return jnp.concatenate([stacked(qg, base, group), mine], axis=1)


def fold_rows(rows, op):
    parts = [fold(rows[at : at + TILE, :], op) for at in range(0, rows.shape[0], TILE)]
    whole = functools.reduce(op, parts)
    reduce = jnp.max if op is jnp.maximum else jnp.sum
    return reduce(whole, axis=0, keepdims=True)


def weigh(scores, top, keep):
    total = None
    for at in range(0, scores.shape[0], TILE):
        part = slice(at, at + TILE)
        e = jnp.exp2(scores[part, :] * exp2_scale - top)
        keep[part, :] = e.astype(BF16)
        e = fold(e, jnp.add)
        total = e if total is None else total + e
    return jnp.sum(total, axis=0, keepdims=True)


def tile_causal(group):
    row_of = lax.broadcasted_iota(jnp.int32, (TILE, TILE), 0)
    col_of = lax.broadcasted_iota(jnp.int32, (TILE, TILE), 1)
    return jnp.concatenate([row_of <= col_of] * group, axis=1)


def own_body(size, core, masks, tok, group, *refs):
    take = taker(refs)
    (seg_k, seg_q), qg_pieces, (kv,) = take(2), take(len(masks)), take(1)
    e_own, out_part, stats = take(3)
    qg, ka, vt, s_scr = take(4)
    wide, tiles = group * TILE, tok // TILE
    place_rows(size, core, masks, qg_pieces, qg)
    ka[:, :HEAD_DIM] = kv[:, :HEAD_DIM]
    ka[:, HEAD_DIM:] = seg_k[WINDOW:, :]
    vt[...] = kv[:, HEAD_DIM:].T
    causal = tile_causal(group)

    def scores(tile):
        queries = query_columns(qg, seg_q, tile * TILE, group)
        s_scr[tile % 2, : (tile + 1) * TILE, :] = dot_t(ka[: (tile + 1) * TILE, :], queries)

    def weights(tile):
        base, turn = tile * TILE, tile % 2
        last = slice(base, base + TILE)
        s_scr[turn, last, :] = jnp.where(causal, s_scr[turn, last, :], FAR)
        rows = s_scr.at[turn, : base + TILE, :]
        top = fold_rows(rows, jnp.maximum) * exp2_scale
        stats[tile : tile + 1, :] = top
        stats[tiles + tile : tiles + tile + 1, :] = weigh(rows, top, e_own.at[own_rows(tile), :])

    def outputs(tile):
        e = e_own[own_rows(tile), :]
        out_part[:, tile * wide : (tile + 1) * wide] = dot(vt[:, : (tile + 1) * TILE], e)

    pipeline(tiles, scores, weights, outputs)


def forward_body(size, core, masks, reach, tok, group, *refs):
    take = taker(refs)
    (seg_k, seg_q), qg_pieces, kvs = take(2), take(len(masks)), take(reach)
    out_own, stats = take(2)
    out_pieces, sent, (outs, own_scale, dq_part) = take(len(masks)), take(reach), take(3)
    qg, ka, va, kt, vt, dk, dv, s_scr, e_scr, dp_scr, ds_scr, g_scr = take(12)
    wide, tiles = group * TILE, tok // TILE
    place_rows(size, core, masks, qg_pieces, qg)
    ka[:, HEAD_DIM:] = seg_k[:WINDOW, :]
    for lag in range(1, reach + 1):
        there = slice((reach - lag) * tok, (reach - lag + 1) * tok)
        kv = kvs[lag - 1][...]
        ka[there, :HEAD_DIM] = kv[:, :HEAD_DIM]
        kt[:, there] = kv[:, :HEAD_DIM].T
        vt[:, there] = kv[:, HEAD_DIM:].T
        set_values(va.at[there, :], kv[:, HEAD_DIM:])
    beyond = ~tile_causal(group)

    def scores(tile):
        base = tile * TILE
        queries = query_columns(qg, seg_q, base, group)
        s_scr[tile % 2, : WINDOW - base, :] = dot_t(ka[base:, :], queries)

    scales = {}

    def weights(tile):
        early = WINDOW - tile * TILE
        turn = tile % 2
        s_scr[turn, :TILE, :] = jnp.where(beyond, s_scr[turn, :TILE, :], FAR)
        rows = s_scr.at[turn, :early, :]
        top_own = stats[tile : tile + 1, :]
        top = jnp.maximum(fold_rows(rows, jnp.maximum) * exp2_scale, top_own)
        total = weigh(rows, top, e_scr.at[tile % 3, :early, :])
        scale = jnp.exp2(top_own - top)
        inv = 1.0 / (total + stats[tiles + tile : tiles + tile + 1, :] * scale)
        own_scale[tile : tile + 1, :] = inv * scale
        scales[tile] = scale, inv

    def outputs(tile):
        base, turn = tile * TILE, tile % 2
        early = WINDOW - base
        scale, inv = scales.pop(tile)
        out = dot(vt[:, base:], e_scr[tile % 3, :early, :])
        out = out + out_own[:, tile * wide : (tile + 1) * wide] * scale
        out = (out * inv).T.astype(BF16)
        unstacked(outs, base, group, out)
        g_scr[turn], g_wide = gradient_rows(qg, base, group, inv, out)
        dp_scr[turn, :early, :] = dot_t(va[base:, :], g_wide)

    def gradients(tile):
        base, turn = tile * TILE, tile % 2
        early = WINDOW - base
        e = e_scr[tile % 3, :early, :]
        old = early if tile else 0
        add_rows(dv, base, old, dot(e, g_scr[turn]))
        score_gradients(ds_scr.at[turn, :early, :], e, dp_scr.at[turn, :early, :])
        ds = ds_scr[turn, :early, :]
        add_rows(dk, base, old, dot(ds, stacked(qg, base, group)))
        dq_part[:, tile * wide : (tile + 1) * wide] = dot(kt[:, base:], ds)

    pipeline(tiles, scores, weights, outputs, gradients)

    for lag in range(1, reach + 1):
        there = slice((reach - lag) * tok, (reach - lag + 1) * tok)
        sent[lag - 1][:, :HEAD_DIM] = (dk[there, :] * logit_scale).astype(BF16)
        sent[lag - 1][:, HEAD_DIM:] = dv[there, :].astype(BF16)
    take_rows(size, core, masks, lambda there: outs[there, :], out_pieces)


def backward_body(size, core, masks, tok, group, *refs):
    take = taker(refs)
    qg_pieces, (kv, e_own, outs, own_scale, dq_part) = take(len(masks)), take(5)
    dq_pieces, (dkv,) = take(len(masks)), take(1)
    qg, dqs, va, kt, dk, dv, dp_scr, ds_scr, g_scr = take(9)
    wide = group * TILE
    place_rows(size, core, masks, qg_pieces, qg)
    kt[...] = kv[:, :HEAD_DIM].T
    set_values(va, kv[:, HEAD_DIM:])

    def products(tile):
        base, turn = tile * TILE, tile % 2
        scale = own_scale[tile : tile + 1, :]
        out = stacked(outs, base, group)
        g_scr[turn], g_wide = gradient_rows(qg, base, group, scale, out)
        dp_scr[turn, : base + TILE, :] = dot_t(va[: base + TILE, :], g_wide)

    def gradients(tile):
        base, turn = tile * TILE, tile % 2
        count = base + TILE
        columns = slice(tile * wide, (tile + 1) * wide)
        e = e_own[own_rows(tile), :]
        add_rows(dv, 0, base, dot(e, g_scr[turn]))
        score_gradients(ds_scr.at[turn, :count, :], e, dp_scr.at[turn, :count, :])
        ds = ds_scr[turn, :count, :]
        add_rows(dk, 0, base, dot(ds, stacked(qg, base, group)))
        dq = (dq_part[:, columns] + dot(kt[:, :count], ds)) * logit_scale
        unstacked(dqs, base, group, dq.T.astype(BF16))

    pipeline(tok // TILE, products, gradients)
    dkv[:, :HEAD_DIM] = dk[...] * logit_scale
    dkv[:, HEAD_DIM:] = dv[...]
    take_rows(size, core, masks, lambda there: dqs[there, :], dq_pieces)


def attend_call(kernel, out_shape, scratch_shapes, flops, name, *args):
    return pl.pallas_call(
        kernel,
        out_shape=out_shape,
        in_specs=[VMEM] * len(args),
        out_specs=[VMEM] * len(out_shape),
        scratch_shapes=scratch_shapes,
        compiler_params=pltpu.CompilerParams(vmem_limit_bytes=24 * 1024 * 1024),
        cost_estimate=pl.CostEstimate(
            flops=flops, bytes_accessed=8 * 1024 * 1024, transcendentals=0
        ),
        name=name,
    )(*args)


def forward_own(documents, qg, kv, size):
    rows, cols = qg[0].shape
    tok = len(qg) * rows
    group = cols // (2 * HEAD_DIM)
    wide, tiles = group * TILE, tok // TILE
    return attend_call(
        functools.partial(own_body, size, core_mask(), chip_masks(size), tok, group),
        [
            jax.ShapeDtypeStruct((own_rows(tiles - 1).stop, wide), BF16),
            jax.ShapeDtypeStruct((HEAD_DIM, tiles * wide), F32),
            jax.ShapeDtypeStruct((2 * tiles, wide), F32),
        ],
        [
            pltpu.VMEM((tok, cols), BF16),
            pltpu.VMEM((tok, 2 * HEAD_DIM), BF16),
            pltpu.VMEM((HEAD_DIM, tok), BF16),
            pltpu.VMEM((2, tok, wide), F32),
        ],
        16 * tok * group * (WINDOW + TILE) * HEAD_DIM,
        "forward_own",
        *documents,
        *qg,
        kv,
    )


def forward(documents, qg, lags, carried, size):
    rows, cols = qg[0].shape
    tok, count, reach = len(qg) * rows, len(qg), len(lags)
    group = cols // (2 * HEAD_DIM)
    wide, tiles = group * TILE, tok // TILE
    half = jax.ShapeDtypeStruct((tok, 2 * HEAD_DIM), BF16)
    out_shape = [jax.ShapeDtypeStruct((rows, cols // 2), BF16)] * count + [half] * reach
    out_shape += [
        jax.ShapeDtypeStruct((tok, cols // 2), BF16),
        jax.ShapeDtypeStruct((tiles, wide), F32),
        jax.ShapeDtypeStruct((HEAD_DIM, tiles * wide), F32),
    ]
    scratch = [
        pltpu.VMEM((tok, cols), BF16),
        pltpu.VMEM((WINDOW, 2 * HEAD_DIM), BF16),
        pltpu.VMEM((WINDOW, 2 * HEAD_DIM), BF16),
        pltpu.VMEM((HEAD_DIM, WINDOW), BF16),
        pltpu.VMEM((HEAD_DIM, WINDOW), BF16),
        pltpu.VMEM((WINDOW, HEAD_DIM), F32),
        pltpu.VMEM((WINDOW, HEAD_DIM), F32),
        pltpu.VMEM((2, WINDOW, wide), F32),
        pltpu.VMEM((3, WINDOW, wide), BF16),
        pltpu.VMEM((2, WINDOW, wide), F32),
        pltpu.VMEM((2, WINDOW, wide), BF16),
        pltpu.VMEM((2, wide, HEAD_DIM), BF16),
    ]
    results = attend_call(
        functools.partial(
            forward_body, size, core_mask(), chip_masks(size), reach, tok, group
        ),
        out_shape,
        scratch,
        6 * tok * group * (WINDOW + TILE) * HEAD_DIM,
        "forward",
        *documents,
        *qg,
        *lags,
        *carried,
    )
    return results[:count], results[count : count + reach], results[count + reach :]


def backward(qg, kv, carried, size):
    rows, cols = qg[0].shape
    tok, count = len(qg) * rows, len(qg)
    group = cols // (2 * HEAD_DIM)
    wide = group * TILE
    results = attend_call(
        functools.partial(backward_body, size, core_mask(), chip_masks(size), tok, group),
        [jax.ShapeDtypeStruct((rows, cols // 2), BF16)] * count
        + [jax.ShapeDtypeStruct((tok, 2 * HEAD_DIM), F32)],
        [
            pltpu.VMEM((tok, cols), BF16),
            pltpu.VMEM((tok, cols // 2), BF16),
            pltpu.VMEM((tok, 2 * HEAD_DIM), BF16),
            pltpu.VMEM((HEAD_DIM, tok), BF16),
            pltpu.VMEM((tok, HEAD_DIM), F32),
            pltpu.VMEM((tok, HEAD_DIM), F32),
            pltpu.VMEM((2, tok, wide), F32),
            pltpu.VMEM((2, tok, wide), BF16),
            pltpu.VMEM((2, wide, HEAD_DIM), BF16),
        ],
        4 * tok * group * (WINDOW + TILE) * HEAD_DIM,
        "backward",
        *qg,
        kv,
        *carried,
    )
    return results[:count], results[count]


def document_columns(segment_ids, tok, size):
    start = (flat_index() // size) * tok
    padded = jnp.concatenate([jnp.full((WINDOW,), -1, jnp.int32), segment_ids])
    keys = lax.dynamic_slice_in_dim(padded, start, WINDOW + tok, 0)
    queries = lax.dynamic_slice_in_dim(segment_ids, start, tok, 0)
    number = jnp.arange(HEAD_DIM, dtype=jnp.int32)[None, :]
    return (
        jnp.where(keys[:, None] == number, 0.0, FAR).astype(BF16),
        jnp.where(queries[:, None] == number, 1.0, 0.0).astype(BF16),
    )


def body(query, key, value, grad_out, segment_ids):
    size = key.shape[1] // HEAD_DIM
    rows = query.shape[0]
    tok = size * rows
    reach = WINDOW // tok
    assert reach * tok == WINDOW and device_count() % size == 0

    got = [swap(array, core_mask()) for array in (key, value, query, grad_out)]
    pieces = list(gather_cores((key, value), got[:2], size))
    pieces[0], query, grad_out, segment_ids = after(pieces[0], query, grad_out, segment_ids)
    documents = document_columns(segment_ids, tok, size)
    kv = join(swap_chips(pieces, size), size)
    lags = [shifted(kv, lag * size) for lag in range(1, reach + 1)]
    qg = swap_chips(gather_cores((query, grad_out), got[2:], size), size)

    e_own, *partial = forward_own(documents, qg, kv, size)
    out, sent, carried = forward(documents, qg, lags, partial, size)
    backs = [shifted(sent[lag - 1], -lag * size) for lag in range(1, reach + 1)]
    out = swap_chips(out, size)
    grad_q, dkv = backward(qg, kv, [e_own, *carried], size)
    both = after(*out, *grad_q)
    out, grad_q = both[: len(out)], both[len(out) :]
    grad_q = swap_chips(grad_q, size)
    grads = swap_chips(combine([dkv, *backs], size), size)
    return tuple(spread_cores([out, grad_q, grads], (1, 1, 2), size))


def solution(mesh):
    placed = P(("pipe", "tensor"), None)
    return jax.shard_map(
        body,
        mesh=mesh,
        in_specs=(placed, placed, placed, placed, P()),
        out_specs=(placed, placed, placed, placed),
        check_vma=False,
    )
```

```python
import functools

import jax
import jax.numpy as jnp
from jax import lax
from jax.experimental import pallas as pl
from jax.experimental.pallas import tpu as pltpu
from jax.sharding import PartitionSpec as P

HEAD_DIM = 128
WINDOW = 1024
TILE = 128

logit_scale = 168.0 ** (-0.5)
exp2_scale = logit_scale * 1.4426950408889634

FAR = -(2.0**30)
SMALL = pltpu.CompilerParams(vmem_limit_bytes=4 * 1024 * 1024)
ANY = pl.BlockSpec(memory_space=pl.ANY)
VMEM = pl.BlockSpec(memory_space=pltpu.VMEM)
F32 = jnp.float32
BF16 = jnp.bfloat16
BOTH = ("pipe", "tensor")


def flat_index():
    return lax.axis_index("pipe") * lax.axis_size("tensor") + lax.axis_index("tensor")


def device_count():
    return lax.axis_size("pipe") * lax.axis_size("tensor")


def swap(value, mask):
    return lax.ppermute(value, BOTH, [(i, i ^ mask) for i in range(device_count())])


def core_mask():
    return lax.axis_size("tensor")


def chip_masks(size):
    return [mask for mask in range(size) if not mask & core_mask()]


def swap_chips(pieces, size):
    return [pieces[0]] + [
        swap(piece, mask) for piece, mask in zip(pieces[1:], chip_masks(size)[1:])
    ]


def shifted(value, step):
    count = device_count()
    pairs = [(i, i + step) for i in range(count) if 0 <= i + step < count]
    return lax.ppermute(value, BOTH, pairs)


def partner(size, j):
    return lax.bitwise_xor(lax.rem(flat_index(), size), j)


def place(index, width):
    return pl.ds(pl.multiple_of(index * width, width), width)


def after(value, *others):
    return lax.optimization_barrier((value, *others))


def run_copies(copies, sems):
    started = []
    for at, (source, target) in enumerate(copies):
        copy = pltpu.make_async_copy(source, target, sems.at[at])
        copy.start()
        started.append(copy)
    for copy in started:
        copy.wait()


def small_call(kernel, out_shape, name, *args):
    return pl.pallas_call(
        kernel,
        out_shape=out_shape,
        in_specs=[VMEM] * len(args),
        out_specs=jax.tree.map(lambda _: VMEM, out_shape),
        compiler_params=SMALL,
        name=name,
    )(*args)


def this_core(array, size):
    core = core_mask()
    width = array.shape[1] // size
    shares = [array[:, r * width : (r + 1) * width] for r in range(size)]
    first, second = (
        jnp.concatenate([share for r, share in enumerate(shares) if (r // core) % 2 == at], axis=1)
        for at in range(2)
    )
    return jnp.where((flat_index() // core) % 2 == 0, first, second)


def stack_body(size, core, masks, count, *refs):
    own, got, pieces = refs[:count], refs[count : 2 * count], refs[2 * count :]
    rows = own[0].shape[0]
    for mask, piece in zip(masks, pieces):
        there = partner(size, mask)
        chip = there // (2 * core) * core + lax.rem(there, core)
        start = 0
        for mine, other in zip(own, got):
            width = other.shape[1] // size
            piece[:rows, start : start + width] = mine[:, place(chip, width)]
            piece[rows:, start : start + width] = other[:, place(there, width)]
            start += width


def gather_cores(arrays, got, size):
    masks = chip_masks(size)
    own = [this_core(array, size) for array in arrays]
    cols = sum(array.shape[1] // size for array in arrays)
    piece = jax.ShapeDtypeStruct((2 * arrays[0].shape[0], cols), BF16)
    kernel = functools.partial(stack_body, size, core_mask(), masks, len(arrays))
    return small_call(kernel, [piece] * len(masks), "stack", *own, *got)


def place_rows(size, core, masks, pieces, out):
    for mask, piece in zip(masks, pieces):
        rows = piece.shape[0] // 2
        out[place(partner(size, mask), rows), :] = piece[:rows, :]
        out[place(partner(size, mask ^ core), rows), :] = piece[rows:, :]


def take_rows(size, core, masks, source, pieces):
    for mask, piece in zip(masks, pieces):
        rows = piece.shape[0] // 2
        piece[:rows, :] = source(place(partner(size, mask), rows))
        piece[rows:, :] = source(place(partner(size, mask ^ core), rows))


def take_halves(size, core, masks, source, own, give):
    rows = own.shape[0] // len(masks)
    for at, mask in enumerate(masks):
        part = slice(at * rows, (at + 1) * rows)
        own[part, :] = source(place(partner(size, mask), rows))
        give[part, :] = source(place(partner(size, mask ^ core), rows))


def take_gradients(size, core, masks, dk, dv, halves):
    def source(there):
        return jnp.concatenate([dk[there, :] * logit_scale, dv[there, :]], axis=1).astype(BF16)

    take_halves(size, core, masks, source, *halves)


def join(pieces, size):
    rows, cols = pieces[0].shape
    core, masks = core_mask(), chip_masks(size)

    def kernel(*refs):
        place_rows(size, core, masks, refs[:-1], refs[-1])

    out = jax.ShapeDtypeStruct((len(pieces) * rows, cols), BF16)
    return small_call(kernel, out, "join", *pieces)


def lay(own, got):
    def kernel(own, got, out):
        rows = own.shape[0]
        out[:rows, :] = own[...]
        out[rows:, :] = got[...]

    both = jax.ShapeDtypeStruct((2 * own.shape[0], own.shape[1]), BF16)
    return small_call(kernel, both, "lay", own, got)


def combine(own, got, backs, size):
    count = len(chip_masks(size))
    half = own.shape[0]
    rows = half // count

    def kernel(*refs):
        terms, pieces = refs[2:-count], refs[-count:]
        for side in (0, 1):
            for at, piece in enumerate(pieces):
                value = refs[side][at * rows : (at + 1) * rows, :].astype(F32)
                start = side * half + at * rows
                for term in terms:
                    value = value + term[start : start + rows, :].astype(F32)
                piece[side * rows : (side + 1) * rows, :] = value.astype(BF16)

    piece = jax.ShapeDtypeStruct((2 * rows, own.shape[1]), BF16)
    return small_call(kernel, [piece] * count, "combine", own, got, *backs)


def bottom_body(*refs):
    count = len(refs) // 3
    for at, piece in enumerate(refs[: 2 * count]):
        rows, width = piece.shape[0] // 2, piece.shape[1]
        start = at % 2 * width
        refs[2 * count + at // 2][:, start : start + width] = piece[rows:, :]


def spread_body(size, core, masks, *refs):
    take = taker(refs)
    sets, got, sems = [take(len(masks)) for _ in range(3)], take(len(masks)), refs[-1]
    sets_out = [refs[-5:-4], refs[-4:-3], refs[-3:-1]]
    copies, hopped = [], 0
    for pieces, outs in zip(sets, sets_out):
        for mask, piece in zip(masks, pieces):
            rows, width = piece.shape[0] // 2, piece.shape[1] // len(outs)
            for at, out in enumerate(outs):
                part = slice(at * width, (at + 1) * width)
                if len(outs) == 1:
                    start = hopped % 2 * width
                    other = got[hopped // 2].at[:, start : start + width]
                    hopped += 1
                else:
                    other = piece.at[rows:, part]
                mine = out.at[:, place(partner(size, mask), width)]
                copies.append((piece.at[:rows, part], mine))
                copies.append((other, out.at[:, place(partner(size, mask ^ core), width)]))
    run_copies(copies, sems)


def spread(out, grad_q, grads, size):
    rows, width = out[0].shape[0] // 2, out[0].shape[1]
    give = [jax.ShapeDtypeStruct((rows, 2 * width), BF16)] * len(out)
    give = small_call(bottom_body, give, "bottom", *out, *grad_q)
    got = [swap(part, core_mask()) for part in give]
    widths = [width, width, grads[0].shape[1] // 2, grads[0].shape[1] // 2]
    pieces = [*out, *grad_q, *grads]
    return pl.pallas_call(
        functools.partial(spread_body, size, core_mask(), chip_masks(size)),
        out_shape=[jax.ShapeDtypeStruct((rows, width * size), BF16) for width in widths],
        in_specs=[ANY] * (len(pieces) + len(got)),
        out_specs=[ANY] * 4,
        scratch_shapes=[pltpu.SemaphoreType.DMA((4 * size,))],
        compiler_params=SMALL,
        name="spread",
    )(*pieces, *got)


def dot(a, b):
    return lax.dot_general(a, b, (((1,), (0,)), ((), ())), preferred_element_type=F32)


def dot_t(a, b):
    return lax.dot_general(a, b, (((1,), (1,)), ((), ())), preferred_element_type=F32)


def fold(x, op):
    parts = [x[at : at + 8] for at in range(0, x.shape[0], 8)]
    while len(parts) > 1:
        parts = [
            op(*parts[at : at + 2]) if at + 1 < len(parts) else parts[at]
            for at in range(0, len(parts), 2)
        ]
    return parts[0]


def taker(refs):
    refs = list(refs)
    return lambda count: [refs.pop(0) for _ in range(count)]


def stacked(rows, base, group, first=0):
    parts = [slice(first + at * HEAD_DIM, first + (at + 1) * HEAD_DIM) for at in range(group)]
    return jnp.concatenate([rows[base : base + TILE, part] for part in parts], axis=0)


def unstacked(rows, base, group, value):
    for at in range(group):
        part = slice(at * TILE, (at + 1) * TILE)
        rows[base : base + TILE, at * HEAD_DIM : (at + 1) * HEAD_DIM] = value[part]


def set_values(va, values):
    lane = lax.broadcasted_iota(jnp.int32, values.shape, 1)
    va[:, :HEAD_DIM] = values
    va[:, HEAD_DIM:] = jnp.where(lane < 2, 1.0, 0.0).astype(BF16)


def add_rows(target, start, old, value):
    if old:
        target[start : start + old, :] += value[:old]
    if old < value.shape[0]:
        target[start + old : start + value.shape[0], :] = value[old:]


def score_gradients(ds_scr, e, dp):
    for at in range(0, e.shape[0], TILE):
        part = slice(at, at + TILE)
        ds_scr[part, :] = (e[part, :].astype(F32) * dp[part, :]).astype(BF16)


def pipeline(tiles, *stages):
    for step in range(tiles + len(stages) - 1):
        for behind, stage in enumerate(stages):
            if 0 <= step - behind < tiles:
                stage(step - behind)


def gradient_rows(qg, base, group, scale, out):
    first = qg.shape[1] // 2
    columns = jnp.broadcast_to(scale, (HEAD_DIM, scale.shape[1])).T
    g2 = (stacked(qg, base, group, first).astype(F32) * columns).astype(BF16)
    delta = jnp.sum(g2.astype(F32) * out.astype(F32), axis=1, keepdims=True)
    high = delta.astype(BF16).astype(F32)
    lane = lax.broadcasted_iota(jnp.int32, g2.shape, 1)
    extra = jnp.where(lane == 0, -high, jnp.where(lane == 1, high - delta, 0.0))
    return g2, jnp.concatenate([g2, extra.astype(BF16)], axis=1)


def own_rows(tile):
    start = tile * (tile + 1) // 2 * TILE
    return slice(start, start + (tile + 1) * TILE)


def query_columns(qg, seg_q, base, group):
    mine = jnp.concatenate([seg_q[base : base + TILE, :]] * group, axis=0)
    return jnp.concatenate([stacked(qg, base, group), mine], axis=1)


def fold_rows(rows, op):
    parts = [fold(rows[at : at + TILE, :], op) for at in range(0, rows.shape[0], TILE)]
    whole = functools.reduce(op, parts)
    reduce = jnp.max if op is jnp.maximum else jnp.sum
    return reduce(whole, axis=0, keepdims=True)


def weigh(scores, top, keep):
    total = None
    for at in range(0, scores.shape[0], TILE):
        part = slice(at, at + TILE)
        e = jnp.exp2(scores[part, :] * exp2_scale - top)
        keep[part, :] = e.astype(BF16)
        e = fold(e, jnp.add)
        total = e if total is None else total + e
    return jnp.sum(total, axis=0, keepdims=True)


def tile_causal(group):
    row_of = lax.broadcasted_iota(jnp.int32, (TILE, TILE), 0)
    col_of = lax.broadcasted_iota(jnp.int32, (TILE, TILE), 1)
    return jnp.concatenate([row_of <= col_of] * group, axis=1)


def own_body(size, core, masks, tok, group, *refs):
    take = taker(refs)
    (seg_k, seg_q), qg_pieces, (kv,) = take(2), take(len(masks)), take(1)
    e_own, out_part, stats = take(3)
    qg, ka, vt, s_scr = take(4)
    wide, tiles = group * TILE, tok // TILE
    place_rows(size, core, masks, qg_pieces, qg)
    ka[:, :HEAD_DIM] = kv[:, :HEAD_DIM]
    ka[:, HEAD_DIM:] = seg_k[WINDOW:, :]
    vt[...] = kv[:, HEAD_DIM:].T
    causal = tile_causal(group)

    def scores(tile):
        queries = query_columns(qg, seg_q, tile * TILE, group)
        s_scr[tile % 2, : (tile + 1) * TILE, :] = dot_t(ka[: (tile + 1) * TILE, :], queries)

    def weights(tile):
        base, turn = tile * TILE, tile % 2
        last = slice(base, base + TILE)
        s_scr[turn, last, :] = jnp.where(causal, s_scr[turn, last, :], FAR)
        rows = s_scr.at[turn, : base + TILE, :]
        top = fold_rows(rows, jnp.maximum) * exp2_scale
        stats[tile : tile + 1, :] = top
        stats[tiles + tile : tiles + tile + 1, :] = weigh(rows, top, e_own.at[own_rows(tile), :])

    def outputs(tile):
        e = e_own[own_rows(tile), :]
        out_part[:, tile * wide : (tile + 1) * wide] = dot(vt[:, : (tile + 1) * TILE], e)

    pipeline(tiles, scores, weights, outputs)


def forward_body(size, core, masks, reach, tok, group, *refs):
    take = taker(refs)
    (seg_k, seg_q), qg_pieces, kvs = take(2), take(len(masks)), take(reach)
    out_own, stats = take(2)
    out_pieces, sent, (outs, own_scale, dq_part) = take(len(masks)), take(2 * reach), take(3)
    qg, ka, va, kt, vt, dk, dv, s_scr, e_scr, dp_scr, ds_scr, g_scr = take(12)
    wide, tiles = group * TILE, tok // TILE
    place_rows(size, core, masks, qg_pieces, qg)
    ka[:, HEAD_DIM:] = seg_k[:WINDOW, :]
    for lag in range(1, reach + 1):
        there = slice((reach - lag) * tok, (reach - lag + 1) * tok)
        kv = kvs[lag - 1][...]
        ka[there, :HEAD_DIM] = kv[:, :HEAD_DIM]
        kt[:, there] = kv[:, :HEAD_DIM].T
        vt[:, there] = kv[:, HEAD_DIM:].T
        set_values(va.at[there, :], kv[:, HEAD_DIM:])
    beyond = ~tile_causal(group)

    def scores(tile):
        base = tile * TILE
        queries = query_columns(qg, seg_q, base, group)
        s_scr[tile % 2, : WINDOW - base, :] = dot_t(ka[base:, :], queries)

    scales = {}

    def weights(tile):
        early = WINDOW - tile * TILE
        turn = tile % 2
        s_scr[turn, :TILE, :] = jnp.where(beyond, s_scr[turn, :TILE, :], FAR)
        rows = s_scr.at[turn, :early, :]
        top_own = stats[tile : tile + 1, :]
        top = jnp.maximum(fold_rows(rows, jnp.maximum) * exp2_scale, top_own)
        total = weigh(rows, top, e_scr.at[tile % 3, :early, :])
        scale = jnp.exp2(top_own - top)
        inv = 1.0 / (total + stats[tiles + tile : tiles + tile + 1, :] * scale)
        own_scale[tile : tile + 1, :] = inv * scale
        scales[tile] = scale, inv

    def outputs(tile):
        base, turn = tile * TILE, tile % 2
        early = WINDOW - base
        scale, inv = scales.pop(tile)
        out = dot(vt[:, base:], e_scr[tile % 3, :early, :])
        out = out + out_own[:, tile * wide : (tile + 1) * wide] * scale
        out = (out * inv).T.astype(BF16)
        unstacked(outs, base, group, out)
        g_scr[turn], g_wide = gradient_rows(qg, base, group, inv, out)
        dp_scr[turn, :early, :] = dot_t(va[base:, :], g_wide)

    def gradients(tile):
        base, turn = tile * TILE, tile % 2
        early = WINDOW - base
        e = e_scr[tile % 3, :early, :]
        old = early if tile else 0
        add_rows(dv, base, old, dot(e, g_scr[turn]))
        score_gradients(ds_scr.at[turn, :early, :], e, dp_scr.at[turn, :early, :])
        ds = ds_scr[turn, :early, :]
        add_rows(dk, base, old, dot(ds, stacked(qg, base, group)))
        dq_part[:, tile * wide : (tile + 1) * wide] = dot(kt[:, base:], ds)

    pipeline(tiles, scores, weights, outputs, gradients)

    for lag in range(1, reach + 1):
        there = slice((reach - lag) * tok, (reach - lag + 1) * tok)
        halves = sent[2 * lag - 2 : 2 * lag]
        take_gradients(size, core, masks, dk.at[there, :], dv.at[there, :], halves)
    take_rows(size, core, masks, lambda there: outs[there, :], out_pieces)


def backward_body(size, core, masks, tok, group, *refs):
    take = taker(refs)
    qg_pieces, (kv, e_own, outs, own_scale, dq_part) = take(len(masks)), take(5)
    dq_pieces, dkv_halves = take(len(masks)), take(2)
    qg, dqs, va, kt, dk, dv, dp_scr, ds_scr, g_scr = take(9)
    wide = group * TILE
    place_rows(size, core, masks, qg_pieces, qg)
    kt[...] = kv[:, :HEAD_DIM].T
    set_values(va, kv[:, HEAD_DIM:])

    def products(tile):
        base, turn = tile * TILE, tile % 2
        scale = own_scale[tile : tile + 1, :]
        out = stacked(outs, base, group)
        g_scr[turn], g_wide = gradient_rows(qg, base, group, scale, out)
        dp_scr[turn, : base + TILE, :] = dot_t(va[: base + TILE, :], g_wide)

    def gradients(tile):
        base, turn = tile * TILE, tile % 2
        count = base + TILE
        columns = slice(tile * wide, (tile + 1) * wide)
        e = e_own[own_rows(tile), :]
        add_rows(dv, 0, base, dot(e, g_scr[turn]))
        score_gradients(ds_scr.at[turn, :count, :], e, dp_scr.at[turn, :count, :])
        ds = ds_scr[turn, :count, :]
        add_rows(dk, 0, base, dot(ds, stacked(qg, base, group)))
        dq = (dq_part[:, columns] + dot(kt[:, :count], ds)) * logit_scale
        unstacked(dqs, base, group, dq.T.astype(BF16))

    pipeline(tok // TILE, products, gradients)
    take_gradients(size, core, masks, dk, dv, dkv_halves)
    take_rows(size, core, masks, lambda there: dqs[there, :], dq_pieces)


def attend_call(kernel, out_shape, scratch_shapes, flops, name, *args):
    return pl.pallas_call(
        kernel,
        out_shape=out_shape,
        in_specs=[VMEM] * len(args),
        out_specs=[VMEM] * len(out_shape),
        scratch_shapes=scratch_shapes,
        compiler_params=pltpu.CompilerParams(vmem_limit_bytes=24 * 1024 * 1024),
        cost_estimate=pl.CostEstimate(
            flops=flops, bytes_accessed=8 * 1024 * 1024, transcendentals=0
        ),
        name=name,
    )(*args)


def forward_own(documents, qg, kv, size):
    rows, cols = qg[0].shape
    tok = len(qg) * rows
    group = cols // (2 * HEAD_DIM)
    wide, tiles = group * TILE, tok // TILE
    return attend_call(
        functools.partial(own_body, size, core_mask(), chip_masks(size), tok, group),
        [
            jax.ShapeDtypeStruct((own_rows(tiles - 1).stop, wide), BF16),
            jax.ShapeDtypeStruct((HEAD_DIM, tiles * wide), F32),
            jax.ShapeDtypeStruct((2 * tiles, wide), F32),
        ],
        [
            pltpu.VMEM((tok, cols), BF16),
            pltpu.VMEM((tok, 2 * HEAD_DIM), BF16),
            pltpu.VMEM((HEAD_DIM, tok), BF16),
            pltpu.VMEM((2, tok, wide), F32),
        ],
        16 * tok * group * (WINDOW + TILE) * HEAD_DIM,
        "forward_own",
        *documents,
        *qg,
        kv,
    )


def forward(documents, qg, lags, carried, size):
    rows, cols = qg[0].shape
    tok, count, reach = len(qg) * rows, len(qg), len(lags)
    group = cols // (2 * HEAD_DIM)
    wide, tiles = group * TILE, tok // TILE
    half = jax.ShapeDtypeStruct((tok // 2, 2 * HEAD_DIM), BF16)
    out_shape = [jax.ShapeDtypeStruct((rows, cols // 2), BF16)] * count + [half] * 2 * reach
    out_shape += [
        jax.ShapeDtypeStruct((tok, cols // 2), BF16),
        jax.ShapeDtypeStruct((tiles, wide), F32),
        jax.ShapeDtypeStruct((HEAD_DIM, tiles * wide), F32),
    ]
    scratch = [
        pltpu.VMEM((tok, cols), BF16),
        pltpu.VMEM((WINDOW, 2 * HEAD_DIM), BF16),
        pltpu.VMEM((WINDOW, 2 * HEAD_DIM), BF16),
        pltpu.VMEM((HEAD_DIM, WINDOW), BF16),
        pltpu.VMEM((HEAD_DIM, WINDOW), BF16),
        pltpu.VMEM((WINDOW, HEAD_DIM), F32),
        pltpu.VMEM((WINDOW, HEAD_DIM), F32),
        pltpu.VMEM((2, WINDOW, wide), F32),
        pltpu.VMEM((3, WINDOW, wide), BF16),
        pltpu.VMEM((2, WINDOW, wide), F32),
        pltpu.VMEM((2, WINDOW, wide), BF16),
        pltpu.VMEM((2, wide, HEAD_DIM), BF16),
    ]
    results = attend_call(
        functools.partial(
            forward_body, size, core_mask(), chip_masks(size), reach, tok, group
        ),
        out_shape,
        scratch,
        6 * tok * group * (WINDOW + TILE) * HEAD_DIM,
        "forward",
        *documents,
        *qg,
        *lags,
        *carried,
    )
    sent, carried = results[count : count + 2 * reach], results[count + 2 * reach :]
    return results[:count], sent, carried


def backward(qg, kv, carried, size):
    rows, cols = qg[0].shape
    tok, count = len(qg) * rows, len(qg)
    group = cols // (2 * HEAD_DIM)
    wide = group * TILE
    results = attend_call(
        functools.partial(backward_body, size, core_mask(), chip_masks(size), tok, group),
        [jax.ShapeDtypeStruct((rows, cols // 2), BF16)] * count
        + [jax.ShapeDtypeStruct((tok // 2, 2 * HEAD_DIM), BF16)] * 2,
        [
            pltpu.VMEM((tok, cols), BF16),
            pltpu.VMEM((tok, cols // 2), BF16),
            pltpu.VMEM((tok, 2 * HEAD_DIM), BF16),
            pltpu.VMEM((HEAD_DIM, tok), BF16),
            pltpu.VMEM((tok, HEAD_DIM), F32),
            pltpu.VMEM((tok, HEAD_DIM), F32),
            pltpu.VMEM((2, tok, wide), F32),
            pltpu.VMEM((2, tok, wide), BF16),
            pltpu.VMEM((2, wide, HEAD_DIM), BF16),
        ],
        4 * tok * group * (WINDOW + TILE) * HEAD_DIM,
        "backward",
        *qg,
        kv,
        *carried,
    )
    return results[:count], results[count:]


def document_columns(segment_ids, tok, size):
    start = (flat_index() // size) * tok
    padded = jnp.concatenate([jnp.full((WINDOW,), -1, jnp.int32), segment_ids])
    keys = lax.dynamic_slice_in_dim(padded, start, WINDOW + tok, 0)
    queries = lax.dynamic_slice_in_dim(segment_ids, start, tok, 0)
    number = jnp.arange(HEAD_DIM, dtype=jnp.int32)[None, :]
    return (
        jnp.where(keys[:, None] == number, 0.0, FAR).astype(BF16),
        jnp.where(queries[:, None] == number, 1.0, 0.0).astype(BF16),
    )


def body(query, key, value, grad_out, segment_ids):
    size = key.shape[1] // HEAD_DIM
    rows = query.shape[0]
    tok = size * rows
    reach = WINDOW // tok
    assert reach * tok == WINDOW and device_count() % size == 0

    got = [swap(array, core_mask()) for array in (key, value, query, grad_out)]
    pieces = list(gather_cores((key, value), got[:2], size))
    pieces[0], query, grad_out, segment_ids = after(pieces[0], query, grad_out, segment_ids)
    documents = document_columns(segment_ids, tok, size)
    kv = join(swap_chips(pieces, size), size)
    lags = [shifted(kv, lag * size) for lag in range(1, reach + 1)]
    qg = swap_chips(gather_cores((query, grad_out), got[2:], size), size)

    e_own, *partial = forward_own(documents, qg, kv, size)
    out, sent, carried = forward(documents, qg, lags, partial, size)
    laid = [
        lay(sent[2 * lag - 2], swap(sent[2 * lag - 1], core_mask()))
        for lag in range(1, reach + 1)
    ]
    backs = [shifted(rows, -lag * size) for lag, rows in enumerate(laid, 1)]
    out = swap_chips(out, size)
    kv, *_ = after(kv, *laid)
    grad_q, dkv = backward(qg, kv, [e_own, *carried], size)
    grad_q = swap_chips(grad_q, size)
    give, *out = after(dkv[1], *out)
    grads = list(combine(dkv[0], swap(give, core_mask()), backs, size))
    grads[0], *both = after(grads[0], *out, *grad_q)
    out, grad_q = both[: len(out)], both[len(out) :]
    return tuple(spread(out, grad_q, swap_chips(grads, size), size))


def solution(mesh):
    placed = P(("pipe", "tensor"), None)
    return jax.shard_map(
        body,
        mesh=mesh,
        in_specs=(placed, placed, placed, placed, P()),
        out_specs=(placed, placed, placed, placed),
        check_vma=False,
    )
```

```python
import functools

import jax
import jax.numpy as jnp
from jax import lax
from jax.experimental import pallas as pl
from jax.experimental.pallas import tpu as pltpu
from jax.sharding import PartitionSpec as P

HEAD_DIM = 128
WINDOW = 1024
TILE = 128

logit_scale = 168.0 ** (-0.5)
exp2_scale = logit_scale * 1.4426950408889634

FAR = -(2.0**30)
SMALL = pltpu.CompilerParams(vmem_limit_bytes=4 * 1024 * 1024)
ANY = pl.BlockSpec(memory_space=pl.ANY)
VMEM = pl.BlockSpec(memory_space=pltpu.VMEM)
F32 = jnp.float32
BF16 = jnp.bfloat16
BOTH = ("pipe", "tensor")


def flat_index():
    return lax.axis_index("pipe") * lax.axis_size("tensor") + lax.axis_index("tensor")


def device_count():
    return lax.axis_size("pipe") * lax.axis_size("tensor")


def swap(value, mask):
    return lax.ppermute(value, BOTH, [(i, i ^ mask) for i in range(device_count())])


def core_mask():
    return lax.axis_size("tensor")


def chip_masks(size):
    masks = [mask for mask in range(size) if not mask & core_mask()]
    order = masks[:1] + masks[2:0:-1] + masks[3:]
    return list(zip(masks, order))


def swap_chips(pieces, size):
    core, received = core_mask(), list(pieces)
    for at, masks in list(enumerate(chip_masks(size)))[1:]:
        pairs = [(i, i ^ masks[i // core % 2]) for i in range(device_count())]
        received[at] = lax.ppermute(pieces[at], BOTH, pairs)
    return received


def shifted(value, step):
    count = device_count()
    pairs = [(i, i + step) for i in range(count) if 0 <= i + step < count]
    return lax.ppermute(value, BOTH, pairs)


def partner(size, masks, flip=0, twin=False):
    core, me = core_mask(), lax.rem(flat_index(), size)
    odd = lax.rem(lax.div(me, core), 2) == 1
    mask = jnp.where(odd != twin, masks[1], masks[0])
    return lax.bitwise_xor(me, lax.bitwise_xor(mask, flip))


def place(index, width):
    return pl.ds(pl.multiple_of(index * width, width), width)


def after(value, *others):
    return lax.optimization_barrier((value, *others))


def run_copies(copies, sems):
    started = []
    for at, (source, target) in enumerate(copies):
        copy = pltpu.make_async_copy(source, target, sems.at[at])
        copy.start()
        started.append(copy)
    for copy in started:
        copy.wait()


def small_call(kernel, out_shape, name, *args):
    return pl.pallas_call(
        kernel,
        out_shape=out_shape,
        in_specs=[VMEM] * len(args),
        out_specs=jax.tree.map(lambda _: VMEM, out_shape),
        compiler_params=SMALL,
        name=name,
    )(*args)


def this_core(array, size):
    core = core_mask()
    width = array.shape[1] // size
    shares = [array[:, r * width : (r + 1) * width] for r in range(size)]
    first, second = (
        jnp.concatenate([share for r, share in enumerate(shares) if (r // core) % 2 == at], axis=1)
        for at in range(2)
    )
    return jnp.where((flat_index() // core) % 2 == 0, first, second)


def stack_body(size, core, masks, count, *refs):
    own, got, pieces = refs[:count], refs[count : 2 * count], refs[2 * count :]
    rows = own[0].shape[0]
    for mask, piece in zip(masks, pieces):
        there = partner(size, mask)
        chip = there // (2 * core) * core + lax.rem(there, core)
        start = 0
        for mine, other in zip(own, got):
            width = other.shape[1] // size
            piece[:rows, start : start + width] = mine[:, place(chip, width)]
            piece[rows:, start : start + width] = other[:, place(there, width)]
            start += width


def gather_cores(arrays, got, size):
    masks = chip_masks(size)
    own = [this_core(array, size) for array in arrays]
    cols = sum(array.shape[1] // size for array in arrays)
    piece = jax.ShapeDtypeStruct((2 * arrays[0].shape[0], cols), BF16)
    kernel = functools.partial(stack_body, size, core_mask(), masks, len(arrays))
    return small_call(kernel, [piece] * len(masks), "stack", *own, *got)


def place_rows(size, core, masks, pieces, out):
    for mask, piece in zip(masks, pieces):
        rows = piece.shape[0] // 2
        out[place(partner(size, mask), rows), :] = piece[:rows, :]
        out[place(partner(size, mask, core), rows), :] = piece[rows:, :]


def take_rows(size, core, masks, source, pieces):
    for mask, piece in zip(masks, pieces):
        rows = piece.shape[0] // 2
        piece[:rows, :] = source(place(partner(size, mask), rows))
        piece[rows:, :] = source(place(partner(size, mask, core), rows))


def join(pieces, size):
    rows, cols = pieces[0].shape
    core, masks = core_mask(), chip_masks(size)

    def kernel(*refs):
        place_rows(size, core, masks, refs[:-1], refs[-1])

    out = jax.ShapeDtypeStruct((len(pieces) * rows, cols), BF16)
    return small_call(kernel, out, "join", *pieces)


def combine(terms, size):
    tok, cols = terms[0].shape
    core, masks = core_mask(), chip_masks(size)

    def kernel(*refs):
        added = refs[: len(terms)]

        def source(there):
            total = added[0][there, :]
            for term in added[1:]:
                total = total + term[there, :].astype(F32)
            return total.astype(BF16)

        take_rows(size, core, masks, source, refs[len(terms) :])

    piece = jax.ShapeDtypeStruct((2 * (tok // size), cols), BF16)
    return small_call(kernel, [piece] * len(masks), "combine", *terms)


def bottom_body(*refs):
    out, start = refs[-1], 0
    for piece in refs[:-1]:
        rows, width = piece.shape[0] // 2, piece.shape[1]
        out[:, start : start + width] = piece[rows:, :]
        start += width


def spread_body(size, core, masks, counts, *refs):
    refs = list(refs)
    take = lambda count: [refs.pop(0) for _ in range(count)]
    sets = [take(len(masks)) for _ in counts]
    (got,), sets_out, (sems,) = take(1), [take(count) for count in counts], take(1)
    copies, start = [], 0
    for pieces, outs in zip(sets, sets_out):
        for mask, piece in zip(masks, pieces):
            rows, width = piece.shape[0] // 2, piece.shape[1] // len(outs)
            for at, out in enumerate(outs):
                mine = out.at[:, place(partner(size, mask), width)]
                other = out.at[:, place(partner(size, mask, core, True), width)]
                copies.append((piece.at[:rows, at * width : (at + 1) * width], mine))
                copies.append((got.at[:, start : start + width], other))
                start += width
    run_copies(copies, sems)


def spread_cores(sets, counts, size):
    pieces = [piece for part in sets for piece in part]
    rows = pieces[0].shape[0] // 2
    give = jax.ShapeDtypeStruct((rows, sum(piece.shape[1] for piece in pieces)), BF16)
    got = swap(small_call(bottom_body, give, "bottom", *pieces), core_mask())
    widths = [part[0].shape[1] // count for part, count in zip(sets, counts) for _ in range(count)]
    return pl.pallas_call(
        functools.partial(spread_body, size, core_mask(), chip_masks(size), counts),
        out_shape=[jax.ShapeDtypeStruct((rows, width * size), BF16) for width in widths],
        in_specs=[ANY] * (len(pieces) + 1),
        out_specs=[ANY] * len(widths),
        scratch_shapes=[pltpu.SemaphoreType.DMA((len(widths) * size,))],
        compiler_params=SMALL,
        name="spread",
    )(*pieces, got)


def dot(a, b):
    return lax.dot_general(a, b, (((1,), (0,)), ((), ())), preferred_element_type=F32)


def dot_t(a, b):
    return lax.dot_general(a, b, (((1,), (1,)), ((), ())), preferred_element_type=F32)


def fold(x, op):
    parts = [x[at : at + 8] for at in range(0, x.shape[0], 8)]
    while len(parts) > 1:
        parts = [
            op(*parts[at : at + 2]) if at + 1 < len(parts) else parts[at]
            for at in range(0, len(parts), 2)
        ]
    return parts[0]


def taker(refs):
    refs = list(refs)
    return lambda count: [refs.pop(0) for _ in range(count)]


def stacked(rows, base, group, first=0):
    parts = [slice(first + at * HEAD_DIM, first + (at + 1) * HEAD_DIM) for at in range(group)]
    return jnp.concatenate([rows[base : base + TILE, part] for part in parts], axis=0)


def unstacked(rows, base, group, value):
    for at in range(group):
        part = slice(at * TILE, (at + 1) * TILE)
        rows[base : base + TILE, at * HEAD_DIM : (at + 1) * HEAD_DIM] = value[part]


def set_values(va, values):
    lane = lax.broadcasted_iota(jnp.int32, values.shape, 1)
    va[:, :HEAD_DIM] = values
    va[:, HEAD_DIM:] = jnp.where(lane < 2, 1.0, 0.0).astype(BF16)


def add_rows(target, start, old, value):
    if old:
        target[start : start + old, :] += value[:old]
    if old < value.shape[0]:
        target[start + old : start + value.shape[0], :] = value[old:]


def score_gradients(ds_scr, e, dp):
    for at in range(0, e.shape[0], TILE):
        part = slice(at, at + TILE)
        ds_scr[part, :] = (e[part, :].astype(F32) * dp[part, :]).astype(BF16)


def pipeline(tiles, *stages):
    for step in range(tiles + len(stages) - 1):
        for behind, stage in enumerate(stages):
            if 0 <= step - behind < tiles:
                stage(step - behind)


def gradient_rows(qg, base, group, scale, out):
    first = qg.shape[1] // 2
    columns = jnp.broadcast_to(scale, (HEAD_DIM, scale.shape[1])).T
    g2 = (stacked(qg, base, group, first).astype(F32) * columns).astype(BF16)
    delta = jnp.sum(g2.astype(F32) * out.astype(F32), axis=1, keepdims=True)
    high = delta.astype(BF16).astype(F32)
    lane = lax.broadcasted_iota(jnp.int32, g2.shape, 1)
    extra = jnp.where(lane == 0, -high, jnp.where(lane == 1, high - delta, 0.0))
    return g2, jnp.concatenate([g2, extra.astype(BF16)], axis=1)


def own_rows(tile):
    start = tile * (tile + 1) // 2 * TILE
    return slice(start, start + (tile + 1) * TILE)


def query_columns(qg, seg_q, base, group):
    mine = jnp.concatenate([seg_q[base : base + TILE, :]] * group, axis=0)
    return jnp.concatenate([stacked(qg, base, group), mine], axis=1)


def fold_rows(rows, op):
    parts = [fold(rows[at : at + TILE, :], op) for at in range(0, rows.shape[0], TILE)]
    whole = functools.reduce(op, parts)
    reduce = jnp.max if op is jnp.maximum else jnp.sum
    return reduce(whole, axis=0, keepdims=True)


def weigh(scores, top, keep):
    total = None
    for at in range(0, scores.shape[0], TILE):
        part = slice(at, at + TILE)
        e = jnp.exp2(scores[part, :] * exp2_scale - top)
        keep[part, :] = e.astype(BF16)
        e = fold(e, jnp.add)
        total = e if total is None else total + e
    return jnp.sum(total, axis=0, keepdims=True)


def tile_causal(group):
    row_of = lax.broadcasted_iota(jnp.int32, (TILE, TILE), 0)
    col_of = lax.broadcasted_iota(jnp.int32, (TILE, TILE), 1)
    return jnp.concatenate([row_of <= col_of] * group, axis=1)


def own_body(size, core, masks, tok, group, *refs):
    take = taker(refs)
    (seg_k, seg_q), qg_pieces, (kv,) = take(2), take(len(masks)), take(1)
    e_own, out_part, stats = take(3)
    qg, ka, vt, s_scr = take(4)
    wide, tiles = group * TILE, tok // TILE
    place_rows(size, core, masks, qg_pieces, qg)
    ka[:, :HEAD_DIM] = kv[:, :HEAD_DIM]
    ka[:, HEAD_DIM:] = seg_k[WINDOW:, :]
    vt[...] = kv[:, HEAD_DIM:].T
    causal = tile_causal(group)

    def scores(tile):
        queries = query_columns(qg, seg_q, tile * TILE, group)
        s_scr[tile % 2, : (tile + 1) * TILE, :] = dot_t(ka[: (tile + 1) * TILE, :], queries)

    def weights(tile):
        base, turn = tile * TILE, tile % 2
        last = slice(base, base + TILE)
        s_scr[turn, last, :] = jnp.where(causal, s_scr[turn, last, :], FAR)
        rows = s_scr.at[turn, : base + TILE, :]
        top = fold_rows(rows, jnp.maximum) * exp2_scale
        stats[tile : tile + 1, :] = top
        stats[tiles + tile : tiles + tile + 1, :] = weigh(rows, top, e_own.at[own_rows(tile), :])

    def outputs(tile):
        e = e_own[own_rows(tile), :]
        out_part[:, tile * wide : (tile + 1) * wide] = dot(vt[:, : (tile + 1) * TILE], e)

    pipeline(tiles, scores, weights, outputs)


def forward_body(size, core, masks, reach, tok, group, *refs):
    take = taker(refs)
    (seg_k, seg_q), qg_pieces, kvs = take(2), take(len(masks)), take(reach)
    out_own, stats = take(2)
    out_pieces, sent, (outs, own_scale, dq_part) = take(len(masks)), take(reach), take(3)
    qg, ka, va, kt, vt, dk, dv, s_scr, e_scr, dp_scr, ds_scr, g_scr = take(12)
    wide, tiles = group * TILE, tok // TILE
    place_rows(size, core, masks, qg_pieces, qg)
    ka[:, HEAD_DIM:] = seg_k[:WINDOW, :]
    for lag in range(1, reach + 1):
        there = slice((reach - lag) * tok, (reach - lag + 1) * tok)
        kv = kvs[lag - 1][...]
        ka[there, :HEAD_DIM] = kv[:, :HEAD_DIM]
        kt[:, there] = kv[:, :HEAD_DIM].T
        vt[:, there] = kv[:, HEAD_DIM:].T
        set_values(va.at[there, :], kv[:, HEAD_DIM:])
    beyond = ~tile_causal(group)

    def scores(tile):
        base = tile * TILE
        queries = query_columns(qg, seg_q, base, group)
        s_scr[tile % 2, : WINDOW - base, :] = dot_t(ka[base:, :], queries)

    scales = {}

    def weights(tile):
        early = WINDOW - tile * TILE
        turn = tile % 2
        s_scr[turn, :TILE, :] = jnp.where(beyond, s_scr[turn, :TILE, :], FAR)
        rows = s_scr.at[turn, :early, :]
        top_own = stats[tile : tile + 1, :]
        top = jnp.maximum(fold_rows(rows, jnp.maximum) * exp2_scale, top_own)
        total = weigh(rows, top, e_scr.at[tile % 3, :early, :])
        scale = jnp.exp2(top_own - top)
        inv = 1.0 / (total + stats[tiles + tile : tiles + tile + 1, :] * scale)
        own_scale[tile : tile + 1, :] = inv * scale
        scales[tile] = scale, inv

    def outputs(tile):
        base, turn = tile * TILE, tile % 2
        early = WINDOW - base
        scale, inv = scales.pop(tile)
        out = dot(vt[:, base:], e_scr[tile % 3, :early, :])
        out = out + out_own[:, tile * wide : (tile + 1) * wide] * scale
        out = (out * inv).T.astype(BF16)
        unstacked(outs, base, group, out)
        g_scr[turn], g_wide = gradient_rows(qg, base, group, inv, out)
        dp_scr[turn, :early, :] = dot_t(va[base:, :], g_wide)

    def gradients(tile):
        base, turn = tile * TILE, tile % 2
        early = WINDOW - base
        e = e_scr[tile % 3, :early, :]
        old = early if tile else 0
        add_rows(dv, base, old, dot(e, g_scr[turn]))
        score_gradients(ds_scr.at[turn, :early, :], e, dp_scr.at[turn, :early, :])
        ds = ds_scr[turn, :early, :]
        add_rows(dk, base, old, dot(ds, stacked(qg, base, group)))
        dq_part[:, tile * wide : (tile + 1) * wide] = dot(kt[:, base:], ds)

    pipeline(tiles, scores, weights, outputs, gradients)

    for lag in range(1, reach + 1):
        there = slice((reach - lag) * tok, (reach - lag + 1) * tok)
        sent[lag - 1][:, :HEAD_DIM] = (dk[there, :] * logit_scale).astype(BF16)
        sent[lag - 1][:, HEAD_DIM:] = dv[there, :].astype(BF16)
    take_rows(size, core, masks, lambda there: outs[there, :], out_pieces)


def backward_body(size, core, masks, tok, group, *refs):
    take = taker(refs)
    qg_pieces, (kv, e_own, outs, own_scale, dq_part) = take(len(masks)), take(5)
    dq_pieces, (dkv,) = take(len(masks)), take(1)
    qg, dqs, va, kt, dk, dv, dp_scr, ds_scr, g_scr = take(9)
    wide = group * TILE
    place_rows(size, core, masks, qg_pieces, qg)
    kt[...] = kv[:, :HEAD_DIM].T
    set_values(va, kv[:, HEAD_DIM:])

    def products(tile):
        base, turn = tile * TILE, tile % 2
        scale = own_scale[tile : tile + 1, :]
        out = stacked(outs, base, group)
        g_scr[turn], g_wide = gradient_rows(qg, base, group, scale, out)
        dp_scr[turn, : base + TILE, :] = dot_t(va[: base + TILE, :], g_wide)

    def gradients(tile):
        base, turn = tile * TILE, tile % 2
        count = base + TILE
        columns = slice(tile * wide, (tile + 1) * wide)
        e = e_own[own_rows(tile), :]
        add_rows(dv, 0, base, dot(e, g_scr[turn]))
        score_gradients(ds_scr.at[turn, :count, :], e, dp_scr.at[turn, :count, :])
        ds = ds_scr[turn, :count, :]
        add_rows(dk, 0, base, dot(ds, stacked(qg, base, group)))
        dq = (dq_part[:, columns] + dot(kt[:, :count], ds)) * logit_scale
        unstacked(dqs, base, group, dq.T.astype(BF16))

    pipeline(tok // TILE, products, gradients)
    dkv[:, :HEAD_DIM] = dk[...] * logit_scale
    dkv[:, HEAD_DIM:] = dv[...]
    take_rows(size, core, masks, lambda there: dqs[there, :], dq_pieces)


def attend_call(kernel, out_shape, scratch_shapes, flops, name, *args):
    return pl.pallas_call(
        kernel,
        out_shape=out_shape,
        in_specs=[VMEM] * len(args),
        out_specs=[VMEM] * len(out_shape),
        scratch_shapes=scratch_shapes,
        compiler_params=pltpu.CompilerParams(vmem_limit_bytes=24 * 1024 * 1024),
        cost_estimate=pl.CostEstimate(
            flops=flops, bytes_accessed=8 * 1024 * 1024, transcendentals=0
        ),
        name=name,
    )(*args)


def forward_own(documents, qg, kv, size):
    rows, cols = qg[0].shape
    tok = len(qg) * rows
    group = cols // (2 * HEAD_DIM)
    wide, tiles = group * TILE, tok // TILE
    return attend_call(
        functools.partial(own_body, size, core_mask(), chip_masks(size), tok, group),
        [
            jax.ShapeDtypeStruct((own_rows(tiles - 1).stop, wide), BF16),
            jax.ShapeDtypeStruct((HEAD_DIM, tiles * wide), F32),
            jax.ShapeDtypeStruct((2 * tiles, wide), F32),
        ],
        [
            pltpu.VMEM((tok, cols), BF16),
            pltpu.VMEM((tok, 2 * HEAD_DIM), BF16),
            pltpu.VMEM((HEAD_DIM, tok), BF16),
            pltpu.VMEM((2, tok, wide), F32),
        ],
        16 * tok * group * (WINDOW + TILE) * HEAD_DIM,
        "forward_own",
        *documents,
        *qg,
        kv,
    )


def forward(documents, qg, lags, carried, size):
    rows, cols = qg[0].shape
    tok, count, reach = len(qg) * rows, len(qg), len(lags)
    group = cols // (2 * HEAD_DIM)
    wide, tiles = group * TILE, tok // TILE
    half = jax.ShapeDtypeStruct((tok, 2 * HEAD_DIM), BF16)
    out_shape = [jax.ShapeDtypeStruct((rows, cols // 2), BF16)] * count + [half] * reach
    out_shape += [
        jax.ShapeDtypeStruct((tok, cols // 2), BF16),
        jax.ShapeDtypeStruct((tiles, wide), F32),
        jax.ShapeDtypeStruct((HEAD_DIM, tiles * wide), F32),
    ]
    scratch = [
        pltpu.VMEM((tok, cols), BF16),
        pltpu.VMEM((WINDOW, 2 * HEAD_DIM), BF16),
        pltpu.VMEM((WINDOW, 2 * HEAD_DIM), BF16),
        pltpu.VMEM((HEAD_DIM, WINDOW), BF16),
        pltpu.VMEM((HEAD_DIM, WINDOW), BF16),
        pltpu.VMEM((WINDOW, HEAD_DIM), F32),
        pltpu.VMEM((WINDOW, HEAD_DIM), F32),
        pltpu.VMEM((2, WINDOW, wide), F32),
        pltpu.VMEM((3, WINDOW, wide), BF16),
        pltpu.VMEM((2, WINDOW, wide), F32),
        pltpu.VMEM((2, WINDOW, wide), BF16),
        pltpu.VMEM((2, wide, HEAD_DIM), BF16),
    ]
    results = attend_call(
        functools.partial(
            forward_body, size, core_mask(), chip_masks(size), reach, tok, group
        ),
        out_shape,
        scratch,
        6 * tok * group * (WINDOW + TILE) * HEAD_DIM,
        "forward",
        *documents,
        *qg,
        *lags,
        *carried,
    )
    return results[:count], results[count : count + reach], results[count + reach :]


def backward(qg, kv, carried, size):
    rows, cols = qg[0].shape
    tok, count = len(qg) * rows, len(qg)
    group = cols // (2 * HEAD_DIM)
    wide = group * TILE
    results = attend_call(
        functools.partial(backward_body, size, core_mask(), chip_masks(size), tok, group),
        [jax.ShapeDtypeStruct((rows, cols // 2), BF16)] * count
        + [jax.ShapeDtypeStruct((tok, 2 * HEAD_DIM), F32)],
        [
            pltpu.VMEM((tok, cols), BF16),
            pltpu.VMEM((tok, cols // 2), BF16),
            pltpu.VMEM((tok, 2 * HEAD_DIM), BF16),
            pltpu.VMEM((HEAD_DIM, tok), BF16),
            pltpu.VMEM((tok, HEAD_DIM), F32),
            pltpu.VMEM((tok, HEAD_DIM), F32),
            pltpu.VMEM((2, tok, wide), F32),
            pltpu.VMEM((2, tok, wide), BF16),
            pltpu.VMEM((2, wide, HEAD_DIM), BF16),
        ],
        4 * tok * group * (WINDOW + TILE) * HEAD_DIM,
        "backward",
        *qg,
        kv,
        *carried,
    )
    return results[:count], results[count]


def document_columns(segment_ids, tok, size):
    start = (flat_index() // size) * tok
    padded = jnp.concatenate([jnp.full((WINDOW,), -1, jnp.int32), segment_ids])
    keys = lax.dynamic_slice_in_dim(padded, start, WINDOW + tok, 0)
    queries = lax.dynamic_slice_in_dim(segment_ids, start, tok, 0)
    number = jnp.arange(HEAD_DIM, dtype=jnp.int32)[None, :]
    return (
        jnp.where(keys[:, None] == number, 0.0, FAR).astype(BF16),
        jnp.where(queries[:, None] == number, 1.0, 0.0).astype(BF16),
    )


def body(query, key, value, grad_out, segment_ids):
    size = key.shape[1] // HEAD_DIM
    rows = query.shape[0]
    tok = size * rows
    reach = WINDOW // tok
    assert reach * tok == WINDOW and device_count() % size == 0

    got = [swap(array, core_mask()) for array in (key, value, query, grad_out)]
    pieces = list(gather_cores((key, value), got[:2], size))
    pieces[0], query, grad_out, segment_ids = after(pieces[0], query, grad_out, segment_ids)
    documents = document_columns(segment_ids, tok, size)
    kv = join(swap_chips(pieces, size), size)
    lags = [shifted(kv, lag * size) for lag in range(1, reach + 1)]
    qg = swap_chips(gather_cores((query, grad_out), got[2:], size), size)

    e_own, *partial = forward_own(documents, qg, kv, size)
    out, sent, carried = forward(documents, qg, lags, partial, size)
    backs = [shifted(sent[lag - 1], -lag * size) for lag in range(1, reach + 1)]
    out = swap_chips(out, size)
    grad_q, dkv = backward(qg, kv, [e_own, *carried], size)
    both = after(*out, *grad_q)
    out, grad_q = both[: len(out)], both[len(out) :]
    grad_q = swap_chips(grad_q, size)
    grads = swap_chips(combine([dkv, *backs], size), size)
    return tuple(spread_cores([out, grad_q, grads], (1, 1, 2), size))


def solution(mesh):
    placed = P(("pipe", "tensor"), None)
    return jax.shard_map(
        body,
        mesh=mesh,
        in_specs=(placed, placed, placed, placed, P()),
        out_specs=(placed, placed, placed, placed),
        check_vma=False,
    )
```

```python
import functools

import jax
import jax.numpy as jnp
from jax import lax
from jax.experimental import pallas as pl
from jax.experimental.pallas import tpu as pltpu
from jax.sharding import PartitionSpec as P

HEAD_DIM = 128
WINDOW = 1024
TILE = 128

logit_scale = 168.0 ** (-0.5)
exp2_scale = logit_scale * 1.4426950408889634

FAR = -(2.0**30)
SMALL = pltpu.CompilerParams(vmem_limit_bytes=4 * 1024 * 1024)
ANY = pl.BlockSpec(memory_space=pl.ANY)
VMEM = pl.BlockSpec(memory_space=pltpu.VMEM)
F32 = jnp.float32
BF16 = jnp.bfloat16
BOTH = ("pipe", "tensor")


def flat_index():
    return lax.axis_index("pipe") * lax.axis_size("tensor") + lax.axis_index("tensor")


def device_count():
    return lax.axis_size("pipe") * lax.axis_size("tensor")


def swap(value, mask):
    return lax.ppermute(value, BOTH, [(i, i ^ mask) for i in range(device_count())])


def core_mask():
    return lax.axis_size("tensor")


def chip_masks(size):
    return [mask for mask in range(size) if not mask & core_mask()]


def swap_chips(pieces, size):
    return [pieces[0]] + [
        swap(piece, mask) for piece, mask in zip(pieces[1:], chip_masks(size)[1:])
    ]


def shifted(value, step):
    count = device_count()
    pairs = [(i, i + step) for i in range(count) if 0 <= i + step < count]
    return lax.ppermute(value, BOTH, pairs)


def partner(size, j):
    return lax.bitwise_xor(lax.rem(flat_index(), size), j)


def place(index, width):
    return pl.ds(pl.multiple_of(index * width, width), width)


def after(value, *others):
    return lax.optimization_barrier((value, *others))


def run_copies(copies, sems):
    started = []
    for at, (source, target) in enumerate(copies):
        copy = pltpu.make_async_copy(source, target, sems.at[at])
        copy.start()
        started.append(copy)
    for copy in started:
        copy.wait()


def small_call(kernel, out_shape, name, *args):
    return pl.pallas_call(
        kernel,
        out_shape=out_shape,
        in_specs=[VMEM] * len(args),
        out_specs=jax.tree.map(lambda _: VMEM, out_shape),
        compiler_params=SMALL,
        name=name,
    )(*args)


def this_core(array, size):
    core = core_mask()
    width = array.shape[1] // size
    shares = [array[:, r * width : (r + 1) * width] for r in range(size)]
    first, second = (
        jnp.concatenate([share for r, share in enumerate(shares) if (r // core) % 2 == at], axis=1)
        for at in range(2)
    )
    return jnp.where((flat_index() // core) % 2 == 0, first, second)


def stack_body(size, core, masks, count, *refs):
    own, got, pieces = refs[:count], refs[count : 2 * count], refs[2 * count :]
    rows = own[0].shape[0]
    for mask, piece in zip(masks, pieces):
        there = partner(size, mask)
        chip = there // (2 * core) * core + lax.rem(there, core)
        start = 0
        for mine, other in zip(own, got):
            width = other.shape[1] // size
            piece[:rows, start : start + width] = mine[:, place(chip, width)]
            piece[rows:, start : start + width] = other[:, place(there, width)]
            start += width


def gather_cores(arrays, got, size):
    masks = chip_masks(size)
    own = [this_core(array, size) for array in arrays]
    cols = sum(array.shape[1] // size for array in arrays)
    piece = jax.ShapeDtypeStruct((2 * arrays[0].shape[0], cols), BF16)
    kernel = functools.partial(stack_body, size, core_mask(), masks, len(arrays))
    return small_call(kernel, [piece] * len(masks), "stack", *own, *got)


def place_rows(size, core, masks, pieces, out):
    for mask, piece in zip(masks, pieces):
        rows = piece.shape[0] // 2
        out[place(partner(size, mask), rows), :] = piece[:rows, :]
        out[place(partner(size, mask ^ core), rows), :] = piece[rows:, :]


def take_rows(size, core, masks, source, pieces):
    for mask, piece in zip(masks, pieces):
        rows = piece.shape[0] // 2
        piece[:rows, :] = source(place(partner(size, mask), rows))
        piece[rows:, :] = source(place(partner(size, mask ^ core), rows))


def join(pieces, size):
    rows, cols = pieces[0].shape
    core, masks = core_mask(), chip_masks(size)

    def kernel(*refs):
        place_rows(size, core, masks, refs[:-1], refs[-1])

    out = jax.ShapeDtypeStruct((len(pieces) * rows, cols), BF16)
    return small_call(kernel, out, "join", *pieces)


def combine(terms, size):
    tok, cols = terms[0].shape
    core, masks = core_mask(), chip_masks(size)

    def kernel(*refs):
        added = refs[: len(terms)]

        def source(there):
            total = added[0][there, :]
            for term in added[1:]:
                total = total + term[there, :].astype(F32)
            return total.astype(BF16)

        take_rows(size, core, masks, source, refs[len(terms) :])

    piece = jax.ShapeDtypeStruct((2 * (tok // size), cols), BF16)
    return small_call(kernel, [piece] * len(masks), "combine", *terms)


def bottom_body(*refs):
    out, start = refs[-1], 0
    for piece in refs[:-1]:
        rows, width = piece.shape[0] // 2, piece.shape[1]
        out[:, start : start + width] = piece[rows:, :]
        start += width


def spread_body(size, core, masks, counts, *refs):
    refs = list(refs)
    take = lambda count: [refs.pop(0) for _ in range(count)]
    sets = [take(len(masks)) for _ in counts]
    (got,), sets_out, (sems,) = take(1), [take(count) for count in counts], take(1)
    copies, start = [], 0
    for pieces, outs in zip(sets, sets_out):
        for mask, piece in zip(masks, pieces):
            rows, width = piece.shape[0] // 2, piece.shape[1] // len(outs)
            for at, out in enumerate(outs):
                mine = out.at[:, place(partner(size, mask), width)]
                other = out.at[:, place(partner(size, mask ^ core), width)]
                copies.append((piece.at[:rows, at * width : (at + 1) * width], mine))
                copies.append((got.at[:, start : start + width], other))
                start += width
    run_copies(copies, sems)


def bottom(pieces):
    shape = (pieces[0].shape[0] // 2, sum(piece.shape[1] for piece in pieces))
    return small_call(bottom_body, jax.ShapeDtypeStruct(shape, BF16), "bottom", *pieces)


def spread_cores(sets, counts, got, size):
    pieces = [piece for part in sets for piece in part]
    rows = pieces[0].shape[0] // 2
    widths = [part[0].shape[1] // count for part, count in zip(sets, counts) for _ in range(count)]
    return pl.pallas_call(
        functools.partial(spread_body, size, core_mask(), chip_masks(size), counts),
        out_shape=[jax.ShapeDtypeStruct((rows, width * size), BF16) for width in widths],
        in_specs=[ANY] * (len(pieces) + 1),
        out_specs=[ANY] * len(widths),
        scratch_shapes=[pltpu.SemaphoreType.DMA((len(widths) * size,))],
        compiler_params=SMALL,
        name="spread",
    )(*pieces, got)


def dot(a, b):
    return lax.dot_general(a, b, (((1,), (0,)), ((), ())), preferred_element_type=F32)


def dot_t(a, b):
    return lax.dot_general(a, b, (((1,), (1,)), ((), ())), preferred_element_type=F32)


def fold(x, op):
    parts = [x[at : at + 8] for at in range(0, x.shape[0], 8)]
    while len(parts) > 1:
        parts = [
            op(*parts[at : at + 2]) if at + 1 < len(parts) else parts[at]
            for at in range(0, len(parts), 2)
        ]
    return parts[0]


def taker(refs):
    refs = list(refs)
    return lambda count: [refs.pop(0) for _ in range(count)]


def stacked(rows, base, group, first=0):
    parts = [slice(first + at * HEAD_DIM, first + (at + 1) * HEAD_DIM) for at in range(group)]
    return jnp.concatenate([rows[base : base + TILE, part] for part in parts], axis=0)


def unstacked(rows, base, group, value):
    for at in range(group):
        part = slice(at * TILE, (at + 1) * TILE)
        rows[base : base + TILE, at * HEAD_DIM : (at + 1) * HEAD_DIM] = value[part]


def set_values(va, values):
    lane = lax.broadcasted_iota(jnp.int32, values.shape, 1)
    va[:, :HEAD_DIM] = values
    va[:, HEAD_DIM:] = jnp.where(lane < 2, 1.0, 0.0).astype(BF16)


def add_rows(target, start, old, value):
    if old:
        target[start : start + old, :] += value[:old]
    if old < value.shape[0]:
        target[start + old : start + value.shape[0], :] = value[old:]


def score_gradients(ds_scr, e, dp):
    for at in range(0, e.shape[0], TILE):
        part = slice(at, at + TILE)
        ds_scr[part, :] = (e[part, :].astype(F32) * dp[part, :]).astype(BF16)


def pipeline(tiles, *stages):
    for step in range(tiles + len(stages) - 1):
        for behind, stage in enumerate(stages):
            if 0 <= step - behind < tiles:
                stage(step - behind)


def gradient_rows(qg, base, group, scale, out):
    first = qg.shape[1] // 2
    columns = jnp.broadcast_to(scale, (HEAD_DIM, scale.shape[1])).T
    g2 = (stacked(qg, base, group, first).astype(F32) * columns).astype(BF16)
    delta = jnp.sum(g2.astype(F32) * out.astype(F32), axis=1, keepdims=True)
    high = delta.astype(BF16).astype(F32)
    lane = lax.broadcasted_iota(jnp.int32, g2.shape, 1)
    extra = jnp.where(lane == 0, -high, jnp.where(lane == 1, high - delta, 0.0))
    return g2, jnp.concatenate([g2, extra.astype(BF16)], axis=1)


def own_rows(tile):
    start = tile * (tile + 1) // 2 * TILE
    return slice(start, start + (tile + 1) * TILE)


def query_columns(qg, seg_q, base, group):
    mine = jnp.concatenate([seg_q[base : base + TILE, :]] * group, axis=0)
    return jnp.concatenate([stacked(qg, base, group), mine], axis=1)


def fold_rows(rows, op):
    parts = [fold(rows[at : at + TILE, :], op) for at in range(0, rows.shape[0], TILE)]
    whole = functools.reduce(op, parts)
    reduce = jnp.max if op is jnp.maximum else jnp.sum
    return reduce(whole, axis=0, keepdims=True)


def weigh(scores, top, keep):
    total = None
    for at in range(0, scores.shape[0], TILE):
        part = slice(at, at + TILE)
        e = jnp.exp2(scores[part, :] * exp2_scale - top)
        keep[part, :] = e.astype(BF16)
        e = fold(e, jnp.add)
        total = e if total is None else total + e
    return jnp.sum(total, axis=0, keepdims=True)


def tile_causal(group):
    row_of = lax.broadcasted_iota(jnp.int32, (TILE, TILE), 0)
    col_of = lax.broadcasted_iota(jnp.int32, (TILE, TILE), 1)
    return jnp.concatenate([row_of <= col_of] * group, axis=1)


def own_body(size, core, masks, tok, group, *refs):
    take = taker(refs)
    (seg_k, seg_q), qg_pieces, (kv,) = take(2), take(len(masks)), take(1)
    e_own, out_part, stats = take(3)
    qg, ka, vt, s_scr = take(4)
    wide, tiles = group * TILE, tok // TILE
    place_rows(size, core, masks, qg_pieces, qg)
    ka[:, :HEAD_DIM] = kv[:, :HEAD_DIM]
    ka[:, HEAD_DIM:] = seg_k[WINDOW:, :]
    vt[...] = kv[:, HEAD_DIM:].T
    causal = tile_causal(group)

    def scores(tile):
        queries = query_columns(qg, seg_q, tile * TILE, group)
        s_scr[tile % 2, : (tile + 1) * TILE, :] = dot_t(ka[: (tile + 1) * TILE, :], queries)

    def weights(tile):
        base, turn = tile * TILE, tile % 2
        last = slice(base, base + TILE)
        s_scr[turn, last, :] = jnp.where(causal, s_scr[turn, last, :], FAR)
        rows = s_scr.at[turn, : base + TILE, :]
        top = fold_rows(rows, jnp.maximum) * exp2_scale
        stats[tile : tile + 1, :] = top
        stats[tiles + tile : tiles + tile + 1, :] = weigh(rows, top, e_own.at[own_rows(tile), :])

    def outputs(tile):
        e = e_own[own_rows(tile), :]
        out_part[:, tile * wide : (tile + 1) * wide] = dot(vt[:, : (tile + 1) * TILE], e)

    pipeline(tiles, scores, weights, outputs)


def forward_body(size, core, masks, reach, tok, group, *refs):
    take = taker(refs)
    (seg_k, seg_q), qg_pieces, kvs = take(2), take(len(masks)), take(reach)
    out_own, stats = take(2)
    out_pieces, sent, (outs, own_scale, dq_part) = take(len(masks)), take(reach), take(3)
    qg, ka, va, kt, vt, dk, dv, s_scr, e_scr, dp_scr, ds_scr, g_scr = take(12)
    wide, tiles = group * TILE, tok // TILE
    place_rows(size, core, masks, qg_pieces, qg)
    ka[:, HEAD_DIM:] = seg_k[:WINDOW, :]
    for lag in range(1, reach + 1):
        there = slice((reach - lag) * tok, (reach - lag + 1) * tok)
        kv = kvs[lag - 1][...]
        ka[there, :HEAD_DIM] = kv[:, :HEAD_DIM]
        kt[:, there] = kv[:, :HEAD_DIM].T
        vt[:, there] = kv[:, HEAD_DIM:].T
        set_values(va.at[there, :], kv[:, HEAD_DIM:])
    beyond = ~tile_causal(group)

    def scores(tile):
        base = tile * TILE
        queries = query_columns(qg, seg_q, base, group)
        s_scr[tile % 2, : WINDOW - base, :] = dot_t(ka[base:, :], queries)

    scales = {}

    def weights(tile):
        early = WINDOW - tile * TILE
        turn = tile % 2
        s_scr[turn, :TILE, :] = jnp.where(beyond, s_scr[turn, :TILE, :], FAR)
        rows = s_scr.at[turn, :early, :]
        top_own = stats[tile : tile + 1, :]
        top = jnp.maximum(fold_rows(rows, jnp.maximum) * exp2_scale, top_own)
        total = weigh(rows, top, e_scr.at[tile % 3, :early, :])
        scale = jnp.exp2(top_own - top)
        inv = 1.0 / (total + stats[tiles + tile : tiles + tile + 1, :] * scale)
        own_scale[tile : tile + 1, :] = inv * scale
        scales[tile] = scale, inv

    def outputs(tile):
        base, turn = tile * TILE, tile % 2
        early = WINDOW - base
        scale, inv = scales.pop(tile)
        out = dot(vt[:, base:], e_scr[tile % 3, :early, :])
        out = out + out_own[:, tile * wide : (tile + 1) * wide] * scale
        out = (out * inv).T.astype(BF16)
        unstacked(outs, base, group, out)
        g_scr[turn], g_wide = gradient_rows(qg, base, group, inv, out)
        dp_scr[turn, :early, :] = dot_t(va[base:, :], g_wide)

    def gradients(tile):
        base, turn = tile * TILE, tile % 2
        early = WINDOW - base
        e = e_scr[tile % 3, :early, :]
        old = early if tile else 0
        add_rows(dv, base, old, dot(e, g_scr[turn]))
        score_gradients(ds_scr.at[turn, :early, :], e, dp_scr.at[turn, :early, :])
        ds = ds_scr[turn, :early, :]
        add_rows(dk, base, old, dot(ds, stacked(qg, base, group)))
        dq_part[:, tile * wide : (tile + 1) * wide] = dot(kt[:, base:], ds)

    pipeline(tiles, scores, weights, outputs, gradients)

    for lag in range(1, reach + 1):
        there = slice((reach - lag) * tok, (reach - lag + 1) * tok)
        sent[lag - 1][:, :HEAD_DIM] = (dk[there, :] * logit_scale).astype(BF16)
        sent[lag - 1][:, HEAD_DIM:] = dv[there, :].astype(BF16)
    take_rows(size, core, masks, lambda there: outs[there, :], out_pieces)


def backward_body(size, core, masks, tok, group, *refs):
    take = taker(refs)
    qg_pieces, (kv, e_own, outs, own_scale, dq_part) = take(len(masks)), take(5)
    dq_pieces, (dkv,) = take(len(masks)), take(1)
    qg, dqs, va, kt, dk, dv, dp_scr, ds_scr, g_scr = take(9)
    wide = group * TILE
    place_rows(size, core, masks, qg_pieces, qg)
    kt[...] = kv[:, :HEAD_DIM].T
    set_values(va, kv[:, HEAD_DIM:])

    def products(tile):
        base, turn = tile * TILE, tile % 2
        scale = own_scale[tile : tile + 1, :]
        out = stacked(outs, base, group)
        g_scr[turn], g_wide = gradient_rows(qg, base, group, scale, out)
        dp_scr[turn, : base + TILE, :] = dot_t(va[: base + TILE, :], g_wide)

    def gradients(tile):
        base, turn = tile * TILE, tile % 2
        count = base + TILE
        columns = slice(tile * wide, (tile + 1) * wide)
        e = e_own[own_rows(tile), :]
        add_rows(dv, 0, base, dot(e, g_scr[turn]))
        score_gradients(ds_scr.at[turn, :count, :], e, dp_scr.at[turn, :count, :])
        ds = ds_scr[turn, :count, :]
        add_rows(dk, 0, base, dot(ds, stacked(qg, base, group)))
        dq = (dq_part[:, columns] + dot(kt[:, :count], ds)) * logit_scale
        unstacked(dqs, base, group, dq.T.astype(BF16))

    pipeline(tok // TILE, products, gradients)
    dkv[:, :HEAD_DIM] = dk[...] * logit_scale
    dkv[:, HEAD_DIM:] = dv[...]
    take_rows(size, core, masks, lambda there: dqs[there, :], dq_pieces)


def attend_call(kernel, out_shape, scratch_shapes, flops, name, *args):
    return pl.pallas_call(
        kernel,
        out_shape=out_shape,
        in_specs=[VMEM] * len(args),
        out_specs=[VMEM] * len(out_shape),
        scratch_shapes=scratch_shapes,
        compiler_params=pltpu.CompilerParams(vmem_limit_bytes=24 * 1024 * 1024),
        cost_estimate=pl.CostEstimate(
            flops=flops, bytes_accessed=8 * 1024 * 1024, transcendentals=0
        ),
        name=name,
    )(*args)


def forward_own(documents, qg, kv, size):
    rows, cols = qg[0].shape
    tok = len(qg) * rows
    group = cols // (2 * HEAD_DIM)
    wide, tiles = group * TILE, tok // TILE
    return attend_call(
        functools.partial(own_body, size, core_mask(), chip_masks(size), tok, group),
        [
            jax.ShapeDtypeStruct((own_rows(tiles - 1).stop, wide), BF16),
            jax.ShapeDtypeStruct((HEAD_DIM, tiles * wide), F32),
            jax.ShapeDtypeStruct((2 * tiles, wide), F32),
        ],
        [
            pltpu.VMEM((tok, cols), BF16),
            pltpu.VMEM((tok, 2 * HEAD_DIM), BF16),
            pltpu.VMEM((HEAD_DIM, tok), BF16),
            pltpu.VMEM((2, tok, wide), F32),
        ],
        16 * tok * group * (WINDOW + TILE) * HEAD_DIM,
        "forward_own",
        *documents,
        *qg,
        kv,
    )


def forward(documents, qg, lags, carried, size):
    rows, cols = qg[0].shape
    tok, count, reach = len(qg) * rows, len(qg), len(lags)
    group = cols // (2 * HEAD_DIM)
    wide, tiles = group * TILE, tok // TILE
    half = jax.ShapeDtypeStruct((tok, 2 * HEAD_DIM), BF16)
    out_shape = [jax.ShapeDtypeStruct((rows, cols // 2), BF16)] * count + [half] * reach
    out_shape += [
        jax.ShapeDtypeStruct((tok, cols // 2), BF16),
        jax.ShapeDtypeStruct((tiles, wide), F32),
        jax.ShapeDtypeStruct((HEAD_DIM, tiles * wide), F32),
    ]
    scratch = [
        pltpu.VMEM((tok, cols), BF16),
        pltpu.VMEM((WINDOW, 2 * HEAD_DIM), BF16),
        pltpu.VMEM((WINDOW, 2 * HEAD_DIM), BF16),
        pltpu.VMEM((HEAD_DIM, WINDOW), BF16),
        pltpu.VMEM((HEAD_DIM, WINDOW), BF16),
        pltpu.VMEM((WINDOW, HEAD_DIM), F32),
        pltpu.VMEM((WINDOW, HEAD_DIM), F32),
        pltpu.VMEM((2, WINDOW, wide), F32),
        pltpu.VMEM((3, WINDOW, wide), BF16),
        pltpu.VMEM((2, WINDOW, wide), F32),
        pltpu.VMEM((2, WINDOW, wide), BF16),
        pltpu.VMEM((2, wide, HEAD_DIM), BF16),
    ]
    results = attend_call(
        functools.partial(
            forward_body, size, core_mask(), chip_masks(size), reach, tok, group
        ),
        out_shape,
        scratch,
        6 * tok * group * (WINDOW + TILE) * HEAD_DIM,
        "forward",
        *documents,
        *qg,
        *lags,
        *carried,
    )
    return results[:count], results[count : count + reach], results[count + reach :]


def backward(qg, kv, carried, size):
    rows, cols = qg[0].shape
    tok, count = len(qg) * rows, len(qg)
    group = cols // (2 * HEAD_DIM)
    wide = group * TILE
    results = attend_call(
        functools.partial(backward_body, size, core_mask(), chip_masks(size), tok, group),
        [jax.ShapeDtypeStruct((rows, cols // 2), BF16)] * count
        + [jax.ShapeDtypeStruct((tok, 2 * HEAD_DIM), F32)],
        [
            pltpu.VMEM((tok, cols), BF16),
            pltpu.VMEM((tok, cols // 2), BF16),
            pltpu.VMEM((tok, 2 * HEAD_DIM), BF16),
            pltpu.VMEM((HEAD_DIM, tok), BF16),
            pltpu.VMEM((tok, HEAD_DIM), F32),
            pltpu.VMEM((tok, HEAD_DIM), F32),
            pltpu.VMEM((2, tok, wide), F32),
            pltpu.VMEM((2, tok, wide), BF16),
            pltpu.VMEM((2, wide, HEAD_DIM), BF16),
        ],
        4 * tok * group * (WINDOW + TILE) * HEAD_DIM,
        "backward",
        *qg,
        kv,
        *carried,
    )
    return results[:count], results[count]


def document_columns(segment_ids, tok, size):
    start = (flat_index() // size) * tok
    padded = jnp.concatenate([jnp.full((WINDOW,), -1, jnp.int32), segment_ids])
    keys = lax.dynamic_slice_in_dim(padded, start, WINDOW + tok, 0)
    queries = lax.dynamic_slice_in_dim(segment_ids, start, tok, 0)
    number = jnp.arange(HEAD_DIM, dtype=jnp.int32)[None, :]
    return (
        jnp.where(keys[:, None] == number, 0.0, FAR).astype(BF16),
        jnp.where(queries[:, None] == number, 1.0, 0.0).astype(BF16),
    )


def body(query, key, value, grad_out, segment_ids):
    size = key.shape[1] // HEAD_DIM
    rows = query.shape[0]
    tok = size * rows
    reach = WINDOW // tok
    assert reach * tok == WINDOW and device_count() % size == 0

    got = [swap(array, core_mask()) for array in (key, value, query, grad_out)]
    pieces = list(gather_cores((key, value), got[:2], size))
    pieces[0], query, grad_out, segment_ids = after(pieces[0], query, grad_out, segment_ids)
    documents = document_columns(segment_ids, tok, size)
    kv = join(swap_chips(pieces, size), size)
    lags = [shifted(kv, lag * size) for lag in range(1, reach + 1)]
    qg = swap_chips(gather_cores((query, grad_out), got[2:], size), size)

    e_own, *partial = forward_own(documents, qg, kv, size)
    out, sent, carried = forward(documents, qg, lags, partial, size)
    backs = [shifted(sent[lag - 1], -lag * size) for lag in range(1, reach + 1)]
    out = swap_chips(out, size)
    grad_q, dkv = backward(qg, kv, [e_own, *carried], size)
    give, *grad_q = after(bottom(out), *grad_q)
    grad_q = swap_chips(grad_q, size)
    dkv, got = after(dkv, swap(give, core_mask()))
    grads = swap_chips(combine([dkv, *backs], size), size)
    (attn_out,) = spread_cores([out], (1,), got, size)
    attn_out, *grad_q = after(attn_out, *grad_q)
    got = swap(bottom([*grad_q, *grads]), core_mask())
    return (attn_out, *spread_cores([grad_q, grads], (1, 2), got, size))


def solution(mesh):
    placed = P(("pipe", "tensor"), None)
    return jax.shard_map(
        body,
        mesh=mesh,
        in_specs=(placed, placed, placed, placed, P()),
        out_specs=(placed, placed, placed, placed),
        check_vma=False,
    )
```

```python
import functools

import jax
import jax.numpy as jnp
from jax import lax
from jax.experimental import pallas as pl
from jax.experimental.pallas import tpu as pltpu
from jax.sharding import PartitionSpec as P

HEAD_DIM = 128
WINDOW = 1024
TILE = 128

logit_scale = 168.0 ** (-0.5)
exp2_scale = logit_scale * 1.4426950408889634

FAR = -(2.0**30)
SMALL = pltpu.CompilerParams(vmem_limit_bytes=4 * 1024 * 1024)
ANY = pl.BlockSpec(memory_space=pl.ANY)
VMEM = pl.BlockSpec(memory_space=pltpu.VMEM)
F32 = jnp.float32
BF16 = jnp.bfloat16
BOTH = ("pipe", "tensor")


def flat_index():
    return lax.axis_index("pipe") * lax.axis_size("tensor") + lax.axis_index("tensor")


def device_count():
    return lax.axis_size("pipe") * lax.axis_size("tensor")


def swap(value, mask):
    return lax.ppermute(value, BOTH, [(i, i ^ mask) for i in range(device_count())])


def core_mask():
    return lax.axis_size("tensor")


def chip_masks(size):
    return [mask for mask in range(size) if not mask & core_mask()]


def swap_chips(pieces, size):
    return [pieces[0]] + [
        swap(piece, mask) for piece, mask in zip(pieces[1:], chip_masks(size)[1:])
    ]


def shifted(value, step):
    count = device_count()
    pairs = [(i, i + step) for i in range(count) if 0 <= i + step < count]
    return lax.ppermute(value, BOTH, pairs)


def partner(size, j):
    return lax.bitwise_xor(lax.rem(flat_index(), size), j)


def place(index, width):
    return pl.ds(pl.multiple_of(index * width, width), width)


def after(value, *others):
    return lax.optimization_barrier((value, *others))


def run_copies(copies, sems):
    started = []
    for at, (source, target) in enumerate(copies):
        copy = pltpu.make_async_copy(source, target, sems.at[at])
        copy.start()
        started.append(copy)
    for copy in started:
        copy.wait()


def small_call(kernel, out_shape, name, *args):
    return pl.pallas_call(
        kernel,
        out_shape=out_shape,
        in_specs=[VMEM] * len(args),
        out_specs=jax.tree.map(lambda _: VMEM, out_shape),
        compiler_params=SMALL,
        name=name,
    )(*args)


def this_core(array, size):
    core = core_mask()
    width = array.shape[1] // size
    shares = [array[:, r * width : (r + 1) * width] for r in range(size)]
    first, second = (
        jnp.concatenate([share for r, share in enumerate(shares) if (r // core) % 2 == at], axis=1)
        for at in range(2)
    )
    return jnp.where((flat_index() // core) % 2 == 0, first, second)


def stack_body(size, core, masks, count, *refs):
    own, got, pieces = refs[:count], refs[count : 2 * count], refs[2 * count :]
    rows = own[0].shape[0]
    for mask, piece in zip(masks, pieces):
        there = partner(size, mask)
        chip = there // (2 * core) * core + lax.rem(there, core)
        start = 0
        for mine, other in zip(own, got):
            width = other.shape[1] // size
            piece[:rows, start : start + width] = mine[:, place(chip, width)]
            piece[rows:, start : start + width] = other[:, place(there, width)]
            start += width


def gather_cores(arrays, got, size):
    masks = chip_masks(size)
    own = [this_core(array, size) for array in arrays]
    cols = sum(array.shape[1] // size for array in arrays)
    piece = jax.ShapeDtypeStruct((2 * arrays[0].shape[0], cols), BF16)
    kernel = functools.partial(stack_body, size, core_mask(), masks, len(arrays))
    return small_call(kernel, [piece] * len(masks), "stack", *own, *got)


def place_rows(size, core, masks, pieces, out):
    for mask, piece in zip(masks, pieces):
        rows = piece.shape[0] // 2
        out[place(partner(size, mask), rows), :] = piece[:rows, :]
        out[place(partner(size, mask ^ core), rows), :] = piece[rows:, :]


def take_rows(size, core, masks, source, pieces):
    for mask, piece in zip(masks, pieces):
        rows = piece.shape[0] // 2
        piece[:rows, :] = source(place(partner(size, mask), rows))
        piece[rows:, :] = source(place(partner(size, mask ^ core), rows))


def join(pieces, size):
    rows, cols = pieces[0].shape
    core, masks = core_mask(), chip_masks(size)

    def kernel(*refs):
        place_rows(size, core, masks, refs[:-1], refs[-1])

    out = jax.ShapeDtypeStruct((len(pieces) * rows, cols), BF16)
    return small_call(kernel, out, "join", *pieces)


def combine(terms, size):
    tok, cols = terms[0].shape
    core, masks = core_mask(), chip_masks(size)

    def kernel(*refs):
        added = refs[: len(terms)]

        def source(there):
            total = added[0][there, :]
            for term in added[1:]:
                total = total + term[there, :].astype(F32)
            return total.astype(BF16)

        take_rows(size, core, masks, source, refs[len(terms) :])

    piece = jax.ShapeDtypeStruct((2 * (tok // size), cols), BF16)
    return small_call(kernel, [piece] * len(masks), "combine", *terms)


def bottom_body(*refs):
    out, start = refs[-1], 0
    for piece in refs[:-1]:
        rows, width = piece.shape[0] // 2, piece.shape[1]
        out[:, start : start + width] = piece[rows:, :]
        start += width


def spread_body(size, core, masks, counts, *refs):
    refs = list(refs)
    take = lambda count: [refs.pop(0) for _ in range(count)]
    sets = [take(len(masks)) for _ in counts]
    (got,), sets_out, (sems,) = take(1), [take(count) for count in counts], take(1)
    copies, start = [], 0
    for pieces, outs in zip(sets, sets_out):
        for mask, piece in zip(masks, pieces):
            rows, width = piece.shape[0] // 2, piece.shape[1] // len(outs)
            for at, out in enumerate(outs):
                mine = out.at[:, place(partner(size, mask), width)]
                other = out.at[:, place(partner(size, mask ^ core), width)]
                copies.append((piece.at[:rows, at * width : (at + 1) * width], mine))
                copies.append((got.at[:, start : start + width], other))
                start += width
    run_copies(copies, sems)


def spread_cores(sets, counts, size):
    pieces = [piece for part in sets for piece in part]
    rows = pieces[0].shape[0] // 2
    give = jax.ShapeDtypeStruct((rows, sum(piece.shape[1] for piece in pieces)), BF16)
    got = swap(small_call(bottom_body, give, "bottom", *pieces), core_mask())
    widths = [part[0].shape[1] // count for part, count in zip(sets, counts) for _ in range(count)]
    return pl.pallas_call(
        functools.partial(spread_body, size, core_mask(), chip_masks(size), counts),
        out_shape=[jax.ShapeDtypeStruct((rows, width * size), BF16) for width in widths],
        in_specs=[ANY] * (len(pieces) + 1),
        out_specs=[ANY] * len(widths),
        scratch_shapes=[pltpu.SemaphoreType.DMA((len(widths) * size,))],
        compiler_params=SMALL,
        name="spread",
    )(*pieces, got)


def dot(a, b):
    return lax.dot_general(a, b, (((1,), (0,)), ((), ())), preferred_element_type=F32)


def dot_t(a, b):
    return lax.dot_general(a, b, (((1,), (1,)), ((), ())), preferred_element_type=F32)


def fold(x, op):
    parts = [x[at : at + 8] for at in range(0, x.shape[0], 8)]
    while len(parts) > 1:
        parts = [
            op(*parts[at : at + 2]) if at + 1 < len(parts) else parts[at]
            for at in range(0, len(parts), 2)
        ]
    return parts[0]


def taker(refs):
    refs = list(refs)
    return lambda count: [refs.pop(0) for _ in range(count)]


def stacked(rows, base, group, first=0):
    parts = [slice(first + at * HEAD_DIM, first + (at + 1) * HEAD_DIM) for at in range(group)]
    return jnp.concatenate([rows[base : base + TILE, part] for part in parts], axis=0)


def unstacked(rows, base, group, value):
    for at in range(group):
        part = slice(at * TILE, (at + 1) * TILE)
        rows[base : base + TILE, at * HEAD_DIM : (at + 1) * HEAD_DIM] = value[part]


def set_values(va, values):
    lane = lax.broadcasted_iota(jnp.int32, values.shape, 1)
    va[:, :HEAD_DIM] = values
    va[:, HEAD_DIM:] = jnp.where(lane < 2, 1.0, 0.0).astype(BF16)


def add_rows(target, start, old, value):
    if old:
        target[start : start + old, :] += value[:old]
    if old < value.shape[0]:
        target[start + old : start + value.shape[0], :] = value[old:]


def score_gradients(ds_scr, e, dp):
    for at in range(0, e.shape[0], TILE):
        part = slice(at, at + TILE)
        ds_scr[part, :] = (e[part, :].astype(F32) * dp[part, :]).astype(BF16)


def pipeline(tiles, *stages):
    for step in range(tiles + len(stages) - 1):
        for behind, stage in enumerate(stages):
            if 0 <= step - behind < tiles:
                stage(step - behind)


def gradient_rows(qg, base, group, scale, out):
    first = qg.shape[1] // 2
    columns = jnp.broadcast_to(scale, (HEAD_DIM, scale.shape[1])).T
    g2 = (stacked(qg, base, group, first).astype(F32) * columns).astype(BF16)
    delta = jnp.sum(g2.astype(F32) * out.astype(F32), axis=1, keepdims=True)
    high = delta.astype(BF16).astype(F32)
    lane = lax.broadcasted_iota(jnp.int32, g2.shape, 1)
    extra = jnp.where(lane == 0, -high, jnp.where(lane == 1, high - delta, 0.0))
    return g2, jnp.concatenate([g2, extra.astype(BF16)], axis=1)


def own_rows(tile):
    start = tile * (tile + 1) // 2 * TILE
    return slice(start, start + (tile + 1) * TILE)


def query_columns(qg, seg_q, base, group):
    mine = jnp.concatenate([seg_q[base : base + TILE, :]] * group, axis=0)
    return jnp.concatenate([stacked(qg, base, group), mine], axis=1)


def fold_rows(rows, op):
    parts = [fold(rows[at : at + TILE, :], op) for at in range(0, rows.shape[0], TILE)]
    whole = functools.reduce(op, parts)
    reduce = jnp.max if op is jnp.maximum else jnp.sum
    return reduce(whole, axis=0, keepdims=True)


def weigh(scores, top, keep):
    total = None
    for at in range(0, scores.shape[0], TILE):
        part = slice(at, at + TILE)
        e = jnp.exp2(scores[part, :] * exp2_scale - top)
        keep[part, :] = e.astype(BF16)
        e = fold(e, jnp.add)
        total = e if total is None else total + e
    return jnp.sum(total, axis=0, keepdims=True)


def tile_causal(group):
    row_of = lax.broadcasted_iota(jnp.int32, (TILE, TILE), 0)
    col_of = lax.broadcasted_iota(jnp.int32, (TILE, TILE), 1)
    return jnp.concatenate([row_of <= col_of] * group, axis=1)


def own_body(size, core, masks, tok, group, *refs):
    take = taker(refs)
    (seg_k, seg_q), qg_pieces, (kv,) = take(2), take(len(masks)), take(1)
    e_own, out_part, stats, qg = take(4)
    ka, vt, s_scr = take(3)
    wide, tiles = group * TILE, tok // TILE
    place_rows(size, core, masks, qg_pieces, qg)
    ka[:, :HEAD_DIM] = kv[:, :HEAD_DIM]
    ka[:, HEAD_DIM:] = seg_k[WINDOW:, :]
    vt[...] = kv[:, HEAD_DIM:].T
    causal = tile_causal(group)

    def scores(tile):
        queries = query_columns(qg, seg_q, tile * TILE, group)
        s_scr[tile % 2, : (tile + 1) * TILE, :] = dot_t(ka[: (tile + 1) * TILE, :], queries)

    def weights(tile):
        base, turn = tile * TILE, tile % 2
        last = slice(base, base + TILE)
        s_scr[turn, last, :] = jnp.where(causal, s_scr[turn, last, :], FAR)
        rows = s_scr.at[turn, : base + TILE, :]
        top = fold_rows(rows, jnp.maximum) * exp2_scale
        stats[tile : tile + 1, :] = top
        stats[tiles + tile : tiles + tile + 1, :] = weigh(rows, top, e_own.at[own_rows(tile), :])

    def outputs(tile):
        e = e_own[own_rows(tile), :]
        out_part[:, tile * wide : (tile + 1) * wide] = dot(vt[:, : (tile + 1) * TILE], e)

    pipeline(tiles, scores, weights, outputs)


def forward_body(size, core, masks, reach, tok, group, *refs):
    take = taker(refs)
    (seg_k, seg_q, qg), kvs, (out_own, stats) = take(3), take(reach), take(2)
    out_pieces, sent, (outs, own_scale, dq_part) = take(len(masks)), take(reach), take(3)
    ka, va, kt, vt, dk, dv, s_scr, e_scr, dp_scr, ds_scr, g_scr = take(11)
    wide, tiles = group * TILE, tok // TILE
    ka[:, HEAD_DIM:] = seg_k[:WINDOW, :]
    for lag in range(1, reach + 1):
        there = slice((reach - lag) * tok, (reach - lag + 1) * tok)
        kv = kvs[lag - 1][...]
        ka[there, :HEAD_DIM] = kv[:, :HEAD_DIM]
        kt[:, there] = kv[:, :HEAD_DIM].T
        vt[:, there] = kv[:, HEAD_DIM:].T
        set_values(va.at[there, :], kv[:, HEAD_DIM:])
    beyond = ~tile_causal(group)

    def scores(tile):
        base = tile * TILE
        queries = query_columns(qg, seg_q, base, group)
        s_scr[tile % 2, : WINDOW - base, :] = dot_t(ka[base:, :], queries)

    scales = {}

    def weights(tile):
        early = WINDOW - tile * TILE
        turn = tile % 2
        s_scr[turn, :TILE, :] = jnp.where(beyond, s_scr[turn, :TILE, :], FAR)
        rows = s_scr.at[turn, :early, :]
        top_own = stats[tile : tile + 1, :]
        top = jnp.maximum(fold_rows(rows, jnp.maximum) * exp2_scale, top_own)
        total = weigh(rows, top, e_scr.at[tile % 3, :early, :])
        scale = jnp.exp2(top_own - top)
        inv = 1.0 / (total + stats[tiles + tile : tiles + tile + 1, :] * scale)
        own_scale[tile : tile + 1, :] = inv * scale
        scales[tile] = scale, inv

    def outputs(tile):
        base, turn = tile * TILE, tile % 2
        early = WINDOW - base
        scale, inv = scales.pop(tile)
        out = dot(vt[:, base:], e_scr[tile % 3, :early, :])
        out = out + out_own[:, tile * wide : (tile + 1) * wide] * scale
        out = (out * inv).T.astype(BF16)
        unstacked(outs, base, group, out)
        g_scr[turn], g_wide = gradient_rows(qg, base, group, inv, out)
        dp_scr[turn, :early, :] = dot_t(va[base:, :], g_wide)

    def gradients(tile):
        base, turn = tile * TILE, tile % 2
        early = WINDOW - base
        e = e_scr[tile % 3, :early, :]
        old = early if tile else 0
        add_rows(dv, base, old, dot(e, g_scr[turn]))
        score_gradients(ds_scr.at[turn, :early, :], e, dp_scr.at[turn, :early, :])
        ds = ds_scr[turn, :early, :]
        add_rows(dk, base, old, dot(ds, stacked(qg, base, group)))
        dq_part[:, tile * wide : (tile + 1) * wide] = dot(kt[:, base:], ds)

    pipeline(tiles, scores, weights, outputs, gradients)

    for lag in range(1, reach + 1):
        there = slice((reach - lag) * tok, (reach - lag + 1) * tok)
        sent[lag - 1][:, :HEAD_DIM] = (dk[there, :] * logit_scale).astype(BF16)
        sent[lag - 1][:, HEAD_DIM:] = dv[there, :].astype(BF16)
    take_rows(size, core, masks, lambda there: outs[there, :], out_pieces)


def backward_body(size, core, masks, tok, group, *refs):
    take = taker(refs)
    qg, kv, e_own, outs, own_scale, dq_part = take(6)
    dq_pieces, (dkv,) = take(len(masks)), take(1)
    dqs, va, kt, dk, dv, dp_scr, ds_scr, g_scr = take(8)
    wide = group * TILE
    kt[...] = kv[:, :HEAD_DIM].T
    set_values(va, kv[:, HEAD_DIM:])

    def products(tile):
        base, turn = tile * TILE, tile % 2
        scale = own_scale[tile : tile + 1, :]
        out = stacked(outs, base, group)
        g_scr[turn], g_wide = gradient_rows(qg, base, group, scale, out)
        dp_scr[turn, : base + TILE, :] = dot_t(va[: base + TILE, :], g_wide)

    def gradients(tile):
        base, turn = tile * TILE, tile % 2
        count = base + TILE
        columns = slice(tile * wide, (tile + 1) * wide)
        e = e_own[own_rows(tile), :]
        add_rows(dv, 0, base, dot(e, g_scr[turn]))
        score_gradients(ds_scr.at[turn, :count, :], e, dp_scr.at[turn, :count, :])
        ds = ds_scr[turn, :count, :]
        add_rows(dk, 0, base, dot(ds, stacked(qg, base, group)))
        dq = (dq_part[:, columns] + dot(kt[:, :count], ds)) * logit_scale
        unstacked(dqs, base, group, dq.T.astype(BF16))

    pipeline(tok // TILE, products, gradients)
    dkv[:, :HEAD_DIM] = dk[...] * logit_scale
    dkv[:, HEAD_DIM:] = dv[...]
    take_rows(size, core, masks, lambda there: dqs[there, :], dq_pieces)


def attend_call(kernel, out_shape, scratch_shapes, flops, name, *args):
    return pl.pallas_call(
        kernel,
        out_shape=out_shape,
        in_specs=[VMEM] * len(args),
        out_specs=[VMEM] * len(out_shape),
        scratch_shapes=scratch_shapes,
        compiler_params=pltpu.CompilerParams(vmem_limit_bytes=24 * 1024 * 1024),
        cost_estimate=pl.CostEstimate(
            flops=flops, bytes_accessed=8 * 1024 * 1024, transcendentals=0
        ),
        name=name,
    )(*args)


def forward_own(documents, qg, kv, size):
    rows, cols = qg[0].shape
    tok = len(qg) * rows
    group = cols // (2 * HEAD_DIM)
    wide, tiles = group * TILE, tok // TILE
    return attend_call(
        functools.partial(own_body, size, core_mask(), chip_masks(size), tok, group),
        [
            jax.ShapeDtypeStruct((own_rows(tiles - 1).stop, wide), BF16),
            jax.ShapeDtypeStruct((HEAD_DIM, tiles * wide), F32),
            jax.ShapeDtypeStruct((2 * tiles, wide), F32),
            jax.ShapeDtypeStruct((tok, cols), BF16),
        ],
        [
            pltpu.VMEM((tok, 2 * HEAD_DIM), BF16),
            pltpu.VMEM((HEAD_DIM, tok), BF16),
            pltpu.VMEM((2, tok, wide), F32),
        ],
        16 * tok * group * (WINDOW + TILE) * HEAD_DIM,
        "forward_own",
        *documents,
        *qg,
        kv,
    )


def forward(documents, qg, lags, carried, size):
    (tok, cols), count, reach = qg.shape, len(chip_masks(size)), len(lags)
    rows = tok // count
    group = cols // (2 * HEAD_DIM)
    wide, tiles = group * TILE, tok // TILE
    half = jax.ShapeDtypeStruct((tok, 2 * HEAD_DIM), BF16)
    out_shape = [jax.ShapeDtypeStruct((rows, cols // 2), BF16)] * count + [half] * reach
    out_shape += [
        jax.ShapeDtypeStruct((tok, cols // 2), BF16),
        jax.ShapeDtypeStruct((tiles, wide), F32),
        jax.ShapeDtypeStruct((HEAD_DIM, tiles * wide), F32),
    ]
    scratch = [
        pltpu.VMEM((WINDOW, 2 * HEAD_DIM), BF16),
        pltpu.VMEM((WINDOW, 2 * HEAD_DIM), BF16),
        pltpu.VMEM((HEAD_DIM, WINDOW), BF16),
        pltpu.VMEM((HEAD_DIM, WINDOW), BF16),
        pltpu.VMEM((WINDOW, HEAD_DIM), F32),
        pltpu.VMEM((WINDOW, HEAD_DIM), F32),
        pltpu.VMEM((2, WINDOW, wide), F32),
        pltpu.VMEM((3, WINDOW, wide), BF16),
        pltpu.VMEM((2, WINDOW, wide), F32),
        pltpu.VMEM((2, WINDOW, wide), BF16),
        pltpu.VMEM((2, wide, HEAD_DIM), BF16),
    ]
    results = attend_call(
        functools.partial(
            forward_body, size, core_mask(), chip_masks(size), reach, tok, group
        ),
        out_shape,
        scratch,
        6 * tok * group * (WINDOW + TILE) * HEAD_DIM,
        "forward",
        *documents,
        qg,
        *lags,
        *carried,
    )
    return results[:count], results[count : count + reach], results[count + reach :]


def backward(qg, kv, carried, size):
    (tok, cols), count = qg.shape, len(chip_masks(size))
    rows = tok // count
    group = cols // (2 * HEAD_DIM)
    wide = group * TILE
    results = attend_call(
        functools.partial(backward_body, size, core_mask(), chip_masks(size), tok, group),
        [jax.ShapeDtypeStruct((rows, cols // 2), BF16)] * count
        + [jax.ShapeDtypeStruct((tok, 2 * HEAD_DIM), F32)],
        [
            pltpu.VMEM((tok, cols // 2), BF16),
            pltpu.VMEM((tok, 2 * HEAD_DIM), BF16),
            pltpu.VMEM((HEAD_DIM, tok), BF16),
            pltpu.VMEM((tok, HEAD_DIM), F32),
            pltpu.VMEM((tok, HEAD_DIM), F32),
            pltpu.VMEM((2, tok, wide), F32),
            pltpu.VMEM((2, tok, wide), BF16),
            pltpu.VMEM((2, wide, HEAD_DIM), BF16),
        ],
        4 * tok * group * (WINDOW + TILE) * HEAD_DIM,
        "backward",
        qg,
        kv,
        *carried,
    )
    return results[:count], results[count]


def document_columns(segment_ids, tok, size):
    start = (flat_index() // size) * tok
    padded = jnp.concatenate([jnp.full((WINDOW,), -1, jnp.int32), segment_ids])
    keys = lax.dynamic_slice_in_dim(padded, start, WINDOW + tok, 0)
    queries = lax.dynamic_slice_in_dim(segment_ids, start, tok, 0)
    number = jnp.arange(HEAD_DIM, dtype=jnp.int32)[None, :]
    return (
        jnp.where(keys[:, None] == number, 0.0, FAR).astype(BF16),
        jnp.where(queries[:, None] == number, 1.0, 0.0).astype(BF16),
    )


def body(query, key, value, grad_out, segment_ids):
    size = key.shape[1] // HEAD_DIM
    rows = query.shape[0]
    tok = size * rows
    reach = WINDOW // tok
    assert reach * tok == WINDOW and device_count() % size == 0

    got = [swap(array, core_mask()) for array in (key, value, query, grad_out)]
    key, value = after(key, value)
    pieces = list(gather_cores((key, value), got[:2], size))
    pieces[0], query, grad_out, segment_ids = after(pieces[0], query, grad_out, segment_ids)
    documents = document_columns(segment_ids, tok, size)
    kv = join(swap_chips(pieces, size), size)
    lags = [shifted(kv, lag * size) for lag in range(1, reach + 1)]
    qg = swap_chips(gather_cores((query, grad_out), got[2:], size), size)

    e_own, *partial, qg = forward_own(documents, qg, kv, size)
    out, sent, carried = forward(documents, qg, lags, partial, size)
    backs = [shifted(sent[lag - 1], -lag * size) for lag in range(1, reach + 1)]
    out = swap_chips(out, size)
    grad_q, dkv = backward(qg, kv, [e_own, *carried], size)
    both = after(*out, *grad_q)
    out, grad_q = both[: len(out)], both[len(out) :]
    grad_q = swap_chips(grad_q, size)
    grads = swap_chips(combine([dkv, *backs], size), size)
    return tuple(spread_cores([out, grad_q, grads], (1, 1, 2), size))


def solution(mesh):
    placed = P(("pipe", "tensor"), None)
    return jax.shard_map(
        body,
        mesh=mesh,
        in_specs=(placed, placed, placed, placed, P()),
        out_specs=(placed, placed, placed, placed),
        check_vma=False,
    )
```

```python
import functools

import jax
import jax.numpy as jnp
from jax import lax
from jax.experimental import pallas as pl
from jax.experimental.pallas import tpu as pltpu
from jax.sharding import PartitionSpec as P

HEAD_DIM = 128
WINDOW = 1024
TILE = 128

logit_scale = 168.0 ** (-0.5)
exp2_scale = logit_scale * 1.4426950408889634

FAR = -(2.0**30)
SMALL = pltpu.CompilerParams(vmem_limit_bytes=4 * 1024 * 1024)
ANY = pl.BlockSpec(memory_space=pl.ANY)
VMEM = pl.BlockSpec(memory_space=pltpu.VMEM)
F32 = jnp.float32
BF16 = jnp.bfloat16
BOTH = ("pipe", "tensor")


def flat_index():
    return lax.axis_index("pipe") * lax.axis_size("tensor") + lax.axis_index("tensor")


def device_count():
    return lax.axis_size("pipe") * lax.axis_size("tensor")


def swap(value, mask):
    return lax.ppermute(value, BOTH, [(i, i ^ mask) for i in range(device_count())])


def core_mask():
    return lax.axis_size("tensor")


def chip_masks(size):
    return [mask for mask in range(size) if not mask & core_mask()]


def swap_chips(pieces, size):
    return [pieces[0]] + [
        swap(piece, mask) for piece, mask in zip(pieces[1:], chip_masks(size)[1:])
    ]


def shifted(value, step):
    count = device_count()
    pairs = [(i, i + step) for i in range(count) if 0 <= i + step < count]
    return lax.ppermute(value, BOTH, pairs)


def partner(size, j):
    return lax.bitwise_xor(lax.rem(flat_index(), size), j)


def place(index, width):
    return pl.ds(pl.multiple_of(index * width, width), width)


def after(value, *others):
    return lax.optimization_barrier((value, *others))


def run_copies(copies, sems):
    started = []
    for at, (source, target) in enumerate(copies):
        copy = pltpu.make_async_copy(source, target, sems.at[at])
        copy.start()
        started.append(copy)
    for copy in started:
        copy.wait()


def small_call(kernel, out_shape, name, *args):
    return pl.pallas_call(
        kernel,
        out_shape=out_shape,
        in_specs=[VMEM] * len(args),
        out_specs=jax.tree.map(lambda _: VMEM, out_shape),
        compiler_params=SMALL,
        name=name,
    )(*args)


def this_core(array, size):
    core = core_mask()
    width = array.shape[1] // size
    shares = [array[:, r * width : (r + 1) * width] for r in range(size)]
    first, second = (
        jnp.concatenate([share for r, share in enumerate(shares) if (r // core) % 2 == at], axis=1)
        for at in range(2)
    )
    return jnp.where((flat_index() // core) % 2 == 0, first, second)


def stack_body(size, core, masks, count, *refs):
    own, got, pieces = refs[:count], refs[count : 2 * count], refs[2 * count :]
    rows = own[0].shape[0]
    for mask, piece in zip(masks, pieces):
        there = partner(size, mask)
        chip = there // (2 * core) * core + lax.rem(there, core)
        start = 0
        for mine, other in zip(own, got):
            width = other.shape[1] // size
            piece[:rows, start : start + width] = mine[:, place(chip, width)]
            piece[rows:, start : start + width] = other[:, place(there, width)]
            start += width


def gather_cores(arrays, got, size):
    masks = chip_masks(size)
    own = [this_core(array, size) for array in arrays]
    cols = sum(array.shape[1] // size for array in arrays)
    piece = jax.ShapeDtypeStruct((2 * arrays[0].shape[0], cols), BF16)
    kernel = functools.partial(stack_body, size, core_mask(), masks, len(arrays))
    return small_call(kernel, [piece] * len(masks), "stack", *own, *got)


def place_rows(size, core, masks, pieces, out):
    for mask, piece in zip(masks, pieces):
        rows = piece.shape[0] // 2
        out[place(partner(size, mask), rows), :] = piece[:rows, :]
        out[place(partner(size, mask ^ core), rows), :] = piece[rows:, :]


def take_rows(size, core, masks, source, pieces):
    for mask, piece in zip(masks, pieces):
        rows = piece.shape[0] // 2
        piece[:rows, :] = source(place(partner(size, mask), rows))
        piece[rows:, :] = source(place(partner(size, mask ^ core), rows))


def join(pieces, size):
    rows, cols = pieces[0].shape
    core, masks = core_mask(), chip_masks(size)

    def kernel(*refs):
        place_rows(size, core, masks, refs[:-1], refs[-1])

    out = jax.ShapeDtypeStruct((len(pieces) * rows, cols), BF16)
    return small_call(kernel, out, "join", *pieces)


def combine(terms, size):
    tok, cols = terms[0].shape
    core, masks = core_mask(), chip_masks(size)

    def kernel(*refs):
        added = refs[: len(terms)]

        def source(there):
            total = added[0][there, :]
            for term in added[1:]:
                total = total + term[there, :].astype(F32)
            return total.astype(BF16)

        take_rows(size, core, masks, source, refs[len(terms) :])

    piece = jax.ShapeDtypeStruct((2 * (tok // size), cols), BF16)
    return small_call(kernel, [piece] * len(masks), "combine", *terms)


def bottom_body(*refs):
    out, start = refs[-1], 0
    for piece in refs[:-1]:
        rows, width = piece.shape[0] // 2, piece.shape[1]
        out[:, start : start + width] = piece[rows:, :]
        start += width


def spread_body(size, core, masks, counts, *refs):
    refs = list(refs)
    take = lambda count: [refs.pop(0) for _ in range(count)]
    sets = [take(len(masks)) for _ in counts]
    (got,), sets_out, (sems,) = take(1), [take(count) for count in counts], take(1)
    copies, start = [], 0
    for pieces, outs in zip(sets, sets_out):
        for mask, piece in zip(masks, pieces):
            rows, width = piece.shape[0] // 2, piece.shape[1] // len(outs)
            for at, out in enumerate(outs):
                mine = out.at[:, place(partner(size, mask), width)]
                other = out.at[:, place(partner(size, mask ^ core), width)]
                copies.append((piece.at[:rows, at * width : (at + 1) * width], mine))
                copies.append((got.at[:, start : start + width], other))
                start += width
    run_copies(copies, sems)


def spread_cores(sets, counts, size):
    pieces = [piece for part in sets for piece in part]
    rows = pieces[0].shape[0] // 2
    give = jax.ShapeDtypeStruct((rows, sum(piece.shape[1] for piece in pieces)), BF16)
    got = swap(small_call(bottom_body, give, "bottom", *pieces), core_mask())
    widths = [part[0].shape[1] // count for part, count in zip(sets, counts) for _ in range(count)]
    return pl.pallas_call(
        functools.partial(spread_body, size, core_mask(), chip_masks(size), counts),
        out_shape=[jax.ShapeDtypeStruct((rows, width * size), BF16) for width in widths],
        in_specs=[ANY] * (len(pieces) + 1),
        out_specs=[ANY] * len(widths),
        scratch_shapes=[pltpu.SemaphoreType.DMA((len(widths) * size,))],
        compiler_params=SMALL,
        name="spread",
    )(*pieces, got)


def dot(a, b):
    return lax.dot_general(a, b, (((1,), (0,)), ((), ())), preferred_element_type=F32)


def dot_t(a, b):
    return lax.dot_general(a, b, (((1,), (1,)), ((), ())), preferred_element_type=F32)


def fold(x, op):
    parts = [x[at : at + 8] for at in range(0, x.shape[0], 8)]
    while len(parts) > 1:
        parts = [
            op(*parts[at : at + 2]) if at + 1 < len(parts) else parts[at]
            for at in range(0, len(parts), 2)
        ]
    return parts[0]


def taker(refs):
    refs = list(refs)
    return lambda count: [refs.pop(0) for _ in range(count)]


def stacked(rows, base, group, first=0):
    parts = [slice(first + at * HEAD_DIM, first + (at + 1) * HEAD_DIM) for at in range(group)]
    return jnp.concatenate([rows[base : base + TILE, part] for part in parts], axis=0)


def unstacked(rows, base, group, value):
    for at in range(group):
        part = slice(at * TILE, (at + 1) * TILE)
        rows[base : base + TILE, at * HEAD_DIM : (at + 1) * HEAD_DIM] = value[part]


def set_values(va, values):
    lane = lax.broadcasted_iota(jnp.int32, values.shape, 1)
    va[:, :HEAD_DIM] = values
    va[:, HEAD_DIM:] = jnp.where(lane < 2, 1.0, 0.0).astype(BF16)


def add_rows(target, start, old, value):
    if old:
        target[start : start + old, :] += value[:old]
    if old < value.shape[0]:
        target[start + old : start + value.shape[0], :] = value[old:]


def score_gradients(ds_scr, e, dp):
    for at in range(0, e.shape[0], TILE):
        part = slice(at, at + TILE)
        ds_scr[part, :] = (e[part, :].astype(F32) * dp[part, :]).astype(BF16)


def pipeline(tiles, *stages):
    for step in range(tiles + len(stages) - 1):
        for behind, stage in enumerate(stages):
            if 0 <= step - behind < tiles:
                stage(step - behind)


def early_rows(tile):
    count = WINDOW // TILE
    start = (tile * count - tile * (tile - 1) // 2) * TILE
    return slice(start, start + (count - tile) * TILE)


def gradient_rows(qg, base, group, scale, out):
    first = qg.shape[1] // 2
    columns = jnp.broadcast_to(scale, (HEAD_DIM, scale.shape[1])).T
    g2 = (stacked(qg, base, group, first).astype(F32) * columns).astype(BF16)
    delta = jnp.sum(g2.astype(F32) * out.astype(F32), axis=1, keepdims=True)
    high = delta.astype(BF16).astype(F32)
    lane = lax.broadcasted_iota(jnp.int32, g2.shape, 1)
    extra = jnp.where(lane == 0, -high, jnp.where(lane == 1, high - delta, 0.0))
    return g2, jnp.concatenate([g2, extra.astype(BF16)], axis=1)


def own_rows(tile):
    start = tile * (tile + 1) // 2 * TILE
    return slice(start, start + (tile + 1) * TILE)


def query_columns(qg, seg_q, base, group):
    mine = jnp.concatenate([seg_q[base : base + TILE, :]] * group, axis=0)
    return jnp.concatenate([stacked(qg, base, group), mine], axis=1)


def fold_rows(rows, op):
    parts = [fold(rows[at : at + TILE, :], op) for at in range(0, rows.shape[0], TILE)]
    whole = functools.reduce(op, parts)
    reduce = jnp.max if op is jnp.maximum else jnp.sum
    return reduce(whole, axis=0, keepdims=True)


def weigh(scores, top, keep):
    total = None
    for at in range(0, scores.shape[0], TILE):
        part = slice(at, at + TILE)
        e = jnp.exp2(scores[part, :] * exp2_scale - top)
        keep[part, :] = e.astype(BF16)
        e = fold(e, jnp.add)
        total = e if total is None else total + e
    return jnp.sum(total, axis=0, keepdims=True)


def tile_causal(group):
    row_of = lax.broadcasted_iota(jnp.int32, (TILE, TILE), 0)
    col_of = lax.broadcasted_iota(jnp.int32, (TILE, TILE), 1)
    return jnp.concatenate([row_of <= col_of] * group, axis=1)


def own_body(size, core, masks, tok, group, *refs):
    take = taker(refs)
    (seg_k, seg_q), qg_pieces, (kv,) = take(2), take(len(masks)), take(1)
    e_own, out_part, stats, qg = take(4)
    ka, vt, s_scr = take(3)
    wide, tiles = group * TILE, tok // TILE
    place_rows(size, core, masks, qg_pieces, qg)
    ka[:, :HEAD_DIM] = kv[:, :HEAD_DIM]
    ka[:, HEAD_DIM:] = seg_k[WINDOW:, :]
    vt[...] = kv[:, HEAD_DIM:].T
    causal = tile_causal(group)

    def scores(tile):
        queries = query_columns(qg, seg_q, tile * TILE, group)
        s_scr[tile % 2, : (tile + 1) * TILE, :] = dot_t(ka[: (tile + 1) * TILE, :], queries)

    def weights(tile):
        base, turn = tile * TILE, tile % 2
        last = slice(base, base + TILE)
        s_scr[turn, last, :] = jnp.where(causal, s_scr[turn, last, :], FAR)
        rows = s_scr.at[turn, : base + TILE, :]
        top = fold_rows(rows, jnp.maximum) * exp2_scale
        stats[tile : tile + 1, :] = top
        stats[tiles + tile : tiles + tile + 1, :] = weigh(rows, top, e_own.at[own_rows(tile), :])

    def outputs(tile):
        e = e_own[own_rows(tile), :]
        out_part[:, tile * wide : (tile + 1) * wide] = dot(vt[:, : (tile + 1) * TILE], e)

    pipeline(tiles, scores, weights, outputs)


def forward_body(size, core, masks, reach, tok, group, *refs):
    take = taker(refs)
    (seg_k, seg_q, qg), kvs, (out_own, stats) = take(3), take(reach), take(2)
    out_pieces, sent, (outs, own_scale, ds_early, kt) = take(len(masks)), take(reach), take(4)
    ka, va, vt, dk, dv, s_scr, e_scr, dp_scr, g_scr = take(9)
    wide, tiles = group * TILE, tok // TILE
    ka[:, HEAD_DIM:] = seg_k[:WINDOW, :]
    for lag in range(1, reach + 1):
        there = slice((reach - lag) * tok, (reach - lag + 1) * tok)
        kv = kvs[lag - 1][...]
        ka[there, :HEAD_DIM] = kv[:, :HEAD_DIM]
        kt[:, there] = kv[:, :HEAD_DIM].T
        vt[:, there] = kv[:, HEAD_DIM:].T
        set_values(va.at[there, :], kv[:, HEAD_DIM:])
    beyond = ~tile_causal(group)

    def scores(tile):
        base = tile * TILE
        queries = query_columns(qg, seg_q, base, group)
        s_scr[tile % 2, : WINDOW - base, :] = dot_t(ka[base:, :], queries)

    scales = {}

    def weights(tile):
        early = WINDOW - tile * TILE
        turn = tile % 2
        s_scr[turn, :TILE, :] = jnp.where(beyond, s_scr[turn, :TILE, :], FAR)
        rows = s_scr.at[turn, :early, :]
        top_own = stats[tile : tile + 1, :]
        top = jnp.maximum(fold_rows(rows, jnp.maximum) * exp2_scale, top_own)
        total = weigh(rows, top, e_scr.at[tile % 3, :early, :])
        scale = jnp.exp2(top_own - top)
        inv = 1.0 / (total + stats[tiles + tile : tiles + tile + 1, :] * scale)
        own_scale[tile : tile + 1, :] = inv * scale
        scales[tile] = scale, inv

    def outputs(tile):
        base, turn = tile * TILE, tile % 2
        early = WINDOW - base
        scale, inv = scales.pop(tile)
        out = dot(vt[:, base:], e_scr[tile % 3, :early, :])
        out = out + out_own[:, tile * wide : (tile + 1) * wide] * scale
        out = (out * inv).T.astype(BF16)
        unstacked(outs, base, group, out)
        g_scr[turn], g_wide = gradient_rows(qg, base, group, inv, out)
        dp_scr[turn, :early, :] = dot_t(va[base:, :], g_wide)

    def gradients(tile):
        base, turn = tile * TILE, tile % 2
        early = WINDOW - base
        e = e_scr[tile % 3, :early, :]
        old = early if tile else 0
        add_rows(dv, base, old, dot(e, g_scr[turn]))
        ds = ds_early.at[early_rows(tile), :]
        score_gradients(ds, e, dp_scr.at[turn, :early, :])
        add_rows(dk, base, old, dot(ds[...], stacked(qg, base, group)))

    pipeline(tiles, scores, weights, outputs, gradients)

    for lag in range(1, reach + 1):
        there = slice((reach - lag) * tok, (reach - lag + 1) * tok)
        sent[lag - 1][:, :HEAD_DIM] = (dk[there, :] * logit_scale).astype(BF16)
        sent[lag - 1][:, HEAD_DIM:] = dv[there, :].astype(BF16)
    take_rows(size, core, masks, lambda there: outs[there, :], out_pieces)


def backward_body(size, core, masks, tok, group, *refs):
    take = taker(refs)
    qg, kv, e_own, outs, own_scale, ds_early, kt_early = take(7)
    dq_pieces, (dkv,) = take(len(masks)), take(1)
    dqs, va, kt, dk, dv, dp_scr, ds_scr, g_scr = take(8)
    wide = group * TILE
    kt[...] = kv[:, :HEAD_DIM].T
    set_values(va, kv[:, HEAD_DIM:])

    def products(tile):
        base, turn = tile * TILE, tile % 2
        scale = own_scale[tile : tile + 1, :]
        out = stacked(outs, base, group)
        g_scr[turn], g_wide = gradient_rows(qg, base, group, scale, out)
        dp_scr[turn, : base + TILE, :] = dot_t(va[: base + TILE, :], g_wide)

    def gradients(tile):
        base, turn = tile * TILE, tile % 2
        count = base + TILE
        e = e_own[own_rows(tile), :]
        add_rows(dv, 0, base, dot(e, g_scr[turn]))
        score_gradients(ds_scr.at[turn, :count, :], e, dp_scr.at[turn, :count, :])
        ds = ds_scr[turn, :count, :]
        add_rows(dk, 0, base, dot(ds, stacked(qg, base, group)))
        dq = dot(kt_early[:, base:], ds_early[early_rows(tile), :]) + dot(kt[:, :count], ds)
        dq = dq * logit_scale
        unstacked(dqs, base, group, dq.T.astype(BF16))

    pipeline(tok // TILE, products, gradients)
    dkv[:, :HEAD_DIM] = dk[...] * logit_scale
    dkv[:, HEAD_DIM:] = dv[...]
    take_rows(size, core, masks, lambda there: dqs[there, :], dq_pieces)


def attend_call(kernel, out_shape, scratch_shapes, flops, name, *args):
    return pl.pallas_call(
        kernel,
        out_shape=out_shape,
        in_specs=[VMEM] * len(args),
        out_specs=[VMEM] * len(out_shape),
        scratch_shapes=scratch_shapes,
        compiler_params=pltpu.CompilerParams(vmem_limit_bytes=24 * 1024 * 1024),
        cost_estimate=pl.CostEstimate(
            flops=flops, bytes_accessed=8 * 1024 * 1024, transcendentals=0
        ),
        name=name,
    )(*args)


def forward_own(documents, qg, kv, size):
    rows, cols = qg[0].shape
    tok = len(qg) * rows
    group = cols // (2 * HEAD_DIM)
    wide, tiles = group * TILE, tok // TILE
    return attend_call(
        functools.partial(own_body, size, core_mask(), chip_masks(size), tok, group),
        [
            jax.ShapeDtypeStruct((own_rows(tiles - 1).stop, wide), BF16),
            jax.ShapeDtypeStruct((HEAD_DIM, tiles * wide), F32),
            jax.ShapeDtypeStruct((2 * tiles, wide), F32),
            jax.ShapeDtypeStruct((tok, cols), BF16),
        ],
        [
            pltpu.VMEM((tok, 2 * HEAD_DIM), BF16),
            pltpu.VMEM((HEAD_DIM, tok), BF16),
            pltpu.VMEM((2, tok, wide), F32),
        ],
        16 * tok * group * (WINDOW + TILE) * HEAD_DIM,
        "forward_own",
        *documents,
        *qg,
        kv,
    )


def forward(documents, qg, lags, carried, size):
    (tok, cols), count, reach = qg.shape, len(chip_masks(size)), len(lags)
    rows = tok // count
    group = cols // (2 * HEAD_DIM)
    wide, tiles = group * TILE, tok // TILE
    half = jax.ShapeDtypeStruct((tok, 2 * HEAD_DIM), BF16)
    out_shape = [jax.ShapeDtypeStruct((rows, cols // 2), BF16)] * count + [half] * reach
    out_shape += [
        jax.ShapeDtypeStruct((tok, cols // 2), BF16),
        jax.ShapeDtypeStruct((tiles, wide), F32),
        jax.ShapeDtypeStruct((early_rows(tiles - 1).stop, wide), BF16),
        jax.ShapeDtypeStruct((HEAD_DIM, WINDOW), BF16),
    ]
    scratch = [
        pltpu.VMEM((WINDOW, 2 * HEAD_DIM), BF16),
        pltpu.VMEM((WINDOW, 2 * HEAD_DIM), BF16),
        pltpu.VMEM((HEAD_DIM, WINDOW), BF16),
        pltpu.VMEM((WINDOW, HEAD_DIM), F32),
        pltpu.VMEM((WINDOW, HEAD_DIM), F32),
        pltpu.VMEM((2, WINDOW, wide), F32),
        pltpu.VMEM((3, WINDOW, wide), BF16),
        pltpu.VMEM((2, WINDOW, wide), F32),
        pltpu.VMEM((2, wide, HEAD_DIM), BF16),
    ]
    results = attend_call(
        functools.partial(
            forward_body, size, core_mask(), chip_masks(size), reach, tok, group
        ),
        out_shape,
        scratch,
        6 * tok * group * (WINDOW + TILE) * HEAD_DIM,
        "forward",
        *documents,
        qg,
        *lags,
        *carried,
    )
    return results[:count], results[count : count + reach], results[count + reach :]


def backward(qg, kv, carried, size):
    (tok, cols), count = qg.shape, len(chip_masks(size))
    rows = tok // count
    group = cols // (2 * HEAD_DIM)
    wide = group * TILE
    results = attend_call(
        functools.partial(backward_body, size, core_mask(), chip_masks(size), tok, group),
        [jax.ShapeDtypeStruct((rows, cols // 2), BF16)] * count
        + [jax.ShapeDtypeStruct((tok, 2 * HEAD_DIM), F32)],
        [
            pltpu.VMEM((tok, cols // 2), BF16),
            pltpu.VMEM((tok, 2 * HEAD_DIM), BF16),
            pltpu.VMEM((HEAD_DIM, tok), BF16),
            pltpu.VMEM((tok, HEAD_DIM), F32),
            pltpu.VMEM((tok, HEAD_DIM), F32),
            pltpu.VMEM((2, tok, wide), F32),
            pltpu.VMEM((2, tok, wide), BF16),
            pltpu.VMEM((2, wide, HEAD_DIM), BF16),
        ],
        4 * tok * group * (WINDOW + TILE) * HEAD_DIM,
        "backward",
        qg,
        kv,
        *carried,
    )
    return results[:count], results[count]


def document_columns(segment_ids, tok, size):
    start = (flat_index() // size) * tok
    padded = jnp.concatenate([jnp.full((WINDOW,), -1, jnp.int32), segment_ids])
    keys = lax.dynamic_slice_in_dim(padded, start, WINDOW + tok, 0)
    queries = lax.dynamic_slice_in_dim(segment_ids, start, tok, 0)
    number = jnp.arange(HEAD_DIM, dtype=jnp.int32)[None, :]
    return (
        jnp.where(keys[:, None] == number, 0.0, FAR).astype(BF16),
        jnp.where(queries[:, None] == number, 1.0, 0.0).astype(BF16),
    )


def body(query, key, value, grad_out, segment_ids):
    size = key.shape[1] // HEAD_DIM
    rows = query.shape[0]
    tok = size * rows
    reach = WINDOW // tok
    assert reach * tok == WINDOW and device_count() % size == 0

    got = [swap(array, core_mask()) for array in (key, value, query, grad_out)]
    key, value = after(key, value)
    pieces = list(gather_cores((key, value), got[:2], size))
    pieces[0], query, grad_out, segment_ids = after(pieces[0], query, grad_out, segment_ids)
    documents = document_columns(segment_ids, tok, size)
    kv = join(swap_chips(pieces, size), size)
    lags = [shifted(kv, lag * size) for lag in range(1, reach + 1)]
    qg = swap_chips(gather_cores((query, grad_out), got[2:], size), size)

    e_own, *partial, qg = forward_own(documents, qg, kv, size)
    out, sent, carried = forward(documents, qg, lags, partial, size)
    backs = [shifted(sent[lag - 1], -lag * size) for lag in range(1, reach + 1)]
    out = swap_chips(out, size)
    grad_q, dkv = backward(qg, kv, [e_own, *carried], size)
    both = after(*out, *grad_q)
    out, grad_q = both[: len(out)], both[len(out) :]
    grad_q = swap_chips(grad_q, size)
    grads = swap_chips(combine([dkv, *backs], size), size)
    return tuple(spread_cores([out, grad_q, grads], (1, 1, 2), size))


def solution(mesh):
    placed = P(("pipe", "tensor"), None)
    return jax.shard_map(
        body,
        mesh=mesh,
        in_specs=(placed, placed, placed, placed, P()),
        out_specs=(placed, placed, placed, placed),
        check_vma=False,
    )
```

```python
import functools

import jax
import jax.numpy as jnp
from jax import lax
from jax.experimental import pallas as pl
from jax.experimental.pallas import tpu as pltpu
from jax.sharding import PartitionSpec as P

HEAD_DIM = 128
WINDOW = 1024
TILE = 128

logit_scale = 168.0 ** (-0.5)
exp2_scale = logit_scale * 1.4426950408889634

FAR = -(2.0**30)
SMALL = pltpu.CompilerParams(vmem_limit_bytes=4 * 1024 * 1024)
ANY = pl.BlockSpec(memory_space=pl.ANY)
VMEM = pl.BlockSpec(memory_space=pltpu.VMEM)
F32 = jnp.float32
BF16 = jnp.bfloat16
BOTH = ("pipe", "tensor")


def flat_index():
    return lax.axis_index("pipe") * lax.axis_size("tensor") + lax.axis_index("tensor")


def device_count():
    return lax.axis_size("pipe") * lax.axis_size("tensor")


def swap(value, mask):
    return lax.ppermute(value, BOTH, [(i, i ^ mask) for i in range(device_count())])


def core_mask():
    return lax.axis_size("tensor")


def chip_masks(size):
    return [mask for mask in range(size) if not mask & core_mask()]


def swap_chips(pieces, size):
    return [pieces[0]] + [
        swap(piece, mask) for piece, mask in zip(pieces[1:], chip_masks(size)[1:])
    ]


def shifted(value, step):
    count = device_count()
    pairs = [(i, i + step) for i in range(count) if 0 <= i + step < count]
    return lax.ppermute(value, BOTH, pairs)


def partner(size, j):
    return lax.bitwise_xor(lax.rem(flat_index(), size), j)


def place(index, width):
    return pl.ds(pl.multiple_of(index * width, width), width)


def after(value, *others):
    return lax.optimization_barrier((value, *others))


def run_copies(copies, sems):
    started = []
    for at, (source, target) in enumerate(copies):
        copy = pltpu.make_async_copy(source, target, sems.at[at])
        copy.start()
        started.append(copy)
    for copy in started:
        copy.wait()


def small_call(kernel, out_shape, name, *args):
    return pl.pallas_call(
        kernel,
        out_shape=out_shape,
        in_specs=[VMEM] * len(args),
        out_specs=jax.tree.map(lambda _: VMEM, out_shape),
        compiler_params=SMALL,
        name=name,
    )(*args)


def this_core(array, size):
    core = core_mask()
    width = array.shape[1] // size
    shares = [array[:, r * width : (r + 1) * width] for r in range(size)]
    first, second = (
        jnp.concatenate([share for r, share in enumerate(shares) if (r // core) % 2 == at], axis=1)
        for at in range(2)
    )
    return jnp.where((flat_index() // core) % 2 == 0, first, second)


def stack_body(size, core, masks, count, *refs):
    own, got, pieces = refs[:count], refs[count : 2 * count], refs[2 * count :]
    rows = own[0].shape[0]
    for mask, piece in zip(masks, pieces):
        there = partner(size, mask)
        chip = there // (2 * core) * core + lax.rem(there, core)
        start = 0
        for mine, other in zip(own, got):
            width = other.shape[1] // size
            piece[:rows, start : start + width] = mine[:, place(chip, width)]
            piece[rows:, start : start + width] = other[:, place(there, width)]
            start += width


def gather_cores(arrays, got, size):
    masks = chip_masks(size)
    own = [this_core(array, size) for array in arrays]
    cols = sum(array.shape[1] // size for array in arrays)
    piece = jax.ShapeDtypeStruct((2 * arrays[0].shape[0], cols), BF16)
    kernel = functools.partial(stack_body, size, core_mask(), masks, len(arrays))
    return small_call(kernel, [piece] * len(masks), "stack", *own, *got)


def place_rows(size, core, masks, pieces, out):
    for mask, piece in zip(masks, pieces):
        rows = piece.shape[0] // 2
        out[place(partner(size, mask), rows), :] = piece[:rows, :]
        out[place(partner(size, mask ^ core), rows), :] = piece[rows:, :]


def take_rows(size, core, masks, source, pieces):
    for mask, piece in zip(masks, pieces):
        rows = piece.shape[0] // 2
        piece[:rows, :] = source(place(partner(size, mask), rows))
        piece[rows:, :] = source(place(partner(size, mask ^ core), rows))


def join(pieces, size):
    rows, cols = pieces[0].shape
    core, masks = core_mask(), chip_masks(size)

    def kernel(*refs):
        place_rows(size, core, masks, refs[:-1], refs[-1])

    out = jax.ShapeDtypeStruct((len(pieces) * rows, cols), BF16)
    return small_call(kernel, out, "join", *pieces)


def combine(terms, size):
    tok, cols = terms[0].shape
    core, masks = core_mask(), chip_masks(size)

    def kernel(*refs):
        added = refs[: len(terms)]

        def source(there):
            total = added[0][there, :]
            for term in added[1:]:
                total = total + term[there, :].astype(F32)
            return total.astype(BF16)

        take_rows(size, core, masks, source, refs[len(terms) :])

    piece = jax.ShapeDtypeStruct((2 * (tok // size), cols), BF16)
    return small_call(kernel, [piece] * len(masks), "combine", *terms)


def bottom_body(*refs):
    out, start = refs[-1], 0
    for piece in refs[:-1]:
        rows, width = piece.shape[0] // 2, piece.shape[1]
        out[:, start : start + width] = piece[rows:, :]
        start += width


def spread_body(size, core, masks, counts, *refs):
    refs = list(refs)
    take = lambda count: [refs.pop(0) for _ in range(count)]
    sets = [take(len(masks)) for _ in counts]
    (got,), sets_out, (sems,) = take(1), [take(count) for count in counts], take(1)
    copies, start = [], 0
    for pieces, outs in zip(sets, sets_out):
        for mask, piece in zip(masks, pieces):
            rows, width = piece.shape[0] // 2, piece.shape[1] // len(outs)
            for at, out in enumerate(outs):
                mine = out.at[:, place(partner(size, mask), width)]
                other = out.at[:, place(partner(size, mask ^ core), width)]
                copies.append((piece.at[:rows, at * width : (at + 1) * width], mine))
                copies.append((got.at[:, start : start + width], other))
                start += width
    run_copies(copies, sems)


def spread_cores(sets, counts, size):
    pieces = [piece for part in sets for piece in part]
    rows = pieces[0].shape[0] // 2
    give = jax.ShapeDtypeStruct((rows, sum(piece.shape[1] for piece in pieces)), BF16)
    got = swap(small_call(bottom_body, give, "bottom", *pieces), core_mask())
    widths = [part[0].shape[1] // count for part, count in zip(sets, counts) for _ in range(count)]
    return pl.pallas_call(
        functools.partial(spread_body, size, core_mask(), chip_masks(size), counts),
        out_shape=[jax.ShapeDtypeStruct((rows, width * size), BF16) for width in widths],
        in_specs=[ANY] * (len(pieces) + 1),
        out_specs=[ANY] * len(widths),
        scratch_shapes=[pltpu.SemaphoreType.DMA((len(widths) * size,))],
        compiler_params=SMALL,
        name="spread",
    )(*pieces, got)


def dot(a, b):
    return lax.dot_general(a, b, (((1,), (0,)), ((), ())), preferred_element_type=F32)


def dot_t(a, b):
    return lax.dot_general(a, b, (((1,), (1,)), ((), ())), preferred_element_type=F32)


def fold(x, op):
    parts = [x[at : at + 8] for at in range(0, x.shape[0], 8)]
    while len(parts) > 1:
        parts = [
            op(*parts[at : at + 2]) if at + 1 < len(parts) else parts[at]
            for at in range(0, len(parts), 2)
        ]
    return parts[0]


def taker(refs):
    refs = list(refs)
    return lambda count: [refs.pop(0) for _ in range(count)]


def stacked(rows, base, group, first=0):
    parts = [slice(first + at * HEAD_DIM, first + (at + 1) * HEAD_DIM) for at in range(group)]
    return jnp.concatenate([rows[base : base + TILE, part] for part in parts], axis=0)


def unstacked(rows, base, group, value):
    for at in range(group):
        part = slice(at * TILE, (at + 1) * TILE)
        rows[base : base + TILE, at * HEAD_DIM : (at + 1) * HEAD_DIM] = value[part]


def set_values(va, values):
    lane = lax.broadcasted_iota(jnp.int32, values.shape, 1)
    va[:, :HEAD_DIM] = values
    va[:, HEAD_DIM:] = jnp.where(lane < 2, 1.0, 0.0).astype(BF16)


def add_rows(target, start, old, value):
    if old:
        target[start : start + old, :] += value[:old]
    if old < value.shape[0]:
        target[start + old : start + value.shape[0], :] = value[old:]


def score_gradients(ds_scr, e, dp):
    for at in range(0, e.shape[0], TILE):
        part = slice(at, at + TILE)
        ds_scr[part, :] = (e[part, :].astype(F32) * dp[part, :]).astype(BF16)


def pipeline(tiles, *stages):
    for step in range(tiles + len(stages) - 1):
        for behind, stage in enumerate(stages):
            if 0 <= step - behind < tiles:
                stage(step - behind)


def early_rows(tile):
    count = WINDOW // TILE
    start = (tile * count - tile * (tile - 1) // 2) * TILE
    return slice(start, start + (count - tile) * TILE)


def gradient_rows(g_rows, base, group, scale, out):
    columns = jnp.broadcast_to(scale, (HEAD_DIM, scale.shape[1])).T
    g2 = (stacked(g_rows, base, group).astype(F32) * columns).astype(BF16)
    delta = jnp.sum(g2.astype(F32) * out.astype(F32), axis=1, keepdims=True)
    high = delta.astype(BF16).astype(F32)
    lane = lax.broadcasted_iota(jnp.int32, g2.shape, 1)
    extra = jnp.where(lane == 0, -high, jnp.where(lane == 1, high - delta, 0.0))
    return g2, jnp.concatenate([g2, extra.astype(BF16)], axis=1)


def own_rows(tile):
    start = tile * (tile + 1) // 2 * TILE
    return slice(start, start + (tile + 1) * TILE)


def query_columns(qg, seg_q, base, group):
    mine = jnp.concatenate([seg_q[base : base + TILE, :]] * group, axis=0)
    return jnp.concatenate([stacked(qg, base, group), mine], axis=1)


def fold_rows(rows, op):
    parts = [fold(rows[at : at + TILE, :], op) for at in range(0, rows.shape[0], TILE)]
    whole = functools.reduce(op, parts)
    reduce = jnp.max if op is jnp.maximum else jnp.sum
    return reduce(whole, axis=0, keepdims=True)


def weigh(scores, top, keep):
    total = None
    for at in range(0, scores.shape[0], TILE):
        part = slice(at, at + TILE)
        e = jnp.exp2(scores[part, :] * exp2_scale - top)
        keep[part, :] = e.astype(BF16)
        e = fold(e, jnp.add)
        total = e if total is None else total + e
    return jnp.sum(total, axis=0, keepdims=True)


def tile_causal(group):
    row_of = lax.broadcasted_iota(jnp.int32, (TILE, TILE), 0)
    col_of = lax.broadcasted_iota(jnp.int32, (TILE, TILE), 1)
    return jnp.concatenate([row_of <= col_of] * group, axis=1)


def own_body(size, core, masks, tok, group, *refs):
    take = taker(refs)
    (seg_k, seg_q), q_pieces, (kv,) = take(2), take(len(masks)), take(1)
    e_own, out_part, stats, q_rows = take(4)
    ka, vt, s_scr = take(3)
    wide, tiles = group * TILE, tok // TILE
    place_rows(size, core, masks, q_pieces, q_rows)
    ka[:, :HEAD_DIM] = kv[:, :HEAD_DIM]
    ka[:, HEAD_DIM:] = seg_k[WINDOW:, :]
    vt[...] = kv[:, HEAD_DIM:].T
    causal = tile_causal(group)

    def scores(tile):
        queries = query_columns(q_rows, seg_q, tile * TILE, group)
        s_scr[tile % 2, : (tile + 1) * TILE, :] = dot_t(ka[: (tile + 1) * TILE, :], queries)

    def weights(tile):
        base, turn = tile * TILE, tile % 2
        last = slice(base, base + TILE)
        s_scr[turn, last, :] = jnp.where(causal, s_scr[turn, last, :], FAR)
        rows = s_scr.at[turn, : base + TILE, :]
        top = fold_rows(rows, jnp.maximum) * exp2_scale
        stats[tile : tile + 1, :] = top
        stats[tiles + tile : tiles + tile + 1, :] = weigh(rows, top, e_own.at[own_rows(tile), :])

    def outputs(tile):
        e = e_own[own_rows(tile), :]
        out_part[:, tile * wide : (tile + 1) * wide] = dot(vt[:, : (tile + 1) * TILE], e)

    pipeline(tiles, scores, weights, outputs)


def forward_body(size, core, masks, reach, tok, group, *refs):
    take = taker(refs)
    (seg_k, seg_q, q_rows), g_pieces, kvs = take(3), take(len(masks)), take(reach)
    out_own, stats = take(2)
    out_pieces, sent, (outs, own_scale, ds_early, kt) = take(len(masks)), take(reach), take(4)
    (g_rows,) = take(1)
    ka, va, vt, dk, dv, s_scr, e_scr, dp_scr, g_scr = take(9)
    wide, tiles = group * TILE, tok // TILE
    place_rows(size, core, masks, g_pieces, g_rows)
    ka[:, HEAD_DIM:] = seg_k[:WINDOW, :]
    for lag in range(1, reach + 1):
        there = slice((reach - lag) * tok, (reach - lag + 1) * tok)
        kv = kvs[lag - 1][...]
        ka[there, :HEAD_DIM] = kv[:, :HEAD_DIM]
        kt[:, there] = kv[:, :HEAD_DIM].T
        vt[:, there] = kv[:, HEAD_DIM:].T
        set_values(va.at[there, :], kv[:, HEAD_DIM:])
    beyond = ~tile_causal(group)

    def scores(tile):
        base = tile * TILE
        queries = query_columns(q_rows, seg_q, base, group)
        s_scr[tile % 2, : WINDOW - base, :] = dot_t(ka[base:, :], queries)

    scales = {}

    def weights(tile):
        early = WINDOW - tile * TILE
        turn = tile % 2
        s_scr[turn, :TILE, :] = jnp.where(beyond, s_scr[turn, :TILE, :], FAR)
        rows = s_scr.at[turn, :early, :]
        top_own = stats[tile : tile + 1, :]
        top = jnp.maximum(fold_rows(rows, jnp.maximum) * exp2_scale, top_own)
        total = weigh(rows, top, e_scr.at[tile % 3, :early, :])
        scale = jnp.exp2(top_own - top)
        inv = 1.0 / (total + stats[tiles + tile : tiles + tile + 1, :] * scale)
        own_scale[tile : tile + 1, :] = inv * scale
        scales[tile] = scale, inv

    def outputs(tile):
        base, turn = tile * TILE, tile % 2
        early = WINDOW - base
        scale, inv = scales.pop(tile)
        out = dot(vt[:, base:], e_scr[tile % 3, :early, :])
        out = out + out_own[:, tile * wide : (tile + 1) * wide] * scale
        out = (out * inv).T.astype(BF16)
        unstacked(outs, base, group, out)
        g_scr[turn], g_wide = gradient_rows(g_rows, base, group, inv, out)
        dp_scr[turn, :early, :] = dot_t(va[base:, :], g_wide)

    def gradients(tile):
        base, turn = tile * TILE, tile % 2
        early = WINDOW - base
        e = e_scr[tile % 3, :early, :]
        old = early if tile else 0
        add_rows(dv, base, old, dot(e, g_scr[turn]))
        ds = ds_early.at[early_rows(tile), :]
        score_gradients(ds, e, dp_scr.at[turn, :early, :])
        add_rows(dk, base, old, dot(ds[...], stacked(q_rows, base, group)))

    pipeline(tiles, scores, weights, outputs, gradients)

    for lag in range(1, reach + 1):
        there = slice((reach - lag) * tok, (reach - lag + 1) * tok)
        sent[lag - 1][:, :HEAD_DIM] = (dk[there, :] * logit_scale).astype(BF16)
        sent[lag - 1][:, HEAD_DIM:] = dv[there, :].astype(BF16)
    take_rows(size, core, masks, lambda there: outs[there, :], out_pieces)


def backward_body(size, core, masks, tok, group, *refs):
    take = taker(refs)
    q_rows, kv, e_own, outs, own_scale, ds_early, kt_early, g_rows = take(8)
    dq_pieces, (dkv,) = take(len(masks)), take(1)
    dqs, va, kt, dk, dv, dp_scr, ds_scr, g_scr = take(8)
    wide = group * TILE
    kt[...] = kv[:, :HEAD_DIM].T
    set_values(va, kv[:, HEAD_DIM:])

    def products(tile):
        base, turn = tile * TILE, tile % 2
        scale = own_scale[tile : tile + 1, :]
        out = stacked(outs, base, group)
        g_scr[turn], g_wide = gradient_rows(g_rows, base, group, scale, out)
        dp_scr[turn, : base + TILE, :] = dot_t(va[: base + TILE, :], g_wide)

    def gradients(tile):
        base, turn = tile * TILE, tile % 2
        count = base + TILE
        e = e_own[own_rows(tile), :]
        add_rows(dv, 0, base, dot(e, g_scr[turn]))
        score_gradients(ds_scr.at[turn, :count, :], e, dp_scr.at[turn, :count, :])
        ds = ds_scr[turn, :count, :]
        add_rows(dk, 0, base, dot(ds, stacked(q_rows, base, group)))
        dq = dot(kt_early[:, base:], ds_early[early_rows(tile), :]) + dot(kt[:, :count], ds)
        dq = dq * logit_scale
        unstacked(dqs, base, group, dq.T.astype(BF16))

    pipeline(tok // TILE, products, gradients)
    dkv[:, :HEAD_DIM] = dk[...] * logit_scale
    dkv[:, HEAD_DIM:] = dv[...]
    take_rows(size, core, masks, lambda there: dqs[there, :], dq_pieces)


def attend_call(kernel, out_shape, scratch_shapes, flops, name, *args):
    return pl.pallas_call(
        kernel,
        out_shape=out_shape,
        in_specs=[VMEM] * len(args),
        out_specs=[VMEM] * len(out_shape),
        scratch_shapes=scratch_shapes,
        compiler_params=pltpu.CompilerParams(vmem_limit_bytes=24 * 1024 * 1024),
        cost_estimate=pl.CostEstimate(
            flops=flops, bytes_accessed=8 * 1024 * 1024, transcendentals=0
        ),
        name=name,
    )(*args)


def forward_own(documents, q_pieces, kv, size):
    rows, cols = q_pieces[0].shape
    tok = len(q_pieces) * rows
    group = cols // HEAD_DIM
    wide, tiles = group * TILE, tok // TILE
    return attend_call(
        functools.partial(own_body, size, core_mask(), chip_masks(size), tok, group),
        [
            jax.ShapeDtypeStruct((own_rows(tiles - 1).stop, wide), BF16),
            jax.ShapeDtypeStruct((HEAD_DIM, tiles * wide), F32),
            jax.ShapeDtypeStruct((2 * tiles, wide), F32),
            jax.ShapeDtypeStruct((tok, cols), BF16),
        ],
        [
            pltpu.VMEM((tok, 2 * HEAD_DIM), BF16),
            pltpu.VMEM((HEAD_DIM, tok), BF16),
            pltpu.VMEM((2, tok, wide), F32),
        ],
        16 * tok * group * (WINDOW + TILE) * HEAD_DIM,
        "forward_own",
        *documents,
        *q_pieces,
        kv,
    )


def forward(documents, q_rows, g_pieces, lags, carried, size):
    (tok, cols), count, reach = q_rows.shape, len(chip_masks(size)), len(lags)
    rows = tok // count
    group = cols // HEAD_DIM
    wide, tiles = group * TILE, tok // TILE
    half = jax.ShapeDtypeStruct((tok, 2 * HEAD_DIM), BF16)
    out_shape = [jax.ShapeDtypeStruct((rows, cols), BF16)] * count + [half] * reach
    out_shape += [
        jax.ShapeDtypeStruct((tok, cols), BF16),
        jax.ShapeDtypeStruct((tiles, wide), F32),
        jax.ShapeDtypeStruct((early_rows(tiles - 1).stop, wide), BF16),
        jax.ShapeDtypeStruct((HEAD_DIM, WINDOW), BF16),
        jax.ShapeDtypeStruct((tok, cols), BF16),
    ]
    scratch = [
        pltpu.VMEM((WINDOW, 2 * HEAD_DIM), BF16),
        pltpu.VMEM((WINDOW, 2 * HEAD_DIM), BF16),
        pltpu.VMEM((HEAD_DIM, WINDOW), BF16),
        pltpu.VMEM((WINDOW, HEAD_DIM), F32),
        pltpu.VMEM((WINDOW, HEAD_DIM), F32),
        pltpu.VMEM((2, WINDOW, wide), F32),
        pltpu.VMEM((3, WINDOW, wide), BF16),
        pltpu.VMEM((2, WINDOW, wide), F32),
        pltpu.VMEM((2, wide, HEAD_DIM), BF16),
    ]
    results = attend_call(
        functools.partial(
            forward_body, size, core_mask(), chip_masks(size), reach, tok, group
        ),
        out_shape,
        scratch,
        6 * tok * group * (WINDOW + TILE) * HEAD_DIM,
        "forward",
        *documents,
        q_rows,
        *g_pieces,
        *lags,
        *carried,
    )
    return results[:count], results[count : count + reach], results[count + reach :]


def backward(q_rows, kv, carried, size):
    (tok, cols), count = q_rows.shape, len(chip_masks(size))
    rows = tok // count
    group = cols // HEAD_DIM
    wide = group * TILE
    results = attend_call(
        functools.partial(backward_body, size, core_mask(), chip_masks(size), tok, group),
        [jax.ShapeDtypeStruct((rows, cols), BF16)] * count
        + [jax.ShapeDtypeStruct((tok, 2 * HEAD_DIM), F32)],
        [
            pltpu.VMEM((tok, cols), BF16),
            pltpu.VMEM((tok, 2 * HEAD_DIM), BF16),
            pltpu.VMEM((HEAD_DIM, tok), BF16),
            pltpu.VMEM((tok, HEAD_DIM), F32),
            pltpu.VMEM((tok, HEAD_DIM), F32),
            pltpu.VMEM((2, tok, wide), F32),
            pltpu.VMEM((2, tok, wide), BF16),
            pltpu.VMEM((2, wide, HEAD_DIM), BF16),
        ],
        4 * tok * group * (WINDOW + TILE) * HEAD_DIM,
        "backward",
        q_rows,
        kv,
        *carried,
    )
    return results[:count], results[count]


def document_columns(segment_ids, tok, size):
    start = (flat_index() // size) * tok
    padded = jnp.concatenate([jnp.full((WINDOW,), -1, jnp.int32), segment_ids])
    keys = lax.dynamic_slice_in_dim(padded, start, WINDOW + tok, 0)
    queries = lax.dynamic_slice_in_dim(segment_ids, start, tok, 0)
    number = jnp.arange(HEAD_DIM, dtype=jnp.int32)[None, :]
    return (
        jnp.where(keys[:, None] == number, 0.0, FAR).astype(BF16),
        jnp.where(queries[:, None] == number, 1.0, 0.0).astype(BF16),
    )


def body(query, key, value, grad_out, segment_ids):
    size = key.shape[1] // HEAD_DIM
    rows = query.shape[0]
    tok = size * rows
    reach = WINDOW // tok
    assert reach * tok == WINDOW and device_count() % size == 0

    got = [swap(array, core_mask()) for array in (key, value, query, grad_out)]
    key, value = after(key, value)
    pieces = list(gather_cores((key, value), got[:2], size))
    pieces[0], query, grad_out, segment_ids = after(pieces[0], query, grad_out, segment_ids)
    documents = document_columns(segment_ids, tok, size)
    kv = join(swap_chips(pieces, size), size)
    lags = [shifted(kv, lag * size) for lag in range(1, reach + 1)]
    q_pieces = swap_chips(gather_cores((query,), got[2:3], size), size)
    g_pieces = swap_chips(gather_cores((grad_out,), got[3:], size), size)

    e_own, *partial, q_rows = forward_own(documents, q_pieces, kv, size)
    out, sent, carried = forward(documents, q_rows, g_pieces, lags, partial, size)
    backs = [shifted(sent[lag - 1], -lag * size) for lag in range(1, reach + 1)]
    out = swap_chips(out, size)
    grad_q, dkv = backward(q_rows, kv, [e_own, *carried], size)
    both = after(*out, *grad_q)
    out, grad_q = both[: len(out)], both[len(out) :]
    grad_q = swap_chips(grad_q, size)
    grads = swap_chips(combine([dkv, *backs], size), size)
    return tuple(spread_cores([out, grad_q, grads], (1, 1, 2), size))


def solution(mesh):
    placed = P(("pipe", "tensor"), None)
    return jax.shard_map(
        body,
        mesh=mesh,
        in_specs=(placed, placed, placed, placed, P()),
        out_specs=(placed, placed, placed, placed),
        check_vma=False,
    )
```

```python
import functools

import jax
import jax.numpy as jnp
from jax import lax
from jax.experimental import pallas as pl
from jax.experimental.pallas import tpu as pltpu
from jax.sharding import PartitionSpec as P

HEAD_DIM = 128
WINDOW = 1024
TILE = 128

logit_scale = 168.0 ** (-0.5)
exp2_scale = logit_scale * 1.4426950408889634

FAR = -(2.0**30)
SMALL = pltpu.CompilerParams(vmem_limit_bytes=4 * 1024 * 1024)
ANY = pl.BlockSpec(memory_space=pl.ANY)
VMEM = pl.BlockSpec(memory_space=pltpu.VMEM)
F32 = jnp.float32
BF16 = jnp.bfloat16
BOTH = ("pipe", "tensor")


def flat_index():
    return lax.axis_index("pipe") * lax.axis_size("tensor") + lax.axis_index("tensor")


def device_count():
    return lax.axis_size("pipe") * lax.axis_size("tensor")


def swap(value, mask):
    return lax.ppermute(value, BOTH, [(i, i ^ mask) for i in range(device_count())])


def core_mask():
    return lax.axis_size("tensor")


def chip_masks(size):
    return [mask for mask in range(size) if not mask & core_mask()]


def swap_chips(pieces, size):
    return [pieces[0]] + [
        swap(piece, mask) for piece, mask in zip(pieces[1:], chip_masks(size)[1:])
    ]


def shifted(value, step):
    count = device_count()
    pairs = [(i, i + step) for i in range(count) if 0 <= i + step < count]
    return lax.ppermute(value, BOTH, pairs)


def partner(size, j):
    return lax.bitwise_xor(lax.rem(flat_index(), size), j)


def place(index, width):
    return pl.ds(pl.multiple_of(index * width, width), width)


def after(value, *others):
    return lax.optimization_barrier((value, *others))


def run_copies(copies, sems):
    started = []
    for at, (source, target) in enumerate(copies):
        copy = pltpu.make_async_copy(source, target, sems.at[at])
        copy.start()
        started.append(copy)
    for copy in started:
        copy.wait()


def small_call(kernel, out_shape, name, *args):
    return pl.pallas_call(
        kernel,
        out_shape=out_shape,
        in_specs=[VMEM] * len(args),
        out_specs=jax.tree.map(lambda _: VMEM, out_shape),
        compiler_params=SMALL,
        name=name,
    )(*args)


def this_core(array, size):
    core = core_mask()
    width = array.shape[1] // size
    shares = [array[:, r * width : (r + 1) * width] for r in range(size)]
    first, second = (
        jnp.concatenate([share for r, share in enumerate(shares) if (r // core) % 2 == at], axis=1)
        for at in range(2)
    )
    return jnp.where((flat_index() // core) % 2 == 0, first, second)


def stack_body(size, core, masks, count, *refs):
    own, got, pieces = refs[:count], refs[count : 2 * count], refs[2 * count :]
    rows = own[0].shape[0]
    for mask, piece in zip(masks, pieces):
        there = partner(size, mask)
        chip = there // (2 * core) * core + lax.rem(there, core)
        start = 0
        for mine, other in zip(own, got):
            width = other.shape[1] // size
            piece[:rows, start : start + width] = mine[:, place(chip, width)]
            piece[rows:, start : start + width] = other[:, place(there, width)]
            start += width


def gather_cores(arrays, got, size):
    masks = chip_masks(size)
    own = [this_core(array, size) for array in arrays]
    cols = sum(array.shape[1] // size for array in arrays)
    piece = jax.ShapeDtypeStruct((2 * arrays[0].shape[0], cols), BF16)
    kernel = functools.partial(stack_body, size, core_mask(), masks, len(arrays))
    return small_call(kernel, [piece] * len(masks), "stack", *own, *got)


def place_rows(size, core, masks, pieces, out):
    for mask, piece in zip(masks, pieces):
        rows = piece.shape[0] // 2
        out[place(partner(size, mask), rows), :] = piece[:rows, :]
        out[place(partner(size, mask ^ core), rows), :] = piece[rows:, :]


def take_rows(size, core, masks, source, pieces):
    for mask, piece in zip(masks, pieces):
        rows = piece.shape[0] // 2
        piece[:rows, :] = source(place(partner(size, mask), rows))
        piece[rows:, :] = source(place(partner(size, mask ^ core), rows))


def join(pieces, size):
    rows, cols = pieces[0].shape
    core, masks = core_mask(), chip_masks(size)

    def kernel(*refs):
        place_rows(size, core, masks, refs[:-1], refs[-1])

    out = jax.ShapeDtypeStruct((len(pieces) * rows, cols), BF16)
    return small_call(kernel, out, "join", *pieces)


def combine(terms, size):
    tok, cols = terms[0].shape
    core, masks = core_mask(), chip_masks(size)

    def kernel(*refs):
        added = refs[: len(terms)]

        def source(there):
            total = added[0][there, :]
            for term in added[1:]:
                total = total + term[there, :].astype(F32)
            return total.astype(BF16)

        take_rows(size, core, masks, source, refs[len(terms) :])

    piece = jax.ShapeDtypeStruct((2 * (tok // size), cols), BF16)
    return small_call(kernel, [piece] * len(masks), "combine", *terms)


def bottom_body(*refs):
    out, start = refs[-1], 0
    for piece in refs[:-1]:
        rows, width = piece.shape[0] // 2, piece.shape[1]
        out[:, start : start + width] = piece[rows:, :]
        start += width


def spread_body(size, core, masks, counts, *refs):
    refs = list(refs)
    take = lambda count: [refs.pop(0) for _ in range(count)]
    sets = [take(len(masks)) for _ in counts]
    (got,), sets_out, (sems,) = take(1), [take(count) for count in counts], take(1)
    copies, start = [], 0
    for pieces, outs in zip(sets, sets_out):
        for mask, piece in zip(masks, pieces):
            rows, width = piece.shape[0] // 2, piece.shape[1] // len(outs)
            for at, out in enumerate(outs):
                mine = out.at[:, place(partner(size, mask), width)]
                other = out.at[:, place(partner(size, mask ^ core), width)]
                copies.append((piece.at[:rows, at * width : (at + 1) * width], mine))
                copies.append((got.at[:, start : start + width], other))
                start += width
    run_copies(copies, sems)


def spread_cores(sets, counts, size):
    pieces = [piece for part in sets for piece in part]
    rows = pieces[0].shape[0] // 2
    give = jax.ShapeDtypeStruct((rows, sum(piece.shape[1] for piece in pieces)), BF16)
    got = swap(small_call(bottom_body, give, "bottom", *pieces), core_mask())
    widths = [part[0].shape[1] // count for part, count in zip(sets, counts) for _ in range(count)]
    return pl.pallas_call(
        functools.partial(spread_body, size, core_mask(), chip_masks(size), counts),
        out_shape=[jax.ShapeDtypeStruct((rows, width * size), BF16) for width in widths],
        in_specs=[ANY] * (len(pieces) + 1),
        out_specs=[ANY] * len(widths),
        scratch_shapes=[pltpu.SemaphoreType.DMA((len(widths) * size,))],
        compiler_params=SMALL,
        name="spread",
    )(*pieces, got)


def dot(a, b):
    return lax.dot_general(a, b, (((1,), (0,)), ((), ())), preferred_element_type=F32)


def dot_t(a, b):
    return lax.dot_general(a, b, (((1,), (1,)), ((), ())), preferred_element_type=F32)


def fold(x, op):
    parts = [x[at : at + 8] for at in range(0, x.shape[0], 8)]
    while len(parts) > 1:
        parts = [
            op(*parts[at : at + 2]) if at + 1 < len(parts) else parts[at]
            for at in range(0, len(parts), 2)
        ]
    return parts[0]


def taker(refs):
    refs = list(refs)
    return lambda count: [refs.pop(0) for _ in range(count)]


def stacked(rows, base, group, first=0):
    parts = [slice(first + at * HEAD_DIM, first + (at + 1) * HEAD_DIM) for at in range(group)]
    return jnp.concatenate([rows[base : base + TILE, part] for part in parts], axis=0)


def unstacked(rows, base, group, value):
    for at in range(group):
        part = slice(at * TILE, (at + 1) * TILE)
        rows[base : base + TILE, at * HEAD_DIM : (at + 1) * HEAD_DIM] = value[part]


def set_values(va, values):
    lane = lax.broadcasted_iota(jnp.int32, values.shape, 1)
    va[:, :HEAD_DIM] = values
    va[:, HEAD_DIM:] = jnp.where(lane < 2, 1.0, 0.0).astype(BF16)


def add_rows(target, start, value, known):
    ends = range(0, value.shape[0] + TILE, TILE)
    first = 0
    for at in ends[1:]:
        last = at == value.shape[0]
        old = (start + at - TILE) in known
        if last or ((start + at) in known) != old:
            part = slice(start + first, start + at)
            if old:
                target[part, :] += value[first:at]
            else:
                target[part, :] = value[first:at]
            first = at
    known.update(range(start, start + value.shape[0], TILE))


def score_gradients(ds_scr, e, dp):
    for at in range(0, e.shape[0], TILE):
        part = slice(at, at + TILE)
        ds_scr[part, :] = (e[part, :].astype(F32) * dp[part, :]).astype(BF16)


def pipeline(order, *stages):
    for step in range(len(order) + len(stages) - 1):
        for behind, stage in enumerate(stages):
            at = step - behind
            if 0 <= at < len(order):
                stage(order[at], at)


def early_rows(tile):
    count = WINDOW // TILE
    start = (tile * count - tile * (tile - 1) // 2) * TILE
    return slice(start, start + (count - tile) * TILE)


def gradient_rows(qg, base, group, scale, out):
    first = qg.shape[1] // 2
    columns = jnp.broadcast_to(scale, (HEAD_DIM, scale.shape[1])).T
    g2 = (stacked(qg, base, group, first).astype(F32) * columns).astype(BF16)
    delta = jnp.sum(g2.astype(F32) * out.astype(F32), axis=1, keepdims=True)
    high = delta.astype(BF16).astype(F32)
    lane = lax.broadcasted_iota(jnp.int32, g2.shape, 1)
    extra = jnp.where(lane == 0, -high, jnp.where(lane == 1, high - delta, 0.0))
    return g2, jnp.concatenate([g2, extra.astype(BF16)], axis=1)


def own_rows(tile):
    start = tile * (tile + 1) // 2 * TILE
    return slice(start, start + (tile + 1) * TILE)


def query_columns(qg, seg_q, base, group):
    mine = jnp.concatenate([seg_q[base : base + TILE, :]] * group, axis=0)
    return jnp.concatenate([stacked(qg, base, group), mine], axis=1)


def fold_rows(rows, op):
    parts = [fold(rows[at : at + TILE, :], op) for at in range(0, rows.shape[0], TILE)]
    whole = functools.reduce(op, parts)
    reduce = jnp.max if op is jnp.maximum else jnp.sum
    return reduce(whole, axis=0, keepdims=True)


def weigh(scores, top, keep):
    total = None
    for at in range(0, scores.shape[0], TILE):
        part = slice(at, at + TILE)
        e = jnp.exp2(scores[part, :] * exp2_scale - top)
        keep[part, :] = e.astype(BF16)
        e = fold(e, jnp.add)
        total = e if total is None else total + e
    return jnp.sum(total, axis=0, keepdims=True)


def tile_causal(group):
    row_of = lax.broadcasted_iota(jnp.int32, (TILE, TILE), 0)
    col_of = lax.broadcasted_iota(jnp.int32, (TILE, TILE), 1)
    return jnp.concatenate([row_of <= col_of] * group, axis=1)


def own_body(size, core, masks, tok, group, *refs):
    take = taker(refs)
    (seg_k, seg_q), qg_pieces, (kv,) = take(2), take(len(masks)), take(1)
    e_own, out_part, stats, qg = take(4)
    ka, vt, s_scr = take(3)
    wide, tiles = group * TILE, tok // TILE
    place_rows(size, core, masks, qg_pieces, qg)
    ka[:, :HEAD_DIM] = kv[:, :HEAD_DIM]
    ka[:, HEAD_DIM:] = seg_k[WINDOW:, :]
    vt[...] = kv[:, HEAD_DIM:].T
    causal = tile_causal(group)

    def scores(tile, at):
        queries = query_columns(qg, seg_q, tile * TILE, group)
        s_scr[at % 2, : (tile + 1) * TILE, :] = dot_t(ka[: (tile + 1) * TILE, :], queries)

    def weights(tile, at):
        base, turn = tile * TILE, at % 2
        last = slice(base, base + TILE)
        s_scr[turn, last, :] = jnp.where(causal, s_scr[turn, last, :], FAR)
        rows = s_scr.at[turn, : base + TILE, :]
        top = fold_rows(rows, jnp.maximum) * exp2_scale
        stats[tile : tile + 1, :] = top
        stats[tiles + tile : tiles + tile + 1, :] = weigh(rows, top, e_own.at[own_rows(tile), :])

    def outputs(tile, at):
        e = e_own[own_rows(tile), :]
        out_part[:, tile * wide : (tile + 1) * wide] = dot(vt[:, : (tile + 1) * TILE], e)

    pipeline([*range(1, tiles), 0], scores, weights, outputs)


def forward_body(size, core, masks, reach, tok, group, *refs):
    take = taker(refs)
    (seg_k, seg_q, qg), kvs, (out_own, stats) = take(3), take(reach), take(2)
    out_pieces, sent, (outs, own_scale, ds_early) = take(len(masks)), take(reach), take(3)
    ka, va, vt, dk, dv, s_scr, e_scr, dp_scr, g_scr = take(9)
    wide, tiles = group * TILE, tok // TILE
    ka[:, HEAD_DIM:] = seg_k[:WINDOW, :]
    for lag in range(1, reach + 1):
        there = slice((reach - lag) * tok, (reach - lag + 1) * tok)
        kv = kvs[lag - 1][...]
        ka[there, :HEAD_DIM] = kv[:, :HEAD_DIM]
        vt[:, there] = kv[:, HEAD_DIM:].T
        set_values(va.at[there, :], kv[:, HEAD_DIM:])
    beyond = ~tile_causal(group)

    def scores(tile, at):
        base = tile * TILE
        queries = query_columns(qg, seg_q, base, group)
        s_scr[at % 2, : WINDOW - base, :] = dot_t(ka[base:, :], queries)

    scales, known = {}, (set(), set())

    def weights(tile, at):
        early = WINDOW - tile * TILE
        turn = at % 2
        s_scr[turn, :TILE, :] = jnp.where(beyond, s_scr[turn, :TILE, :], FAR)
        rows = s_scr.at[turn, :early, :]
        top_own = stats[tile : tile + 1, :]
        top = jnp.maximum(fold_rows(rows, jnp.maximum) * exp2_scale, top_own)
        total = weigh(rows, top, e_scr.at[at % 3, :early, :])
        scale = jnp.exp2(top_own - top)
        inv = 1.0 / (total + stats[tiles + tile : tiles + tile + 1, :] * scale)
        own_scale[tile : tile + 1, :] = inv * scale
        scales[tile] = scale, inv

    def outputs(tile, at):
        base, turn = tile * TILE, at % 2
        early = WINDOW - base
        scale, inv = scales.pop(tile)
        out = dot(vt[:, base:], e_scr[at % 3, :early, :])
        out = out + out_own[:, tile * wide : (tile + 1) * wide] * scale
        out = (out * inv).T.astype(BF16)
        unstacked(outs, base, group, out)
        g_scr[turn], g_wide = gradient_rows(qg, base, group, inv, out)
        dp_scr[turn, :early, :] = dot_t(va[base:, :], g_wide)

    def gradients(tile, at):
        base, turn = tile * TILE, at % 2
        early = WINDOW - base
        e = e_scr[at % 3, :early, :]
        add_rows(dv, base, dot(e, g_scr[turn]), known[0])
        ds = ds_early.at[early_rows(tile), :]
        score_gradients(ds, e, dp_scr.at[turn, :early, :])
        add_rows(dk, base, dot(ds[...], stacked(qg, base, group)), known[1])

    order = [tiles - 1, *range(tiles - 1)]
    pipeline(order, scores, weights, outputs, gradients)

    for lag in range(1, reach + 1):
        there = slice((reach - lag) * tok, (reach - lag + 1) * tok)
        sent[lag - 1][:, :HEAD_DIM] = (dk[there, :] * logit_scale).astype(BF16)
        sent[lag - 1][:, HEAD_DIM:] = dv[there, :].astype(BF16)
    take_rows(size, core, masks, lambda there: outs[there, :], out_pieces)


def backward_body(size, core, masks, reach, tok, group, *refs):
    take = taker(refs)
    qg, kv, e_own, outs, own_scale, ds_early = take(6)
    lags = take(reach)
    dq_pieces, (dkv,) = take(len(masks)), take(1)
    dqs, va, kt, kt_early, dk, dv, dp_scr, ds_scr, g_scr = take(9)
    wide = group * TILE
    kt[...] = kv[:, :HEAD_DIM].T
    for lag in range(1, reach + 1):
        there = slice((reach - lag) * tok, (reach - lag + 1) * tok)
        kt_early[:, there] = lags[lag - 1][:, :HEAD_DIM].T
    set_values(va, kv[:, HEAD_DIM:])

    known = (set(), set())

    def products(tile, at):
        base, turn = tile * TILE, at % 2
        scale = own_scale[tile : tile + 1, :]
        out = stacked(outs, base, group)
        g_scr[turn], g_wide = gradient_rows(qg, base, group, scale, out)
        dp_scr[turn, : base + TILE, :] = dot_t(va[: base + TILE, :], g_wide)

    def gradients(tile, at):
        base, turn = tile * TILE, at % 2
        count = base + TILE
        e = e_own[own_rows(tile), :]
        add_rows(dv, 0, dot(e, g_scr[turn]), known[0])
        score_gradients(ds_scr.at[turn, :count, :], e, dp_scr.at[turn, :count, :])
        ds = ds_scr[turn, :count, :]
        add_rows(dk, 0, dot(ds, stacked(qg, base, group)), known[1])
        dq = dot(kt_early[:, base:], ds_early[early_rows(tile), :]) + dot(kt[:, :count], ds)
        dq = dq * logit_scale
        unstacked(dqs, base, group, dq.T.astype(BF16))

    pipeline([*range(1, tok // TILE), 0], products, gradients)
    dkv[:, :HEAD_DIM] = dk[...] * logit_scale
    dkv[:, HEAD_DIM:] = dv[...]
    take_rows(size, core, masks, lambda there: dqs[there, :], dq_pieces)


def attend_call(kernel, out_shape, scratch_shapes, flops, name, *args):
    return pl.pallas_call(
        kernel,
        out_shape=out_shape,
        in_specs=[VMEM] * len(args),
        out_specs=[VMEM] * len(out_shape),
        scratch_shapes=scratch_shapes,
        compiler_params=pltpu.CompilerParams(vmem_limit_bytes=24 * 1024 * 1024),
        cost_estimate=pl.CostEstimate(
            flops=flops, bytes_accessed=8 * 1024 * 1024, transcendentals=0
        ),
        name=name,
    )(*args)


def forward_own(documents, qg, kv, size):
    rows, cols = qg[0].shape
    tok = len(qg) * rows
    group = cols // (2 * HEAD_DIM)
    wide, tiles = group * TILE, tok // TILE
    return attend_call(
        functools.partial(own_body, size, core_mask(), chip_masks(size), tok, group),
        [
            jax.ShapeDtypeStruct((own_rows(tiles - 1).stop, wide), BF16),
            jax.ShapeDtypeStruct((HEAD_DIM, tiles * wide), F32),
            jax.ShapeDtypeStruct((2 * tiles, wide), F32),
            jax.ShapeDtypeStruct((tok, cols), BF16),
        ],
        [
            pltpu.VMEM((tok, 2 * HEAD_DIM), BF16),
            pltpu.VMEM((HEAD_DIM, tok), BF16),
            pltpu.VMEM((2, tok, wide), F32),
        ],
        16 * tok * group * (WINDOW + TILE) * HEAD_DIM,
        "forward_own",
        *documents,
        *qg,
        kv,
    )


def forward(documents, qg, lags, carried, size):
    (tok, cols), count, reach = qg.shape, len(chip_masks(size)), len(lags)
    rows = tok // count
    group = cols // (2 * HEAD_DIM)
    wide, tiles = group * TILE, tok // TILE
    half = jax.ShapeDtypeStruct((tok, 2 * HEAD_DIM), BF16)
    out_shape = [jax.ShapeDtypeStruct((rows, cols // 2), BF16)] * count + [half] * reach
    out_shape += [
        jax.ShapeDtypeStruct((tok, cols // 2), BF16),
        jax.ShapeDtypeStruct((tiles, wide), F32),
        jax.ShapeDtypeStruct((early_rows(tiles - 1).stop, wide), BF16),
    ]
    scratch = [
        pltpu.VMEM((WINDOW, 2 * HEAD_DIM), BF16),
        pltpu.VMEM((WINDOW, 2 * HEAD_DIM), BF16),
        pltpu.VMEM((HEAD_DIM, WINDOW), BF16),
        pltpu.VMEM((WINDOW, HEAD_DIM), F32),
        pltpu.VMEM((WINDOW, HEAD_DIM), F32),
        pltpu.VMEM((2, WINDOW, wide), F32),
        pltpu.VMEM((3, WINDOW, wide), BF16),
        pltpu.VMEM((2, WINDOW, wide), F32),
        pltpu.VMEM((2, wide, HEAD_DIM), BF16),
    ]
    results = attend_call(
        functools.partial(
            forward_body, size, core_mask(), chip_masks(size), reach, tok, group
        ),
        out_shape,
        scratch,
        6 * tok * group * (WINDOW + TILE) * HEAD_DIM,
        "forward",
        *documents,
        qg,
        *lags,
        *carried,
    )
    return results[:count], results[count : count + reach], results[count + reach :]


def backward(qg, kv, carried, lags, size):
    (tok, cols), count = qg.shape, len(chip_masks(size))
    rows = tok // count
    group = cols // (2 * HEAD_DIM)
    wide = group * TILE
    results = attend_call(
        functools.partial(
            backward_body, size, core_mask(), chip_masks(size), len(lags), tok, group
        ),
        [jax.ShapeDtypeStruct((rows, cols // 2), BF16)] * count
        + [jax.ShapeDtypeStruct((tok, 2 * HEAD_DIM), F32)],
        [
            pltpu.VMEM((tok, cols // 2), BF16),
            pltpu.VMEM((tok, 2 * HEAD_DIM), BF16),
            pltpu.VMEM((HEAD_DIM, tok), BF16),
            pltpu.VMEM((HEAD_DIM, WINDOW), BF16),
            pltpu.VMEM((tok, HEAD_DIM), F32),
            pltpu.VMEM((tok, HEAD_DIM), F32),
            pltpu.VMEM((2, tok, wide), F32),
            pltpu.VMEM((2, tok, wide), BF16),
            pltpu.VMEM((2, wide, HEAD_DIM), BF16),
        ],
        4 * tok * group * (WINDOW + TILE) * HEAD_DIM,
        "backward",
        qg,
        kv,
        *carried,
        *lags,
    )
    return results[:count], results[count]


def document_columns(segment_ids, tok, size):
    start = (flat_index() // size) * tok
    padded = jnp.concatenate([jnp.full((WINDOW,), -1, jnp.int32), segment_ids])
    keys = lax.dynamic_slice_in_dim(padded, start, WINDOW + tok, 0)
    queries = lax.dynamic_slice_in_dim(segment_ids, start, tok, 0)
    number = jnp.arange(HEAD_DIM, dtype=jnp.int32)[None, :]
    return (
        jnp.where(keys[:, None] == number, 0.0, FAR).astype(BF16),
        jnp.where(queries[:, None] == number, 1.0, 0.0).astype(BF16),
    )


def body(query, key, value, grad_out, segment_ids):
    size = key.shape[1] // HEAD_DIM
    rows = query.shape[0]
    tok = size * rows
    reach = WINDOW // tok
    assert reach * tok == WINDOW and device_count() % size == 0

    got = [swap(array, core_mask()) for array in (key, value, query, grad_out)]
    key, value = after(key, value)
    pieces = list(gather_cores((key, value), got[:2], size))
    pieces[0], query, grad_out, segment_ids = after(pieces[0], query, grad_out, segment_ids)
    documents = document_columns(segment_ids, tok, size)
    kv = join(swap_chips(pieces, size), size)
    lags = [shifted(kv, lag * size) for lag in range(1, reach + 1)]
    qg = swap_chips(gather_cores((query, grad_out), got[2:], size), size)

    e_own, *partial, qg = forward_own(documents, qg, kv, size)
    out, sent, carried = forward(documents, qg, lags, partial, size)
    backs = [shifted(sent[lag - 1], -lag * size) for lag in range(1, reach + 1)]
    out = swap_chips(out, size)
    grad_q, dkv = backward(qg, kv, [e_own, *carried], lags, size)
    both = after(*out, *grad_q)
    out, grad_q = both[: len(out)], both[len(out) :]
    grad_q = swap_chips(grad_q, size)
    grads = swap_chips(combine([dkv, *backs], size), size)
    return tuple(spread_cores([out, grad_q, grads], (1, 1, 2), size))


def solution(mesh):
    placed = P(("pipe", "tensor"), None)
    return jax.shard_map(
        body,
        mesh=mesh,
        in_specs=(placed, placed, placed, placed, P()),
        out_specs=(placed, placed, placed, placed),
        check_vma=False,
    )
```

```python
import functools

import jax
import jax.numpy as jnp
from jax import lax
from jax.experimental import pallas as pl
from jax.experimental.pallas import tpu as pltpu
from jax.sharding import PartitionSpec as P

HEAD_DIM = 128
WINDOW = 1024
TILE = 128

logit_scale = 168.0 ** (-0.5)
exp2_scale = logit_scale * 1.4426950408889634

FAR = -(2.0**30)
SMALL = pltpu.CompilerParams(vmem_limit_bytes=4 * 1024 * 1024)
ANY = pl.BlockSpec(memory_space=pl.ANY)
VMEM = pl.BlockSpec(memory_space=pltpu.VMEM)
F32 = jnp.float32
BF16 = jnp.bfloat16
BOTH = ("pipe", "tensor")


def flat_index():
    return lax.axis_index("pipe") * lax.axis_size("tensor") + lax.axis_index("tensor")


def device_count():
    return lax.axis_size("pipe") * lax.axis_size("tensor")


def swap(value, mask):
    return lax.ppermute(value, BOTH, [(i, i ^ mask) for i in range(device_count())])


def core_mask():
    return lax.axis_size("tensor")


def chip_masks(size):
    return [mask for mask in range(size) if not mask & core_mask()]


def swap_chips(pieces, size):
    return [pieces[0]] + [
        swap(piece, mask) for piece, mask in zip(pieces[1:], chip_masks(size)[1:])
    ]


def shifted(value, step):
    count = device_count()
    pairs = [(i, i + step) for i in range(count) if 0 <= i + step < count]
    return lax.ppermute(value, BOTH, pairs)


def partner(size, j):
    return lax.bitwise_xor(lax.rem(flat_index(), size), j)


def place(index, width):
    return pl.ds(pl.multiple_of(index * width, width), width)


def after(value, *others):
    return lax.optimization_barrier((value, *others))


def run_copies(copies, sems):
    started = []
    for at, (source, target) in enumerate(copies):
        copy = pltpu.make_async_copy(source, target, sems.at[at])
        copy.start()
        started.append(copy)
    for copy in started:
        copy.wait()


def small_call(kernel, out_shape, name, *args):
    return pl.pallas_call(
        kernel,
        out_shape=out_shape,
        in_specs=[VMEM] * len(args),
        out_specs=jax.tree.map(lambda _: VMEM, out_shape),
        compiler_params=SMALL,
        name=name,
    )(*args)


def this_core(array, size):
    core = core_mask()
    width = array.shape[1] // size
    shares = [array[:, r * width : (r + 1) * width] for r in range(size)]
    first, second = (
        jnp.concatenate([share for r, share in enumerate(shares) if (r // core) % 2 == at], axis=1)
        for at in range(2)
    )
    return jnp.where((flat_index() // core) % 2 == 0, first, second)


def stack_body(size, core, masks, count, *refs):
    own, got, pieces = refs[:count], refs[count : 2 * count], refs[2 * count :]
    rows = own[0].shape[0]
    for mask, piece in zip(masks, pieces):
        there = partner(size, mask)
        chip = there // (2 * core) * core + lax.rem(there, core)
        start = 0
        for mine, other in zip(own, got):
            width = other.shape[1] // size
            piece[:rows, start : start + width] = mine[:, place(chip, width)]
            piece[rows:, start : start + width] = other[:, place(there, width)]
            start += width


def gather_cores(arrays, got, size):
    masks = chip_masks(size)
    own = [this_core(array, size) for array in arrays]
    cols = sum(array.shape[1] // size for array in arrays)
    piece = jax.ShapeDtypeStruct((2 * arrays[0].shape[0], cols), BF16)
    kernel = functools.partial(stack_body, size, core_mask(), masks, len(arrays))
    return small_call(kernel, [piece] * len(masks), "stack", *own, *got)


def place_rows(size, core, masks, pieces, out):
    for mask, piece in zip(masks, pieces):
        rows = piece.shape[0] // 2
        out[place(partner(size, mask), rows), :] = piece[:rows, :]
        out[place(partner(size, mask ^ core), rows), :] = piece[rows:, :]


def take_rows(size, core, masks, source, pieces):
    for mask, piece in zip(masks, pieces):
        rows = piece.shape[0] // 2
        piece[:rows, :] = source(place(partner(size, mask), rows))
        piece[rows:, :] = source(place(partner(size, mask ^ core), rows))


def join(pieces, size):
    rows, cols = pieces[0].shape
    core, masks = core_mask(), chip_masks(size)

    def kernel(*refs):
        place_rows(size, core, masks, refs[:-1], refs[-1])

    out = jax.ShapeDtypeStruct((len(pieces) * rows, cols), BF16)
    return small_call(kernel, out, "join", *pieces)


def combine(terms, size):
    tok, cols = terms[0].shape
    core, masks = core_mask(), chip_masks(size)

    def kernel(*refs):
        added = refs[: len(terms)]

        def source(there):
            total = added[0][there, :]
            for term in added[1:]:
                total = total + term[there, :].astype(F32)
            return total.astype(BF16)

        take_rows(size, core, masks, source, refs[len(terms) :])

    piece = jax.ShapeDtypeStruct((2 * (tok // size), cols), BF16)
    return small_call(kernel, [piece] * len(masks), "combine", *terms)


def bottom_body(*refs):
    out, start = refs[-1], 0
    for piece in refs[:-1]:
        rows, width = piece.shape[0] // 2, piece.shape[1]
        out[:, start : start + width] = piece[rows:, :]
        start += width


def spread_body(size, core, masks, counts, *refs):
    refs = list(refs)
    take = lambda count: [refs.pop(0) for _ in range(count)]
    sets = [take(len(masks)) for _ in counts]
    (got,), sets_out, (sems,) = take(1), [take(count) for count in counts], take(1)
    copies, start = [], 0
    for pieces, outs in zip(sets, sets_out):
        for mask, piece in zip(masks, pieces):
            rows, width = piece.shape[0] // 2, piece.shape[1] // len(outs)
            for at, out in enumerate(outs):
                mine = out.at[:, place(partner(size, mask), width)]
                other = out.at[:, place(partner(size, mask ^ core), width)]
                copies.append((piece.at[:rows, at * width : (at + 1) * width], mine))
                copies.append((got.at[:, start : start + width], other))
                start += width
    run_copies(copies, sems)


def spread_cores(sets, counts, size):
    pieces = [piece for part in sets for piece in part]
    rows = pieces[0].shape[0] // 2
    give = jax.ShapeDtypeStruct((rows, sum(piece.shape[1] for piece in pieces)), BF16)
    got = swap(small_call(bottom_body, give, "bottom", *pieces), core_mask())
    widths = [part[0].shape[1] // count for part, count in zip(sets, counts) for _ in range(count)]
    return pl.pallas_call(
        functools.partial(spread_body, size, core_mask(), chip_masks(size), counts),
        out_shape=[jax.ShapeDtypeStruct((rows, width * size), BF16) for width in widths],
        in_specs=[ANY] * (len(pieces) + 1),
        out_specs=[ANY] * len(widths),
        scratch_shapes=[pltpu.SemaphoreType.DMA((len(widths) * size,))],
        compiler_params=SMALL,
        name="spread",
    )(*pieces, got)


def dot(a, b):
    return lax.dot_general(a, b, (((1,), (0,)), ((), ())), preferred_element_type=F32)


def dot_t(a, b):
    return lax.dot_general(a, b, (((1,), (1,)), ((), ())), preferred_element_type=F32)


def fold(x, op):
    parts = [x[at : at + 8] for at in range(0, x.shape[0], 8)]
    while len(parts) > 1:
        parts = [
            op(*parts[at : at + 2]) if at + 1 < len(parts) else parts[at]
            for at in range(0, len(parts), 2)
        ]
    return parts[0]


def taker(refs):
    refs = list(refs)
    return lambda count: [refs.pop(0) for _ in range(count)]


def stacked(rows, base, group, first=0):
    parts = [slice(first + at * HEAD_DIM, first + (at + 1) * HEAD_DIM) for at in range(group)]
    return jnp.concatenate([rows[base : base + TILE, part] for part in parts], axis=0)


def unstacked(rows, base, group, value):
    for at in range(group):
        part = slice(at * TILE, (at + 1) * TILE)
        rows[base : base + TILE, at * HEAD_DIM : (at + 1) * HEAD_DIM] = value[part]


def set_values(va, values):
    lane = lax.broadcasted_iota(jnp.int32, values.shape, 1)
    va[:, :HEAD_DIM] = values
    va[:, HEAD_DIM:] = jnp.where(lane < 2, 1.0, 0.0).astype(BF16)


def add_rows(target, start, value, known):
    ends = range(0, value.shape[0] + TILE, TILE)
    first = 0
    for at in ends[1:]:
        last = at == value.shape[0]
        old = (start + at - TILE) in known
        if last or ((start + at) in known) != old:
            part = slice(start + first, start + at)
            if old:
                target[part, :] += value[first:at]
            else:
                target[part, :] = value[first:at]
            first = at
    known.update(range(start, start + value.shape[0], TILE))


def score_gradients(ds_scr, e, dp):
    for at in range(0, e.shape[0], TILE):
        part = slice(at, at + TILE)
        ds_scr[part, :] = (e[part, :].astype(F32) * dp[part, :]).astype(BF16)


def pipeline(order, *stages):
    for step in range(len(order) + len(stages) - 1):
        for behind, stage in enumerate(stages):
            at = step - behind
            if 0 <= at < len(order):
                stage(order[at], at)


def early_rows(tile):
    count = WINDOW // TILE
    start = (tile * count - tile * (tile - 1) // 2) * TILE
    return slice(start, start + (count - tile) * TILE)


def gradient_rows(qg, base, group, scale, out):
    first = qg.shape[1] // 2
    columns = jnp.broadcast_to(scale, (HEAD_DIM, scale.shape[1])).T
    g2 = (stacked(qg, base, group, first).astype(F32) * columns).astype(BF16)
    delta = jnp.sum(g2.astype(F32) * out.astype(F32), axis=1, keepdims=True)
    high = delta.astype(BF16).astype(F32)
    lane = lax.broadcasted_iota(jnp.int32, g2.shape, 1)
    extra = jnp.where(lane == 0, -high, jnp.where(lane == 1, high - delta, 0.0))
    return g2, jnp.concatenate([g2, extra.astype(BF16)], axis=1)


def own_rows(tile):
    start = tile * (tile + 1) // 2 * TILE
    return slice(start, start + (tile + 1) * TILE)


def query_columns(qg, seg_q, base, group):
    mine = jnp.concatenate([seg_q[base : base + TILE, :]] * group, axis=0)
    return jnp.concatenate([stacked(qg, base, group), mine], axis=1)


def fold_rows(rows, op):
    parts = [fold(rows[at : at + TILE, :], op) for at in range(0, rows.shape[0], TILE)]
    whole = functools.reduce(op, parts)
    reduce = jnp.max if op is jnp.maximum else jnp.sum
    return reduce(whole, axis=0, keepdims=True)


def weigh(scores, top, keep):
    total = None
    for at in range(0, scores.shape[0], TILE):
        part = slice(at, at + TILE)
        e = jnp.exp2(scores[part, :] * exp2_scale - top)
        keep[part, :] = e.astype(BF16)
        e = fold(e, jnp.add)
        total = e if total is None else total + e
    return jnp.sum(total, axis=0, keepdims=True)


def tile_causal(group):
    row_of = lax.broadcasted_iota(jnp.int32, (TILE, TILE), 0)
    col_of = lax.broadcasted_iota(jnp.int32, (TILE, TILE), 1)
    return jnp.concatenate([row_of <= col_of] * group, axis=1)


def own_body(size, core, masks, tok, group, *refs):
    take = taker(refs)
    (seg_k, seg_q), qg_pieces, (kv,) = take(2), take(len(masks)), take(1)
    e_own, out_part, stats, qg = take(4)
    ka, vt, s_scr = take(3)
    wide, tiles = group * TILE, tok // TILE
    place_rows(size, core, masks, qg_pieces, qg)
    ka[:, :HEAD_DIM] = kv[:, :HEAD_DIM]
    ka[:, HEAD_DIM:] = seg_k[WINDOW:, :]
    vt[...] = kv[:, HEAD_DIM:].T
    causal = tile_causal(group)

    def scores(tile, at):
        queries = query_columns(qg, seg_q, tile * TILE, group)
        s_scr[at % 2, : (tile + 1) * TILE, :] = dot_t(ka[: (tile + 1) * TILE, :], queries)

    def weights(tile, at):
        base, turn = tile * TILE, at % 2
        last = slice(base, base + TILE)
        s_scr[turn, last, :] = jnp.where(causal, s_scr[turn, last, :], FAR)
        rows = s_scr.at[turn, : base + TILE, :]
        top = fold_rows(rows, jnp.maximum) * exp2_scale
        stats[tile : tile + 1, :] = top
        stats[tiles + tile : tiles + tile + 1, :] = weigh(rows, top, e_own.at[own_rows(tile), :])

    def outputs(tile, at):
        e = e_own[own_rows(tile), :]
        out_part[:, tile * wide : (tile + 1) * wide] = dot(vt[:, : (tile + 1) * TILE], e)

    pipeline([*range(1, tiles), 0], scores, weights, outputs)


def forward_body(size, core, masks, reach, tok, group, *refs):
    take = taker(refs)
    (seg_k, seg_q, qg), kvs, (out_own, stats) = take(3), take(reach), take(2)
    out_pieces, sent, (outs, own_scale, ds_early) = take(len(masks)), take(reach), take(3)
    ka, va, vt, dk, dv, s_scr, e_scr, dp_scr, g_scr = take(9)
    wide, tiles = group * TILE, tok // TILE
    ka[:, HEAD_DIM:] = seg_k[:WINDOW, :]
    for lag in range(1, reach + 1):
        there = slice((reach - lag) * tok, (reach - lag + 1) * tok)
        kv = kvs[lag - 1][...]
        ka[there, :HEAD_DIM] = kv[:, :HEAD_DIM]
        vt[:, there] = kv[:, HEAD_DIM:].T
        set_values(va.at[there, :], kv[:, HEAD_DIM:])
    beyond = ~tile_causal(group)

    def scores(tile, at):
        base = tile * TILE
        queries = query_columns(qg, seg_q, base, group)
        s_scr[at % 2, : WINDOW - base, :] = dot_t(ka[base:, :], queries)

    scales, known = {}, (set(), set())

    def weights(tile, at):
        early = WINDOW - tile * TILE
        turn = at % 2
        s_scr[turn, :TILE, :] = jnp.where(beyond, s_scr[turn, :TILE, :], FAR)
        rows = s_scr.at[turn, :early, :]
        top_own = stats[tile : tile + 1, :]
        top = jnp.maximum(fold_rows(rows, jnp.maximum) * exp2_scale, top_own)
        total = weigh(rows, top, e_scr.at[at % 3, :early, :])
        scale = jnp.exp2(top_own - top)
        inv = 1.0 / (total + stats[tiles + tile : tiles + tile + 1, :] * scale)
        own_scale[tile : tile + 1, :] = inv * scale
        scales[tile] = scale, inv

    def outputs(tile, at):
        base, turn = tile * TILE, at % 2
        early = WINDOW - base
        scale, inv = scales.pop(tile)
        out = dot(vt[:, base:], e_scr[at % 3, :early, :])
        out = out + out_own[:, tile * wide : (tile + 1) * wide] * scale
        out = (out * inv).T.astype(BF16)
        unstacked(outs, base, group, out)
        g_scr[turn], g_wide = gradient_rows(qg, base, group, inv, out)
        dp_scr[turn, :early, :] = dot_t(va[base:, :], g_wide)

    def gradients(tile, at):
        base, turn = tile * TILE, at % 2
        early = WINDOW - base
        e = e_scr[at % 3, :early, :]
        add_rows(dv, base, dot(e, g_scr[turn]), known[0])
        ds = ds_early.at[early_rows(tile), :]
        score_gradients(ds, e, dp_scr.at[turn, :early, :])
        add_rows(dk, base, dot(ds[...], stacked(qg, base, group)), known[1])

    pipeline(range(tiles), scores, weights, outputs, gradients)

    for lag in range(1, reach + 1):
        there = slice((reach - lag) * tok, (reach - lag + 1) * tok)
        sent[lag - 1][:, :HEAD_DIM] = (dk[there, :] * logit_scale).astype(BF16)
        sent[lag - 1][:, HEAD_DIM:] = dv[there, :].astype(BF16)
    take_rows(size, core, masks, lambda there: outs[there, :], out_pieces)


def backward_body(size, core, masks, reach, tok, group, *refs):
    take = taker(refs)
    qg, kv, e_own, outs, own_scale, ds_early = take(6)
    lags = take(reach)
    dq_pieces, (dkv,) = take(len(masks)), take(1)
    dqs, va, kt, kt_early, dk, dv, dp_scr, ds_scr, g_scr = take(9)
    wide = group * TILE
    kt[...] = kv[:, :HEAD_DIM].T
    for lag in range(1, reach + 1):
        there = slice((reach - lag) * tok, (reach - lag + 1) * tok)
        kt_early[:, there] = lags[lag - 1][:, :HEAD_DIM].T
    set_values(va, kv[:, HEAD_DIM:])

    known = (set(), set())

    def products(tile, at):
        base, turn = tile * TILE, at % 2
        scale = own_scale[tile : tile + 1, :]
        out = stacked(outs, base, group)
        g_scr[turn], g_wide = gradient_rows(qg, base, group, scale, out)
        dp_scr[turn, : base + TILE, :] = dot_t(va[: base + TILE, :], g_wide)

    def gradients(tile, at):
        base, turn = tile * TILE, at % 2
        count = base + TILE
        e = e_own[own_rows(tile), :]
        add_rows(dv, 0, dot(e, g_scr[turn]), known[0])
        score_gradients(ds_scr.at[turn, :count, :], e, dp_scr.at[turn, :count, :])
        ds = ds_scr[turn, :count, :]
        add_rows(dk, 0, dot(ds, stacked(qg, base, group)), known[1])
        dq = dot(kt_early[:, base:], ds_early[early_rows(tile), :]) + dot(kt[:, :count], ds)
        dq = dq * logit_scale
        unstacked(dqs, base, group, dq.T.astype(BF16))

    pipeline([*range(1, tok // TILE), 0], products, gradients)
    dkv[:, :HEAD_DIM] = dk[...] * logit_scale
    dkv[:, HEAD_DIM:] = dv[...]
    take_rows(size, core, masks, lambda there: dqs[there, :], dq_pieces)


def attend_call(kernel, out_shape, scratch_shapes, flops, name, *args):
    return pl.pallas_call(
        kernel,
        out_shape=out_shape,
        in_specs=[VMEM] * len(args),
        out_specs=[VMEM] * len(out_shape),
        scratch_shapes=scratch_shapes,
        compiler_params=pltpu.CompilerParams(vmem_limit_bytes=24 * 1024 * 1024),
        cost_estimate=pl.CostEstimate(
            flops=flops, bytes_accessed=8 * 1024 * 1024, transcendentals=0
        ),
        name=name,
    )(*args)


def forward_own(documents, qg, kv, size):
    rows, cols = qg[0].shape
    tok = len(qg) * rows
    group = cols // (2 * HEAD_DIM)
    wide, tiles = group * TILE, tok // TILE
    return attend_call(
        functools.partial(own_body, size, core_mask(), chip_masks(size), tok, group),
        [
            jax.ShapeDtypeStruct((own_rows(tiles - 1).stop, wide), BF16),
            jax.ShapeDtypeStruct((HEAD_DIM, tiles * wide), F32),
            jax.ShapeDtypeStruct((2 * tiles, wide), F32),
            jax.ShapeDtypeStruct((tok, cols), BF16),
        ],
        [
            pltpu.VMEM((tok, 2 * HEAD_DIM), BF16),
            pltpu.VMEM((HEAD_DIM, tok), BF16),
            pltpu.VMEM((2, tok, wide), F32),
        ],
        16 * tok * group * (WINDOW + TILE) * HEAD_DIM,
        "forward_own",
        *documents,
        *qg,
        kv,
    )


def forward(documents, qg, lags, carried, size):
    (tok, cols), count, reach = qg.shape, len(chip_masks(size)), len(lags)
    rows = tok // count
    group = cols // (2 * HEAD_DIM)
    wide, tiles = group * TILE, tok // TILE
    half = jax.ShapeDtypeStruct((tok, 2 * HEAD_DIM), BF16)
    out_shape = [jax.ShapeDtypeStruct((rows, cols // 2), BF16)] * count + [half] * reach
    out_shape += [
        jax.ShapeDtypeStruct((tok, cols // 2), BF16),
        jax.ShapeDtypeStruct((tiles, wide), F32),
        jax.ShapeDtypeStruct((early_rows(tiles - 1).stop, wide), BF16),
    ]
    scratch = [
        pltpu.VMEM((WINDOW, 2 * HEAD_DIM), BF16),
        pltpu.VMEM((WINDOW, 2 * HEAD_DIM), BF16),
        pltpu.VMEM((HEAD_DIM, WINDOW), BF16),
        pltpu.VMEM((WINDOW, HEAD_DIM), F32),
        pltpu.VMEM((WINDOW, HEAD_DIM), F32),
        pltpu.VMEM((2, WINDOW, wide), F32),
        pltpu.VMEM((3, WINDOW, wide), BF16),
        pltpu.VMEM((2, WINDOW, wide), F32),
        pltpu.VMEM((2, wide, HEAD_DIM), BF16),
    ]
    results = attend_call(
        functools.partial(
            forward_body, size, core_mask(), chip_masks(size), reach, tok, group
        ),
        out_shape,
        scratch,
        6 * tok * group * (WINDOW + TILE) * HEAD_DIM,
        "forward",
        *documents,
        qg,
        *lags,
        *carried,
    )
    return results[:count], results[count : count + reach], results[count + reach :]


def backward(qg, kv, carried, lags, size):
    (tok, cols), count = qg.shape, len(chip_masks(size))
    rows = tok // count
    group = cols // (2 * HEAD_DIM)
    wide = group * TILE
    results = attend_call(
        functools.partial(
            backward_body, size, core_mask(), chip_masks(size), len(lags), tok, group
        ),
        [jax.ShapeDtypeStruct((rows, cols // 2), BF16)] * count
        + [jax.ShapeDtypeStruct((tok, 2 * HEAD_DIM), F32)],
        [
            pltpu.VMEM((tok, cols // 2), BF16),
            pltpu.VMEM((tok, 2 * HEAD_DIM), BF16),
            pltpu.VMEM((HEAD_DIM, tok), BF16),
            pltpu.VMEM((HEAD_DIM, WINDOW), BF16),
            pltpu.VMEM((tok, HEAD_DIM), F32),
            pltpu.VMEM((tok, HEAD_DIM), F32),
            pltpu.VMEM((2, tok, wide), F32),
            pltpu.VMEM((2, tok, wide), BF16),
            pltpu.VMEM((2, wide, HEAD_DIM), BF16),
        ],
        4 * tok * group * (WINDOW + TILE) * HEAD_DIM,
        "backward",
        qg,
        kv,
        *carried,
        *lags,
    )
    return results[:count], results[count]


def document_columns(segment_ids, tok, size):
    start = (flat_index() // size) * tok
    padded = jnp.concatenate([jnp.full((WINDOW,), -1, jnp.int32), segment_ids])
    keys = lax.dynamic_slice_in_dim(padded, start, WINDOW + tok, 0)
    queries = lax.dynamic_slice_in_dim(segment_ids, start, tok, 0)
    number = jnp.arange(HEAD_DIM, dtype=jnp.int32)[None, :]
    return (
        jnp.where(keys[:, None] == number, 0.0, FAR).astype(BF16),
        jnp.where(queries[:, None] == number, 1.0, 0.0).astype(BF16),
    )


def body(query, key, value, grad_out, segment_ids):
    size = key.shape[1] // HEAD_DIM
    rows = query.shape[0]
    tok = size * rows
    reach = WINDOW // tok
    assert reach * tok == WINDOW and device_count() % size == 0

    got = [swap(array, core_mask()) for array in (key, value, query, grad_out)]
    key, value = after(key, value)
    pieces = list(gather_cores((key, value), got[:2], size))
    pieces[0], query, grad_out, segment_ids = after(pieces[0], query, grad_out, segment_ids)
    documents = document_columns(segment_ids, tok, size)
    kv = join(swap_chips(pieces, size), size)
    lags = [shifted(kv, lag * size) for lag in range(1, reach + 1)]
    qg = swap_chips(gather_cores((query, grad_out), got[2:], size), size)

    e_own, *partial, qg = forward_own(documents, qg, kv, size)
    out, sent, carried = forward(documents, qg, lags, partial, size)
    backs = [shifted(sent[lag - 1], -lag * size) for lag in range(1, reach + 1)]
    out = swap_chips(out, size)
    grad_q, dkv = backward(qg, kv, [e_own, *carried], lags, size)
    both = after(*out, *grad_q)
    out, grad_q = both[: len(out)], both[len(out) :]
    grad_q = swap_chips(grad_q, size)
    grads = swap_chips(combine([dkv, *backs], size), size)
    return tuple(spread_cores([out, grad_q, grads], (1, 1, 2), size))


def solution(mesh):
    placed = P(("pipe", "tensor"), None)
    return jax.shard_map(
        body,
        mesh=mesh,
        in_specs=(placed, placed, placed, placed, P()),
        out_specs=(placed, placed, placed, placed),
        check_vma=False,
    )
```

```python
import functools

import jax
import jax.numpy as jnp
from jax import lax
from jax.experimental import pallas as pl
from jax.experimental.pallas import tpu as pltpu
from jax.sharding import PartitionSpec as P

HEAD_DIM = 128
WINDOW = 1024
TILE = 128

logit_scale = 168.0 ** (-0.5)
exp2_scale = logit_scale * 1.4426950408889634

FAR = -(2.0**30)
SMALL = pltpu.CompilerParams(vmem_limit_bytes=4 * 1024 * 1024)
ANY = pl.BlockSpec(memory_space=pl.ANY)
VMEM = pl.BlockSpec(memory_space=pltpu.VMEM)
F32 = jnp.float32
BF16 = jnp.bfloat16
BOTH = ("pipe", "tensor")


def flat_index():
    return lax.axis_index("pipe") * lax.axis_size("tensor") + lax.axis_index("tensor")


def device_count():
    return lax.axis_size("pipe") * lax.axis_size("tensor")


def swap(value, mask):
    return lax.ppermute(value, BOTH, [(i, i ^ mask) for i in range(device_count())])


def core_mask():
    return lax.axis_size("tensor")


def chip_masks(size):
    return [mask for mask in range(size) if not mask & core_mask()]


def swap_chips(pieces, size):
    return [pieces[0]] + [
        swap(piece, mask) for piece, mask in zip(pieces[1:], chip_masks(size)[1:])
    ]


def shifted(value, step):
    count = device_count()
    pairs = [(i, i + step) for i in range(count) if 0 <= i + step < count]
    return lax.ppermute(value, BOTH, pairs)


def partner(size, j):
    return lax.bitwise_xor(lax.rem(flat_index(), size), j)


def place(index, width):
    return pl.ds(pl.multiple_of(index * width, width), width)


def after(value, *others):
    return lax.optimization_barrier((value, *others))


def run_copies(copies, sems):
    started = []
    for at, (source, target) in enumerate(copies):
        copy = pltpu.make_async_copy(source, target, sems.at[at])
        copy.start()
        started.append(copy)
    for copy in started:
        copy.wait()


def small_call(kernel, out_shape, name, *args):
    return pl.pallas_call(
        kernel,
        out_shape=out_shape,
        in_specs=[VMEM] * len(args),
        out_specs=jax.tree.map(lambda _: VMEM, out_shape),
        compiler_params=SMALL,
        name=name,
    )(*args)


def this_core(array, size):
    core = core_mask()
    width = array.shape[1] // size
    shares = [array[:, r * width : (r + 1) * width] for r in range(size)]
    first, second = (
        jnp.concatenate([share for r, share in enumerate(shares) if (r // core) % 2 == at], axis=1)
        for at in range(2)
    )
    return jnp.where((flat_index() // core) % 2 == 0, first, second)


def stack_body(size, core, masks, count, *refs):
    own, got, pieces = refs[:count], refs[count : 2 * count], refs[2 * count :]
    rows = own[0].shape[0]
    for mask, piece in zip(masks, pieces):
        there = partner(size, mask)
        chip = there // (2 * core) * core + lax.rem(there, core)
        start = 0
        for mine, other in zip(own, got):
            width = other.shape[1] // size
            piece[:rows, start : start + width] = mine[:, place(chip, width)]
            piece[rows:, start : start + width] = other[:, place(there, width)]
            start += width


def gather_cores(arrays, got, size):
    masks = chip_masks(size)
    own = [this_core(array, size) for array in arrays]
    cols = sum(array.shape[1] // size for array in arrays)
    piece = jax.ShapeDtypeStruct((2 * arrays[0].shape[0], cols), BF16)
    kernel = functools.partial(stack_body, size, core_mask(), masks, len(arrays))
    return small_call(kernel, [piece] * len(masks), "stack", *own, *got)


def place_rows(size, core, masks, pieces, out):
    for mask, piece in zip(masks, pieces):
        rows = piece.shape[0] // 2
        out[place(partner(size, mask), rows), :] = piece[:rows, :]
        out[place(partner(size, mask ^ core), rows), :] = piece[rows:, :]


def take_rows(size, core, masks, source, pieces):
    for mask, piece in zip(masks, pieces):
        rows = piece.shape[0] // 2
        piece[:rows, :] = source(place(partner(size, mask), rows))
        piece[rows:, :] = source(place(partner(size, mask ^ core), rows))


def join(pieces, size):
    rows, cols = pieces[0].shape
    core, masks = core_mask(), chip_masks(size)

    def kernel(*refs):
        place_rows(size, core, masks, refs[:-1], refs[-1])

    out = jax.ShapeDtypeStruct((len(pieces) * rows, cols), BF16)
    return small_call(kernel, out, "join", *pieces)


def combine(terms, size):
    tok, cols = terms[0].shape
    core, masks = core_mask(), chip_masks(size)

    def kernel(*refs):
        added = refs[: len(terms)]

        def source(there):
            total = added[0][there, :]
            for term in added[1:]:
                total = total + term[there, :].astype(F32)
            return total.astype(BF16)

        take_rows(size, core, masks, source, refs[len(terms) :])

    piece = jax.ShapeDtypeStruct((2 * (tok // size), cols), BF16)
    return small_call(kernel, [piece] * len(masks), "combine", *terms)


def bottom_body(*refs):
    out, start = refs[-1], 0
    for piece in refs[:-1]:
        rows, width = piece.shape[0] // 2, piece.shape[1]
        out[:, start : start + width] = piece[rows:, :]
        start += width


def spread_body(size, core, masks, counts, *refs):
    refs = list(refs)
    take = lambda count: [refs.pop(0) for _ in range(count)]
    sets = [take(len(masks)) for _ in counts]
    (got,), sets_out, (sems,) = take(1), [take(count) for count in counts], take(1)
    copies, start = [], 0
    for pieces, outs in zip(sets, sets_out):
        for mask, piece in zip(masks, pieces):
            rows, width = piece.shape[0] // 2, piece.shape[1] // len(outs)
            for at, out in enumerate(outs):
                mine = out.at[:, place(partner(size, mask), width)]
                other = out.at[:, place(partner(size, mask ^ core), width)]
                copies.append((piece.at[:rows, at * width : (at + 1) * width], mine))
                copies.append((got.at[:, start : start + width], other))
                start += width
    run_copies(copies, sems)


def spread_cores(sets, counts, size):
    pieces = [piece for part in sets for piece in part]
    rows = pieces[0].shape[0] // 2
    give = jax.ShapeDtypeStruct((rows, sum(piece.shape[1] for piece in pieces)), BF16)
    got = swap(small_call(bottom_body, give, "bottom", *pieces), core_mask())
    widths = [part[0].shape[1] // count for part, count in zip(sets, counts) for _ in range(count)]
    return pl.pallas_call(
        functools.partial(spread_body, size, core_mask(), chip_masks(size), counts),
        out_shape=[jax.ShapeDtypeStruct((rows, width * size), BF16) for width in widths],
        in_specs=[ANY] * (len(pieces) + 1),
        out_specs=[ANY] * len(widths),
        scratch_shapes=[pltpu.SemaphoreType.DMA((len(widths) * size,))],
        compiler_params=SMALL,
        name="spread",
    )(*pieces, got)


def dot(a, b):
    return lax.dot_general(a, b, (((1,), (0,)), ((), ())), preferred_element_type=F32)


def dot_t(a, b):
    return lax.dot_general(a, b, (((1,), (1,)), ((), ())), preferred_element_type=F32)


def fold(x, op):
    parts = [x[at : at + 8] for at in range(0, x.shape[0], 8)]
    while len(parts) > 1:
        parts = [
            op(*parts[at : at + 2]) if at + 1 < len(parts) else parts[at]
            for at in range(0, len(parts), 2)
        ]
    return parts[0]


def taker(refs):
    refs = list(refs)
    return lambda count: [refs.pop(0) for _ in range(count)]


def stacked(rows, base, group, first=0):
    parts = [slice(first + at * HEAD_DIM, first + (at + 1) * HEAD_DIM) for at in range(group)]
    return jnp.concatenate([rows[base : base + TILE, part] for part in parts], axis=0)


def unstacked(rows, base, group, value):
    for at in range(group):
        part = slice(at * TILE, (at + 1) * TILE)
        rows[base : base + TILE, at * HEAD_DIM : (at + 1) * HEAD_DIM] = value[part]


def set_values(va, values):
    lane = lax.broadcasted_iota(jnp.int32, values.shape, 1)
    va[:, :HEAD_DIM] = values
    va[:, HEAD_DIM:] = jnp.where(lane < 2, 1.0, 0.0).astype(BF16)


def add_rows(target, start, old, value):
    if old:
        target[start : start + old, :] += value[:old]
    if old < value.shape[0]:
        target[start + old : start + value.shape[0], :] = value[old:]


def score_gradients(ds_scr, e, dp):
    for at in range(0, e.shape[0], TILE):
        part = slice(at, at + TILE)
        ds_scr[part, :] = (e[part, :].astype(F32) * dp[part, :]).astype(BF16)


def pipeline(tiles, *stages):
    for step in range(tiles + len(stages) - 1):
        for behind, stage in enumerate(stages):
            if 0 <= step - behind < tiles:
                stage(step - behind)


def early_rows(tile):
    count = WINDOW // TILE
    start = (tile * count - tile * (tile - 1) // 2) * TILE
    return slice(start, start + (count - tile) * TILE)


def gradient_rows(qg, base, group, scale, out):
    first = qg.shape[1] // 2
    columns = jnp.broadcast_to(scale, (HEAD_DIM, scale.shape[1])).T
    g2 = (stacked(qg, base, group, first).astype(F32) * columns).astype(BF16)
    delta = jnp.sum(g2.astype(F32) * out.astype(F32), axis=1, keepdims=True)
    high = delta.astype(BF16).astype(F32)
    lane = lax.broadcasted_iota(jnp.int32, g2.shape, 1)
    extra = jnp.where(lane == 0, -high, jnp.where(lane == 1, high - delta, 0.0))
    return g2, jnp.concatenate([g2, extra.astype(BF16)], axis=1)


def own_rows(tile):
    start = tile * (tile + 1) // 2 * TILE
    return slice(start, start + (tile + 1) * TILE)


def query_columns(qg, seg_q, base, group):
    mine = jnp.concatenate([seg_q[base : base + TILE, :]] * group, axis=0)
    return jnp.concatenate([stacked(qg, base, group), mine], axis=1)


def fold_rows(rows, op):
    parts = [fold(rows[at : at + TILE, :], op) for at in range(0, rows.shape[0], TILE)]
    whole = functools.reduce(op, parts)
    reduce = jnp.max if op is jnp.maximum else jnp.sum
    return reduce(whole, axis=0, keepdims=True)


def weigh(scores, top, keep):
    total = None
    for at in range(0, scores.shape[0], TILE):
        part = slice(at, at + TILE)
        e = jnp.exp2(scores[part, :] * exp2_scale - top)
        keep[part, :] = e.astype(BF16)
        e = fold(e, jnp.add)
        total = e if total is None else total + e
    return jnp.sum(total, axis=0, keepdims=True)


def tile_causal(group):
    row_of = lax.broadcasted_iota(jnp.int32, (TILE, TILE), 0)
    col_of = lax.broadcasted_iota(jnp.int32, (TILE, TILE), 1)
    return jnp.concatenate([row_of <= col_of] * group, axis=1)


def own_body(size, core, masks, tok, group, *refs):
    take = taker(refs)
    (seg_k, seg_q), qg_pieces, (kv,) = take(2), take(len(masks)), take(1)
    e_own, out_part, stats, qg = take(4)
    ka, vt, s_scr = take(3)
    wide, tiles = group * TILE, tok // TILE
    place_rows(size, core, masks, qg_pieces, qg)
    ka[:, :HEAD_DIM] = kv[:, :HEAD_DIM]
    ka[:, HEAD_DIM:] = seg_k[WINDOW:, :]
    vt[...] = kv[:, HEAD_DIM:].T
    causal = tile_causal(group)

    def scores(tile):
        queries = query_columns(qg, seg_q, tile * TILE, group)
        s_scr[tile % 2, : (tile + 1) * TILE, :] = dot_t(ka[: (tile + 1) * TILE, :], queries)

    def weights(tile):
        base, turn = tile * TILE, tile % 2
        last = slice(base, base + TILE)
        s_scr[turn, last, :] = jnp.where(causal, s_scr[turn, last, :], FAR)
        rows = s_scr.at[turn, : base + TILE, :]
        top = fold_rows(rows, jnp.maximum) * exp2_scale
        stats[tile : tile + 1, :] = top
        stats[tiles + tile : tiles + tile + 1, :] = weigh(rows, top, e_own.at[own_rows(tile), :])

    def outputs(tile):
        e = e_own[own_rows(tile), :]
        out_part[:, tile * wide : (tile + 1) * wide] = dot(vt[:, : (tile + 1) * TILE], e)

    pipeline(tiles, scores, weights, outputs)


def forward_body(size, core, masks, reach, tok, group, *refs):
    take = taker(refs)
    (seg_k, seg_q, qg), kvs, (out_own, stats) = take(3), take(reach), take(2)
    out_pieces, sent, (outs, own_scale, ds_early, kt) = take(len(masks)), take(reach), take(4)
    ka, va, vt, dk, dv, s_scr, e_scr, dp_scr, g_scr = take(9)
    wide, tiles = group * TILE, tok // TILE
    ka[:, HEAD_DIM:] = seg_k[:WINDOW, :]
    for lag in range(1, reach + 1):
        there = slice((reach - lag) * tok, (reach - lag + 1) * tok)
        kv = kvs[lag - 1][...]
        ka[there, :HEAD_DIM] = kv[:, :HEAD_DIM]
        kt[:, there] = kv[:, :HEAD_DIM].T
        vt[:, there] = kv[:, HEAD_DIM:].T
        set_values(va.at[there, :], kv[:, HEAD_DIM:])
    beyond = ~tile_causal(group)

    def scores(tile):
        base = tile * TILE
        queries = query_columns(qg, seg_q, base, group)
        s_scr[tile % 2, : WINDOW - base, :] = dot_t(ka[base:, :], queries)

    scales = {}

    def weights(tile):
        early = WINDOW - tile * TILE
        turn = tile % 2
        s_scr[turn, :TILE, :] = jnp.where(beyond, s_scr[turn, :TILE, :], FAR)
        rows = s_scr.at[turn, :early, :]
        top_own = stats[tile : tile + 1, :]
        top = jnp.maximum(fold_rows(rows, jnp.maximum) * exp2_scale, top_own)
        total = weigh(rows, top, e_scr.at[tile % 3, :early, :])
        scale = jnp.exp2(top_own - top)
        inv = 1.0 / (total + stats[tiles + tile : tiles + tile + 1, :] * scale)
        own_scale[tile : tile + 1, :] = inv * scale
        scales[tile] = scale, inv

    def outputs(tile):
        base, turn = tile * TILE, tile % 2
        early = WINDOW - base
        scale, inv = scales.pop(tile)
        out = dot(vt[:, base:], e_scr[tile % 3, :early, :])
        out = out + out_own[:, tile * wide : (tile + 1) * wide] * scale
        out = (out * inv).T.astype(BF16)
        unstacked(outs, base, group, out)
        g_scr[turn], g_wide = gradient_rows(qg, base, group, inv, out)
        dp_scr[turn, :early, :] = dot_t(va[base:, :], g_wide)

    def gradients(tile):
        base, turn = tile * TILE, tile % 2
        early = WINDOW - base
        e = e_scr[tile % 3, :early, :]
        old = early if tile else 0
        add_rows(dv, base, old, dot(e, g_scr[turn]))
        ds = ds_early.at[early_rows(tile), :]
        score_gradients(ds, e, dp_scr.at[turn, :early, :])
        add_rows(dk, base, old, dot(ds[...], stacked(qg, base, group)))

    pipeline(tiles, scores, weights, outputs, gradients)

    for lag in range(1, reach + 1):
        there = slice((reach - lag) * tok, (reach - lag + 1) * tok)
        sent[lag - 1][:, :HEAD_DIM] = (dk[there, :] * logit_scale).astype(BF16)
        sent[lag - 1][:, HEAD_DIM:] = dv[there, :].astype(BF16)
    take_rows(size, core, masks, lambda there: outs[there, :], out_pieces)


def backward_body(size, core, masks, tok, group, *refs):
    take = taker(refs)
    qg, kv, e_own, outs, own_scale, ds_early, kt_early = take(7)
    dq_pieces, (dkv,) = take(len(masks)), take(1)
    dqs, va, kt, dk, dv, dp_scr, ds_scr, g_scr = take(8)
    wide = group * TILE
    kt[...] = kv[:, :HEAD_DIM].T
    set_values(va, kv[:, HEAD_DIM:])

    def products(tile):
        base, turn = tile * TILE, tile % 2
        scale = own_scale[tile : tile + 1, :]
        out = stacked(outs, base, group)
        g_scr[turn], g_wide = gradient_rows(qg, base, group, scale, out)
        dp_scr[turn, : base + TILE, :] = dot_t(va[: base + TILE, :], g_wide)

    def gradients(tile):
        base, turn = tile * TILE, tile % 2
        count = base + TILE
        e = e_own[own_rows(tile), :]
        add_rows(dv, 0, base, dot(e, g_scr[turn]))
        score_gradients(ds_scr.at[turn, :count, :], e, dp_scr.at[turn, :count, :])
        ds = ds_scr[turn, :count, :]
        add_rows(dk, 0, base, dot(ds, stacked(qg, base, group)))
        dq = dot(kt_early[:, base:], ds_early[early_rows(tile), :]) + dot(kt[:, :count], ds)
        dq = dq * logit_scale
        unstacked(dqs, base, group, dq.T.astype(BF16))

    pipeline(tok // TILE, products, gradients)
    dkv[:, :HEAD_DIM] = dk[...] * logit_scale
    dkv[:, HEAD_DIM:] = dv[...]
    take_rows(size, core, masks, lambda there: dqs[there, :], dq_pieces)


def attend_call(kernel, out_shape, scratch_shapes, flops, name, *args):
    return pl.pallas_call(
        kernel,
        out_shape=out_shape,
        in_specs=[VMEM] * len(args),
        out_specs=[VMEM] * len(out_shape),
        scratch_shapes=scratch_shapes,
        compiler_params=pltpu.CompilerParams(vmem_limit_bytes=24 * 1024 * 1024),
        cost_estimate=pl.CostEstimate(
            flops=flops, bytes_accessed=8 * 1024 * 1024, transcendentals=0
        ),
        name=name,
    )(*args)


def forward_own(documents, qg, kv, size):
    rows, cols = qg[0].shape
    tok = len(qg) * rows
    group = cols // (2 * HEAD_DIM)
    wide, tiles = group * TILE, tok // TILE
    return attend_call(
        functools.partial(own_body, size, core_mask(), chip_masks(size), tok, group),
        [
            jax.ShapeDtypeStruct((own_rows(tiles - 1).stop, wide), BF16),
            jax.ShapeDtypeStruct((HEAD_DIM, tiles * wide), F32),
            jax.ShapeDtypeStruct((2 * tiles, wide), F32),
            jax.ShapeDtypeStruct((tok, cols), BF16),
        ],
        [
            pltpu.VMEM((tok, 2 * HEAD_DIM), BF16),
            pltpu.VMEM((HEAD_DIM, tok), BF16),
            pltpu.VMEM((2, tok, wide), F32),
        ],
        16 * tok * group * (WINDOW + TILE) * HEAD_DIM,
        "forward_own",
        *documents,
        *qg,
        kv,
    )


def forward(documents, qg, lags, carried, size):
    (tok, cols), count, reach = qg.shape, len(chip_masks(size)), len(lags)
    rows = tok // count
    group = cols // (2 * HEAD_DIM)
    wide, tiles = group * TILE, tok // TILE
    half = jax.ShapeDtypeStruct((tok, 2 * HEAD_DIM), BF16)
    out_shape = [jax.ShapeDtypeStruct((rows, cols // 2), BF16)] * count + [half] * reach
    out_shape += [
        jax.ShapeDtypeStruct((tok, cols // 2), BF16),
        jax.ShapeDtypeStruct((tiles, wide), F32),
        jax.ShapeDtypeStruct((early_rows(tiles - 1).stop, wide), BF16),
        jax.ShapeDtypeStruct((HEAD_DIM, WINDOW), BF16),
    ]
    scratch = [
        pltpu.VMEM((WINDOW, 2 * HEAD_DIM), BF16),
        pltpu.VMEM((WINDOW, 2 * HEAD_DIM), BF16),
        pltpu.VMEM((HEAD_DIM, WINDOW), BF16),
        pltpu.VMEM((WINDOW, HEAD_DIM), F32),
        pltpu.VMEM((WINDOW, HEAD_DIM), F32),
        pltpu.VMEM((2, WINDOW, wide), F32),
        pltpu.VMEM((3, WINDOW, wide), BF16),
        pltpu.VMEM((2, WINDOW, wide), F32),
        pltpu.VMEM((2, wide, HEAD_DIM), BF16),
    ]
    results = attend_call(
        functools.partial(
            forward_body, size, core_mask(), chip_masks(size), reach, tok, group
        ),
        out_shape,
        scratch,
        6 * tok * group * (WINDOW + TILE) * HEAD_DIM,
        "forward",
        *documents,
        qg,
        *lags,
        *carried,
    )
    return results[:count], results[count : count + reach], results[count + reach :]


def backward(qg, kv, carried, size):
    (tok, cols), count = qg.shape, len(chip_masks(size))
    rows = tok // count
    group = cols // (2 * HEAD_DIM)
    wide = group * TILE
    results = attend_call(
        functools.partial(backward_body, size, core_mask(), chip_masks(size), tok, group),
        [jax.ShapeDtypeStruct((rows, cols // 2), BF16)] * count
        + [jax.ShapeDtypeStruct((tok, 2 * HEAD_DIM), F32)],
        [
            pltpu.VMEM((tok, cols // 2), BF16),
            pltpu.VMEM((tok, 2 * HEAD_DIM), BF16),
            pltpu.VMEM((HEAD_DIM, tok), BF16),
            pltpu.VMEM((tok, HEAD_DIM), F32),
            pltpu.VMEM((tok, HEAD_DIM), F32),
            pltpu.VMEM((2, tok, wide), F32),
            pltpu.VMEM((2, tok, wide), BF16),
            pltpu.VMEM((2, wide, HEAD_DIM), BF16),
        ],
        4 * tok * group * (WINDOW + TILE) * HEAD_DIM,
        "backward",
        qg,
        kv,
        *carried,
    )
    return results[:count], results[count]


def document_columns(segment_ids, tok, size):
    start = (flat_index() // size) * tok
    padded = jnp.concatenate([jnp.full((WINDOW,), -1, jnp.int32), segment_ids])
    keys = lax.dynamic_slice_in_dim(padded, start, WINDOW + tok, 0)
    queries = lax.dynamic_slice_in_dim(segment_ids, start, tok, 0)
    number = jnp.arange(HEAD_DIM, dtype=jnp.int32)[None, :]
    return (
        jnp.where(keys[:, None] == number, 0.0, FAR).astype(BF16),
        jnp.where(queries[:, None] == number, 1.0, 0.0).astype(BF16),
    )


def body(query, key, value, grad_out, segment_ids):
    size = key.shape[1] // HEAD_DIM
    rows = query.shape[0]
    tok = size * rows
    reach = WINDOW // tok
    assert reach * tok == WINDOW and device_count() % size == 0

    got = [swap(array, core_mask()) for array in (key, value, query, grad_out)]
    key, value = after(key, value)
    pieces = list(gather_cores((key, value), got[:2], size))
    pieces[0], query, grad_out, segment_ids = after(pieces[0], query, grad_out, segment_ids)
    documents = document_columns(segment_ids, tok, size)
    kv = join(swap_chips(pieces, size), size)
    lags = [shifted(kv, lag * size) for lag in range(1, reach + 1)]
    qg = swap_chips(gather_cores((query, grad_out), got[2:], size), size)

    e_own, *partial, qg = forward_own(documents, qg, kv, size)
    out, sent, carried = forward(documents, qg, lags, partial, size)
    backs = [shifted(sent[lag - 1], -lag * size) for lag in range(1, reach + 1)]
    out = swap_chips(out, size)
    grad_q, dkv = backward(qg, kv, [e_own, *carried], size)
    both = after(*out[:-1], *grad_q)
    out, grad_q = [*both[: len(out) - 1], out[-1]], both[len(out) - 1 :]
    grad_q = swap_chips(grad_q, size)
    grads = swap_chips(combine([dkv, *backs], size), size)
    return tuple(spread_cores([out, grad_q, grads], (1, 1, 2), size))


def solution(mesh):
    placed = P(("pipe", "tensor"), None)
    return jax.shard_map(
        body,
        mesh=mesh,
        in_specs=(placed, placed, placed, placed, P()),
        out_specs=(placed, placed, placed, placed),
        check_vma=False,
    )
```
